32 devices in a mesh: ctx: 8 (over z, y), pipe: 4 (over x, core).
Axes of the slice: x: 2, y: 2, z: 4, core: 2. Of those that a mesh axis runs over, the one named last changes fastest.
Arguments:
- queries: bfloat16 [4, 4096, 2048], P('pipe', 'ctx'), may hold values from -400 to 400
- keys: bfloat16 [4, 4096, 2048], P('pipe', 'ctx'), may hold values from -12 to 12
- values: bfloat16 [4, 4096, 2048], P('pipe', 'ctx'), may hold values from -15 to 15
- picks: int32 [4, 8, 16, 2], P('pipe'), may hold values from -1 to 6, as said below
Outputs:
- passed: bfloat16 [4, 4096, 2048], P('pipe', 'ctx')
The draws below stay inside these ranges and needn't reach their ends.
Inputs may be any that keep to these rules, and one draw needn't show every extreme that they name: Each entry is -1 (no block) or a block earlier than its query block; a head's 2 entries differ unless -1; within one section and query block no block is named more than 4 times over all heads and picks, and this bound is reached; query block 0 names nothing and every later query block names its preceding block at least once.
All inputs are finite; a program needn't handle non-finite values.
Results may differ from the reference program's by a relative error of at most 0.0048.
Values may be sent and summed in bfloat16 or wider, within the bound.
No kernel may reach another device: no remote copies, remote signals or barrier semaphores. Data moves between devices by JAX's collectives and lax.ppermute only.
A program may use at most 128 MiB of HBM per device.

```python
import jax
import jax.numpy as jnp
from jax import lax

HEADS = 16
HD = 128
D = 2048
BLOCK = 512
PICKS = 2
NB = 8
TOKENS = 4096
CAP = 4
N_PIPE = 4


def shared_draw(key):
    base_key = jax.random.fold_in(key, 1013)
    key_first, key_second = jax.random.split(base_key, 2)
    full_shape = (N_PIPE, TOKENS, D)
    key_part = jax.random.truncated_normal(key_first, -4.0, 4.0, full_shape, jnp.float32)
    query_part = 2.0 * jax.random.truncated_normal(key_second, -4.0, 4.0, full_shape, jnp.float32)
    return (query_part, key_part)


def draw_queries(key, part):
    return shared_draw(key)[0].astype(jnp.bfloat16)


def draw_keys(key, part):
    return shared_draw(key)[1].astype(jnp.bfloat16)


def pick_block(layer_key, block_index):
    block_key = jax.random.fold_in(layer_key, block_index)
    key_order, key_heads = jax.random.split(block_key)
    owner_ids = lax.iota(jnp.int32, NB)
    noise = jax.random.randint(key_order, (NB,), 0, 1 << 20) * NB + owner_ids
    noise = jnp.where(owner_ids == block_index - 1, -1, noise)
    noise = jnp.where(owner_ids < block_index, noise, 1 << 30)
    ranked = jnp.argsort(noise).astype(jnp.int32)
    pick_ids = lax.iota(jnp.int32, HEADS * PICKS)
    is_live = (pick_ids < block_index * CAP) & ((block_index >= 2) | (pick_ids % PICKS == 0))
    chosen = ranked[pick_ids % jnp.maximum(block_index, 1)]
    chosen = jnp.where(is_live, chosen, -1).reshape(HEADS, PICKS)
    shuffle = jax.random.permutation(key_heads, HEADS)
    return chosen[shuffle]


def draw_picks(key, part):
    base_key = jax.random.fold_in(key, 2027)

    def one_layer(layer_index):
        layer_key = jax.random.fold_in(base_key, layer_index)
        return jax.vmap(lambda block_index: pick_block(layer_key, block_index))(lax.iota(jnp.int32, NB))
    return jax.vmap(one_layer)(lax.iota(jnp.int32, N_PIPE))


def block_scale(rng, shape, cuts, least, largest):
    def one(dim, parts):
        steps = jax.random.uniform(jax.random.fold_in(jax.random.fold_in(rng, 6), dim), (parts,), jnp.float32, least / len(cuts), largest / len(cuts))
        return jnp.repeat(jnp.exp(steps), shape[dim] // parts).reshape((-1,) + (1,) * (len(shape) - dim - 1))

    loudness = one(*cuts[0])
    for cut in cuts[1:]:
        loudness = loudness * one(*cut)
    return loudness


def scatter_about(stream_key, extent, scale, reach, cuts=(), kind=jnp.bfloat16):
    values = scale * jax.random.normal(stream_key, extent, jnp.float32)
    if cuts:
        values = values * block_scale(stream_key, extent, cuts, -0.22, 0.18)
    return jnp.clip(values, -reach, reach).astype(kind)


def setup_inputs(seed: int = 0) -> dict:
    key_list = jax.random.split(jax.random.key(seed), 5)
    return {
        "queries": draw_queries(jax.random.fold_in(key_list[4], 71), 0),
        "keys": draw_keys(jax.random.fold_in(key_list[4], 71), 0),
        "values": scatter_about(key_list[2], (N_PIPE, TOKENS, D), 3.0, 15.0, ((0, 4), (1, 8))),
        "picks": draw_picks(jax.random.fold_in(key_list[4], 71), 0),
    }


def attend_block(query_rows, key_blocks, value_blocks, chosen, block_index):
    score_scale = HD ** -0.5
    head_index = jnp.arange(HEADS, dtype=jnp.int32)[:, None]
    safe_blocks = jnp.maximum(chosen, 0)
    remote_keys = key_blocks[safe_blocks, :, head_index, :]
    remote_values = value_blocks[safe_blocks, :, head_index, :]
    own_keys = key_blocks[block_index].transpose(1, 0, 2)
    own_values = value_blocks[block_index].transpose(1, 0, 2)
    all_keys = jnp.concatenate([own_keys, remote_keys.reshape(HEADS, PICKS * BLOCK, HD)], axis=1).astype(jnp.float32)
    all_values = jnp.concatenate([own_values, remote_values.reshape(HEADS, PICKS * BLOCK, HD)], axis=1).astype(jnp.float32)
    query_heads = query_rows.reshape(BLOCK, HEADS, HD).transpose(1, 0, 2).astype(jnp.float32)
    scores = jnp.einsum("hqd,hkd->hqk", query_heads, all_keys, precision=lax.Precision.HIGHEST) * score_scale
    positions = jnp.arange(BLOCK, dtype=jnp.int32)
    causal = positions[:, None] >= positions[None, :]
    remote_mask = jnp.repeat(chosen >= 0, BLOCK, axis=1)
    allowed = jnp.concatenate([jnp.broadcast_to(causal[None], (HEADS, BLOCK, BLOCK)), jnp.broadcast_to(remote_mask[:, None, :], (HEADS, BLOCK, PICKS * BLOCK))], axis=2)
    scores = jnp.where(allowed, scores, -jnp.inf)
    row_top = jnp.max(scores, axis=2, keepdims=True)
    weights = jnp.exp(scores - row_top)
    prob_rows = (weights / jnp.sum(weights, axis=2, keepdims=True)).astype(jnp.bfloat16)
    prob_rows = lax.optimization_barrier(prob_rows).astype(jnp.float32)
    mixed_rows = jnp.einsum("hqk,hkd->hqd", prob_rows, all_values, precision=lax.Precision.HIGHEST)
    return mixed_rows.astype(jnp.bfloat16).transpose(1, 0, 2).reshape(BLOCK, HEADS * HD)


def reference(queries, keys, values, picks):
    sections = []
    for layer_index in range(N_PIPE):
        key_blocks = keys[layer_index].reshape(NB, BLOCK, HEADS, HD)
        value_blocks = values[layer_index].reshape(NB, BLOCK, HEADS, HD)
        query_blocks = queries[layer_index].reshape(NB, BLOCK, HEADS * HD)

        def one_block(block_items, key_blocks=key_blocks, value_blocks=value_blocks):
            query_rows, chosen, block_index = block_items
            return attend_block(query_rows, key_blocks, value_blocks, chosen, block_index)

        attended = lax.map(one_block, (query_blocks, picks[layer_index], jnp.arange(NB, dtype=jnp.int32)))
        sections.append(attended.reshape(TOKENS, HEADS * HD))
    stacked = jnp.stack(sections)
    return jnp.roll(stacked, 1, axis=0)
```

```python
import functools
import math

import jax
import jax.numpy as jnp
from jax import lax
from jax.experimental import pallas as pl
from jax.experimental.pallas import tpu as pltpu
from jax.sharding import PartitionSpec as P

HEADS = 16
HD = 128
PICKS = 2
EXP2_SCALE = HD ** -0.5 * math.log2(math.e)
LANES = 128
STAT_ROWS = 16
VMEM_BYTES = 48 * 1024 * 1024


def passed_along(value, axis, steps):
    count = lax.axis_size(axis)
    pairs = [(source, (source + steps) % count) for source in range(count)]
    return lax.ppermute(value, axis, pairs)


def request_table(chosen, owners, slot_count):
    pick_count = chosen.shape[1]
    pick_ids = lax.iota(jnp.int32, pick_count)
    is_live = chosen >= 0
    earlier = pick_ids[None, :] < pick_ids[:, None]
    same_owner = (chosen[:, :, None] == chosen[:, None, :]) & earlier[None]
    pick_order = jnp.sum(same_owner.astype(jnp.int32), axis=2)
    head_ids = pick_ids // PICKS
    slot_ranks = lax.iota(jnp.int32, slot_count)
    matches = (
        is_live[:, None, None, :]
        & (chosen[:, None, None, :] == owners[None, :, None, None])
        & (pick_order[:, None, None, :] == slot_ranks[None, None, :, None])
    )
    was_found = jnp.any(matches, axis=3)
    head_table = jnp.sum(jnp.where(matches, head_ids[None, None, None, :], 0), axis=3)
    return (jnp.where(was_found, head_table, -1), pick_order)


def pack_kernel(plan_ref, *refs, copies, source_count):
    sources = refs[:source_count]
    outputs = refs[source_count:-1]
    sems = refs[-1]
    started = []
    for number, (source, plan_at, target, place) in enumerate(copies):
        head = jnp.maximum(plan_ref[plan_at], 0)
        columns = pl.ds(pl.multiple_of(head * HD, HD), HD)
        copy = pltpu.make_async_copy(
            sources[source].at[:, columns], outputs[target].at[place], sems.at[number]
        )
        copy.start()
        started.append(copy)
    for copy in started:
        copy.wait()


def pack(plan, sources, copies, places):
    rows = sources[0].shape[0]
    return pl.pallas_call(
        functools.partial(pack_kernel, copies=copies, source_count=len(sources)),
        grid_spec=pltpu.PrefetchScalarGridSpec(
            num_scalar_prefetch=1,
            grid=(1,),
            in_specs=[pl.BlockSpec(memory_space=pl.ANY)] * len(sources),
            out_specs=[pl.BlockSpec(memory_space=pl.ANY)] * len(places),
            scratch_shapes=[pltpu.SemaphoreType.DMA((len(copies),))],
        ),
        out_shape=[jax.ShapeDtypeStruct((count, rows, HD), jnp.bfloat16) for count in places],
        compiler_params=pltpu.CompilerParams(vmem_limit_bytes=VMEM_BYTES),
        cost_estimate=pl.CostEstimate(
            flops=0, bytes_accessed=4 * rows * HD * len(copies), transcendentals=0
        ),
    )(plan, *sources)


def diagonal():
    shape = (LANES, LANES)
    return lax.broadcasted_iota(jnp.int32, shape, 0) == lax.broadcasted_iota(jnp.int32, shape, 1)


def raw_scores(query_rows, key_rows):
    return lax.dot_general(
        query_rows, key_rows, (((1,), (1,)), ((), ())), preferred_element_type=jnp.float32
    )


def with_ones(value_rows):
    return jnp.concatenate([value_rows, jnp.ones_like(value_rows)], axis=1)


def soft_part(score_parts, value_parts):
    top = functools.reduce(
        jnp.maximum, [jnp.max(scores, axis=1, keepdims=True) for scores in score_parts]
    )
    total = None
    for scores, value_rows in zip(score_parts, value_parts):
        weights = jnp.exp2((scores - top) * EXP2_SCALE).astype(jnp.bfloat16)
        part = jnp.dot(weights, value_rows, preferred_element_type=jnp.float32)
        total = part if total is None else total + part
    sums = total[:, HD:]
    return total[:, :HD] / sums, top * EXP2_SCALE + jnp.log2(sums)


def across_lanes(column):
    eye = diagonal()
    return [
        jnp.sum(jnp.where(eye, column[at : at + LANES], 0.0), axis=0, keepdims=True)
        for at in range(0, column.shape[0], LANES)
    ]


def three_parts(stat_rows):
    stats = jnp.concatenate(stat_rows, axis=0)
    first = stats.astype(jnp.bfloat16).astype(jnp.float32)
    second = (stats - first).astype(jnp.bfloat16).astype(jnp.float32)
    third = stats - first - second
    parts = jnp.concatenate([first, second, third], axis=0)
    pad = jnp.zeros((STAT_ROWS - parts.shape[0], LANES), jnp.float32)
    return jnp.concatenate([parts, pad], axis=0).astype(jnp.bfloat16)


def attend_kernel(plan_ref, query_ref, key_ref, value_ref, out_ref, *, plan_at, tile):
    head = plan_ref[plan_at + pl.program_id(0)]
    rows = query_ref.shape[1]

    @pl.when(head >= 0)
    def _():
        key_rows = key_ref[...]
        value_rows = with_ones(value_ref[...])
        stat_rows = []
        for at in range(0, rows, tile):
            scores = raw_scores(query_ref[0, at : at + tile, :], key_rows)
            outputs, sums = soft_part([scores], [value_rows])
            out_ref[0, at : at + tile, :] = outputs.astype(jnp.bfloat16)
            stat_rows += across_lanes(sums)
        out_ref[0, rows:, :] = three_parts(stat_rows)


def attend(plan, plan_at, queries, keys, values):
    slots, rows, _ = queries.shape
    head_column = lambda slot, plan_ref: (0, jnp.maximum(plan_ref[plan_at + slot], 0))
    return pl.pallas_call(
        functools.partial(attend_kernel, plan_at=plan_at, tile=min(rows, 256)),
        grid_spec=pltpu.PrefetchScalarGridSpec(
            num_scalar_prefetch=1,
            grid=(slots,),
            in_specs=[
                pl.BlockSpec((1, rows, HD), lambda slot, plan_ref: (slot, 0, 0)),
                pl.BlockSpec((rows, HD), head_column),
                pl.BlockSpec((rows, HD), head_column),
            ],
            out_specs=pl.BlockSpec((1, rows + STAT_ROWS, HD), lambda slot, plan_ref: (slot, 0, 0)),
        ),
        out_shape=jax.ShapeDtypeStruct((slots, rows + STAT_ROWS, HD), jnp.bfloat16),
        compiler_params=pltpu.CompilerParams(vmem_limit_bytes=VMEM_BYTES),
        cost_estimate=pl.CostEstimate(
            flops=4 * slots * rows * rows * HD,
            bytes_accessed=8 * slots * rows * HD,
            transcendentals=slots * rows * rows,
        ),
    )(plan, queries, keys, values)


def own_kernel(plan_ref, query_ref, key_ref, value_ref, near_ref, out_ref, *, plan_at, tile):
    slot = plan_ref[plan_at + pl.program_id(0)]
    rows = query_ref.shape[0]

    def run(use_near):
        value_rows = with_ones(value_ref[...])
        if use_near:
            near_keys = near_ref[0]
            near_values = with_ones(near_ref[1])
        stat_rows = []
        for at in range(0, rows, tile):
            reach = at + tile
            query_rows = query_ref[at:reach, :]
            scores = raw_scores(query_rows, key_ref[:reach, :])
            shape = scores.shape
            causal = lax.broadcasted_iota(jnp.int32, shape, 0) + at >= lax.broadcasted_iota(
                jnp.int32, shape, 1
            )
            score_parts = [jnp.where(causal, scores, -jnp.inf)]
            value_parts = [value_rows[:reach]]
            if use_near:
                score_parts.append(raw_scores(query_rows, near_keys))
                value_parts.append(near_values)
            outputs, sums = soft_part(score_parts, value_parts)
            out_ref[0, at:reach, :] = outputs.astype(jnp.bfloat16)
            stat_rows += across_lanes(sums)
        out_ref[0, rows:, :] = three_parts(stat_rows)

    @pl.when(slot >= 0)
    def _():
        run(True)

    @pl.when(slot < 0)
    def _():
        run(False)


def own_part(plan, plan_at, queries, keys, values, near):
    rows = queries.shape[0]
    column = lambda head, plan_ref: (0, head)
    return pl.pallas_call(
        functools.partial(own_kernel, plan_at=plan_at, tile=min(rows, 256)),
        grid_spec=pltpu.PrefetchScalarGridSpec(
            num_scalar_prefetch=1,
            grid=(HEADS,),
            in_specs=[
                pl.BlockSpec((rows, HD), column),
                pl.BlockSpec((rows, HD), column),
                pl.BlockSpec((rows, HD), column),
                pl.BlockSpec(
                    (2, rows, HD),
                    lambda head, plan_ref: (jnp.maximum(plan_ref[plan_at + head], 0), 0, 0),
                ),
            ],
            out_specs=pl.BlockSpec((1, rows + STAT_ROWS, HD), lambda head, plan_ref: (head, 0, 0)),
        ),
        out_shape=jax.ShapeDtypeStruct((HEADS, rows + STAT_ROWS, HD), jnp.bfloat16),
        compiler_params=pltpu.CompilerParams(vmem_limit_bytes=VMEM_BYTES),
        cost_estimate=pl.CostEstimate(
            flops=4 * HEADS * rows * rows * HD,
            bytes_accessed=8 * HEADS * rows * HD,
            transcendentals=HEADS * rows * rows,
        ),
    )(plan, queries, keys, values, near)


def merge_kernel(plan_ref, own_ref, *refs, places):
    parts, out_ref, held, sems = refs[: len(places)], refs[-3], refs[-2], refs[-1]
    rows = out_ref.shape[0]
    groups = rows // LANES
    copies = [
        pltpu.make_async_copy(part, held.at[pl.ds(place, part.shape[0])], sems.at[number])
        for number, (part, place) in enumerate(zip(parts, places))
    ]
    for copy in copies:
        copy.start()
    for copy in copies:
        copy.wait()

    def stats_of(block):
        stats = block.astype(jnp.float32)
        return stats[:groups] + stats[groups : 2 * groups] + stats[2 * groups : 3 * groups]

    def one_head(head, carry):
        found = [plan_ref[head * PICKS + pick] for pick in range(PICKS)]
        spots = [jnp.maximum(spot, 0) for spot in found]
        sums = [stats_of(own_ref[head, rows:, :])]
        for spot, safe in zip(found, spots):
            sums.append(jnp.where(spot >= 0, stats_of(held[safe, rows:, :]), -jnp.inf))
        top = functools.reduce(jnp.maximum, sums)
        shares = [jnp.exp2(part - top) for part in sums]
        whole = functools.reduce(jnp.add, shares)
        shares = [share / whole for share in shares]
        eye = diagonal()
        columns = pl.ds(pl.multiple_of(head * HD, HD), HD)
        for group in range(groups):
            lines = pl.ds(group * LANES, LANES)
            blocks = [own_ref[head, lines, :].astype(jnp.float32)]
            for spot, safe in zip(found, spots):
                block = held[safe, lines, :].astype(jnp.float32)
                blocks.append(jnp.where(spot >= 0, block, 0.0))
            mixed = None
            for block, share in zip(blocks, shares):
                spread = jnp.broadcast_to(share[group : group + 1, :], (LANES, LANES))
                column = jnp.sum(jnp.where(eye, spread, 0.0), axis=1, keepdims=True)
                term = block * column
                mixed = term if mixed is None else mixed + term
            out_ref[lines, columns] = mixed.astype(jnp.bfloat16)
        return carry

    lax.fori_loop(0, HEADS, one_head, 0)


def merge(plan, own, parts, places, slot_total):
    rows = own.shape[1] - STAT_ROWS
    whole = lambda step, plan_ref: (0, 0, 0)
    return pl.pallas_call(
        functools.partial(merge_kernel, places=places),
        grid_spec=pltpu.PrefetchScalarGridSpec(
            num_scalar_prefetch=1,
            grid=(1,),
            in_specs=[pl.BlockSpec(own.shape, whole)]
            + [pl.BlockSpec(memory_space=pl.ANY)] * len(parts),
            out_specs=pl.BlockSpec((rows, HEADS * HD), lambda step, plan_ref: (0, 0)),
            scratch_shapes=[
                pltpu.VMEM((slot_total, rows + STAT_ROWS, HD), jnp.bfloat16),
                pltpu.SemaphoreType.DMA((len(parts),)),
            ],
        ),
        out_shape=jax.ShapeDtypeStruct((rows, HEADS * HD), jnp.bfloat16),
        compiler_params=pltpu.CompilerParams(vmem_limit_bytes=VMEM_BYTES),
        cost_estimate=pl.CostEstimate(
            flops=6 * HEADS * rows * HD,
            bytes_accessed=2 * (HEADS * 2 + slot_total) * rows * HD,
            transcendentals=0,
        ),
    )(plan, own, *parts)


def travelling_queries(queries, keys, values, picks):
    width = lax.axis_size("ctx")
    sections = lax.axis_size("pipe")
    here = lax.axis_index("ctx")
    slots = max(1, PICKS * HEADS // width)
    queries, keys, values = queries[0], keys[0], values[0]

    shifts = lax.iota(jnp.int32, width)
    every_pick = picks[0].reshape(width, HEADS * PICKS)
    table, every_order = request_table(every_pick, shifts, slots)
    asking = here - shifts
    ask = lax.dynamic_index_in_dim(table, here, 0, keepdims=False)[jnp.maximum(asking, 0)]
    ask = jnp.where((asking >= 0)[:, None], ask, -1)
    asked_by = here + shifts
    asked = lax.dynamic_index_in_dim(table, here, 1, keepdims=False)
    asked = asked[jnp.minimum(asked_by, width - 1)]
    asked = jnp.where((asked_by < width)[:, None], asked, -1)
    chosen = lax.dynamic_index_in_dim(every_pick, here, 0, keepdims=False)
    order = lax.dynamic_index_in_dim(every_order, here, 0, keepdims=False)
    is_near = (chosen >= 0) & (chosen == here - 1)
    near_slot = jnp.max(jnp.where(is_near, order, -1).reshape(HEADS, PICKS), axis=1)
    plan = jnp.concatenate([ask.reshape(-1), asked.reshape(-1), near_slot])
    asked_at = width * slots
    near_at = 2 * width * slots

    before = passed_along(picks, "pipe", 1)[0].reshape(width, HEADS * PICKS)
    before = lax.dynamic_index_in_dim(before, here, 0, keepdims=True)
    before_order = request_table(before, shifts, slots)[1][0]
    distance = here - before[0]
    merge_plan = jnp.where(
        (before[0] >= 0) & (distance >= 2), (distance - 2) * slots + before_order, -1
    )

    pieces = [(shift, 0, slots) for shift in piece_order(width)]
    copies = []
    for number, (shift, first, count) in enumerate(pieces):
        copies += [(0, shift * slots + first + slot, number, slot) for slot in range(count)]
    near_copies = []
    for slot in range(slots):
        near_copies += [
            (0, asked_at + slots + slot, 0, 2 * slot),
            (1, asked_at + slots + slot, 0, 2 * slot + 1),
        ]
    near_send = pack(plan, [keys, values], near_copies, [2 * slots])[0]
    near = lax.ppermute(near_send, "ctx", [(at, at + 1) for at in range(width - 1)])
    sends = pack(plan, [queries], copies, [count for _, _, count in pieces])

    own = own_part(plan, near_at, queries, keys, values, near)
    own = passed_along(own, "pipe", 1)

    arrived, returned = [], []
    for number, (shift, first, count) in enumerate(pieces):
        send = sends[number]
        if number >= 2:
            send, arrived[number - 2] = lax.optimization_barrier((send, arrived[number - 2]))
        pairs = [(at, at - shift) for at in range(shift, width)]
        arrived.append(lax.ppermute(send, "ctx", pairs))
    for number, (shift, first, count) in enumerate(pieces):
        part = attend(plan, asked_at + shift * slots + first, arrived[number], keys, values)
        pairs = [
            (at * sections + section, (at + shift) * sections + (section + 1) % sections)
            for at in range(width - shift)
            for section in range(sections)
        ]
        returned.append(lax.ppermute(part, ("ctx", "pipe"), pairs))
    places = [(shift - 2) * slots + first for shift, first, _ in pieces]
    return merge(merge_plan, own, returned, places, (width - 2) * slots)[None]


def piece_order(width):
    middle = sorted(range(2, width - 1), key=lambda shift: abs(shift - width // 2))
    return [width - 1] + middle


def travelling_keys(queries, keys, values, picks):
    ctx_width = lax.axis_size("ctx")
    rank_here = lax.axis_index("ctx")
    slot_count = max(1, PICKS * HEADS // ctx_width)
    block_rows = queries.shape[1]
    score_scale = HD ** (-0.5)
    every_pick = picks[0].reshape(ctx_width, HEADS * PICKS)
    chosen = lax.dynamic_slice_in_dim(every_pick, rank_here, 1, 0)
    pick_order = request_table(chosen, lax.iota(jnp.int32, ctx_width), slot_count)[1]
    asked_table = request_table(every_pick, rank_here.reshape(1), slot_count)[0]
    asked_heads = asked_table[:, 0, :]
    safe_asked = jnp.maximum(asked_heads, 0)
    query_heads = queries[0].reshape(block_rows, HEADS, HD).transpose(1, 0, 2)
    key_heads = keys[0].reshape(block_rows, HEADS, HD).transpose(1, 0, 2)
    value_heads = values[0].reshape(block_rows, HEADS, HD).transpose(1, 0, 2)
    is_live = chosen[0] >= 0
    flat_slot = jnp.where(is_live, chosen[0] * slot_count + pick_order[0], 0)
    remote_mask = jnp.repeat(is_live.reshape(HEADS, PICKS), block_rows, axis=1)
    row_index = lax.iota(jnp.int32, block_rows)
    causal = row_index[:, None] >= row_index[None, :]

    def masked_scores(query_head, key_rows, mask_row):
        scores = lax.dot_general(
            query_head, key_rows, (((1,), (1,)), ((), ())), preferred_element_type=jnp.float32
        )
        allowed = jnp.concatenate(
            [causal, jnp.broadcast_to(mask_row[None, :], (block_rows, PICKS * block_rows))], axis=1
        )
        return jnp.where(allowed, scores * score_scale, -jnp.inf)

    def row_stats(scores):
        row_top = jnp.max(scores, axis=1)
        row_total = jnp.sum(jnp.exp(scores - row_top[:, None]), axis=1)
        return (row_top, row_total)

    def weighted(scores, row_top, row_total, value_rows):
        prob_rows = (jnp.exp(scores - row_top[:, None]) / row_total[:, None]).astype(jnp.bfloat16)
        return jnp.dot(prob_rows, value_rows, preferred_element_type=jnp.float32).astype(
            jnp.bfloat16
        )

    send_both = jnp.concatenate([key_heads, value_heads], axis=2)[safe_asked]
    got_slots = lax.all_to_all(send_both, "ctx", split_axis=0, concat_axis=0, tiled=True)
    last_width = 2 * HD
    flat_slots = got_slots.reshape(ctx_width * slot_count, block_rows, last_width)
    remote_both = flat_slots[flat_slot].reshape(HEADS, PICKS * block_rows, last_width)
    all_keys = jnp.concatenate([key_heads, remote_both[:, :, :HD]], axis=1)
    all_values = jnp.concatenate([value_heads, remote_both[:, :, HD:]], axis=1)

    def per_head(head_items):
        query_head, key_rows, value_rows, mask_row = head_items
        scores = masked_scores(query_head, key_rows, mask_row)
        row_top, row_total = row_stats(scores)
        return weighted(scores, row_top, row_total, value_rows)

    outputs = lax.map(per_head, (query_heads, all_keys, all_values, remote_mask))
    merged = outputs.transpose(1, 0, 2).reshape(1, block_rows, HEADS * HD)
    return passed_along(merged, "pipe", 1)


def per_device(queries, keys, values, picks):
    few_shifts = lax.axis_size("ctx") <= 16
    run = travelling_queries if few_shifts else travelling_keys
    return run(queries, keys, values, picks)


def solution(mesh):
    placed = (
        P("pipe", "ctx", None),
        P("pipe", "ctx", None),
        P("pipe", "ctx", None),
        P("pipe", None, None, None),
    )
    return jax.shard_map(
        per_device, mesh=mesh, in_specs=placed, out_specs=P("pipe", "ctx", None), check_vma=False
    )
```

```python
import functools
import math

import jax
import jax.numpy as jnp
from jax import lax
from jax.experimental import pallas as pl
from jax.experimental.pallas import tpu as pltpu
from jax.sharding import PartitionSpec as P

HEADS = 16
HD = 128
PICKS = 2
EXP2_SCALE = HD ** -0.5 * math.log2(math.e)
LANES = 128
STAT_ROWS = 16
VMEM_BYTES = 48 * 1024 * 1024


def passed_along(value, axis, steps):
    count = lax.axis_size(axis)
    pairs = [(source, (source + steps) % count) for source in range(count)]
    return lax.ppermute(value, axis, pairs)


def request_table(chosen, owners, slot_count):
    pick_count = chosen.shape[1]
    pick_ids = lax.iota(jnp.int32, pick_count)
    is_live = chosen >= 0
    earlier = pick_ids[None, :] < pick_ids[:, None]
    same_owner = (chosen[:, :, None] == chosen[:, None, :]) & earlier[None]
    pick_order = jnp.sum(same_owner.astype(jnp.int32), axis=2)
    head_ids = pick_ids // PICKS
    slot_ranks = lax.iota(jnp.int32, slot_count)
    matches = (
        is_live[:, None, None, :]
        & (chosen[:, None, None, :] == owners[None, :, None, None])
        & (pick_order[:, None, None, :] == slot_ranks[None, None, :, None])
    )
    was_found = jnp.any(matches, axis=3)
    head_table = jnp.sum(jnp.where(matches, head_ids[None, None, None, :], 0), axis=3)
    return (jnp.where(was_found, head_table, -1), pick_order)


def call(kernel, name_space, outputs, out_specs, scratch=(), flops=0, moved=0, exps=0):
    return pl.pallas_call(
        kernel,
        in_specs=name_space,
        out_specs=out_specs,
        out_shape=outputs,
        scratch_shapes=list(scratch),
        compiler_params=pltpu.CompilerParams(vmem_limit_bytes=VMEM_BYTES),
        cost_estimate=pl.CostEstimate(flops=20 * flops, bytes_accessed=moved, transcendentals=exps),
    )


SCALARS = pl.BlockSpec(memory_space=pltpu.SMEM)
IN_HBM = pl.BlockSpec(memory_space=pltpu.HBM)
IN_VMEM = pl.BlockSpec(memory_space=pltpu.VMEM)


def list_heads(heads_ref, start, picks_ref, block, owner, slots):
    width = picks_ref.shape[0]
    for slot in range(slots):
        heads_ref[start + slot] = -1
    valid = (block >= 0) & (block < width) & (owner >= 0) & (owner < width)
    row = jnp.clip(block, 0, width - 1)

    def look(number, found):
        pick, head = number // HEADS, number % HEADS
        hit = valid & (picks_ref[row, pick, head] == owner)

        @pl.when(hit)
        def _():
            heads_ref[start + found] = head

        return found + hit.astype(jnp.int32)

    lax.fori_loop(0, PICKS * HEADS, look, jnp.int32(0))


def pack_kernel(here_ref, picks_ref, *refs, jobs, slots):
    sources, outputs = refs[:3], refs[3 : 3 + len(jobs)]
    heads_ref, sems = refs[-2], refs[-1]
    here = here_ref[0]
    listed = {}
    for shift, first, count, is_near in jobs:
        key = (shift, is_near)
        if key not in listed:
            listed[key] = len(listed) * slots
            block, owner = (here + shift, here) if is_near else (here, here - shift)
            list_heads(heads_ref, listed[key], picks_ref, block, owner, slots)
    copies = []
    for (shift, first, count, is_near), output in zip(jobs, outputs):
        for slot in range(count):
            head = jnp.maximum(heads_ref[listed[shift, is_near] + first + slot], 0)
            columns = pl.ds(pl.multiple_of(head * HD, HD), HD)
            for place, source in enumerate(sources[1:] if is_near else sources[:1]):
                target = output.at[2 * slot + place if is_near else slot]
                copy = pltpu.make_async_copy(
                    source.at[:, columns], target, sems.at[len(copies)]
                )
                copy.start()
                copies.append(copy)
    for copy in copies:
        copy.wait()


def pack(here, picks, queries, keys, values, jobs, slots):
    rows = queries.shape[0]
    sizes = [2 * count if is_near else count for _, _, count, is_near in jobs]
    return call(
        functools.partial(pack_kernel, jobs=jobs, slots=slots),
        [SCALARS, SCALARS, IN_HBM, IN_HBM, IN_HBM],
        [jax.ShapeDtypeStruct((size, rows, HD), jnp.bfloat16) for size in sizes],
        [IN_HBM] * len(sizes),
        [pltpu.SMEM((len(jobs) * slots,), jnp.int32), pltpu.SemaphoreType.DMA((sum(sizes),))],
        moved=4 * rows * HD * sum(sizes),
    )(here, picks, queries, keys, values)


def diagonal():
    shape = (LANES, LANES)
    return lax.broadcasted_iota(jnp.int32, shape, 0) == lax.broadcasted_iota(jnp.int32, shape, 1)


def raw_scores(query_rows, key_rows):
    return lax.dot_general(
        query_rows, key_rows, (((1,), (1,)), ((), ())), preferred_element_type=jnp.float32
    )


def with_ones(value_rows):
    return jnp.concatenate([value_rows, jnp.ones_like(value_rows)], axis=1)


def soft_part(scores, value_rows):
    top = jnp.max(scores, axis=1, keepdims=True)
    weights = jnp.exp2((scores - top) * EXP2_SCALE).astype(jnp.bfloat16)
    total = jnp.dot(weights, value_rows, preferred_element_type=jnp.float32)
    sums = total[:, HD:]
    return total[:, :HD] / sums, top * EXP2_SCALE + jnp.log2(sums)


def across_lanes(column):
    eye = diagonal()
    return [
        jnp.sum(jnp.where(eye, column[at : at + LANES], 0.0), axis=0, keepdims=True)
        for at in range(0, column.shape[0], LANES)
    ]


def down_rows(line):
    spread = jnp.broadcast_to(line, (LANES, LANES))
    return jnp.sum(jnp.where(diagonal(), spread, 0.0), axis=1, keepdims=True)


def three_parts(stats):
    first = stats.astype(jnp.bfloat16).astype(jnp.float32)
    second = (stats - first).astype(jnp.bfloat16).astype(jnp.float32)
    third = stats - first - second
    parts = jnp.concatenate([first, second, third], axis=0)
    pad = jnp.zeros((STAT_ROWS - parts.shape[0], LANES), jnp.float32)
    return jnp.concatenate([parts, pad], axis=0).astype(jnp.bfloat16)


def stats_of(block, groups):
    stats = block.astype(jnp.float32)
    return stats[:groups] + stats[groups : 2 * groups] + stats[2 * groups : 3 * groups]


def attend_rows(query_rows, key_rows, value_rows, tile):
    outputs, lines = [], []
    for at in range(0, query_rows.shape[0], tile):
        part, sums = soft_part(raw_scores(query_rows[at : at + tile], key_rows), value_rows)
        outputs.append(part)
        lines += across_lanes(sums)
    return jnp.concatenate(outputs, axis=0), jnp.concatenate(lines, axis=0)


def head_columns(head):
    return pl.ds(pl.multiple_of(head * HD, HD), HD)


def attend_kernel(here_ref, picks_ref, key_ref, value_ref, *refs, group, slots):
    heads_ref = refs[-1]
    here = here_ref[0]
    for number, (shift, first, count) in enumerate(group):
        query_ref, out_ref = refs[number], refs[len(group) + number]
        rows = query_ref.shape[1]
        list_heads(heads_ref, 0, picks_ref, here + shift, here, slots)
        for slot in range(count):
            head = heads_ref[first + slot]

            @pl.when(head >= 0)
            def _():
                columns = head_columns(head)
                outputs, lines = attend_rows(
                    query_ref[slot],
                    key_ref[:, columns],
                    with_ones(value_ref[:, columns]),
                    min(rows, 256),
                )
                out_ref[slot, :rows, :] = outputs.astype(jnp.bfloat16)
                out_ref[slot, rows:, :] = three_parts(lines)


def attend(here, picks, keys, values, arrived, group, slots):
    rows = keys.shape[0]
    total = sum(count for _, _, count in group)
    return call(
        functools.partial(attend_kernel, group=group, slots=slots),
        [SCALARS, SCALARS, IN_VMEM, IN_VMEM] + [IN_VMEM] * len(group),
        [
            jax.ShapeDtypeStruct((count, rows + STAT_ROWS, HD), jnp.bfloat16)
            for _, _, count in group
        ],
        [IN_VMEM] * len(group),
        [pltpu.SMEM((slots,), jnp.int32)],
        flops=4 * total * rows * rows * HD,
        moved=8 * total * rows * HD,
        exps=total * rows * rows,
    )(here, picks, keys, values, *arrived)


def own_kernel(here_ref, query_ref, key_ref, value_ref, out_ref):
    rows = query_ref.shape[0]
    tile = min(rows, 256)

    def one_head(head, carry):
        columns = head_columns(head)
        value_rows = with_ones(value_ref[:, columns])
        lines = []
        for at in range(0, rows, tile):
            reach = at + tile
            scores = raw_scores(query_ref[at:reach, columns], key_ref[:reach, columns])
            row_ids = lax.broadcasted_iota(jnp.int32, scores.shape, 0) + at
            seen = row_ids >= lax.broadcasted_iota(jnp.int32, scores.shape, 1)
            outputs, sums = soft_part(jnp.where(seen, scores, -jnp.inf), value_rows[:reach])
            out_ref[head, at:reach, :] = outputs.astype(jnp.bfloat16)
            lines += across_lanes(sums)
        out_ref[head, rows:, :] = three_parts(jnp.concatenate(lines, axis=0))
        return carry

    lax.fori_loop(0, HEADS, one_head, 0)


def own_part(here, queries, keys, values):
    rows = queries.shape[0]
    return call(
        own_kernel,
        [SCALARS, IN_VMEM, IN_VMEM, IN_VMEM],
        jax.ShapeDtypeStruct((HEADS, rows + STAT_ROWS, HD), jnp.bfloat16),
        IN_VMEM,
        flops=4 * HEADS * rows * rows * HD,
        moved=8 * HEADS * rows * HD,
        exps=HEADS * rows * rows,
    )(here, queries, keys, values)


def near_kernel(here_ref, picks_ref, query_ref, own_ref, *refs, shifts, slots):
    near_refs, out_ref, heads_ref = refs[: len(shifts)], refs[-2], refs[-1]
    rows = query_ref.shape[0]

    def keep(head, carry):
        out_ref[head] = own_ref[head]
        return carry

    lax.fori_loop(0, HEADS, keep, 0)
    groups = rows // LANES
    here = here_ref[0]
    for shift, near_ref in zip(shifts, near_refs):
        list_heads(heads_ref, 0, picks_ref, here, here - shift, slots)
        for slot in range(slots):
            head = heads_ref[slot]

            @pl.when(head >= 0)
            def _():
                outputs, lines = attend_rows(
                    query_ref[:, head_columns(head)],
                    near_ref[2 * slot],
                    with_ones(near_ref[2 * slot + 1]),
                    min(rows, 256),
                )
                before = stats_of(out_ref[head, rows:, :], groups)
                top = jnp.maximum(before, lines)
                after = top + jnp.log2(jnp.exp2(before - top) + jnp.exp2(lines - top))
                share = jnp.exp2(lines - after)
                for group in range(groups):
                    span = pl.ds(group * LANES, LANES)
                    old = out_ref[head, span, :].astype(jnp.float32)
                    new = outputs[group * LANES : (group + 1) * LANES]
                    mixed = old + (new - old) * down_rows(share[group : group + 1, :])
                    out_ref[head, span, :] = mixed.astype(jnp.bfloat16)
                out_ref[head, rows:, :] = three_parts(after)


def add_near(here, picks, queries, own, near, shifts, slots):
    rows = queries.shape[0]
    count = len(shifts) * slots
    return call(
        functools.partial(near_kernel, shifts=shifts, slots=slots),
        [SCALARS, SCALARS, IN_VMEM, IN_VMEM] + [IN_VMEM] * len(shifts),
        jax.ShapeDtypeStruct(own.shape, own.dtype),
        IN_VMEM,
        [pltpu.SMEM((slots,), jnp.int32)],
        flops=4 * count * rows * rows * HD,
        moved=12 * count * rows * HD,
        exps=count * rows * rows,
    )(here, picks, queries, own, *near)


def merge_kernel(here_ref, picks_ref, own_ref, *refs, places, skipped, slots):
    count = len(places)
    parts, out_ref, held, spots_ref, found_ref, sems = refs[:count], *refs[count:]
    rows = out_ref.shape[0]
    groups = rows // LANES
    width = picks_ref.shape[0]
    here = here_ref[0]
    copies = [
        pltpu.make_async_copy(part, held.at[pl.ds(place, part.shape[0])], sems.at[number])
        for number, (part, place) in enumerate(zip(parts, places))
    ]
    for copy in copies:
        copy.start()
    for owner in range(width):
        found_ref[owner] = 0

    def look(number, carry):
        pick, head = number // HEADS, number % HEADS
        owner = picks_ref[here, pick, head]
        safe = jnp.maximum(owner, 0)
        shift = here - safe
        order = found_ref[safe]
        found_ref[safe] = order + (owner >= 0).astype(jnp.int32)
        is_held = owner >= 0
        for left_out in skipped:
            is_held = is_held & (shift != left_out)
        spots_ref[head * PICKS + pick] = jnp.where(is_held, shift * slots + order, -1)
        return carry

    lax.fori_loop(0, PICKS * HEADS, look, 0)
    for copy in copies:
        copy.wait()

    def one_head(head, carry):
        found = [spots_ref[head * PICKS + pick] for pick in range(PICKS)]
        spots = [jnp.maximum(spot, 0) for spot in found]
        sums = [stats_of(own_ref[head, rows:, :], groups)]
        for spot, safe in zip(found, spots):
            sums.append(jnp.where(spot >= 0, stats_of(held[safe, rows:, :], groups), -jnp.inf))
        top = functools.reduce(jnp.maximum, sums)
        shares = [jnp.exp2(part - top) for part in sums]
        whole = functools.reduce(jnp.add, shares)
        shares = [share / whole for share in shares]
        columns = head_columns(head)
        for group in range(groups):
            span = pl.ds(group * LANES, LANES)
            mixed = own_ref[head, span, :].astype(jnp.float32)
            mixed = mixed * down_rows(shares[0][group : group + 1, :])
            for spot, safe, share in zip(found, spots, shares[1:]):
                block = jnp.where(spot >= 0, held[safe, span, :].astype(jnp.float32), 0.0)
                mixed = mixed + block * down_rows(share[group : group + 1, :])
            out_ref[span, columns] = mixed.astype(jnp.bfloat16)
        return carry

    lax.fori_loop(0, HEADS, one_head, 0)


def merge(here, picks, own, parts, places, skipped, slots):
    rows = own.shape[1] - STAT_ROWS
    width = picks.shape[0]
    return call(
        functools.partial(merge_kernel, places=places, skipped=skipped, slots=slots),
        [SCALARS, SCALARS, IN_VMEM] + [pl.BlockSpec(memory_space=pl.ANY)] * len(parts),
        jax.ShapeDtypeStruct((rows, HEADS * HD), jnp.bfloat16),
        pl.BlockSpec((rows, HEADS * HD), lambda: (0, 0)),
        [
            pltpu.VMEM((width * slots, rows + STAT_ROWS, HD), jnp.bfloat16),
            pltpu.SMEM((PICKS * HEADS,), jnp.int32),
            pltpu.SMEM((width,), jnp.int32),
            pltpu.SemaphoreType.DMA((len(parts),)),
        ],
        flops=6 * HEADS * rows * HD,
        moved=2 * (HEADS * 2 + width * slots) * rows * HD,
    )(here, picks, own, *parts)


def after(value, *earlier):
    return lax.optimization_barrier((value,) + earlier)[0]


def groups_in_order(width, slots):
    middle = width // 2
    groups = []
    for low in range(2, middle):
        size = max(1, slots // 2) if low == middle - 1 else slots
        for first in range(0, slots, size):
            count = min(size, slots - first)
            groups.append([(low, first, count), (width - low, first, count)])
    return groups + [[(middle, 0, slots)]]


def travelling_queries(queries, keys, values, picks):
    width = lax.axis_size("ctx")
    sections = lax.axis_size("pipe")
    slots = max(1, PICKS * HEADS // width)
    here = lax.axis_index("ctx").astype(jnp.int32).reshape(1)
    queries, keys, values = queries[0], keys[0], values[0]
    own_picks = picks[0].transpose(0, 2, 1)

    groups = groups_in_order(width, slots)
    near_shifts = (1, width - 1)
    first_jobs = [(shift, 0, slots, True) for shift in near_shifts]
    first_jobs += [piece + (False,) for piece in groups[0]]
    later_jobs = [piece + (False,) for group in groups[1:] for piece in group]

    def up(value, shift):
        return lax.ppermute(value, "ctx", [(at, at + shift) for at in range(width - shift)])

    def down(value, shift):
        return lax.ppermute(value, "ctx", [(at, at - shift) for at in range(shift, width)])

    def up_and_on(value, shift):
        pairs = [
            (at * sections + section, (at + shift) * sections + (section + 1) % sections)
            for at in range(width - shift)
            for section in range(sections)
        ]
        return lax.ppermute(value, ("ctx", "pipe"), pairs)

    sends = dict(zip(first_jobs, pack(here, own_picks, queries, keys, values, first_jobs, slots)))
    near = [up(sends[job], job[0]) for job in first_jobs if job[3]]
    arrived = [down(sends[piece + (False,)], piece[0]) for piece in groups[0]]
    before = passed_along(own_picks, "pipe", 1)
    now = after(here, *[sends[job] for job in first_jobs])
    sends |= zip(later_jobs, pack(now, own_picks, queries, keys, values, later_jobs, slots))

    own = own_part(after(here, before, sends[later_jobs[0]]), queries, keys, values)
    last, returned = own, {}
    for number, group in enumerate(groups):
        current = arrived
        if number + 1 < len(groups):
            waits = [last] + current
            if number >= 2:
                waits += [returned[piece] for piece in groups[number - 2]]
            arrived = [
                down(after(sends[piece + (False,)], *waits), piece[0])
                for piece in groups[number + 1]
            ]
        waits = [last] + (near if number == 0 else [])
        if number >= 2:
            waits += [returned[piece] for piece in groups[number - 2]]
        parts = attend(
            after(here, *waits), own_picks, keys, values, current, tuple(group), slots
        )
        last = parts[0]
        for piece, part in zip(group, parts):
            if number >= 1:
                part = after(part, *[returned[earlier] for earlier in groups[number - 1]])
            returned[piece] = up_and_on(part, piece[0])
        if number == 1:
            own = add_near(after(here, last, *[returned[piece] for piece in groups[0]]), own_picks, queries, own, near, near_shifts, slots)
            own_back = passed_along(own, "pipe", 1)
            last = own
    places = [shift * slots + first for shift, first, _ in returned]
    parts = list(returned.values())
    return merge(here, before, own_back, parts, places, near_shifts, slots)[None]


def travelling_keys(queries, keys, values, picks):
    ctx_width = lax.axis_size("ctx")
    rank_here = lax.axis_index("ctx")
    slot_count = max(1, PICKS * HEADS // ctx_width)
    block_rows = queries.shape[1]
    score_scale = HD ** (-0.5)
    every_pick = picks[0].reshape(ctx_width, HEADS * PICKS)
    chosen = lax.dynamic_slice_in_dim(every_pick, rank_here, 1, 0)
    pick_order = request_table(chosen, lax.iota(jnp.int32, ctx_width), slot_count)[1]
    asked_table = request_table(every_pick, rank_here.reshape(1), slot_count)[0]
    asked_heads = asked_table[:, 0, :]
    safe_asked = jnp.maximum(asked_heads, 0)
    query_heads = queries[0].reshape(block_rows, HEADS, HD).transpose(1, 0, 2)
    key_heads = keys[0].reshape(block_rows, HEADS, HD).transpose(1, 0, 2)
    value_heads = values[0].reshape(block_rows, HEADS, HD).transpose(1, 0, 2)
    is_live = chosen[0] >= 0
    flat_slot = jnp.where(is_live, chosen[0] * slot_count + pick_order[0], 0)
    remote_mask = jnp.repeat(is_live.reshape(HEADS, PICKS), block_rows, axis=1)
    row_index = lax.iota(jnp.int32, block_rows)
    causal = row_index[:, None] >= row_index[None, :]

    def masked_scores(query_head, key_rows, mask_row):
        scores = lax.dot_general(
            query_head, key_rows, (((1,), (1,)), ((), ())), preferred_element_type=jnp.float32
        )
        allowed = jnp.concatenate(
            [causal, jnp.broadcast_to(mask_row[None, :], (block_rows, PICKS * block_rows))], axis=1
        )
        return jnp.where(allowed, scores * score_scale, -jnp.inf)

    def row_stats(scores):
        row_top = jnp.max(scores, axis=1)
        row_total = jnp.sum(jnp.exp(scores - row_top[:, None]), axis=1)
        return (row_top, row_total)

    def weighted(scores, row_top, row_total, value_rows):
        prob_rows = (jnp.exp(scores - row_top[:, None]) / row_total[:, None]).astype(jnp.bfloat16)
        return jnp.dot(prob_rows, value_rows, preferred_element_type=jnp.float32).astype(
            jnp.bfloat16
        )

    send_both = jnp.concatenate([key_heads, value_heads], axis=2)[safe_asked]
    got_slots = lax.all_to_all(send_both, "ctx", split_axis=0, concat_axis=0, tiled=True)
    last_width = 2 * HD
    flat_slots = got_slots.reshape(ctx_width * slot_count, block_rows, last_width)
    remote_both = flat_slots[flat_slot].reshape(HEADS, PICKS * block_rows, last_width)
    all_keys = jnp.concatenate([key_heads, remote_both[:, :, :HD]], axis=1)
    all_values = jnp.concatenate([value_heads, remote_both[:, :, HD:]], axis=1)

    def per_head(head_items):
        query_head, key_rows, value_rows, mask_row = head_items
        scores = masked_scores(query_head, key_rows, mask_row)
        row_top, row_total = row_stats(scores)
        return weighted(scores, row_top, row_total, value_rows)

    outputs = lax.map(per_head, (query_heads, all_keys, all_values, remote_mask))
    merged = outputs.transpose(1, 0, 2).reshape(1, block_rows, HEADS * HD)
    return passed_along(merged, "pipe", 1)


def per_device(queries, keys, values, picks):
    few_shifts = 4 <= lax.axis_size("ctx") <= 16
    run = travelling_queries if few_shifts else travelling_keys
    return run(queries, keys, values, picks)


def solution(mesh):
    placed = (
        P("pipe", "ctx", None),
        P("pipe", "ctx", None),
        P("pipe", "ctx", None),
        P("pipe", None, None, None),
    )
    return jax.shard_map(
        per_device, mesh=mesh, in_specs=placed, out_specs=P("pipe", "ctx", None), check_vma=False
    )
```

```python
import functools
import math

import jax
import jax.numpy as jnp
from jax import lax
from jax.experimental import pallas as pl
from jax.experimental.pallas import tpu as pltpu
from jax.sharding import PartitionSpec as P

HEADS = 16
HD = 128
PICKS = 2
EXP2_SCALE = HD ** -0.5 * math.log2(math.e)
LANES = 128
STAT_ROWS = 16
VMEM_BYTES = 48 * 1024 * 1024


def passed_along(value, axis, steps):
    count = lax.axis_size(axis)
    pairs = [(source, (source + steps) % count) for source in range(count)]
    return lax.ppermute(value, axis, pairs)


def request_table(chosen, owners, slot_count):
    pick_count = chosen.shape[1]
    pick_ids = lax.iota(jnp.int32, pick_count)
    is_live = chosen >= 0
    earlier = pick_ids[None, :] < pick_ids[:, None]
    same_owner = (chosen[:, :, None] == chosen[:, None, :]) & earlier[None]
    pick_order = jnp.sum(same_owner.astype(jnp.int32), axis=2)
    head_ids = pick_ids // PICKS
    slot_ranks = lax.iota(jnp.int32, slot_count)
    matches = (
        is_live[:, None, None, :]
        & (chosen[:, None, None, :] == owners[None, :, None, None])
        & (pick_order[:, None, None, :] == slot_ranks[None, None, :, None])
    )
    was_found = jnp.any(matches, axis=3)
    head_table = jnp.sum(jnp.where(matches, head_ids[None, None, None, :], 0), axis=3)
    return (jnp.where(was_found, head_table, -1), pick_order)


def call(kernel, name_space, outputs, out_specs, scratch=(), flops=0, moved=0, exps=0):
    return pl.pallas_call(
        kernel,
        in_specs=name_space,
        out_specs=out_specs,
        out_shape=outputs,
        scratch_shapes=list(scratch),
        compiler_params=pltpu.CompilerParams(vmem_limit_bytes=VMEM_BYTES),
        cost_estimate=pl.CostEstimate(flops=flops, bytes_accessed=moved, transcendentals=exps),
    )


SCALARS = pl.BlockSpec(memory_space=pltpu.SMEM)
IN_HBM = pl.BlockSpec(memory_space=pltpu.HBM)
IN_VMEM = pl.BlockSpec(memory_space=pltpu.VMEM)


def tick_kernel(here_ref, out_ref):
    out_ref[0] = here_ref[0]


def tick(here, *earlier, flops=10**12):
    return call(
        tick_kernel,
        [SCALARS],
        jax.ShapeDtypeStruct((1,), jnp.int32),
        SCALARS,
        flops=flops,
    )(after(here, *earlier))


def list_heads(heads_ref, start, picks_ref, block, owner, slots):
    width = picks_ref.shape[0]
    for slot in range(slots):
        heads_ref[start + slot] = -1
    valid = (block >= 0) & (block < width) & (owner >= 0) & (owner < width)
    row = jnp.clip(block, 0, width - 1)

    def look(number, found):
        pick, head = number // HEADS, number % HEADS
        hit = valid & (picks_ref[row, pick, head] == owner)

        @pl.when(hit)
        def _():
            heads_ref[start + found] = head

        return found + hit.astype(jnp.int32)

    lax.fori_loop(0, PICKS * HEADS, look, jnp.int32(0))


def pack_kernel(here_ref, picks_ref, *refs, jobs, slots):
    sources, outputs = refs[:3], refs[3 : 3 + len(jobs)]
    heads_ref, sems = refs[-2], refs[-1]
    here = here_ref[0]
    listed = {}
    for shift, first, count, is_near in jobs:
        key = (shift, is_near)
        if key not in listed:
            listed[key] = len(listed) * slots
            block, owner = (here + shift, here) if is_near else (here, here - shift)
            list_heads(heads_ref, listed[key], picks_ref, block, owner, slots)
    copies = []
    for (shift, first, count, is_near), output in zip(jobs, outputs):
        for slot in range(count):
            head = jnp.maximum(heads_ref[listed[shift, is_near] + first + slot], 0)
            columns = pl.ds(pl.multiple_of(head * HD, HD), HD)
            for place, source in enumerate(sources[1:] if is_near else sources[:1]):
                target = output.at[2 * slot + place if is_near else slot]
                copy = pltpu.make_async_copy(
                    source.at[:, columns], target, sems.at[len(copies)]
                )
                copy.start()
                copies.append(copy)
    for copy in copies:
        copy.wait()


def pack(here, picks, queries, keys, values, jobs, slots):
    rows = queries.shape[0]
    sizes = [2 * count if is_near else count for _, _, count, is_near in jobs]
    return call(
        functools.partial(pack_kernel, jobs=jobs, slots=slots),
        [SCALARS, SCALARS, IN_HBM, IN_HBM, IN_HBM],
        [jax.ShapeDtypeStruct((size, rows, HD), jnp.bfloat16) for size in sizes],
        [IN_HBM] * len(sizes),
        [pltpu.SMEM((len(jobs) * slots,), jnp.int32), pltpu.SemaphoreType.DMA((sum(sizes),))],
        moved=4 * rows * HD * sum(sizes),
    )(here, picks, queries, keys, values)


def diagonal():
    shape = (LANES, LANES)
    return lax.broadcasted_iota(jnp.int32, shape, 0) == lax.broadcasted_iota(jnp.int32, shape, 1)


def raw_scores(query_rows, key_rows):
    return lax.dot_general(
        query_rows, key_rows, (((1,), (1,)), ((), ())), preferred_element_type=jnp.float32
    )


def with_ones(value_rows):
    return jnp.concatenate([value_rows, jnp.ones_like(value_rows)], axis=1)


def soft_part(scores, value_rows):
    top = jnp.max(scores, axis=1, keepdims=True)
    weights = jnp.exp2((scores - top) * EXP2_SCALE).astype(jnp.bfloat16)
    total = jnp.dot(weights, value_rows, preferred_element_type=jnp.float32)
    sums = total[:, HD:]
    return total[:, :HD] * pl.reciprocal(sums), top * EXP2_SCALE, sums


def across_lanes(column):
    eye = diagonal()
    spread = jnp.broadcast_to(column, (column.shape[0], LANES))
    return [
        jnp.sum(jnp.where(eye, spread[at : at + LANES], 0.0), axis=0, keepdims=True)
        for at in range(0, column.shape[0], LANES)
    ]


def down_rows(line):
    spread = jnp.broadcast_to(line, (LANES, LANES))
    return jnp.sum(jnp.where(diagonal(), spread, 0.0), axis=1, keepdims=True)


def three_parts(stats):
    first = stats.astype(jnp.bfloat16).astype(jnp.float32)
    second = (stats - first).astype(jnp.bfloat16).astype(jnp.float32)
    third = stats - first - second
    parts = jnp.concatenate([first, second, third], axis=0)
    pad = jnp.zeros((STAT_ROWS - parts.shape[0], LANES), jnp.float32)
    return jnp.concatenate([parts, pad], axis=0).astype(jnp.bfloat16)


def stats_of(block, groups):
    stats = block.astype(jnp.float32)
    return stats[:groups] + stats[groups : 2 * groups] + stats[2 * groups : 3 * groups]


def log_sums(tops, sums):
    top_lines = [line for top in tops for line in across_lanes(top)]
    sum_lines = [line for part in sums for line in across_lanes(part)]
    return jnp.concatenate(top_lines, axis=0) + jnp.log2(jnp.concatenate(sum_lines, axis=0))


def attend_rows(query_rows, key_rows, value_rows, tile):
    found = [
        soft_part(raw_scores(query_rows[at : at + tile], key_rows), value_rows)
        for at in range(0, query_rows.shape[0], tile)
    ]
    outputs, tops, sums = zip(*found)
    return jnp.concatenate(outputs, axis=0), log_sums(tops, sums)


def head_columns(head):
    return pl.ds(pl.multiple_of(head * HD, HD), HD)


def attend_kernel(here_ref, picks_ref, key_ref, value_ref, *refs, group, slots):
    heads_ref = refs[-1]
    here = here_ref[0]
    for number, (shift, first, count) in enumerate(group):
        query_ref, out_ref = refs[number], refs[len(group) + number]
        rows = query_ref.shape[1]
        list_heads(heads_ref, 0, picks_ref, here + shift, here, slots)
        for slot in range(count):
            columns = head_columns(jnp.maximum(heads_ref[first + slot], 0))
            outputs, lines = attend_rows(
                query_ref[slot], key_ref[:, columns], with_ones(value_ref[:, columns]), min(rows, 256)
            )
            out_ref[slot, :rows, :] = outputs.astype(jnp.bfloat16)
            out_ref[slot, rows:, :] = three_parts(lines)


def attend(here, picks, keys, values, arrived, group, slots):
    rows = keys.shape[0]
    total = sum(count for _, _, count in group)
    return call(
        functools.partial(attend_kernel, group=group, slots=slots),
        [SCALARS, SCALARS, IN_VMEM, IN_VMEM] + [IN_VMEM] * len(group),
        [
            jax.ShapeDtypeStruct((count, rows + STAT_ROWS, HD), jnp.bfloat16)
            for _, _, count in group
        ],
        [IN_VMEM] * len(group),
        [pltpu.SMEM((slots,), jnp.int32)],
        flops=4 * total * rows * rows * HD,
        moved=8 * total * rows * HD,
        exps=total * rows * rows,
    )(here, picks, keys, values, *arrived)


def own_kernel(here_ref, query_ref, key_ref, value_ref, out_ref):
    rows = query_ref.shape[0]
    tile = min(rows, 256)

    def one_head(head, carry):
        columns = head_columns(head)
        value_rows = with_ones(value_ref[:, columns])
        tops, all_sums = [], []
        for at in range(0, rows, tile):
            reach = at + tile
            scores = raw_scores(query_ref[at:reach, columns], key_ref[:reach, columns])
            row_ids = lax.broadcasted_iota(jnp.int32, scores.shape, 0) + at
            seen = row_ids >= lax.broadcasted_iota(jnp.int32, scores.shape, 1)
            outputs, top, sums = soft_part(jnp.where(seen, scores, -jnp.inf), value_rows[:reach])
            out_ref[head, at:reach, :] = outputs.astype(jnp.bfloat16)
            tops.append(top)
            all_sums.append(sums)
        out_ref[head, rows:, :] = three_parts(log_sums(tops, all_sums))
        return carry

    lax.fori_loop(0, HEADS, one_head, 0, unroll=4)


def own_part(here, queries, keys, values):
    rows = queries.shape[0]
    return call(
        own_kernel,
        [SCALARS, IN_VMEM, IN_VMEM, IN_VMEM],
        jax.ShapeDtypeStruct((HEADS, rows + STAT_ROWS, HD), jnp.bfloat16),
        IN_VMEM,
        flops=4 * HEADS * rows * rows * HD,
        moved=8 * HEADS * rows * HD,
        exps=HEADS * rows * rows,
    )(here, queries, keys, values)


def near_kernel(here_ref, picks_ref, query_ref, own_ref, *refs, shifts, slots):
    near_refs, out_ref, heads_ref = refs[: len(shifts)], refs[-2], refs[-1]
    rows = query_ref.shape[0]

    def keep(head, carry):
        out_ref[head] = own_ref[head]
        return carry

    lax.fori_loop(0, HEADS, keep, 0)
    groups = rows // LANES
    here = here_ref[0]
    for shift, near_ref in zip(shifts, near_refs):
        list_heads(heads_ref, 0, picks_ref, here, here - shift, slots)
        for slot in range(slots):
            head = heads_ref[slot]

            @pl.when(head >= 0)
            def _():
                outputs, lines = attend_rows(
                    query_ref[:, head_columns(head)],
                    near_ref[2 * slot],
                    with_ones(near_ref[2 * slot + 1]),
                    min(rows, 256),
                )
                before = stats_of(out_ref[head, rows:, :], groups)
                top = jnp.maximum(before, lines)
                after = top + jnp.log2(jnp.exp2(before - top) + jnp.exp2(lines - top))
                share = jnp.exp2(lines - after)
                for group in range(groups):
                    span = pl.ds(group * LANES, LANES)
                    old = out_ref[head, span, :].astype(jnp.float32)
                    new = outputs[group * LANES : (group + 1) * LANES]
                    mixed = old + (new - old) * down_rows(share[group : group + 1, :])
                    out_ref[head, span, :] = mixed.astype(jnp.bfloat16)
                out_ref[head, rows:, :] = three_parts(after)


def add_near(here, picks, queries, own, near, shifts, slots):
    rows = queries.shape[0]
    count = len(shifts) * slots
    return call(
        functools.partial(near_kernel, shifts=shifts, slots=slots),
        [SCALARS, SCALARS, IN_VMEM, IN_VMEM] + [IN_VMEM] * len(shifts),
        jax.ShapeDtypeStruct(own.shape, own.dtype),
        IN_VMEM,
        [pltpu.SMEM((slots,), jnp.int32)],
        flops=4 * count * rows * rows * HD,
        moved=12 * count * rows * HD,
        exps=count * rows * rows,
    )(here, picks, queries, own, *near)


def find_spots(spots_ref, found_ref, picks_ref, here, shifts, slots):
    for owner in range(picks_ref.shape[0]):
        found_ref[owner] = 0

    def look(number, carry):
        pick, head = number // HEADS, number % HEADS
        owner = picks_ref[here, pick, head]
        safe = jnp.maximum(owner, 0)
        order = found_ref[safe]
        found_ref[safe] = order + (owner >= 0).astype(jnp.int32)
        spot = jnp.int32(-1)
        for place, shift in enumerate(shifts):
            spot = jnp.where(here - safe == shift, place * slots + order, spot)
        spots_ref[head * PICKS + pick] = jnp.where(owner >= 0, spot, -1)
        return carry

    lax.fori_loop(0, PICKS * HEADS, look, 0)


def merge_kernel(here_ref, picks_ref, *refs, places, shifts, slots):
    count = len(places)
    parts = refs[: count + 1]
    out_ref, sums_ref, held, spots_ref, found_ref, sems = refs[count + 1 :]
    groups = sums_ref.shape[1]
    rows = groups * LANES
    copies = [
        pltpu.make_async_copy(part, held.at[pl.ds(place, part.shape[0])], sems.at[number])
        for number, (part, place) in enumerate(zip(parts, (0,) + places))
    ]
    for copy in copies:
        copy.start()
    find_spots(spots_ref, found_ref, picks_ref, here_ref[0], shifts, slots)
    for copy in copies:
        copy.wait()

    def one_head(head, carry):
        found = [spots_ref[head * PICKS + pick] for pick in range(PICKS)]
        spots = [head] + [jnp.where(spot >= 0, HEADS + spot, head) for spot in found]
        sums = [stats_of(held[spot, rows:, :], groups) for spot in spots]
        for pick, spot in enumerate(found):
            sums[1 + pick] = jnp.where(spot >= 0, sums[1 + pick], -jnp.inf)
        top = functools.reduce(jnp.maximum, sums)
        shares = [jnp.exp2(part - top) for part in sums]
        whole = functools.reduce(jnp.add, shares)
        sums_ref[head] = top + jnp.log2(whole)
        for group in range(groups):
            span = pl.ds(group * LANES, LANES)
            own = held[head, span, :].astype(jnp.float32)
            mixed = own
            for spot, share in zip(spots[1:], shares[1:]):
                weight = down_rows((share / whole)[group : group + 1, :])
                mixed = mixed + (held[spot, span, :].astype(jnp.float32) - own) * weight
            out_ref[head, span, :] = mixed
        return carry

    lax.fori_loop(0, HEADS, one_head, 0, unroll=2)


def merge(here, picks, own, parts, places, shifts, slots):
    rows = own.shape[1] - STAT_ROWS
    width = picks.shape[0]
    total = HEADS + len(shifts) * slots
    return call(
        functools.partial(
            merge_kernel, places=tuple(HEADS + place for place in places), shifts=shifts, slots=slots
        ),
        [SCALARS, SCALARS] + [pl.BlockSpec(memory_space=pl.ANY)] * (1 + len(parts)),
        [
            jax.ShapeDtypeStruct((HEADS, rows, HD), jnp.float32),
            jax.ShapeDtypeStruct((HEADS, rows // LANES, LANES), jnp.float32),
        ],
        [IN_VMEM, IN_VMEM],
        [
            pltpu.VMEM((total, rows + STAT_ROWS, HD), jnp.bfloat16),
            pltpu.SMEM((PICKS * HEADS,), jnp.int32),
            pltpu.SMEM((width,), jnp.int32),
            pltpu.SemaphoreType.DMA((1 + len(parts),)),
        ],
        flops=6 * HEADS * rows * HD,
        moved=2 * (HEADS * 2 + total) * rows * HD,
    )(here, picks, own, *parts)


def finish_kernel(
    here_ref, picks_ref, mixed_ref, sums_ref, part_ref, out_ref, spots_ref, found_ref, *, shift, slots
):
    groups = sums_ref.shape[1]
    rows = groups * LANES
    step = pl.program_id(0)
    per_step = HEADS // pl.num_programs(0)

    @pl.when(step == 0)
    def _():
        find_spots(spots_ref, found_ref, picks_ref, here_ref[0], (shift,), slots)

    for place in range(per_step):
        head = step * per_step + place
        spot = jnp.maximum(spots_ref[head * PICKS], spots_ref[head * PICKS + 1])
        columns = pl.ds(place * HD, HD)

        @pl.when(spot < 0)
        def _():
            out_ref[:, columns] = mixed_ref[head].astype(jnp.bfloat16)

        @pl.when(spot >= 0)
        def _():
            before = sums_ref[head]
            added = stats_of(part_ref[spot, rows:, :], groups)
            share = 1.0 / (1.0 + jnp.exp2(before - added))
            for group in range(groups):
                span = pl.ds(group * LANES, LANES)
                old = mixed_ref[head, span, :]
                new = part_ref[spot, span, :].astype(jnp.float32)
                mixed = old + (new - old) * down_rows(share[group : group + 1, :])
                out_ref[span, columns] = mixed.astype(jnp.bfloat16)


def finish(here, picks, mixed, sums, part, shift, slots):
    heads, rows, _ = mixed.shape
    width = picks.shape[0]
    steps = 4
    return pl.pallas_call(
        functools.partial(finish_kernel, shift=shift, slots=slots),
        grid=(steps,),
        in_specs=[SCALARS, SCALARS, IN_VMEM, IN_VMEM, IN_VMEM],
        out_specs=pl.BlockSpec((rows, heads // steps * HD), lambda step: (0, step)),
        out_shape=jax.ShapeDtypeStruct((rows, heads * HD), jnp.bfloat16),
        scratch_shapes=[
            pltpu.SMEM((PICKS * HEADS,), jnp.int32),
            pltpu.SMEM((width,), jnp.int32),
        ],
        compiler_params=pltpu.CompilerParams(vmem_limit_bytes=VMEM_BYTES),
        cost_estimate=pl.CostEstimate(
            flops=2 * heads * rows * HD, bytes_accessed=8 * heads * rows * HD, transcendentals=0
        ),
    )(here, picks, mixed, sums, part)


def after(value, *earlier):
    return lax.optimization_barrier((value,) + earlier)[0]


def groups_in_order(width, slots):
    middle = width // 2
    groups = [[(1, 0, slots)], [(shift, 0, slots) for shift in (width - 2, width - 1)]]
    for low in range(3, middle):
        size = max(1, slots // 2)
        for first in range(0, slots, size):
            count = min(size, slots - first)
            groups.append([(low, first, count), (width - low, first, count)])
    return groups + [[(middle, 0, slots)]]


def travelling_queries(queries, keys, values, picks):
    width = lax.axis_size("ctx")
    sections = lax.axis_size("pipe")
    slots = max(1, PICKS * HEADS // width)
    here = lax.axis_index("ctx").astype(jnp.int32).reshape(1)
    queries, keys, values = queries[0], keys[0], values[0]
    own_picks = picks[0].transpose(0, 2, 1)

    groups = groups_in_order(width, slots)
    near_shifts = (2,)
    first_jobs = [(shift, 0, slots, True) for shift in near_shifts]
    first_jobs += [piece + (False,) for group in groups[:2] for piece in group]
    later_jobs = [piece + (False,) for group in groups[2:] for piece in group]

    def up(value, shift):
        return lax.ppermute(value, "ctx", [(at, at + shift) for at in range(width - shift)])

    def down(value, shift):
        return lax.ppermute(value, "ctx", [(at, at - shift) for at in range(shift, width)])

    def up_and_on(value, shift):
        pairs = [
            (at * sections + section, (at + shift) * sections + (section + 1) % sections)
            for at in range(width - shift)
            for section in range(sections)
        ]
        return lax.ppermute(value, ("ctx", "pipe"), pairs)

    sends = dict(zip(first_jobs, pack(here, own_picks, queries, keys, values, first_jobs, slots)))
    near = [up(sends[job], job[0]) for job in first_jobs if job[3]]
    arrived = {
        piece: down(sends[piece + (False,)], piece[0]) for group in groups[:2] for piece in group
    }
    before = passed_along(own_picks, "pipe", 1)
    now = after(here, *[sends[job] for job in first_jobs])
    sends |= zip(later_jobs, pack(now, own_picks, queries, keys, values, later_jobs, slots))

    def attend_group(token, group):
        return dict(
            zip(
                group,
                attend(
                    token,
                    own_picks,
                    keys,
                    values,
                    [arrived[piece] for piece in group],
                    tuple(group),
                    slots,
                ),
            )
        )

    def ask_for(group, *earlier):
        for piece in group:
            arrived[piece] = down(after(sends[piece + (False,)], *earlier), piece[0])

    def send_back(parts, *earlier):
        for piece, part in parts.items():
            returned[piece] = up_and_on(after(part, *earlier) if earlier else part, piece[0])

    def those(found, group):
        return [found[piece] for piece in group]

    returned = {}
    own = own_part(after(here, before, sends[later_jobs[0]]), queries, keys, values)
    parts = attend_group(after(here, own), groups[0])
    send_back(parts)
    parts_next = attend_group(after(here, *parts.values(), *near), groups[1])
    send_back(parts_next)
    ask_for(groups[2], *parts_next.values(), *arrived.values())
    now = tick(here, *parts_next.values())
    own = add_near(now, own_picks, queries, own, near, near_shifts, slots)
    before_last = groups[0] + groups[1]
    for number in range(2, len(groups)):
        group = groups[number]
        waits = [own] if number == 2 else []
        waits += [own_back] if number == len(groups) - 1 else []
        parts = attend_group(after(now, *waits), group)
        now = tick(now, *parts.values(), flops=0)
        if number == 2:
            ask_for(groups[number + 1], *parts.values(), *those(arrived, group))
        send_back(parts, *those(returned, before_last))
        if number == 2:
            own_back = passed_along(after(own, *those(returned, before_last)), "pipe", 1)
        now = tick(now, *those(returned, before_last))
        before_last = group
        if 2 <= number < len(groups) - 2:
            ask_for(groups[number + 2], now, *those(arrived, groups[number + 1]))

    final = groups[-1][0]
    merged_shifts = tuple(shift for shift in range(1, width) if shift not in (2, final[0]))
    pieces = [piece for piece in returned if piece != final]
    places = [merged_shifts.index(shift) * slots + first for shift, first, _ in pieces]
    parts = [returned[piece] for piece in pieces]
    mixed, sums = merge(now, before, own_back, parts, places, merged_shifts, slots)
    return finish(now, before, mixed, sums, returned[final], final[0], slots)[None]


def travelling_keys(queries, keys, values, picks):
    ctx_width = lax.axis_size("ctx")
    rank_here = lax.axis_index("ctx")
    slot_count = max(1, PICKS * HEADS // ctx_width)
    block_rows = queries.shape[1]
    score_scale = HD ** (-0.5)
    every_pick = picks[0].reshape(ctx_width, HEADS * PICKS)
    chosen = lax.dynamic_slice_in_dim(every_pick, rank_here, 1, 0)
    pick_order = request_table(chosen, lax.iota(jnp.int32, ctx_width), slot_count)[1]
    asked_table = request_table(every_pick, rank_here.reshape(1), slot_count)[0]
    asked_heads = asked_table[:, 0, :]
    safe_asked = jnp.maximum(asked_heads, 0)
    query_heads = queries[0].reshape(block_rows, HEADS, HD).transpose(1, 0, 2)
    key_heads = keys[0].reshape(block_rows, HEADS, HD).transpose(1, 0, 2)
    value_heads = values[0].reshape(block_rows, HEADS, HD).transpose(1, 0, 2)
    is_live = chosen[0] >= 0
    flat_slot = jnp.where(is_live, chosen[0] * slot_count + pick_order[0], 0)
    remote_mask = jnp.repeat(is_live.reshape(HEADS, PICKS), block_rows, axis=1)
    row_index = lax.iota(jnp.int32, block_rows)
    causal = row_index[:, None] >= row_index[None, :]

    def masked_scores(query_head, key_rows, mask_row):
        scores = lax.dot_general(
            query_head, key_rows, (((1,), (1,)), ((), ())), preferred_element_type=jnp.float32
        )
        allowed = jnp.concatenate(
            [causal, jnp.broadcast_to(mask_row[None, :], (block_rows, PICKS * block_rows))], axis=1
        )
        return jnp.where(allowed, scores * score_scale, -jnp.inf)

    def row_stats(scores):
        row_top = jnp.max(scores, axis=1)
        row_total = jnp.sum(jnp.exp(scores - row_top[:, None]), axis=1)
        return (row_top, row_total)

    def weighted(scores, row_top, row_total, value_rows):
        prob_rows = (jnp.exp(scores - row_top[:, None]) / row_total[:, None]).astype(jnp.bfloat16)
        return jnp.dot(prob_rows, value_rows, preferred_element_type=jnp.float32).astype(
            jnp.bfloat16
        )

    send_both = jnp.concatenate([key_heads, value_heads], axis=2)[safe_asked]
    got_slots = lax.all_to_all(send_both, "ctx", split_axis=0, concat_axis=0, tiled=True)
    last_width = 2 * HD
    flat_slots = got_slots.reshape(ctx_width * slot_count, block_rows, last_width)
    remote_both = flat_slots[flat_slot].reshape(HEADS, PICKS * block_rows, last_width)
    all_keys = jnp.concatenate([key_heads, remote_both[:, :, :HD]], axis=1)
    all_values = jnp.concatenate([value_heads, remote_both[:, :, HD:]], axis=1)

    def per_head(head_items):
        query_head, key_rows, value_rows, mask_row = head_items
        scores = masked_scores(query_head, key_rows, mask_row)
        row_top, row_total = row_stats(scores)
        return weighted(scores, row_top, row_total, value_rows)

    outputs = lax.map(per_head, (query_heads, all_keys, all_values, remote_mask))
    merged = outputs.transpose(1, 0, 2).reshape(1, block_rows, HEADS * HD)
    return passed_along(merged, "pipe", 1)


def per_device(queries, keys, values, picks):
    few_shifts = 8 <= lax.axis_size("ctx") <= 16
    run = travelling_queries if few_shifts else travelling_keys
    return run(queries, keys, values, picks)


def solution(mesh):
    placed = (
        P("pipe", "ctx", None),
        P("pipe", "ctx", None),
        P("pipe", "ctx", None),
        P("pipe", None, None, None),
    )
    return jax.shard_map(
        per_device, mesh=mesh, in_specs=placed, out_specs=P("pipe", "ctx", None), check_vma=False
    )
```

```python
import functools
import math

import jax
import jax.numpy as jnp
from jax import lax
from jax.experimental import pallas as pl
from jax.experimental.pallas import tpu as pltpu
from jax.sharding import PartitionSpec as P

HEADS = 16
HD = 128
PICKS = 2
EXP2_SCALE = HD ** -0.5 * math.log2(math.e)
LANES = 128
STAT_ROWS = 16
VMEM_BYTES = 24 * 1024 * 1024
HIGH_COST = 10**12


def passed_along(value, axis, steps):
    count = lax.axis_size(axis)
    pairs = [(source, (source + steps) % count) for source in range(count)]
    return lax.ppermute(value, axis, pairs)


def request_table(chosen, owners, slot_count):
    pick_count = chosen.shape[1]
    pick_ids = lax.iota(jnp.int32, pick_count)
    is_live = chosen >= 0
    earlier = pick_ids[None, :] < pick_ids[:, None]
    same_owner = (chosen[:, :, None] == chosen[:, None, :]) & earlier[None]
    pick_order = jnp.sum(same_owner.astype(jnp.int32), axis=2)
    head_ids = pick_ids // PICKS
    slot_ranks = lax.iota(jnp.int32, slot_count)
    matches = (
        is_live[:, None, None, :]
        & (chosen[:, None, None, :] == owners[None, :, None, None])
        & (pick_order[:, None, None, :] == slot_ranks[None, None, :, None])
    )
    was_found = jnp.any(matches, axis=3)
    head_table = jnp.sum(jnp.where(matches, head_ids[None, None, None, :], 0), axis=3)
    return (jnp.where(was_found, head_table, -1), pick_order)


def call(kernel, name_space, outputs, out_specs, scratch=(), flops=0, moved=0, exps=0):
    return pl.pallas_call(
        kernel,
        in_specs=name_space,
        out_specs=out_specs,
        out_shape=outputs,
        scratch_shapes=list(scratch),
        compiler_params=pltpu.CompilerParams(vmem_limit_bytes=VMEM_BYTES),
        cost_estimate=pl.CostEstimate(flops=flops, bytes_accessed=moved, transcendentals=exps),
    )


SCALARS = pl.BlockSpec(memory_space=pltpu.SMEM)
IN_HBM = pl.BlockSpec(memory_space=pltpu.HBM)
IN_VMEM = pl.BlockSpec(memory_space=pltpu.VMEM)


def tick_kernel(here_ref, out_ref):
    out_ref[0] = here_ref[0]


def tick(here, *earlier):
    return call(
        tick_kernel,
        [SCALARS],
        jax.ShapeDtypeStruct((1,), jnp.int32),
        SCALARS,
        flops=HIGH_COST,
    )(after(here, *earlier))


def list_heads(heads_ref, start, picks_ref, block, owner, slots):
    width = picks_ref.shape[0]
    spare = heads_ref.shape[0] - 1
    for slot in range(slots):
        heads_ref[start + slot] = -1
    valid = (block >= 0) & (block < width) & (owner >= 0) & (owner < width)
    row = jnp.clip(block, 0, width - 1)
    wanted = jnp.where(valid, owner, -2)
    found = jnp.int32(0)
    for pick in range(PICKS):
        for head in range(HEADS):
            hit = picks_ref[row, pick, head] == wanted
            heads_ref[jnp.where(hit, start + found, spare)] = head
            found = found + hit.astype(jnp.int32)


def pack_kernel(here_ref, picks_ref, *refs, jobs, slots):
    sources, outputs = refs[:3], refs[3 : 3 + len(jobs)]
    heads_ref, sems = refs[-2], refs[-1]
    here = here_ref[0]
    listed = {}
    for shift, first, count, is_near in jobs:
        key = (shift, is_near)
        if key not in listed:
            listed[key] = len(listed) * slots
            block, owner = (here + shift, here) if is_near else (here, here - shift)
            list_heads(heads_ref, listed[key], picks_ref, block, owner, slots)
    copies = []
    for (shift, first, count, is_near), output in zip(jobs, outputs):
        for slot in range(count):
            head = jnp.maximum(heads_ref[listed[shift, is_near] + first + slot], 0)
            columns = pl.ds(pl.multiple_of(head * HD, HD), HD)
            for place, source in enumerate(sources[1:] if is_near else sources[:1]):
                target = output.at[2 * slot + place if is_near else slot]
                copy = pltpu.make_async_copy(
                    source.at[:, columns], target, sems.at[len(copies)]
                )
                copy.start()
                copies.append(copy)
    for copy in copies:
        copy.wait()


def pack(here, picks, queries, keys, values, jobs, slots):
    rows = queries.shape[0]
    sizes = [2 * count if is_near else count for _, _, count, is_near in jobs]
    return call(
        functools.partial(pack_kernel, jobs=jobs, slots=slots),
        [SCALARS, SCALARS, IN_HBM, IN_HBM, IN_HBM],
        [jax.ShapeDtypeStruct((size, rows, HD), jnp.bfloat16) for size in sizes],
        [IN_HBM] * len(sizes),
        [pltpu.SMEM((len(jobs) * slots + 1,), jnp.int32), pltpu.SemaphoreType.DMA((sum(sizes),))],
        moved=4 * rows * HD * sum(sizes),
    )(here, picks, queries, keys, values)


def diagonal():
    shape = (LANES, LANES)
    return lax.broadcasted_iota(jnp.int32, shape, 0) == lax.broadcasted_iota(jnp.int32, shape, 1)


def raw_scores(query_rows, key_rows):
    return lax.dot_general(
        query_rows, key_rows, (((1,), (1,)), ((), ())), preferred_element_type=jnp.float32
    )


def with_ones(value_rows):
    return jnp.concatenate([value_rows, jnp.ones_like(value_rows)], axis=1)


def soft_part(scores, value_rows):
    top = jnp.max(scores, axis=1, keepdims=True)
    weights = jnp.exp2((scores - top) * EXP2_SCALE).astype(jnp.bfloat16)
    total = jnp.dot(weights, value_rows, preferred_element_type=jnp.float32)
    sums = total[:, HD:]
    return total[:, :HD] * pl.reciprocal(sums), top * EXP2_SCALE, sums


def across_lanes(column):
    eye = diagonal()
    spread = jnp.broadcast_to(column, (column.shape[0], LANES))
    return [
        jnp.sum(jnp.where(eye, spread[at : at + LANES], 0.0), axis=0, keepdims=True)
        for at in range(0, column.shape[0], LANES)
    ]


def down_rows(line):
    spread = jnp.broadcast_to(line, (LANES, LANES))
    return jnp.sum(jnp.where(diagonal(), spread, 0.0), axis=1, keepdims=True)


def three_parts(stats):
    first = stats.astype(jnp.bfloat16).astype(jnp.float32)
    second = (stats - first).astype(jnp.bfloat16).astype(jnp.float32)
    third = stats - first - second
    parts = jnp.concatenate([first, second, third], axis=0)
    pad = jnp.zeros((STAT_ROWS - parts.shape[0], LANES), jnp.float32)
    return jnp.concatenate([parts, pad], axis=0).astype(jnp.bfloat16)


def stats_of(block, groups):
    stats = block.astype(jnp.float32)
    return stats[:groups] + stats[groups : 2 * groups] + stats[2 * groups : 3 * groups]


def log_sums(tops, sums):
    top_lines = [line for top in tops for line in across_lanes(top)]
    sum_lines = [line for part in sums for line in across_lanes(part)]
    return jnp.concatenate(top_lines, axis=0) + jnp.log2(jnp.concatenate(sum_lines, axis=0))


def attend_rows(query_rows, key_rows, value_rows, tile):
    found = [
        soft_part(raw_scores(query_rows[at : at + tile], key_rows), value_rows)
        for at in range(0, query_rows.shape[0], tile)
    ]
    outputs, tops, sums = zip(*found)
    return jnp.concatenate(outputs, axis=0), log_sums(tops, sums)


def head_columns(head):
    return pl.ds(pl.multiple_of(head * HD, HD), HD)


def attend_kernel(here_ref, picks_ref, key_ref, value_ref, *refs, group, slots):
    heads_ref = refs[-1]
    here = here_ref[0]
    for number, (shift, first, count) in enumerate(group):
        query_ref, out_ref = refs[number], refs[len(group) + number]
        rows = query_ref.shape[1]
        list_heads(heads_ref, 0, picks_ref, here + shift, here, slots)
        for slot in range(count):
            columns = head_columns(jnp.maximum(heads_ref[first + slot], 0))
            outputs, lines = attend_rows(
                query_ref[slot], key_ref[:, columns], with_ones(value_ref[:, columns]), rows
            )
            out_ref[slot, :rows, :] = outputs.astype(jnp.bfloat16)
            out_ref[slot, rows:, :] = three_parts(lines)


def attend(here, picks, keys, values, arrived, group, slots):
    rows = keys.shape[0]
    total = sum(count for _, _, count in group)
    return call(
        functools.partial(attend_kernel, group=group, slots=slots),
        [SCALARS, SCALARS, IN_VMEM, IN_VMEM] + [IN_VMEM] * len(group),
        [
            jax.ShapeDtypeStruct((count, rows + STAT_ROWS, HD), jnp.bfloat16)
            for _, _, count in group
        ],
        [IN_VMEM] * len(group),
        [pltpu.SMEM((slots + 1,), jnp.int32)],
        flops=4 * total * rows * rows * HD,
        moved=8 * total * rows * HD,
        exps=total * rows * rows,
    )(here, picks, keys, values, *arrived)


def own_kernel(here_ref, query_ref, key_ref, value_ref, out_ref):
    rows = query_ref.shape[0]
    tile = min(rows, 256)

    def one_head(head, carry):
        columns = head_columns(head)
        value_rows = with_ones(value_ref[:, columns])
        tops, all_sums = [], []
        for at in range(0, rows, tile):
            reach = at + tile
            scores = raw_scores(query_ref[at:reach, columns], key_ref[:reach, columns])
            row_ids = lax.broadcasted_iota(jnp.int32, scores.shape, 0) + at
            seen = row_ids >= lax.broadcasted_iota(jnp.int32, scores.shape, 1)
            outputs, top, sums = soft_part(jnp.where(seen, scores, -jnp.inf), value_rows[:reach])
            out_ref[head, at:reach, :] = outputs.astype(jnp.bfloat16)
            tops.append(top)
            all_sums.append(sums)
        out_ref[head, rows:, :] = three_parts(log_sums(tops, all_sums))
        return carry

    lax.fori_loop(0, HEADS, one_head, 0, unroll=4)


def own_part(here, queries, keys, values):
    rows = queries.shape[0]
    return call(
        own_kernel,
        [SCALARS, IN_VMEM, IN_VMEM, IN_VMEM],
        jax.ShapeDtypeStruct((HEADS, rows + STAT_ROWS, HD), jnp.bfloat16),
        IN_VMEM,
        flops=4 * HEADS * rows * rows * HD,
        moved=8 * HEADS * rows * HD,
        exps=HEADS * rows * rows,
    )(here, queries, keys, values)


def near_kernel(here_ref, picks_ref, query_ref, own_ref, near_ref, out_ref, heads_ref, *, shift, slots):
    rows = query_ref.shape[0]
    here = here_ref[0]
    list_heads(heads_ref, 0, picks_ref, here, here - shift, slots)
    for head in range(HEADS):
        out_ref[head] = own_ref[head]
    for slot in range(slots):
        columns = head_columns(jnp.maximum(heads_ref[slot], 0))
        outputs, lines = attend_rows(
            query_ref[:, columns], near_ref[2 * slot], with_ones(near_ref[2 * slot + 1]), rows
        )
        out_ref[HEADS + slot, :rows, :] = outputs.astype(jnp.bfloat16)
        out_ref[HEADS + slot, rows:, :] = three_parts(lines)


def add_near(here, picks, queries, own, near, shift, slots):
    rows = queries.shape[0]
    return call(
        functools.partial(near_kernel, shift=shift, slots=slots),
        [SCALARS, SCALARS, IN_VMEM, IN_VMEM, IN_VMEM],
        jax.ShapeDtypeStruct((HEADS + slots,) + own.shape[1:], own.dtype),
        IN_VMEM,
        [pltpu.SMEM((slots + 1,), jnp.int32)],
        flops=HIGH_COST,
        moved=12 * slots * rows * HD,
        exps=slots * rows * rows,
    )(here, picks, queries, own, near)


def find_spots(spots_ref, found_ref, picks_ref, here, shifts, slots):
    for owner in range(picks_ref.shape[0]):
        found_ref[owner] = 0

    for pick in range(PICKS):
        for head in range(HEADS):
            owner = picks_ref[here, pick, head]
            safe = jnp.maximum(owner, 0)
            order = found_ref[safe]
            found_ref[safe] = order + (owner >= 0).astype(jnp.int32)
            spot = jnp.int32(-1)
            for place, shift in enumerate(shifts):
                spot = jnp.where(here - safe == shift, place * slots + order, spot)
            spots_ref[head * PICKS + pick] = jnp.where(owner >= 0, spot, -1)


def merge_kernel(here_ref, picks_ref, *refs, places, shifts, slots):
    count = len(places)
    parts = refs[:count]
    out_ref, sums_ref, held, spots_ref, found_ref, sems = refs[count:]
    groups = sums_ref.shape[1]
    rows = groups * LANES
    copies = [
        pltpu.make_async_copy(part, held.at[pl.ds(place, part.shape[0])], sems.at[number])
        for number, (part, place) in enumerate(zip(parts, places))
    ]
    for copy in copies:
        copy.start()
    find_spots(spots_ref, found_ref, picks_ref, here_ref[0], shifts, slots)
    for copy in copies:
        copy.wait()

    def one_head(head, carry):
        found = [spots_ref[head * PICKS + pick] for pick in range(PICKS)]
        spots = [head] + [jnp.where(spot >= 0, HEADS + spot, head) for spot in found]
        sums = [stats_of(held[spot, rows:, :], groups) for spot in spots]
        for pick, spot in enumerate(found):
            sums[1 + pick] = jnp.where(spot >= 0, sums[1 + pick], -jnp.inf)
        top = functools.reduce(jnp.maximum, sums)
        shares = [jnp.exp2(part - top) for part in sums]
        whole = functools.reduce(jnp.add, shares)
        sums_ref[head] = top + jnp.log2(whole)
        for group in range(groups):
            span = pl.ds(group * LANES, LANES)
            own = held[head, span, :].astype(jnp.float32)
            mixed = own
            for spot, share in zip(spots[1:], shares[1:]):
                weight = down_rows((share / whole)[group : group + 1, :])
                mixed = mixed + (held[spot, span, :].astype(jnp.float32) - own) * weight
            out_ref[head, span, :] = mixed
        return carry

    lax.fori_loop(0, HEADS, one_head, 0, unroll=2)


def merge(here, picks, parts, places, shifts, slots):
    rows = parts[0].shape[1] - STAT_ROWS
    width = picks.shape[0]
    total = HEADS + len(shifts) * slots
    return call(
        functools.partial(merge_kernel, places=tuple(places), shifts=shifts, slots=slots),
        [SCALARS, SCALARS] + [pl.BlockSpec(memory_space=pl.ANY)] * len(parts),
        [
            jax.ShapeDtypeStruct((HEADS, rows, HD), jnp.float32),
            jax.ShapeDtypeStruct((HEADS, rows // LANES, LANES), jnp.float32),
        ],
        [IN_VMEM, IN_VMEM],
        [
            pltpu.VMEM((total, rows + STAT_ROWS, HD), jnp.bfloat16),
            pltpu.SMEM((PICKS * HEADS,), jnp.int32),
            pltpu.SMEM((width,), jnp.int32),
            pltpu.SemaphoreType.DMA((len(parts),)),
        ],
        flops=HIGH_COST,
        moved=2 * (HEADS * 2 + total) * rows * HD,
    )(here, picks, *parts)


def finish_kernel(
    here_ref, picks_ref, mixed_ref, sums_ref, part_ref, out_ref, spots_ref, found_ref, *, shift, slots
):
    groups = sums_ref.shape[1]
    rows = groups * LANES
    step = pl.program_id(0)
    per_step = HEADS // pl.num_programs(0)

    @pl.when(step == 0)
    def _():
        find_spots(spots_ref, found_ref, picks_ref, here_ref[0], (shift,), slots)

    for place in range(per_step):
        head = step * per_step + place
        spot = jnp.maximum(spots_ref[head * PICKS], spots_ref[head * PICKS + 1])
        columns = pl.ds(place * HD, HD)

        @pl.when(spot < 0)
        def _():
            out_ref[:, columns] = mixed_ref[head].astype(jnp.bfloat16)

        @pl.when(spot >= 0)
        def _():
            before = sums_ref[head]
            added = stats_of(part_ref[spot, rows:, :], groups)
            share = 1.0 / (1.0 + jnp.exp2(before - added))
            for group in range(groups):
                span = pl.ds(group * LANES, LANES)
                old = mixed_ref[head, span, :]
                new = part_ref[spot, span, :].astype(jnp.float32)
                mixed = old + (new - old) * down_rows(share[group : group + 1, :])
                out_ref[span, columns] = mixed.astype(jnp.bfloat16)


def finish(here, picks, mixed, sums, part, shift, slots):
    heads, rows, _ = mixed.shape
    width = picks.shape[0]
    steps = 4
    return pl.pallas_call(
        functools.partial(finish_kernel, shift=shift, slots=slots),
        grid=(steps,),
        in_specs=[SCALARS, SCALARS, IN_VMEM, IN_VMEM, IN_VMEM],
        out_specs=pl.BlockSpec((rows, heads // steps * HD), lambda step: (0, step)),
        out_shape=jax.ShapeDtypeStruct((rows, heads * HD), jnp.bfloat16),
        scratch_shapes=[
            pltpu.SMEM((PICKS * HEADS,), jnp.int32),
            pltpu.SMEM((width,), jnp.int32),
        ],
        compiler_params=pltpu.CompilerParams(vmem_limit_bytes=VMEM_BYTES),
        cost_estimate=pl.CostEstimate(
            flops=2 * heads * rows * HD, bytes_accessed=8 * heads * rows * HD, transcendentals=0
        ),
    )(here, picks, mixed, sums, part)


def after(value, *earlier):
    return lax.optimization_barrier((value,) + earlier)[0]


def groups_in_order(width, slots):
    middle = width // 2
    groups = [[(1, 0, slots)], [(shift, 0, slots) for shift in (width - 2, width - 1)]]
    for low in range(3, middle):
        size = max(1, slots // 2)
        for first in range(0, slots, size):
            count = min(size, slots - first)
            groups.append([(low, first, count), (width - low, first, count)])
    return groups + [[(middle, 0, slots)]]


def travelling_queries(queries, keys, values, picks):
    width = lax.axis_size("ctx")
    sections = lax.axis_size("pipe")
    slots = max(1, PICKS * HEADS // width)
    here = lax.axis_index("ctx").astype(jnp.int32).reshape(1)
    queries, keys, values = queries[0], keys[0], values[0]
    own_picks = picks[0].transpose(0, 2, 1)

    groups = groups_in_order(width, slots)
    near_shifts = (2,)
    first_jobs = [(shift, 0, slots, True) for shift in near_shifts]
    first_jobs += [piece + (False,) for group in groups[:2] for piece in group]
    later_jobs = [piece + (False,) for group in groups[2:] for piece in group]

    def up(value, shift):
        return lax.ppermute(value, "ctx", [(at, at + shift) for at in range(width - shift)])

    def down(value, shift):
        return lax.ppermute(value, "ctx", [(at, at - shift) for at in range(shift, width)])

    def up_and_on(value, shift):
        pairs = [
            (at * sections + section, (at + shift) * sections + (section + 1) % sections)
            for at in range(width - shift)
            for section in range(sections)
        ]
        return lax.ppermute(value, ("ctx", "pipe"), pairs)

    sends = dict(zip(first_jobs, pack(here, own_picks, queries, keys, values, first_jobs, slots)))
    near = [up(sends[job], job[0]) for job in first_jobs if job[3]]
    arrived = {
        piece: down(sends[piece + (False,)], piece[0]) for group in groups[:2] for piece in group
    }
    before = passed_along(own_picks, "pipe", 1)
    now = after(here, *[sends[job] for job in first_jobs])
    sends |= zip(later_jobs, pack(now, own_picks, queries, keys, values, later_jobs, slots))

    def attend_group(token, group):
        return dict(
            zip(
                group,
                attend(
                    token,
                    own_picks,
                    keys,
                    values,
                    [arrived[piece] for piece in group],
                    tuple(group),
                    slots,
                ),
            )
        )

    def ask_for(group, *earlier):
        for piece in group:
            arrived[piece] = down(after(sends[piece + (False,)], *earlier), piece[0])

    def send_back(parts, *earlier):
        for piece, part in parts.items():
            returned[piece] = up_and_on(after(part, *earlier) if earlier else part, piece[0])

    def those(found, group):
        return [found[piece] for piece in group]

    returned = {}
    own = own_part(after(here, before, sends[later_jobs[0]]), queries, keys, values)
    parts = attend_group(after(here, own), groups[0])
    send_back(parts)
    parts = attend_group(after(here, *parts.values(), *near), groups[1])
    send_back(parts)
    ask_for(groups[2], *parts.values(), *arrived.values())
    now = after(here, *parts.values())
    before_last = groups[0] + groups[1]
    for number in range(2, len(groups)):
        group = groups[number]
        if number == len(groups) - 1:
            now = tick(now, *those(returned, groups[number - 2]))
            now = after(now, own_back)
        parts = attend_group(now, group)
        if number == 2:
            ask_for(groups[number + 1], *parts.values(), *those(arrived, group))
        send_back(parts, *those(returned, before_last))
        now = after(now, *parts.values())
        if number == 2:
            now = after(now, *those(returned, before_last))
            own = add_near(now, own_picks, queries, own, near[0], near_shifts[0], slots)
            own_back = passed_along(own, "pipe", 1)
            now = after(now, own)
        if 2 <= number < len(groups) - 2:
            ask_for(groups[number + 2], now, *those(arrived, groups[number + 1]))
        before_last = group
    now = after(now, *those(returned, groups[-2]))

    final = groups[-1][0]
    others = [shift for shift in range(1, width) if shift not in near_shifts + final[:1]]
    merged_shifts = near_shifts + tuple(others)
    pieces = [piece for piece in returned if piece != final]
    places = [HEADS + merged_shifts.index(shift) * slots + first for shift, first, _ in pieces]
    parts = [own_back] + [returned[piece] for piece in pieces]
    mixed, sums = merge(now, before, parts, [0] + places, merged_shifts, slots)
    return finish(now, before, mixed, sums, returned[final], final[0], slots)[None]


def travelling_keys(queries, keys, values, picks):
    ctx_width = lax.axis_size("ctx")
    rank_here = lax.axis_index("ctx")
    slot_count = max(1, PICKS * HEADS // ctx_width)
    block_rows = queries.shape[1]
    score_scale = HD ** (-0.5)
    every_pick = picks[0].reshape(ctx_width, HEADS * PICKS)
    chosen = lax.dynamic_slice_in_dim(every_pick, rank_here, 1, 0)
    pick_order = request_table(chosen, lax.iota(jnp.int32, ctx_width), slot_count)[1]
    asked_table = request_table(every_pick, rank_here.reshape(1), slot_count)[0]
    asked_heads = asked_table[:, 0, :]
    safe_asked = jnp.maximum(asked_heads, 0)
    query_heads = queries[0].reshape(block_rows, HEADS, HD).transpose(1, 0, 2)
    key_heads = keys[0].reshape(block_rows, HEADS, HD).transpose(1, 0, 2)
    value_heads = values[0].reshape(block_rows, HEADS, HD).transpose(1, 0, 2)
    is_live = chosen[0] >= 0
    flat_slot = jnp.where(is_live, chosen[0] * slot_count + pick_order[0], 0)
    remote_mask = jnp.repeat(is_live.reshape(HEADS, PICKS), block_rows, axis=1)
    row_index = lax.iota(jnp.int32, block_rows)
    causal = row_index[:, None] >= row_index[None, :]

    def masked_scores(query_head, key_rows, mask_row):
        scores = lax.dot_general(
            query_head, key_rows, (((1,), (1,)), ((), ())), preferred_element_type=jnp.float32
        )
        allowed = jnp.concatenate(
            [causal, jnp.broadcast_to(mask_row[None, :], (block_rows, PICKS * block_rows))], axis=1
        )
        return jnp.where(allowed, scores * score_scale, -jnp.inf)

    def row_stats(scores):
        row_top = jnp.max(scores, axis=1)
        row_total = jnp.sum(jnp.exp(scores - row_top[:, None]), axis=1)
        return (row_top, row_total)

    def weighted(scores, row_top, row_total, value_rows):
        prob_rows = (jnp.exp(scores - row_top[:, None]) / row_total[:, None]).astype(jnp.bfloat16)
        return jnp.dot(prob_rows, value_rows, preferred_element_type=jnp.float32).astype(
            jnp.bfloat16
        )

    send_both = jnp.concatenate([key_heads, value_heads], axis=2)[safe_asked]
    got_slots = lax.all_to_all(send_both, "ctx", split_axis=0, concat_axis=0, tiled=True)
    last_width = 2 * HD
    flat_slots = got_slots.reshape(ctx_width * slot_count, block_rows, last_width)
    remote_both = flat_slots[flat_slot].reshape(HEADS, PICKS * block_rows, last_width)
    all_keys = jnp.concatenate([key_heads, remote_both[:, :, :HD]], axis=1)
    all_values = jnp.concatenate([value_heads, remote_both[:, :, HD:]], axis=1)

    def per_head(head_items):
        query_head, key_rows, value_rows, mask_row = head_items
        scores = masked_scores(query_head, key_rows, mask_row)
        row_top, row_total = row_stats(scores)
        return weighted(scores, row_top, row_total, value_rows)

    outputs = lax.map(per_head, (query_heads, all_keys, all_values, remote_mask))
    merged = outputs.transpose(1, 0, 2).reshape(1, block_rows, HEADS * HD)
    return passed_along(merged, "pipe", 1)


def per_device(queries, keys, values, picks):
    few_shifts = 8 <= lax.axis_size("ctx") <= 16
    run = travelling_queries if few_shifts else travelling_keys
    return run(queries, keys, values, picks)


def solution(mesh):
    placed = (
        P("pipe", "ctx", None),
        P("pipe", "ctx", None),
        P("pipe", "ctx", None),
        P("pipe", None, None, None),
    )
    return jax.shard_map(
        per_device, mesh=mesh, in_specs=placed, out_specs=P("pipe", "ctx", None), check_vma=False
    )
```

```python
import functools
import math

import jax
import jax.numpy as jnp
from jax import lax
from jax.experimental import pallas as pl
from jax.experimental.pallas import tpu as pltpu
from jax.sharding import PartitionSpec as P

HEADS = 16
HD = 128
PICKS = 2
EXP2_SCALE = HD ** -0.5 * math.log2(math.e)
LANES = 128
STAT_ROWS = 16
VMEM_BYTES = 24 * 1024 * 1024
ALL_VMEM_BYTES = 62 * 1024 * 1024
HIGH_COST = 10**12


def passed_along(value, axis, steps):
    count = lax.axis_size(axis)
    pairs = [(source, (source + steps) % count) for source in range(count)]
    return lax.ppermute(value, axis, pairs)


def request_table(chosen, owners, slot_count):
    pick_count = chosen.shape[1]
    pick_ids = lax.iota(jnp.int32, pick_count)
    is_live = chosen >= 0
    earlier = pick_ids[None, :] < pick_ids[:, None]
    same_owner = (chosen[:, :, None] == chosen[:, None, :]) & earlier[None]
    pick_order = jnp.sum(same_owner.astype(jnp.int32), axis=2)
    head_ids = pick_ids // PICKS
    slot_ranks = lax.iota(jnp.int32, slot_count)
    matches = (
        is_live[:, None, None, :]
        & (chosen[:, None, None, :] == owners[None, :, None, None])
        & (pick_order[:, None, None, :] == slot_ranks[None, None, :, None])
    )
    was_found = jnp.any(matches, axis=3)
    head_table = jnp.sum(jnp.where(matches, head_ids[None, None, None, :], 0), axis=3)
    return (jnp.where(was_found, head_table, -1), pick_order)


def call(
    kernel, name_space, outputs, out_specs, scratch=(), flops=0, moved=0, exps=0, vmem=VMEM_BYTES
):
    return pl.pallas_call(
        kernel,
        in_specs=name_space,
        out_specs=out_specs,
        out_shape=outputs,
        scratch_shapes=list(scratch),
        compiler_params=pltpu.CompilerParams(vmem_limit_bytes=vmem),
        cost_estimate=pl.CostEstimate(flops=flops, bytes_accessed=moved, transcendentals=exps),
    )


SCALARS = pl.BlockSpec(memory_space=pltpu.SMEM)
IN_HBM = pl.BlockSpec(memory_space=pltpu.HBM)
IN_VMEM = pl.BlockSpec(memory_space=pltpu.VMEM)


def tick_kernel(here_ref, out_ref):
    out_ref[0] = here_ref[0]


def tick(here, *earlier):
    return call(
        tick_kernel,
        [SCALARS],
        jax.ShapeDtypeStruct((1,), jnp.int32),
        SCALARS,
        flops=HIGH_COST,
    )(after(here, *earlier))


def list_heads(heads_ref, start, picks_ref, block, owner, slots):
    width = picks_ref.shape[0]
    spare = heads_ref.shape[0] - 1
    for slot in range(slots):
        heads_ref[start + slot] = -1
    valid = (block >= 0) & (block < width) & (owner >= 0) & (owner < width)
    row = jnp.clip(block, 0, width - 1)
    wanted = jnp.where(valid, owner, -2)
    found = jnp.int32(0)
    for pick in range(PICKS):
        for head in range(HEADS):
            hit = picks_ref[row, pick, head] == wanted
            heads_ref[jnp.where(hit, start + found, spare)] = head
            found = found + hit.astype(jnp.int32)


def pack_kernel(here_ref, picks_ref, *refs, jobs, slots):
    sources, outputs = refs[:3], refs[3 : 3 + len(jobs)]
    heads_ref, sems = refs[-2], refs[-1]
    here = here_ref[0]
    listed = {}
    for shift, first, count, is_near in jobs:
        key = (shift, is_near)
        if key not in listed:
            listed[key] = len(listed) * slots
            block, owner = (here + shift, here) if is_near else (here, here - shift)
            list_heads(heads_ref, listed[key], picks_ref, block, owner, slots)
    copies = []
    for (shift, first, count, is_near), output in zip(jobs, outputs):
        for slot in range(count):
            head = jnp.maximum(heads_ref[listed[shift, is_near] + first + slot], 0)
            columns = pl.ds(pl.multiple_of(head * HD, HD), HD)
            for place, source in enumerate(sources[1:] if is_near else sources[:1]):
                target = output.at[2 * slot + place if is_near else slot]
                copy = pltpu.make_async_copy(
                    source.at[:, columns], target, sems.at[len(copies)]
                )
                copy.start()
                copies.append(copy)
    for copy in copies:
        copy.wait()


def pack(here, picks, queries, keys, values, jobs, slots):
    rows = queries.shape[0]
    sizes = [2 * count if is_near else count for _, _, count, is_near in jobs]
    return call(
        functools.partial(pack_kernel, jobs=jobs, slots=slots),
        [SCALARS, SCALARS, IN_HBM, IN_HBM, IN_HBM],
        [jax.ShapeDtypeStruct((size, rows, HD), jnp.bfloat16) for size in sizes],
        [IN_HBM] * len(sizes),
        [pltpu.SMEM((len(jobs) * slots + 1,), jnp.int32), pltpu.SemaphoreType.DMA((sum(sizes),))],
        moved=4 * rows * HD * sum(sizes),
        vmem=ALL_VMEM_BYTES,
    )(here, picks, queries, keys, values)


def diagonal():
    shape = (LANES, LANES)
    return lax.broadcasted_iota(jnp.int32, shape, 0) == lax.broadcasted_iota(jnp.int32, shape, 1)


def raw_scores(query_rows, key_rows):
    return lax.dot_general(
        query_rows, key_rows, (((1,), (1,)), ((), ())), preferred_element_type=jnp.float32
    )


def with_ones(value_rows):
    return jnp.concatenate([value_rows, jnp.ones_like(value_rows)], axis=1)


def soft_part(scores, value_rows):
    top = jnp.max(scores, axis=1, keepdims=True)
    weights = jnp.exp2((scores - top) * EXP2_SCALE).astype(jnp.bfloat16)
    total = jnp.dot(weights, value_rows, preferred_element_type=jnp.float32)
    sums = total[:, HD:]
    return total[:, :HD] * pl.reciprocal(sums), top * EXP2_SCALE, sums


def across_lanes(column):
    eye = diagonal()
    spread = jnp.broadcast_to(column, (column.shape[0], LANES))
    return [
        jnp.sum(jnp.where(eye, spread[at : at + LANES], 0.0), axis=0, keepdims=True)
        for at in range(0, column.shape[0], LANES)
    ]


def down_rows(line):
    spread = jnp.broadcast_to(line, (LANES, LANES))
    return jnp.sum(jnp.where(diagonal(), spread, 0.0), axis=1, keepdims=True)


def three_parts(stats):
    first = stats.astype(jnp.bfloat16).astype(jnp.float32)
    second = (stats - first).astype(jnp.bfloat16).astype(jnp.float32)
    third = stats - first - second
    parts = jnp.concatenate([first, second, third], axis=0)
    pad = jnp.zeros((STAT_ROWS - parts.shape[0], LANES), jnp.float32)
    return jnp.concatenate([parts, pad], axis=0).astype(jnp.bfloat16)


def stats_of(block, groups):
    stats = block.astype(jnp.float32)
    return stats[:groups] + stats[groups : 2 * groups] + stats[2 * groups : 3 * groups]


def log_sums(tops, sums):
    top_lines = [line for top in tops for line in across_lanes(top)]
    sum_lines = [line for part in sums for line in across_lanes(part)]
    return jnp.concatenate(top_lines, axis=0) + jnp.log2(jnp.concatenate(sum_lines, axis=0))


def attend_rows(query_rows, key_rows, value_rows, tile):
    found = [
        soft_part(raw_scores(query_rows[at : at + tile], key_rows), value_rows)
        for at in range(0, query_rows.shape[0], tile)
    ]
    outputs, tops, sums = zip(*found)
    return jnp.concatenate(outputs, axis=0), log_sums(tops, sums)


def head_columns(head):
    return pl.ds(pl.multiple_of(head * HD, HD), HD)


def attend_kernel(here_ref, picks_ref, key_ref, value_ref, *refs, group, slots):
    heads_ref = refs[-1]
    here = here_ref[0]
    for number, (shift, first, count) in enumerate(group):
        query_ref, out_ref = refs[number], refs[len(group) + number]
        rows = query_ref.shape[1]
        list_heads(heads_ref, 0, picks_ref, here + shift, here, slots)
        for slot in range(count):
            columns = head_columns(jnp.maximum(heads_ref[first + slot], 0))
            outputs, lines = attend_rows(
                query_ref[slot], key_ref[:, columns], with_ones(value_ref[:, columns]), rows
            )
            out_ref[slot, :rows, :] = outputs.astype(jnp.bfloat16)
            out_ref[slot, rows:, :] = three_parts(lines)


def attend(here, picks, keys, values, arrived, group, slots, is_anchor):
    rows = keys.shape[0]
    total = sum(count for _, _, count in group)
    return call(
        functools.partial(attend_kernel, group=group, slots=slots),
        [SCALARS, SCALARS, IN_VMEM, IN_VMEM] + [IN_VMEM] * len(group),
        [
            jax.ShapeDtypeStruct((count, rows + STAT_ROWS, HD), jnp.bfloat16)
            for _, _, count in group
        ],
        [IN_VMEM] * len(group),
        [pltpu.SMEM((slots + 1,), jnp.int32)],
        flops=HIGH_COST if is_anchor else 4 * total * rows * rows * HD,
        moved=8 * total * rows * HD,
        exps=total * rows * rows,
    )(here, picks, keys, values, *arrived)


def own_kernel(here_ref, query_ref, key_ref, value_ref, out_ref):
    rows = query_ref.shape[0]
    tile = min(rows, 256)

    def one_head(head, carry):
        columns = head_columns(head)
        value_rows = with_ones(value_ref[:, columns])
        tops, all_sums = [], []
        for at in range(0, rows, tile):
            reach = at + tile
            scores = raw_scores(query_ref[at:reach, columns], key_ref[:reach, columns])
            row_ids = lax.broadcasted_iota(jnp.int32, scores.shape, 0) + at
            seen = row_ids >= lax.broadcasted_iota(jnp.int32, scores.shape, 1)
            outputs, top, sums = soft_part(jnp.where(seen, scores, -jnp.inf), value_rows[:reach])
            out_ref[head, at:reach, :] = outputs.astype(jnp.bfloat16)
            tops.append(top)
            all_sums.append(sums)
        out_ref[head, rows:, :] = three_parts(log_sums(tops, all_sums))
        return carry

    lax.fori_loop(0, HEADS, one_head, 0, unroll=4)


def own_part(here, queries, keys, values):
    rows = queries.shape[0]
    return call(
        own_kernel,
        [SCALARS, IN_VMEM, IN_VMEM, IN_VMEM],
        jax.ShapeDtypeStruct((HEADS, rows + STAT_ROWS, HD), jnp.bfloat16),
        IN_VMEM,
        flops=4 * HEADS * rows * rows * HD,
        moved=8 * HEADS * rows * HD,
        exps=HEADS * rows * rows,
    )(here, queries, keys, values)


def near_kernel(here_ref, picks_ref, query_ref, own_ref, near_ref, out_ref, heads_ref, *, shift, slots):
    rows = query_ref.shape[0]
    here = here_ref[0]
    list_heads(heads_ref, 0, picks_ref, here, here - shift, slots)
    for head in range(HEADS):
        out_ref[head] = own_ref[head]
    for slot in range(slots):
        columns = head_columns(jnp.maximum(heads_ref[slot], 0))
        outputs, lines = attend_rows(
            query_ref[:, columns], near_ref[2 * slot], with_ones(near_ref[2 * slot + 1]), rows
        )
        out_ref[HEADS + slot, :rows, :] = outputs.astype(jnp.bfloat16)
        out_ref[HEADS + slot, rows:, :] = three_parts(lines)


def add_near(here, picks, queries, own, near, shift, slots):
    rows = queries.shape[0]
    return call(
        functools.partial(near_kernel, shift=shift, slots=slots),
        [SCALARS, SCALARS, IN_VMEM, IN_VMEM, IN_VMEM],
        jax.ShapeDtypeStruct((HEADS + slots,) + own.shape[1:], own.dtype),
        IN_VMEM,
        [pltpu.SMEM((slots + 1,), jnp.int32)],
        flops=HIGH_COST,
        moved=12 * slots * rows * HD,
        exps=slots * rows * rows,
    )(here, picks, queries, own, near)


def find_spots(spots_ref, found_ref, picks_ref, here, shifts, slots):
    for owner in range(picks_ref.shape[0]):
        found_ref[owner] = 0

    for pick in range(PICKS):
        for head in range(HEADS):
            owner = picks_ref[here, pick, head]
            safe = jnp.maximum(owner, 0)
            order = found_ref[safe]
            found_ref[safe] = order + (owner >= 0).astype(jnp.int32)
            spot = jnp.int32(-1)
            for place, shift in enumerate(shifts):
                spot = jnp.where(here - safe == shift, place * slots + order, spot)
            spots_ref[head * PICKS + pick] = jnp.where(owner >= 0, spot, -1)


def merge_kernel(here_ref, picks_ref, *refs, places, shifts, slots):
    count = len(places)
    parts = refs[:count]
    out_ref, sums_ref, held, spots_ref, found_ref, sems = refs[count:]
    groups = sums_ref.shape[1]
    rows = groups * LANES
    copies = [
        pltpu.make_async_copy(part, held.at[pl.ds(place, part.shape[0])], sems.at[number])
        for number, (part, place) in enumerate(zip(parts, places))
    ]
    for copy in copies:
        copy.start()
    find_spots(spots_ref, found_ref, picks_ref, here_ref[0], shifts, slots)
    for copy in copies:
        copy.wait()

    def one_head(head, carry):
        found = [spots_ref[head * PICKS + pick] for pick in range(PICKS)]
        spots = [head] + [jnp.where(spot >= 0, HEADS + spot, head) for spot in found]
        sums = [stats_of(held[spot, rows:, :], groups) for spot in spots]
        for pick, spot in enumerate(found):
            sums[1 + pick] = jnp.where(spot >= 0, sums[1 + pick], -jnp.inf)
        top = functools.reduce(jnp.maximum, sums)
        shares = [jnp.exp2(part - top) for part in sums]
        whole = functools.reduce(jnp.add, shares)
        sums_ref[head] = top + jnp.log2(whole)
        for group in range(groups):
            span = pl.ds(group * LANES, LANES)
            own = held[head, span, :].astype(jnp.float32)
            mixed = own
            for spot, share in zip(spots[1:], shares[1:]):
                weight = down_rows((share / whole)[group : group + 1, :])
                mixed = mixed + (held[spot, span, :].astype(jnp.float32) - own) * weight
            out_ref[head, span, :] = mixed
        return carry

    lax.fori_loop(0, HEADS, one_head, 0, unroll=2)


def merge(here, picks, parts, places, shifts, slots):
    rows = parts[0].shape[1] - STAT_ROWS
    width = picks.shape[0]
    total = HEADS + len(shifts) * slots
    return call(
        functools.partial(merge_kernel, places=tuple(places), shifts=shifts, slots=slots),
        [SCALARS, SCALARS] + [pl.BlockSpec(memory_space=pl.ANY)] * len(parts),
        [
            jax.ShapeDtypeStruct((HEADS, rows, HD), jnp.float32),
            jax.ShapeDtypeStruct((HEADS, rows // LANES, LANES), jnp.float32),
        ],
        [IN_VMEM, IN_VMEM],
        [
            pltpu.VMEM((total, rows + STAT_ROWS, HD), jnp.bfloat16),
            pltpu.SMEM((PICKS * HEADS,), jnp.int32),
            pltpu.SMEM((width,), jnp.int32),
            pltpu.SemaphoreType.DMA((len(parts),)),
        ],
        flops=HIGH_COST,
        moved=2 * (HEADS * 2 + total) * rows * HD,
    )(here, picks, *parts)


def finish_kernel(
    here_ref, picks_ref, mixed_ref, sums_ref, part_ref, out_ref, spots_ref, found_ref, *, shift, slots
):
    groups = sums_ref.shape[1]
    rows = groups * LANES
    step = pl.program_id(0)
    per_step = HEADS // pl.num_programs(0)

    @pl.when(step == 0)
    def _():
        find_spots(spots_ref, found_ref, picks_ref, here_ref[0], (shift,), slots)

    for place in range(per_step):
        head = step * per_step + place
        spot = jnp.maximum(spots_ref[head * PICKS], spots_ref[head * PICKS + 1])
        columns = pl.ds(place * HD, HD)

        @pl.when(spot < 0)
        def _():
            out_ref[:, columns] = mixed_ref[head].astype(jnp.bfloat16)

        @pl.when(spot >= 0)
        def _():
            before = sums_ref[head]
            added = stats_of(part_ref[spot, rows:, :], groups)
            share = 1.0 / (1.0 + jnp.exp2(before - added))
            for group in range(groups):
                span = pl.ds(group * LANES, LANES)
                old = mixed_ref[head, span, :]
                new = part_ref[spot, span, :].astype(jnp.float32)
                mixed = old + (new - old) * down_rows(share[group : group + 1, :])
                out_ref[span, columns] = mixed.astype(jnp.bfloat16)


def finish(here, picks, mixed, sums, part, shift, slots):
    heads, rows, _ = mixed.shape
    width = picks.shape[0]
    steps = 4
    return pl.pallas_call(
        functools.partial(finish_kernel, shift=shift, slots=slots),
        grid=(steps,),
        in_specs=[SCALARS, SCALARS, IN_VMEM, IN_VMEM, IN_VMEM],
        out_specs=pl.BlockSpec((rows, heads // steps * HD), lambda step: (0, step)),
        out_shape=jax.ShapeDtypeStruct((rows, heads * HD), jnp.bfloat16),
        scratch_shapes=[
            pltpu.SMEM((PICKS * HEADS,), jnp.int32),
            pltpu.SMEM((width,), jnp.int32),
        ],
        compiler_params=pltpu.CompilerParams(vmem_limit_bytes=VMEM_BYTES),
        cost_estimate=pl.CostEstimate(
            flops=2 * heads * rows * HD, bytes_accessed=8 * heads * rows * HD, transcendentals=0
        ),
    )(here, picks, mixed, sums, part)


def after(value, *earlier):
    return lax.optimization_barrier((value,) + earlier)[0]


def groups_in_order(width, slots):
    middle = width // 2
    groups = [[(1, 0, slots)], [(shift, 0, slots) for shift in (width - 2, width - 1)]]
    for low in range(3, middle):
        size = max(1, slots // 2)
        for first in range(0, slots, size):
            count = min(size, slots - first)
            groups.append([(low, first, count), (width - low, first, count)])
    return groups + [[(middle, 0, slots)]]


def travelling_queries(queries, keys, values, picks):
    width = lax.axis_size("ctx")
    sections = lax.axis_size("pipe")
    slots = max(1, PICKS * HEADS // width)
    here = lax.axis_index("ctx").astype(jnp.int32).reshape(1)
    queries, keys, values = queries[0], keys[0], values[0]
    own_picks = picks[0].transpose(0, 2, 1)

    groups = groups_in_order(width, slots)
    near_shifts = (2,)
    first_jobs = [(shift, 0, slots, True) for shift in near_shifts]
    first_jobs += [piece + (False,) for group in groups[:2] for piece in group]
    later_jobs = [piece + (False,) for group in groups[2:] for piece in group]

    def up(value, shift):
        return lax.ppermute(value, "ctx", [(at, at + shift) for at in range(width - shift)])

    def down(value, shift):
        return lax.ppermute(value, "ctx", [(at, at - shift) for at in range(shift, width)])

    def up_and_on(value, shift):
        pairs = [
            (at * sections + section, (at + shift) * sections + (section + 1) % sections)
            for at in range(width - shift)
            for section in range(sections)
        ]
        return lax.ppermute(value, ("ctx", "pipe"), pairs)

    sends = dict(zip(first_jobs, pack(here, own_picks, queries, keys, values, first_jobs, slots)))
    near = [up(sends[job], job[0]) for job in first_jobs if job[3]]
    arrived = {
        piece: down(sends[piece + (False,)], piece[0]) for group in groups[:2] for piece in group
    }
    before = passed_along(own_picks, "pipe", 1)
    now = after(here, *[sends[job] for job in first_jobs])
    sends |= zip(later_jobs, pack(now, own_picks, queries, keys, values, later_jobs, slots))

    def attend_group(token, group, is_anchor=False):
        return dict(
            zip(
                group,
                attend(
                    token,
                    own_picks,
                    keys,
                    values,
                    [arrived[piece] for piece in group],
                    tuple(group),
                    slots,
                    is_anchor,
                ),
            )
        )

    def ask_for(group, *earlier):
        for piece in group:
            arrived[piece] = down(after(sends[piece + (False,)], *earlier), piece[0])

    def send_back(parts, *earlier):
        for piece, part in parts.items():
            returned[piece] = up_and_on(after(part, *earlier) if earlier else part, piece[0])

    def those(found, group):
        return [found[piece] for piece in group]

    returned = {}
    own = own_part(after(here, before, sends[later_jobs[0]]), queries, keys, values)
    ask_for(groups[2][:1], own, *those(arrived, groups[0]))
    parts = attend_group(after(here, own), groups[0])
    send_back(parts)
    ask_for(groups[2][1:], *parts.values(), *near, *those(arrived, groups[1]))
    parts = attend_group(after(here, *parts.values(), *near), groups[1], is_anchor=True)
    send_back(parts)
    now = after(here, *parts.values())
    before_last = groups[0] + groups[1]
    for number in range(2, len(groups)):
        group = groups[number]
        if number == len(groups) - 1:
            now = tick(now, *those(returned, groups[number - 2]))
            now = after(now, own_back)
        if number == 2:
            ask_for(groups[number + 1], now, *those(arrived, group))
        parts = attend_group(now, group, is_anchor=number == 2)
        send_back(parts, *those(returned, before_last))
        now = after(now, *parts.values())
        if number == 2:
            now = after(now, *those(returned, before_last))
            own = add_near(now, own_picks, queries, own, near[0], near_shifts[0], slots)
            own_back = passed_along(own, "pipe", 1)
            now = after(now, own)
        if 2 <= number < len(groups) - 2:
            ask_for(groups[number + 2], now, *those(arrived, groups[number + 1]))
        before_last = group
    now = after(now, *those(returned, groups[-2]))

    final = groups[-1][0]
    others = [shift for shift in range(1, width) if shift not in near_shifts + final[:1]]
    merged_shifts = near_shifts + tuple(others)
    pieces = [piece for piece in returned if piece != final]
    places = [HEADS + merged_shifts.index(shift) * slots + first for shift, first, _ in pieces]
    parts = [own_back] + [returned[piece] for piece in pieces]
    mixed, sums = merge(now, before, parts, [0] + places, merged_shifts, slots)
    return finish(now, before, mixed, sums, returned[final], final[0], slots)[None]


def travelling_keys(queries, keys, values, picks):
    ctx_width = lax.axis_size("ctx")
    rank_here = lax.axis_index("ctx")
    slot_count = max(1, PICKS * HEADS // ctx_width)
    block_rows = queries.shape[1]
    score_scale = HD ** (-0.5)
    every_pick = picks[0].reshape(ctx_width, HEADS * PICKS)
    chosen = lax.dynamic_slice_in_dim(every_pick, rank_here, 1, 0)
    pick_order = request_table(chosen, lax.iota(jnp.int32, ctx_width), slot_count)[1]
    asked_table = request_table(every_pick, rank_here.reshape(1), slot_count)[0]
    asked_heads = asked_table[:, 0, :]
    safe_asked = jnp.maximum(asked_heads, 0)
    query_heads = queries[0].reshape(block_rows, HEADS, HD).transpose(1, 0, 2)
    key_heads = keys[0].reshape(block_rows, HEADS, HD).transpose(1, 0, 2)
    value_heads = values[0].reshape(block_rows, HEADS, HD).transpose(1, 0, 2)
    is_live = chosen[0] >= 0
    flat_slot = jnp.where(is_live, chosen[0] * slot_count + pick_order[0], 0)
    remote_mask = jnp.repeat(is_live.reshape(HEADS, PICKS), block_rows, axis=1)
    row_index = lax.iota(jnp.int32, block_rows)
    causal = row_index[:, None] >= row_index[None, :]

    def masked_scores(query_head, key_rows, mask_row):
        scores = lax.dot_general(
            query_head, key_rows, (((1,), (1,)), ((), ())), preferred_element_type=jnp.float32
        )
        allowed = jnp.concatenate(
            [causal, jnp.broadcast_to(mask_row[None, :], (block_rows, PICKS * block_rows))], axis=1
        )
        return jnp.where(allowed, scores * score_scale, -jnp.inf)

    def row_stats(scores):
        row_top = jnp.max(scores, axis=1)
        row_total = jnp.sum(jnp.exp(scores - row_top[:, None]), axis=1)
        return (row_top, row_total)

    def weighted(scores, row_top, row_total, value_rows):
        prob_rows = (jnp.exp(scores - row_top[:, None]) / row_total[:, None]).astype(jnp.bfloat16)
        return jnp.dot(prob_rows, value_rows, preferred_element_type=jnp.float32).astype(
            jnp.bfloat16
        )

    send_both = jnp.concatenate([key_heads, value_heads], axis=2)[safe_asked]
    got_slots = lax.all_to_all(send_both, "ctx", split_axis=0, concat_axis=0, tiled=True)
    last_width = 2 * HD
    flat_slots = got_slots.reshape(ctx_width * slot_count, block_rows, last_width)
    remote_both = flat_slots[flat_slot].reshape(HEADS, PICKS * block_rows, last_width)
    all_keys = jnp.concatenate([key_heads, remote_both[:, :, :HD]], axis=1)
    all_values = jnp.concatenate([value_heads, remote_both[:, :, HD:]], axis=1)

    def per_head(head_items):
        query_head, key_rows, value_rows, mask_row = head_items
        scores = masked_scores(query_head, key_rows, mask_row)
        row_top, row_total = row_stats(scores)
        return weighted(scores, row_top, row_total, value_rows)

    outputs = lax.map(per_head, (query_heads, all_keys, all_values, remote_mask))
    merged = outputs.transpose(1, 0, 2).reshape(1, block_rows, HEADS * HD)
    return passed_along(merged, "pipe", 1)


def per_device(queries, keys, values, picks):
    few_shifts = 8 <= lax.axis_size("ctx") <= 16
    run = travelling_queries if few_shifts else travelling_keys
    return run(queries, keys, values, picks)


def solution(mesh):
    placed = (
        P("pipe", "ctx", None),
        P("pipe", "ctx", None),
        P("pipe", "ctx", None),
        P("pipe", None, None, None),
    )
    return jax.shard_map(
        per_device, mesh=mesh, in_specs=placed, out_specs=P("pipe", "ctx", None), check_vma=False
    )
```

```python
import functools
import math

import jax
import jax.numpy as jnp
from jax import lax
from jax.experimental import pallas as pl
from jax.experimental.pallas import tpu as pltpu
from jax.sharding import PartitionSpec as P

HEADS = 16
HD = 128
PICKS = 2
EXP2_SCALE = HD ** -0.5 * math.log2(math.e)
LANES = 128
STAT_ROWS = 16
VMEM_BYTES = 24 * 1024 * 1024
ALL_VMEM_BYTES = 62 * 1024 * 1024
HIGH_COST = 10**12


def passed_along(value, axis, steps):
    count = lax.axis_size(axis)
    pairs = [(source, (source + steps) % count) for source in range(count)]
    return lax.ppermute(value, axis, pairs)


def request_table(chosen, owners, slot_count):
    pick_count = chosen.shape[1]
    pick_ids = lax.iota(jnp.int32, pick_count)
    is_live = chosen >= 0
    earlier = pick_ids[None, :] < pick_ids[:, None]
    same_owner = (chosen[:, :, None] == chosen[:, None, :]) & earlier[None]
    pick_order = jnp.sum(same_owner.astype(jnp.int32), axis=2)
    head_ids = pick_ids // PICKS
    slot_ranks = lax.iota(jnp.int32, slot_count)
    matches = (
        is_live[:, None, None, :]
        & (chosen[:, None, None, :] == owners[None, :, None, None])
        & (pick_order[:, None, None, :] == slot_ranks[None, None, :, None])
    )
    was_found = jnp.any(matches, axis=3)
    head_table = jnp.sum(jnp.where(matches, head_ids[None, None, None, :], 0), axis=3)
    return (jnp.where(was_found, head_table, -1), pick_order)


def call(
    kernel, name_space, outputs, out_specs, scratch=(), flops=0, moved=0, exps=0, vmem=VMEM_BYTES
):
    return pl.pallas_call(
        kernel,
        in_specs=name_space,
        out_specs=out_specs,
        out_shape=outputs,
        scratch_shapes=list(scratch),
        compiler_params=pltpu.CompilerParams(vmem_limit_bytes=vmem),
        cost_estimate=pl.CostEstimate(flops=flops, bytes_accessed=moved, transcendentals=exps),
    )


SCALARS = pl.BlockSpec(memory_space=pltpu.SMEM)
IN_HBM = pl.BlockSpec(memory_space=pltpu.HBM)
IN_VMEM = pl.BlockSpec(memory_space=pltpu.VMEM)


def tick_kernel(here_ref, out_ref):
    out_ref[0] = here_ref[0]


def tick(here, *earlier):
    return call(
        tick_kernel,
        [SCALARS],
        jax.ShapeDtypeStruct((1,), jnp.int32),
        SCALARS,
        flops=HIGH_COST,
    )(after(here, *earlier))


def list_heads(heads_ref, start, picks_ref, block, owner, slots):
    width = picks_ref.shape[0]
    spare = heads_ref.shape[0] - 1
    for slot in range(slots):
        heads_ref[start + slot] = -1
    valid = (block >= 0) & (block < width) & (owner >= 0) & (owner < width)
    row = jnp.clip(block, 0, width - 1)
    wanted = jnp.where(valid, owner, -2)
    found = jnp.int32(0)
    for pick in range(PICKS):
        for head in range(HEADS):
            hit = picks_ref[row, pick, head] == wanted
            heads_ref[jnp.where(hit, start + found, spare)] = head
            found = found + hit.astype(jnp.int32)


def pack_kernel(here_ref, picks_ref, *refs, jobs, slots):
    sources, outputs = refs[:3], refs[3 : 3 + len(jobs)]
    heads_ref, sems = refs[-2], refs[-1]
    here = here_ref[0]
    listed = {}
    for shift, first, count, is_near in jobs:
        key = (shift, is_near)
        if key not in listed:
            listed[key] = len(listed) * slots
            block, owner = (here + shift, here) if is_near else (here, here - shift)
            list_heads(heads_ref, listed[key], picks_ref, block, owner, slots)
    copies = []
    for (shift, first, count, is_near), output in zip(jobs, outputs):
        for slot in range(count):
            head = jnp.maximum(heads_ref[listed[shift, is_near] + first + slot], 0)
            columns = pl.ds(pl.multiple_of(head * HD, HD), HD)
            for place, source in enumerate(sources[1:] if is_near else sources[:1]):
                target = output.at[2 * slot + place if is_near else slot]
                copy = pltpu.make_async_copy(
                    source.at[:, columns], target, sems.at[len(copies)]
                )
                copy.start()
                copies.append(copy)
    for copy in copies:
        copy.wait()


def pack(here, picks, queries, keys, values, jobs, slots, vmem=VMEM_BYTES):
    rows = queries.shape[0]
    sizes = [2 * count if is_near else count for _, _, count, is_near in jobs]
    return call(
        functools.partial(pack_kernel, jobs=jobs, slots=slots),
        [SCALARS, SCALARS, IN_HBM, IN_HBM, IN_HBM],
        [jax.ShapeDtypeStruct((size, rows, HD), jnp.bfloat16) for size in sizes],
        [IN_VMEM] * len(sizes),
        [pltpu.SMEM((len(jobs) * slots + 1,), jnp.int32), pltpu.SemaphoreType.DMA((sum(sizes),))],
        moved=4 * rows * HD * sum(sizes),
        vmem=vmem,
    )(here, picks, queries, keys, values)


def diagonal():
    shape = (LANES, LANES)
    return lax.broadcasted_iota(jnp.int32, shape, 0) == lax.broadcasted_iota(jnp.int32, shape, 1)


def raw_scores(query_rows, key_rows):
    return lax.dot_general(
        query_rows, key_rows, (((1,), (1,)), ((), ())), preferred_element_type=jnp.float32
    )


def with_ones(value_rows):
    return jnp.concatenate([value_rows, jnp.ones_like(value_rows)], axis=1)


def soft_part(scores, value_rows):
    top = jnp.max(scores, axis=1, keepdims=True)
    weights = jnp.exp2((scores - top) * EXP2_SCALE).astype(jnp.bfloat16)
    total = jnp.dot(weights, value_rows, preferred_element_type=jnp.float32)
    sums = total[:, HD:]
    return total[:, :HD] * pl.reciprocal(sums), top * EXP2_SCALE, sums


def across_lanes(column):
    eye = diagonal()
    spread = jnp.broadcast_to(column, (column.shape[0], LANES))
    return [
        jnp.sum(jnp.where(eye, spread[at : at + LANES], 0.0), axis=0, keepdims=True)
        for at in range(0, column.shape[0], LANES)
    ]


def down_rows(line):
    spread = jnp.broadcast_to(line, (LANES, LANES))
    return jnp.sum(jnp.where(diagonal(), spread, 0.0), axis=1, keepdims=True)


def three_parts(stats):
    first = stats.astype(jnp.bfloat16).astype(jnp.float32)
    second = (stats - first).astype(jnp.bfloat16).astype(jnp.float32)
    third = stats - first - second
    parts = jnp.concatenate([first, second, third], axis=0)
    pad = jnp.zeros((STAT_ROWS - parts.shape[0], LANES), jnp.float32)
    return jnp.concatenate([parts, pad], axis=0).astype(jnp.bfloat16)


def stats_of(block, groups):
    stats = block.astype(jnp.float32)
    return stats[:groups] + stats[groups : 2 * groups] + stats[2 * groups : 3 * groups]


def log_sums(tops, sums):
    top_lines = [line for top in tops for line in across_lanes(top)]
    sum_lines = [line for part in sums for line in across_lanes(part)]
    return jnp.concatenate(top_lines, axis=0) + jnp.log2(jnp.concatenate(sum_lines, axis=0))


def attend_rows(query_rows, key_rows, value_rows, tile):
    found = [
        soft_part(raw_scores(query_rows[at : at + tile], key_rows), value_rows)
        for at in range(0, query_rows.shape[0], tile)
    ]
    outputs, tops, sums = zip(*found)
    return jnp.concatenate(outputs, axis=0), log_sums(tops, sums)


def head_columns(head):
    return pl.ds(pl.multiple_of(head * HD, HD), HD)


def attend_kernel(here_ref, picks_ref, key_ref, value_ref, *refs, group, slots):
    heads_ref = refs[-1]
    here = here_ref[0]
    for number, (shift, first, count) in enumerate(group):
        query_ref, out_ref = refs[number], refs[len(group) + number]
        rows = query_ref.shape[1]
        list_heads(heads_ref, 0, picks_ref, here + shift, here, slots)
        for slot in range(count):
            columns = head_columns(jnp.maximum(heads_ref[first + slot], 0))
            outputs, lines = attend_rows(
                query_ref[slot], key_ref[:, columns], with_ones(value_ref[:, columns]), rows
            )
            out_ref[slot, :rows, :] = outputs.astype(jnp.bfloat16)
            out_ref[slot, rows:, :] = three_parts(lines)


def attend(here, picks, keys, values, arrived, group, slots, is_anchor):
    rows = keys.shape[0]
    total = sum(count for _, _, count in group)
    return call(
        functools.partial(attend_kernel, group=group, slots=slots),
        [SCALARS, SCALARS, IN_VMEM, IN_VMEM] + [IN_VMEM] * len(group),
        [
            jax.ShapeDtypeStruct((count, rows + STAT_ROWS, HD), jnp.bfloat16)
            for _, _, count in group
        ],
        [IN_VMEM] * len(group),
        [pltpu.SMEM((slots + 1,), jnp.int32)],
        flops=HIGH_COST if is_anchor else 4 * total * rows * rows * HD,
        moved=8 * total * rows * HD,
        exps=total * rows * rows,
    )(here, picks, keys, values, *arrived)


def own_kernel(here_ref, query_ref, key_ref, value_ref, out_ref):
    rows = query_ref.shape[0]
    tile = min(rows, 256)

    def one_head(head, carry):
        columns = head_columns(head)
        value_rows = with_ones(value_ref[:, columns])
        tops, all_sums = [], []
        for at in range(0, rows, tile):
            reach = at + tile
            scores = raw_scores(query_ref[at:reach, columns], key_ref[:reach, columns])
            row_ids = lax.broadcasted_iota(jnp.int32, scores.shape, 0) + at
            seen = row_ids >= lax.broadcasted_iota(jnp.int32, scores.shape, 1)
            outputs, top, sums = soft_part(jnp.where(seen, scores, -jnp.inf), value_rows[:reach])
            out_ref[head, at:reach, :] = outputs.astype(jnp.bfloat16)
            tops.append(top)
            all_sums.append(sums)
        out_ref[head, rows:, :] = three_parts(log_sums(tops, all_sums))
        return carry

    lax.fori_loop(0, HEADS, one_head, 0, unroll=4)


def own_part(here, queries, keys, values):
    rows = queries.shape[0]
    return call(
        own_kernel,
        [SCALARS, IN_VMEM, IN_VMEM, IN_VMEM],
        jax.ShapeDtypeStruct((HEADS, rows + STAT_ROWS, HD), jnp.bfloat16),
        IN_VMEM,
        flops=4 * HEADS * rows * rows * HD,
        moved=8 * HEADS * rows * HD,
        exps=HEADS * rows * rows,
    )(here, queries, keys, values)


def near_kernel(here_ref, picks_ref, query_ref, near_ref, out_ref, heads_ref, *, shift, slots):
    rows = query_ref.shape[0]
    here = here_ref[0]
    list_heads(heads_ref, 0, picks_ref, here, here - shift, slots)
    for slot in range(slots):
        columns = head_columns(jnp.maximum(heads_ref[slot], 0))
        outputs, lines = attend_rows(
            query_ref[:, columns], near_ref[2 * slot], with_ones(near_ref[2 * slot + 1]), rows
        )
        out_ref[slot, :rows, :] = outputs.astype(jnp.bfloat16)
        out_ref[slot, rows:, :] = three_parts(lines)


def near_part(here, picks, queries, near, shift, slots):
    rows = queries.shape[0]
    return call(
        functools.partial(near_kernel, shift=shift, slots=slots),
        [SCALARS, SCALARS, IN_VMEM, IN_VMEM],
        jax.ShapeDtypeStruct((slots, rows + STAT_ROWS, HD), jnp.bfloat16),
        IN_VMEM,
        [pltpu.SMEM((slots + 1,), jnp.int32)],
        flops=HIGH_COST,
        moved=12 * slots * rows * HD,
        exps=slots * rows * rows,
    )(here, picks, queries, near)


def find_spots(spots_ref, found_ref, picks_ref, here, shifts, slots):
    for owner in range(picks_ref.shape[0]):
        found_ref[owner] = 0

    for pick in range(PICKS):
        for head in range(HEADS):
            owner = picks_ref[here, pick, head]
            safe = jnp.maximum(owner, 0)
            order = found_ref[safe]
            found_ref[safe] = order + (owner >= 0).astype(jnp.int32)
            spot = jnp.int32(-1)
            for place, shift in enumerate(shifts):
                spot = jnp.where(here - safe == shift, place * slots + order, spot)
            spots_ref[head * PICKS + pick] = jnp.where(owner >= 0, spot, -1)


def merge_kernel(here_ref, picks_ref, *refs, places, shifts, slots):
    count = len(places)
    parts = refs[:count]
    out_ref, sums_ref, held, spots_ref, found_ref, sems = refs[count:]
    groups = sums_ref.shape[1]
    rows = groups * LANES
    copies = [
        pltpu.make_async_copy(part, held.at[pl.ds(place, part.shape[0])], sems.at[number])
        for number, (part, place) in enumerate(zip(parts, places))
    ]
    for copy in copies:
        copy.start()
    find_spots(spots_ref, found_ref, picks_ref, here_ref[0], shifts, slots)
    for copy in copies:
        copy.wait()

    def one_head(head, carry):
        found = [spots_ref[head * PICKS + pick] for pick in range(PICKS)]
        spots = [head] + [jnp.where(spot >= 0, HEADS + spot, head) for spot in found]
        sums = [stats_of(held[spot, rows:, :], groups) for spot in spots]
        for pick, spot in enumerate(found):
            sums[1 + pick] = jnp.where(spot >= 0, sums[1 + pick], -jnp.inf)
        top = functools.reduce(jnp.maximum, sums)
        shares = [jnp.exp2(part - top) for part in sums]
        whole = functools.reduce(jnp.add, shares)
        sums_ref[head] = top + jnp.log2(whole)
        for group in range(groups):
            span = pl.ds(group * LANES, LANES)
            own = held[head, span, :].astype(jnp.float32)
            mixed = own
            for spot, share in zip(spots[1:], shares[1:]):
                weight = down_rows((share / whole)[group : group + 1, :])
                mixed = mixed + (held[spot, span, :].astype(jnp.float32) - own) * weight
            out_ref[head, span, :] = mixed
        return carry

    lax.fori_loop(0, HEADS, one_head, 0, unroll=2)


def merge(here, picks, parts, places, shifts, slots):
    rows = parts[0].shape[1] - STAT_ROWS
    width = picks.shape[0]
    total = HEADS + len(shifts) * slots
    return call(
        functools.partial(merge_kernel, places=tuple(places), shifts=shifts, slots=slots),
        [SCALARS, SCALARS] + [pl.BlockSpec(memory_space=pl.ANY)] * len(parts),
        [
            jax.ShapeDtypeStruct((HEADS, rows, HD), jnp.float32),
            jax.ShapeDtypeStruct((HEADS, rows // LANES, LANES), jnp.float32),
        ],
        [IN_VMEM, IN_VMEM],
        [
            pltpu.VMEM((total, rows + STAT_ROWS, HD), jnp.bfloat16),
            pltpu.SMEM((PICKS * HEADS,), jnp.int32),
            pltpu.SMEM((width,), jnp.int32),
            pltpu.SemaphoreType.DMA((len(parts),)),
        ],
        flops=HIGH_COST,
        moved=2 * (HEADS * 2 + total) * rows * HD,
    )(here, picks, *parts)


def finish_kernel(
    here_ref, picks_ref, mixed_ref, sums_ref, part_ref, out_ref, spots_ref, found_ref, *, shift, slots
):
    groups = sums_ref.shape[1]
    rows = groups * LANES
    step = pl.program_id(0)
    per_step = HEADS // pl.num_programs(0)

    @pl.when(step == 0)
    def _():
        find_spots(spots_ref, found_ref, picks_ref, here_ref[0], (shift,), slots)

    for place in range(per_step):
        head = step * per_step + place
        spot = jnp.maximum(spots_ref[head * PICKS], spots_ref[head * PICKS + 1])
        columns = pl.ds(place * HD, HD)

        @pl.when(spot < 0)
        def _():
            out_ref[:, columns] = mixed_ref[head].astype(jnp.bfloat16)

        @pl.when(spot >= 0)
        def _():
            before = sums_ref[head]
            added = stats_of(part_ref[spot, rows:, :], groups)
            share = 1.0 / (1.0 + jnp.exp2(before - added))
            for group in range(groups):
                span = pl.ds(group * LANES, LANES)
                old = mixed_ref[head, span, :]
                new = part_ref[spot, span, :].astype(jnp.float32)
                mixed = old + (new - old) * down_rows(share[group : group + 1, :])
                out_ref[span, columns] = mixed.astype(jnp.bfloat16)


def finish(here, picks, mixed, sums, part, shift, slots):
    heads, rows, _ = mixed.shape
    width = picks.shape[0]
    steps = 4
    return pl.pallas_call(
        functools.partial(finish_kernel, shift=shift, slots=slots),
        grid=(steps,),
        in_specs=[SCALARS, SCALARS, IN_VMEM, IN_VMEM, IN_VMEM],
        out_specs=pl.BlockSpec((rows, heads // steps * HD), lambda step: (0, step)),
        out_shape=jax.ShapeDtypeStruct((rows, heads * HD), jnp.bfloat16),
        scratch_shapes=[
            pltpu.SMEM((PICKS * HEADS,), jnp.int32),
            pltpu.SMEM((width,), jnp.int32),
        ],
        compiler_params=pltpu.CompilerParams(vmem_limit_bytes=VMEM_BYTES),
        cost_estimate=pl.CostEstimate(
            flops=2 * heads * rows * HD, bytes_accessed=8 * heads * rows * HD, transcendentals=0
        ),
    )(here, picks, mixed, sums, part)


def after(value, *earlier):
    return lax.optimization_barrier((value,) + earlier)[0]


def groups_in_order(width, slots):
    middle = width // 2
    groups = [[(1, 0, slots)], [(shift, 0, slots) for shift in (width - 2, width - 1)]]
    for low in range(3, middle):
        size = max(1, slots // 2)
        for first in range(0, slots, size):
            count = min(size, slots - first)
            groups.append([(low, first, count), (width - low, first, count)])
    return groups + [[(middle, 0, slots)]]


def travelling_queries(queries, keys, values, picks):
    width = lax.axis_size("ctx")
    sections = lax.axis_size("pipe")
    slots = max(1, PICKS * HEADS // width)
    here = lax.axis_index("ctx").astype(jnp.int32).reshape(1)
    queries, keys, values = queries[0], keys[0], values[0]
    own_picks = picks[0].transpose(0, 2, 1)

    groups = groups_in_order(width, slots)
    near_shifts = (2,)
    first_jobs = [(shift, 0, slots, True) for shift in near_shifts]
    first_jobs += [piece + (False,) for group in groups[:2] for piece in group]
    later_jobs = [piece + (False,) for group in groups[2:] for piece in group]

    def up(value, shift):
        return lax.ppermute(value, "ctx", [(at, at + shift) for at in range(width - shift)])

    def down(value, shift):
        return lax.ppermute(value, "ctx", [(at, at - shift) for at in range(shift, width)])

    def up_and_on(value, shift):
        pairs = [
            (at * sections + section, (at + shift) * sections + (section + 1) % sections)
            for at in range(width - shift)
            for section in range(sections)
        ]
        return lax.ppermute(value, ("ctx", "pipe"), pairs)

    packed = pack(
        here, own_picks, queries, keys, values, first_jobs, slots, vmem=ALL_VMEM_BYTES
    )
    sends = dict(zip(first_jobs, packed))
    near = [up(sends[job], job[0]) for job in first_jobs if job[3]]
    arrived = {
        piece: down(sends[piece + (False,)], piece[0]) for group in groups[:2] for piece in group
    }
    before = passed_along(own_picks, "pipe", 1)
    now = after(here, *[sends[job] for job in first_jobs])
    sends |= zip(later_jobs, pack(now, own_picks, queries, keys, values, later_jobs, slots))

    def attend_group(token, group, is_anchor=False):
        return dict(
            zip(
                group,
                attend(
                    token,
                    own_picks,
                    keys,
                    values,
                    [arrived[piece] for piece in group],
                    tuple(group),
                    slots,
                    is_anchor,
                ),
            )
        )

    def ask_for(group, *earlier):
        for piece in group:
            arrived[piece] = down(after(sends[piece + (False,)], *earlier), piece[0])

    def send_back(parts, *earlier):
        for piece, part in parts.items():
            returned[piece] = up_and_on(after(part, *earlier) if earlier else part, piece[0])

    def those(found, group):
        return [found[piece] for piece in group]

    returned = {}
    own = own_part(after(here, before, sends[later_jobs[0]]), queries, keys, values)
    own_back = passed_along(own, "pipe", 1)
    ask_for(groups[2][:1], own, *those(arrived, groups[0]))
    parts = attend_group(after(here, own), groups[0])
    send_back(parts)
    ask_for(groups[2][1:], *parts.values(), *near, *those(arrived, groups[1]))
    parts = attend_group(after(here, *parts.values(), *near), groups[1], is_anchor=True)
    send_back(parts)
    now = after(here, *parts.values())
    before_last = groups[0] + groups[1]
    for number in range(2, len(groups)):
        group = groups[number]
        if number == len(groups) - 1:
            now = tick(now, *those(returned, groups[number - 2]))
            now = after(now, near_back)
        if number == 2:
            ask_for(groups[number + 1], now, *those(arrived, group))
            now = after(now, own_back)
        parts = attend_group(now, group, is_anchor=number == 2)
        send_back(parts, *those(returned, before_last))
        now = after(now, *parts.values())
        if number == 2:
            now = after(now, *those(returned, before_last))
            beside = near_part(now, own_picks, queries, near[0], near_shifts[0], slots)
            near_back = passed_along(beside, "pipe", 1)
            now = after(now, beside)
        if 2 <= number < len(groups) - 2:
            ask_for(groups[number + 2], now, *those(arrived, groups[number + 1]))
        before_last = group
    now = after(now, *those(returned, groups[-2]))

    final = groups[-1][0]
    others = [shift for shift in range(1, width) if shift not in near_shifts + final[:1]]
    merged_shifts = near_shifts + tuple(others)
    pieces = [piece for piece in returned if piece != final]
    places = [HEADS + merged_shifts.index(shift) * slots + first for shift, first, _ in pieces]
    parts = [own_back, near_back] + [returned[piece] for piece in pieces]
    mixed, sums = merge(now, before, parts, [0, HEADS] + places, merged_shifts, slots)
    return finish(now, before, mixed, sums, returned[final], final[0], slots)[None]


def travelling_keys(queries, keys, values, picks):
    ctx_width = lax.axis_size("ctx")
    rank_here = lax.axis_index("ctx")
    slot_count = max(1, PICKS * HEADS // ctx_width)
    block_rows = queries.shape[1]
    score_scale = HD ** (-0.5)
    every_pick = picks[0].reshape(ctx_width, HEADS * PICKS)
    chosen = lax.dynamic_slice_in_dim(every_pick, rank_here, 1, 0)
    pick_order = request_table(chosen, lax.iota(jnp.int32, ctx_width), slot_count)[1]
    asked_table = request_table(every_pick, rank_here.reshape(1), slot_count)[0]
    asked_heads = asked_table[:, 0, :]
    safe_asked = jnp.maximum(asked_heads, 0)
    query_heads = queries[0].reshape(block_rows, HEADS, HD).transpose(1, 0, 2)
    key_heads = keys[0].reshape(block_rows, HEADS, HD).transpose(1, 0, 2)
    value_heads = values[0].reshape(block_rows, HEADS, HD).transpose(1, 0, 2)
    is_live = chosen[0] >= 0
    flat_slot = jnp.where(is_live, chosen[0] * slot_count + pick_order[0], 0)
    remote_mask = jnp.repeat(is_live.reshape(HEADS, PICKS), block_rows, axis=1)
    row_index = lax.iota(jnp.int32, block_rows)
    causal = row_index[:, None] >= row_index[None, :]

    def masked_scores(query_head, key_rows, mask_row):
        scores = lax.dot_general(
            query_head, key_rows, (((1,), (1,)), ((), ())), preferred_element_type=jnp.float32
        )
        allowed = jnp.concatenate(
            [causal, jnp.broadcast_to(mask_row[None, :], (block_rows, PICKS * block_rows))], axis=1
        )
        return jnp.where(allowed, scores * score_scale, -jnp.inf)

    def row_stats(scores):
        row_top = jnp.max(scores, axis=1)
        row_total = jnp.sum(jnp.exp(scores - row_top[:, None]), axis=1)
        return (row_top, row_total)

    def weighted(scores, row_top, row_total, value_rows):
        prob_rows = (jnp.exp(scores - row_top[:, None]) / row_total[:, None]).astype(jnp.bfloat16)
        return jnp.dot(prob_rows, value_rows, preferred_element_type=jnp.float32).astype(
            jnp.bfloat16
        )

    send_both = jnp.concatenate([key_heads, value_heads], axis=2)[safe_asked]
    got_slots = lax.all_to_all(send_both, "ctx", split_axis=0, concat_axis=0, tiled=True)
    last_width = 2 * HD
    flat_slots = got_slots.reshape(ctx_width * slot_count, block_rows, last_width)
    remote_both = flat_slots[flat_slot].reshape(HEADS, PICKS * block_rows, last_width)
    all_keys = jnp.concatenate([key_heads, remote_both[:, :, :HD]], axis=1)
    all_values = jnp.concatenate([value_heads, remote_both[:, :, HD:]], axis=1)

    def per_head(head_items):
        query_head, key_rows, value_rows, mask_row = head_items
        scores = masked_scores(query_head, key_rows, mask_row)
        row_top, row_total = row_stats(scores)
        return weighted(scores, row_top, row_total, value_rows)

    outputs = lax.map(per_head, (query_heads, all_keys, all_values, remote_mask))
    merged = outputs.transpose(1, 0, 2).reshape(1, block_rows, HEADS * HD)
    return passed_along(merged, "pipe", 1)


def per_device(queries, keys, values, picks):
    few_shifts = 8 <= lax.axis_size("ctx") <= 16
    run = travelling_queries if few_shifts else travelling_keys
    return run(queries, keys, values, picks)


def solution(mesh):
    placed = (
        P("pipe", "ctx", None),
        P("pipe", "ctx", None),
        P("pipe", "ctx", None),
        P("pipe", None, None, None),
    )
    return jax.shard_map(
        per_device, mesh=mesh, in_specs=placed, out_specs=P("pipe", "ctx", None), check_vma=False
    )
```

```python
import functools
import math

import jax
import jax.numpy as jnp
from jax import lax
from jax.experimental import pallas as pl
from jax.experimental.pallas import tpu as pltpu
from jax.sharding import PartitionSpec as P

HEADS = 16
HD = 128
PICKS = 2
EXP2_SCALE = HD ** -0.5 * math.log2(math.e)
LANES = 128
STAT_ROWS = 16
VMEM_BYTES = 24 * 1024 * 1024
HIGH_COST = 10**12


def passed_along(value, axis, steps):
    count = lax.axis_size(axis)
    pairs = [(source, (source + steps) % count) for source in range(count)]
    return lax.ppermute(value, axis, pairs)


def request_table(chosen, owners, slot_count):
    pick_count = chosen.shape[1]
    pick_ids = lax.iota(jnp.int32, pick_count)
    is_live = chosen >= 0
    earlier = pick_ids[None, :] < pick_ids[:, None]
    same_owner = (chosen[:, :, None] == chosen[:, None, :]) & earlier[None]
    pick_order = jnp.sum(same_owner.astype(jnp.int32), axis=2)
    head_ids = pick_ids // PICKS
    slot_ranks = lax.iota(jnp.int32, slot_count)
    matches = (
        is_live[:, None, None, :]
        & (chosen[:, None, None, :] == owners[None, :, None, None])
        & (pick_order[:, None, None, :] == slot_ranks[None, None, :, None])
    )
    was_found = jnp.any(matches, axis=3)
    head_table = jnp.sum(jnp.where(matches, head_ids[None, None, None, :], 0), axis=3)
    return (jnp.where(was_found, head_table, -1), pick_order)


def call(
    kernel, name_space, outputs, out_specs, scratch=(), flops=0, moved=0, exps=0
):
    return pl.pallas_call(
        kernel,
        in_specs=name_space,
        out_specs=out_specs,
        out_shape=outputs,
        scratch_shapes=list(scratch),
        compiler_params=pltpu.CompilerParams(vmem_limit_bytes=VMEM_BYTES),
        cost_estimate=pl.CostEstimate(flops=flops, bytes_accessed=moved, transcendentals=exps),
    )


SCALARS = pl.BlockSpec(memory_space=pltpu.SMEM)
IN_HBM = pl.BlockSpec(memory_space=pltpu.HBM)
IN_VMEM = pl.BlockSpec(memory_space=pltpu.VMEM)


def tick_kernel(here_ref, out_ref):
    out_ref[0] = here_ref[0]


def tick(here, *earlier):
    return call(
        tick_kernel,
        [SCALARS],
        jax.ShapeDtypeStruct((1,), jnp.int32),
        SCALARS,
        flops=HIGH_COST,
    )(after(here, *earlier))


def list_heads(heads_ref, start, picks_ref, block, owner, slots):
    width = picks_ref.shape[0]
    spare = heads_ref.shape[0] - 1
    for slot in range(slots):
        heads_ref[start + slot] = -1
    valid = (block >= 0) & (block < width) & (owner >= 0) & (owner < width)
    row = jnp.clip(block, 0, width - 1)
    wanted = jnp.where(valid, owner, -2)
    found = jnp.int32(0)
    for pick in range(PICKS):
        for head in range(HEADS):
            hit = picks_ref[row, pick, head] == wanted
            heads_ref[jnp.where(hit, start + found, spare)] = head
            found = found + hit.astype(jnp.int32)


def pack_kernel(here_ref, picks_ref, *refs, jobs, slots):
    is_near = jobs[0][3]
    sources = refs[: 1 + is_near]
    outputs = refs[1 + is_near : 1 + is_near + len(jobs)]
    heads_ref, sems = refs[-2], refs[-1]
    here = here_ref[0]
    listed = {}
    for shift, first, count, is_near in jobs:
        key = (shift, is_near)
        if key not in listed:
            listed[key] = len(listed) * slots
            block, owner = (here + shift, here) if is_near else (here, here - shift)
            list_heads(heads_ref, listed[key], picks_ref, block, owner, slots)
    copies = []
    for (shift, first, count, is_near), output in zip(jobs, outputs):
        for slot in range(count):
            head = jnp.maximum(heads_ref[listed[shift, is_near] + first + slot], 0)
            columns = pl.ds(pl.multiple_of(head * HD, HD), HD)
            for place, source in enumerate(sources):
                target = output.at[2 * slot + place if is_near else slot]
                copy = pltpu.make_async_copy(
                    source.at[:, columns], target, sems.at[len(copies)]
                )
                copy.start()
                copies.append(copy)
    for copy in copies:
        copy.wait()


def pack(here, picks, sources, jobs, slots):
    rows = sources[0].shape[0]
    sizes = [len(sources) * count for _, _, count, _ in jobs]
    return call(
        functools.partial(pack_kernel, jobs=jobs, slots=slots),
        [SCALARS, SCALARS] + [IN_VMEM] * len(sources),
        [jax.ShapeDtypeStruct((size, rows, HD), jnp.bfloat16) for size in sizes],
        [IN_VMEM] * len(sizes),
        [pltpu.SMEM((len(jobs) * slots + 1,), jnp.int32), pltpu.SemaphoreType.DMA((sum(sizes),))],
        moved=4 * rows * HD * sum(sizes),
    )(here, picks, *sources)


def diagonal():
    shape = (LANES, LANES)
    return lax.broadcasted_iota(jnp.int32, shape, 0) == lax.broadcasted_iota(jnp.int32, shape, 1)


def raw_scores(query_rows, key_rows):
    return lax.dot_general(
        query_rows, key_rows, (((1,), (1,)), ((), ())), preferred_element_type=jnp.float32
    )


def with_ones(value_rows):
    return jnp.concatenate([value_rows, jnp.ones_like(value_rows)], axis=1)


def soft_part(scores, value_rows):
    top = jnp.max(scores, axis=1, keepdims=True)
    weights = jnp.exp2((scores - top) * EXP2_SCALE).astype(jnp.bfloat16)
    total = jnp.dot(weights, value_rows, preferred_element_type=jnp.float32)
    sums = total[:, HD:]
    return total[:, :HD] * pl.reciprocal(sums), top * EXP2_SCALE, sums


def across_lanes(column):
    eye = diagonal()
    spread = jnp.broadcast_to(column, (column.shape[0], LANES))
    return [
        jnp.sum(jnp.where(eye, spread[at : at + LANES], 0.0), axis=0, keepdims=True)
        for at in range(0, column.shape[0], LANES)
    ]


def down_rows(line):
    spread = jnp.broadcast_to(line, (LANES, LANES))
    return jnp.sum(jnp.where(diagonal(), spread, 0.0), axis=1, keepdims=True)


def three_parts(stats):
    first = stats.astype(jnp.bfloat16).astype(jnp.float32)
    second = (stats - first).astype(jnp.bfloat16).astype(jnp.float32)
    third = stats - first - second
    parts = jnp.concatenate([first, second, third], axis=0)
    pad = jnp.zeros((STAT_ROWS - parts.shape[0], LANES), jnp.float32)
    return jnp.concatenate([parts, pad], axis=0).astype(jnp.bfloat16)


def stats_of(block, groups):
    stats = block.astype(jnp.float32)
    return stats[:groups] + stats[groups : 2 * groups] + stats[2 * groups : 3 * groups]


def log_sums(tops, sums):
    top_lines = [line for top in tops for line in across_lanes(top)]
    sum_lines = [line for part in sums for line in across_lanes(part)]
    return jnp.concatenate(top_lines, axis=0) + jnp.log2(jnp.concatenate(sum_lines, axis=0))


def attend_rows(query_rows, key_rows, value_rows, tile):
    found = [
        soft_part(raw_scores(query_rows[at : at + tile], key_rows), value_rows)
        for at in range(0, query_rows.shape[0], tile)
    ]
    outputs, tops, sums = zip(*found)
    return jnp.concatenate(outputs, axis=0), log_sums(tops, sums)


def head_columns(head):
    return pl.ds(pl.multiple_of(head * HD, HD), HD)


def attend_kernel(here_ref, picks_ref, key_ref, value_ref, *refs, group, slots):
    heads_ref = refs[-1]
    here = here_ref[0]
    for number, (shift, first, count) in enumerate(group):
        query_ref, out_ref = refs[number], refs[len(group) + number]
        rows = query_ref.shape[1]
        list_heads(heads_ref, 0, picks_ref, here + shift, here, slots)
        for slot in range(count):
            columns = head_columns(jnp.maximum(heads_ref[first + slot], 0))
            outputs, lines = attend_rows(
                query_ref[slot], key_ref[:, columns], with_ones(value_ref[:, columns]), rows
            )
            out_ref[slot, :rows, :] = outputs.astype(jnp.bfloat16)
            out_ref[slot, rows:, :] = three_parts(lines)


def attend(here, picks, keys, values, arrived, group, slots, is_anchor):
    rows = keys.shape[0]
    total = sum(count for _, _, count in group)
    return call(
        functools.partial(attend_kernel, group=group, slots=slots),
        [SCALARS, SCALARS, IN_VMEM, IN_VMEM] + [IN_VMEM] * len(group),
        [
            jax.ShapeDtypeStruct((count, rows + STAT_ROWS, HD), jnp.bfloat16)
            for _, _, count in group
        ],
        [IN_VMEM] * len(group),
        [pltpu.SMEM((slots + 1,), jnp.int32)],
        flops=HIGH_COST if is_anchor else 4 * total * rows * rows * HD,
        moved=8 * total * rows * HD,
        exps=total * rows * rows,
    )(here, picks, keys, values, *arrived)


def own_heads(query_ref, key_ref, value_ref, out_ref, heads):
    rows = query_ref.shape[0]
    tile = min(rows, 256)

    def one_head(place, carry):
        columns = head_columns(heads[0] + place)
        value_rows = with_ones(value_ref[:, columns])
        tops, all_sums = [], []
        for at in range(0, rows, tile):
            reach = at + tile
            scores = raw_scores(query_ref[at:reach, columns], key_ref[:reach, columns])
            row_ids = lax.broadcasted_iota(jnp.int32, scores.shape, 0) + at
            seen = row_ids >= lax.broadcasted_iota(jnp.int32, scores.shape, 1)
            outputs, top, sums = soft_part(jnp.where(seen, scores, -jnp.inf), value_rows[:reach])
            out_ref[place, at:reach, :] = outputs.astype(jnp.bfloat16)
            tops.append(top)
            all_sums.append(sums)
        out_ref[place, rows:, :] = three_parts(log_sums(tops, all_sums))
        return carry

    lax.fori_loop(0, len(heads), one_head, 0, unroll=4)


def own_kernel(here_ref, query_ref, key_ref, value_ref, out_ref, *, heads):
    own_heads(query_ref, key_ref, value_ref, out_ref, heads)


def own_part(here, queries, keys, values, heads):
    rows = queries.shape[0]
    return call(
        functools.partial(own_kernel, heads=heads),
        [SCALARS, IN_VMEM, IN_VMEM, IN_VMEM],
        jax.ShapeDtypeStruct((len(heads), rows + STAT_ROWS, HD), jnp.bfloat16),
        IN_VMEM,
        flops=4 * len(heads) * rows * rows * HD,
        moved=8 * len(heads) * rows * HD,
        exps=len(heads) * rows * rows,
    )(here, queries, keys, values)


def near_kernel(
    here_ref, picks_ref, query_ref, key_ref, value_ref, near_ref, out_ref, heads_ref, *, heads, shift, slots
):
    rows = query_ref.shape[0]
    here = here_ref[0]
    list_heads(heads_ref, 0, picks_ref, here, here - shift, slots)
    own_heads(query_ref, key_ref, value_ref, out_ref, heads)
    for slot in range(slots):
        columns = head_columns(jnp.maximum(heads_ref[slot], 0))
        outputs, lines = attend_rows(
            query_ref[:, columns], near_ref[2 * slot], with_ones(near_ref[2 * slot + 1]), rows
        )
        out_ref[len(heads) + slot, :rows, :] = outputs.astype(jnp.bfloat16)
        out_ref[len(heads) + slot, rows:, :] = three_parts(lines)


def near_part(here, picks, queries, keys, values, near, heads, shift, slots):
    rows = queries.shape[0]
    total = len(heads) + slots
    return call(
        functools.partial(near_kernel, heads=heads, shift=shift, slots=slots),
        [SCALARS, SCALARS, IN_VMEM, IN_VMEM, IN_VMEM, IN_VMEM],
        jax.ShapeDtypeStruct((total, rows + STAT_ROWS, HD), jnp.bfloat16),
        IN_VMEM,
        [pltpu.SMEM((slots + 1,), jnp.int32)],
        flops=HIGH_COST,
        moved=12 * total * rows * HD,
        exps=total * rows * rows,
    )(here, picks, queries, keys, values, near)


def find_spots(spots_ref, found_ref, picks_ref, here, shifts, slots):
    for owner in range(picks_ref.shape[0]):
        found_ref[owner] = 0

    for pick in range(PICKS):
        for head in range(HEADS):
            owner = picks_ref[here, pick, head]
            safe = jnp.maximum(owner, 0)
            order = found_ref[safe]
            found_ref[safe] = order + (owner >= 0).astype(jnp.int32)
            spot = jnp.int32(-1)
            for place, shift in enumerate(shifts):
                spot = jnp.where(here - safe == shift, place * slots + order, spot)
            spots_ref[head * PICKS + pick] = jnp.where(owner >= 0, spot, -1)


def merge_kernel(here_ref, picks_ref, *refs, places, shifts, slots):
    count = len(places)
    parts = refs[:count]
    out_ref, sums_ref, held, spots_ref, found_ref, sems = refs[count:]
    groups = sums_ref.shape[1]
    rows = groups * LANES
    copies = [
        pltpu.make_async_copy(part, held.at[pl.ds(place, part.shape[0])], sems.at[number])
        for number, (part, place) in enumerate(zip(parts, places))
    ]
    for copy in copies:
        copy.start()
    find_spots(spots_ref, found_ref, picks_ref, here_ref[0], shifts, slots)
    for copy in copies:
        copy.wait()

    def one_head(head, carry):
        found = [spots_ref[head * PICKS + pick] for pick in range(PICKS)]
        spots = [head] + [jnp.where(spot >= 0, HEADS + spot, head) for spot in found]
        sums = [stats_of(held[spot, rows:, :], groups) for spot in spots]
        for pick, spot in enumerate(found):
            sums[1 + pick] = jnp.where(spot >= 0, sums[1 + pick], -jnp.inf)
        top = functools.reduce(jnp.maximum, sums)
        shares = [jnp.exp2(part - top) for part in sums]
        whole = functools.reduce(jnp.add, shares)
        sums_ref[head] = top + jnp.log2(whole)
        for group in range(groups):
            span = pl.ds(group * LANES, LANES)
            own = held[head, span, :].astype(jnp.float32)
            mixed = own
            for spot, share in zip(spots[1:], shares[1:]):
                weight = down_rows((share / whole)[group : group + 1, :])
                mixed = mixed + (held[spot, span, :].astype(jnp.float32) - own) * weight
            out_ref[head, span, :] = mixed
        return carry

    lax.fori_loop(0, HEADS, one_head, 0, unroll=2)


def merge(here, picks, parts, places, shifts, slots):
    rows = parts[0].shape[1] - STAT_ROWS
    width = picks.shape[0]
    total = HEADS + len(shifts) * slots
    return call(
        functools.partial(merge_kernel, places=tuple(places), shifts=shifts, slots=slots),
        [SCALARS, SCALARS] + [pl.BlockSpec(memory_space=pl.ANY)] * len(parts),
        [
            jax.ShapeDtypeStruct((HEADS, rows, HD), jnp.float32),
            jax.ShapeDtypeStruct((HEADS, rows // LANES, LANES), jnp.float32),
        ],
        [IN_VMEM, IN_VMEM],
        [
            pltpu.VMEM((total, rows + STAT_ROWS, HD), jnp.bfloat16),
            pltpu.SMEM((PICKS * HEADS,), jnp.int32),
            pltpu.SMEM((width,), jnp.int32),
            pltpu.SemaphoreType.DMA((len(parts),)),
        ],
        flops=6 * HEADS * rows * HD,
        moved=2 * (HEADS * 2 + total) * rows * HD,
    )(here, picks, *parts)


def finish_kernel(
    here_ref, picks_ref, mixed_ref, sums_ref, part_ref, out_ref, spots_ref, found_ref, *, shift, slots
):
    groups = sums_ref.shape[1]
    rows = groups * LANES
    step = pl.program_id(0)
    per_step = HEADS // pl.num_programs(0)

    @pl.when(step == 0)
    def _():
        find_spots(spots_ref, found_ref, picks_ref, here_ref[0], (shift,), slots)

    for place in range(per_step):
        head = step * per_step + place
        spot = jnp.maximum(spots_ref[head * PICKS], spots_ref[head * PICKS + 1])
        columns = pl.ds(place * HD, HD)

        @pl.when(spot < 0)
        def _():
            out_ref[:, columns] = mixed_ref[head].astype(jnp.bfloat16)

        @pl.when(spot >= 0)
        def _():
            before = sums_ref[head]
            added = stats_of(part_ref[spot, rows:, :], groups)
            share = 1.0 / (1.0 + jnp.exp2(before - added))
            for group in range(groups):
                span = pl.ds(group * LANES, LANES)
                old = mixed_ref[head, span, :]
                new = part_ref[spot, span, :].astype(jnp.float32)
                mixed = old + (new - old) * down_rows(share[group : group + 1, :])
                out_ref[span, columns] = mixed.astype(jnp.bfloat16)


def finish(here, picks, mixed, sums, part, shift, slots):
    heads, rows, _ = mixed.shape
    width = picks.shape[0]
    steps = 4
    return pl.pallas_call(
        functools.partial(finish_kernel, shift=shift, slots=slots),
        grid=(steps,),
        in_specs=[SCALARS, SCALARS, IN_VMEM, IN_VMEM, IN_VMEM],
        out_specs=pl.BlockSpec((rows, heads // steps * HD), lambda step: (0, step)),
        out_shape=jax.ShapeDtypeStruct((rows, heads * HD), jnp.bfloat16),
        scratch_shapes=[
            pltpu.SMEM((PICKS * HEADS,), jnp.int32),
            pltpu.SMEM((width,), jnp.int32),
        ],
        compiler_params=pltpu.CompilerParams(vmem_limit_bytes=VMEM_BYTES),
        cost_estimate=pl.CostEstimate(
            flops=2 * heads * rows * HD, bytes_accessed=8 * heads * rows * HD, transcendentals=0
        ),
    )(here, picks, mixed, sums, part)


def after(value, *earlier):
    return lax.optimization_barrier((value,) + earlier)[0]


def groups_in_order(width, slots):
    middle = width // 2
    groups = [[(1, 0, slots)], [(shift, 0, slots) for shift in (width - 2, width - 1)]]
    for low in range(3, middle):
        size = max(1, slots // 2)
        for first in range(0, slots, size):
            count = min(size, slots - first)
            groups.append([(low, first, count), (width - low, first, count)])
    return groups + [[(middle, 0, slots)]]


def travelling_queries(queries, keys, values, picks):
    width = lax.axis_size("ctx")
    sections = lax.axis_size("pipe")
    slots = max(1, PICKS * HEADS // width)
    here = lax.axis_index("ctx").astype(jnp.int32).reshape(1)
    queries, keys, values = queries[0], keys[0], values[0]
    own_picks = picks[0].transpose(0, 2, 1)

    groups = groups_in_order(width, slots)
    near_shift = 2
    near_jobs = [(near_shift, 0, slots, True)]
    query_jobs = [piece + (False,) for group in groups for piece in group]

    def up(value, shift):
        return lax.ppermute(value, "ctx", [(at, at + shift) for at in range(width - shift)])

    def down(value, shift):
        return lax.ppermute(value, "ctx", [(at, at - shift) for at in range(shift, width)])

    def up_and_on(value, shift):
        pairs = [
            (at * sections + section, (at + shift) * sections + (section + 1) % sections)
            for at in range(width - shift)
            for section in range(sections)
        ]
        return lax.ppermute(value, ("ctx", "pipe"), pairs)

    near_send = pack(here, own_picks, [keys, values], near_jobs, slots)[0]
    near = up(near_send, near_shift)
    now = after(here, near_send)
    packed = pack(now, own_picks, [queries], query_jobs, slots)
    sends = {job[:3]: send for job, send in zip(query_jobs, packed)}
    arrived = {
        piece: down(sends[piece], piece[0]) for group in groups[:2] for piece in group
    }
    before = passed_along(own_picks, "pipe", 1)

    def attend_group(token, group, is_anchor=False):
        return dict(
            zip(
                group,
                attend(
                    token,
                    own_picks,
                    keys,
                    values,
                    [arrived[piece] for piece in group],
                    tuple(group),
                    slots,
                    is_anchor,
                ),
            )
        )

    def ask_for(group, *earlier):
        for piece in group:
            arrived[piece] = down(after(sends[piece], *earlier), piece[0])

    def send_back(parts):
        for piece, part in parts.items():
            if len(returned) >= 3:
                part = after(part, list(returned.values())[-3])
            returned[piece] = up_and_on(part, piece[0])

    def those(found, group):
        return [found[piece] for piece in group]

    returned = {}
    first_heads, other_heads = range(HEADS // 2), range(HEADS // 2, HEADS)
    own = own_part(
        after(here, before, sends[groups[0][0]]), queries, keys, values, first_heads
    )
    own_back = passed_along(own, "pipe", 1)
    ask_for(groups[2][:1], own, *those(arrived, groups[0]))
    parts = attend_group(after(here, own), groups[0])
    send_back(parts)
    ask_for(groups[2][1:], *parts.values(), near, *those(arrived, groups[1]))
    parts = attend_group(after(here, near, *parts.values()), groups[1], is_anchor=True)
    send_back(parts)
    now = after(here, *parts.values())
    for number in range(2, len(groups)):
        group = groups[number]
        if number == len(groups) - 1:
            now = tick(now, list(returned.values())[-4])
        if number == 2:
            ask_for(groups[number + 1], now, *those(arrived, group))
            now = after(now, own_back)
        parts = attend_group(now, group, is_anchor=number == 2)
        send_back(parts)
        now = after(now, *parts.values())
        if number == 2:
            now = after(now, list(returned.values())[-4])
            beside = near_part(
                now, own_picks, queries, keys, values, near, other_heads, near_shift, slots
            )
            beside_back = passed_along(after(beside, *those(arrived, groups[3])), "pipe", 1)
            now = after(now, beside)
        if 2 <= number < len(groups) - 2:
            ask_for(groups[number + 2], now, *those(arrived, groups[number + 1]))
    now = tick(now)

    final = groups[-1][0]
    others = [shift for shift in range(1, width) if shift not in (near_shift, final[0])]
    merged_shifts = (near_shift,) + tuple(others)
    pieces = [piece for piece in returned if piece != final]
    places = [HEADS + merged_shifts.index(shift) * slots + first for shift, first, _ in pieces]
    parts = [own_back, beside_back] + [returned[piece] for piece in pieces]
    mixed, sums = merge(now, before, parts, [0, len(first_heads)] + places, merged_shifts, slots)
    return finish(now, before, mixed, sums, returned[final], final[0], slots)[None]


def travelling_keys(queries, keys, values, picks):
    ctx_width = lax.axis_size("ctx")
    rank_here = lax.axis_index("ctx")
    slot_count = max(1, PICKS * HEADS // ctx_width)
    block_rows = queries.shape[1]
    score_scale = HD ** (-0.5)
    every_pick = picks[0].reshape(ctx_width, HEADS * PICKS)
    chosen = lax.dynamic_slice_in_dim(every_pick, rank_here, 1, 0)
    pick_order = request_table(chosen, lax.iota(jnp.int32, ctx_width), slot_count)[1]
    asked_table = request_table(every_pick, rank_here.reshape(1), slot_count)[0]
    asked_heads = asked_table[:, 0, :]
    safe_asked = jnp.maximum(asked_heads, 0)
    query_heads = queries[0].reshape(block_rows, HEADS, HD).transpose(1, 0, 2)
    key_heads = keys[0].reshape(block_rows, HEADS, HD).transpose(1, 0, 2)
    value_heads = values[0].reshape(block_rows, HEADS, HD).transpose(1, 0, 2)
    is_live = chosen[0] >= 0
    flat_slot = jnp.where(is_live, chosen[0] * slot_count + pick_order[0], 0)
    remote_mask = jnp.repeat(is_live.reshape(HEADS, PICKS), block_rows, axis=1)
    row_index = lax.iota(jnp.int32, block_rows)
    causal = row_index[:, None] >= row_index[None, :]

    def masked_scores(query_head, key_rows, mask_row):
        scores = lax.dot_general(
            query_head, key_rows, (((1,), (1,)), ((), ())), preferred_element_type=jnp.float32
        )
        allowed = jnp.concatenate(
            [causal, jnp.broadcast_to(mask_row[None, :], (block_rows, PICKS * block_rows))], axis=1
        )
        return jnp.where(allowed, scores * score_scale, -jnp.inf)

    def row_stats(scores):
        row_top = jnp.max(scores, axis=1)
        row_total = jnp.sum(jnp.exp(scores - row_top[:, None]), axis=1)
        return (row_top, row_total)

    def weighted(scores, row_top, row_total, value_rows):
        prob_rows = (jnp.exp(scores - row_top[:, None]) / row_total[:, None]).astype(jnp.bfloat16)
        return jnp.dot(prob_rows, value_rows, preferred_element_type=jnp.float32).astype(
            jnp.bfloat16
        )

    send_both = jnp.concatenate([key_heads, value_heads], axis=2)[safe_asked]
    got_slots = lax.all_to_all(send_both, "ctx", split_axis=0, concat_axis=0, tiled=True)
    last_width = 2 * HD
    flat_slots = got_slots.reshape(ctx_width * slot_count, block_rows, last_width)
    remote_both = flat_slots[flat_slot].reshape(HEADS, PICKS * block_rows, last_width)
    all_keys = jnp.concatenate([key_heads, remote_both[:, :, :HD]], axis=1)
    all_values = jnp.concatenate([value_heads, remote_both[:, :, HD:]], axis=1)

    def per_head(head_items):
        query_head, key_rows, value_rows, mask_row = head_items
        scores = masked_scores(query_head, key_rows, mask_row)
        row_top, row_total = row_stats(scores)
        return weighted(scores, row_top, row_total, value_rows)

    outputs = lax.map(per_head, (query_heads, all_keys, all_values, remote_mask))
    merged = outputs.transpose(1, 0, 2).reshape(1, block_rows, HEADS * HD)
    return passed_along(merged, "pipe", 1)


def per_device(queries, keys, values, picks):
    few_shifts = 8 <= lax.axis_size("ctx") <= 16
    run = travelling_queries if few_shifts else travelling_keys
    return run(queries, keys, values, picks)


def solution(mesh):
    placed = (
        P("pipe", "ctx", None),
        P("pipe", "ctx", None),
        P("pipe", "ctx", None),
        P("pipe", None, None, None),
    )
    return jax.shard_map(
        per_device, mesh=mesh, in_specs=placed, out_specs=P("pipe", "ctx", None), check_vma=False
    )
```

```python
import functools
import math

import jax
import jax.numpy as jnp
from jax import lax
from jax.experimental import pallas as pl
from jax.experimental.pallas import tpu as pltpu
from jax.sharding import PartitionSpec as P

HEADS = 16
HD = 128
PICKS = 2
EXP2_SCALE = HD ** -0.5 * math.log2(math.e)
LANES = 128
STAT_ROWS = 16
VMEM_BYTES = 24 * 1024 * 1024
HIGH_COST = 10**12


def passed_along(value, axis, steps):
    count = lax.axis_size(axis)
    pairs = [(source, (source + steps) % count) for source in range(count)]
    return lax.ppermute(value, axis, pairs)


def request_table(chosen, owners, slot_count):
    pick_count = chosen.shape[1]
    pick_ids = lax.iota(jnp.int32, pick_count)
    is_live = chosen >= 0
    earlier = pick_ids[None, :] < pick_ids[:, None]
    same_owner = (chosen[:, :, None] == chosen[:, None, :]) & earlier[None]
    pick_order = jnp.sum(same_owner.astype(jnp.int32), axis=2)
    head_ids = pick_ids // PICKS
    slot_ranks = lax.iota(jnp.int32, slot_count)
    matches = (
        is_live[:, None, None, :]
        & (chosen[:, None, None, :] == owners[None, :, None, None])
        & (pick_order[:, None, None, :] == slot_ranks[None, None, :, None])
    )
    was_found = jnp.any(matches, axis=3)
    head_table = jnp.sum(jnp.where(matches, head_ids[None, None, None, :], 0), axis=3)
    return (jnp.where(was_found, head_table, -1), pick_order)


def call(
    kernel, name_space, outputs, out_specs, scratch=(), flops=0, moved=0, exps=0
):
    return pl.pallas_call(
        kernel,
        in_specs=name_space,
        out_specs=out_specs,
        out_shape=outputs,
        scratch_shapes=list(scratch),
        compiler_params=pltpu.CompilerParams(vmem_limit_bytes=VMEM_BYTES),
        cost_estimate=pl.CostEstimate(flops=flops, bytes_accessed=moved, transcendentals=exps),
    )


SCALARS = pl.BlockSpec(memory_space=pltpu.SMEM)
IN_HBM = pl.BlockSpec(memory_space=pltpu.HBM)
IN_VMEM = pl.BlockSpec(memory_space=pltpu.VMEM)


def tick_kernel(here_ref, out_ref):
    out_ref[0] = here_ref[0]


def tick(here, *earlier):
    return call(
        tick_kernel,
        [SCALARS],
        jax.ShapeDtypeStruct((1,), jnp.int32),
        SCALARS,
        flops=HIGH_COST,
    )(after(here, *earlier))


def list_heads(heads_ref, start, picks_ref, block, owner, slots):
    width = picks_ref.shape[0]
    spare = heads_ref.shape[0] - 1
    for slot in range(slots):
        heads_ref[start + slot] = -1
    valid = (block >= 0) & (block < width) & (owner >= 0) & (owner < width)
    row = jnp.clip(block, 0, width - 1)
    wanted = jnp.where(valid, owner, -2)
    found = jnp.int32(0)
    for pick in range(PICKS):
        for head in range(HEADS):
            hit = picks_ref[row, pick, head] == wanted
            heads_ref[jnp.where(hit, start + found, spare)] = head
            found = found + hit.astype(jnp.int32)


def pack_kernel(here_ref, picks_ref, *refs, jobs, slots):
    is_near = jobs[0][3]
    sources = refs[: 1 + is_near]
    outputs = refs[1 + is_near : 1 + is_near + len(jobs)]
    heads_ref, sems = refs[-2], refs[-1]
    here = here_ref[0]
    listed = {}
    for shift, first, count, is_near in jobs:
        key = (shift, is_near)
        if key not in listed:
            listed[key] = len(listed) * slots
            block, owner = (here + shift, here) if is_near else (here, here - shift)
            list_heads(heads_ref, listed[key], picks_ref, block, owner, slots)
    copies = []
    for (shift, first, count, is_near), output in zip(jobs, outputs):
        for slot in range(count):
            head = jnp.maximum(heads_ref[listed[shift, is_near] + first + slot], 0)
            columns = pl.ds(pl.multiple_of(head * HD, HD), HD)
            for place, source in enumerate(sources):
                target = output.at[2 * slot + place if is_near else slot]
                copy = pltpu.make_async_copy(
                    source.at[:, columns], target, sems.at[len(copies)]
                )
                copy.start()
                copies.append(copy)
    for copy in copies:
        copy.wait()


def pack(here, picks, sources, jobs, slots):
    rows = sources[0].shape[0]
    sizes = [len(sources) * count for _, _, count, _ in jobs]
    return call(
        functools.partial(pack_kernel, jobs=jobs, slots=slots),
        [SCALARS, SCALARS] + [IN_VMEM] * len(sources),
        [jax.ShapeDtypeStruct((size, rows, HD), jnp.bfloat16) for size in sizes],
        [IN_VMEM] * len(sizes),
        [pltpu.SMEM((len(jobs) * slots + 1,), jnp.int32), pltpu.SemaphoreType.DMA((sum(sizes),))],
        moved=4 * rows * HD * sum(sizes),
    )(here, picks, *sources)


def diagonal():
    shape = (LANES, LANES)
    return lax.broadcasted_iota(jnp.int32, shape, 0) == lax.broadcasted_iota(jnp.int32, shape, 1)


def raw_scores(query_rows, key_rows):
    return lax.dot_general(
        query_rows, key_rows, (((1,), (1,)), ((), ())), preferred_element_type=jnp.float32
    )


def with_ones(value_rows):
    return jnp.concatenate([value_rows, jnp.ones_like(value_rows)], axis=1)


def soft_part(scores, value_rows):
    top = jnp.max(scores, axis=1, keepdims=True)
    weights = jnp.exp2((scores - top) * EXP2_SCALE).astype(jnp.bfloat16)
    total = jnp.dot(weights, value_rows, preferred_element_type=jnp.float32)
    sums = total[:, HD:]
    return total[:, :HD] * pl.reciprocal(sums), top * EXP2_SCALE, sums


def across_lanes(column):
    eye = diagonal()
    spread = jnp.broadcast_to(column, (column.shape[0], LANES))
    return [
        jnp.sum(jnp.where(eye, spread[at : at + LANES], 0.0), axis=0, keepdims=True)
        for at in range(0, column.shape[0], LANES)
    ]


def down_rows(line):
    spread = jnp.broadcast_to(line, (LANES, LANES))
    return jnp.sum(jnp.where(diagonal(), spread, 0.0), axis=1, keepdims=True)


def three_parts(stats):
    first = stats.astype(jnp.bfloat16).astype(jnp.float32)
    second = (stats - first).astype(jnp.bfloat16).astype(jnp.float32)
    third = stats - first - second
    parts = jnp.concatenate([first, second, third], axis=0)
    pad = jnp.zeros((STAT_ROWS - parts.shape[0], LANES), jnp.float32)
    return jnp.concatenate([parts, pad], axis=0).astype(jnp.bfloat16)


def stats_of(block, groups):
    stats = block.astype(jnp.float32)
    return stats[:groups] + stats[groups : 2 * groups] + stats[2 * groups : 3 * groups]


def log_sums(tops, sums):
    top_lines = [line for top in tops for line in across_lanes(top)]
    sum_lines = [line for part in sums for line in across_lanes(part)]
    return jnp.concatenate(top_lines, axis=0) + jnp.log2(jnp.concatenate(sum_lines, axis=0))


def attend_rows(query_rows, key_rows, value_rows, tile):
    found = [
        soft_part(raw_scores(query_rows[at : at + tile], key_rows), value_rows)
        for at in range(0, query_rows.shape[0], tile)
    ]
    outputs, tops, sums = zip(*found)
    return jnp.concatenate(outputs, axis=0), log_sums(tops, sums)


def head_columns(head):
    return pl.ds(pl.multiple_of(head * HD, HD), HD)


def attend_kernel(here_ref, picks_ref, key_ref, value_ref, *refs, group, slots):
    heads_ref = refs[-1]
    here = here_ref[0]
    for number, (shift, first, count) in enumerate(group):
        query_ref, out_ref = refs[number], refs[len(group) + number]
        rows = query_ref.shape[1]
        list_heads(heads_ref, 0, picks_ref, here + shift, here, slots)
        for slot in range(count):
            columns = head_columns(jnp.maximum(heads_ref[first + slot], 0))
            outputs, lines = attend_rows(
                query_ref[slot], key_ref[:, columns], with_ones(value_ref[:, columns]), rows
            )
            out_ref[slot, :rows, :] = outputs.astype(jnp.bfloat16)
            out_ref[slot, rows:, :] = three_parts(lines)


def attend(here, picks, keys, values, arrived, group, slots, is_anchor):
    rows = keys.shape[0]
    total = sum(count for _, _, count in group)
    return call(
        functools.partial(attend_kernel, group=group, slots=slots),
        [SCALARS, SCALARS, IN_VMEM, IN_VMEM] + [IN_VMEM] * len(group),
        [
            jax.ShapeDtypeStruct((count, rows + STAT_ROWS, HD), jnp.bfloat16)
            for _, _, count in group
        ],
        [IN_VMEM] * len(group),
        [pltpu.SMEM((slots + 1,), jnp.int32)],
        flops=HIGH_COST if is_anchor else 4 * total * rows * rows * HD,
        moved=8 * total * rows * HD,
        exps=total * rows * rows,
    )(here, picks, keys, values, *arrived)


def own_kernel(here_ref, query_ref, key_ref, value_ref, out_ref):
    rows = query_ref.shape[0]
    tile = min(rows, 256)

    def one_head(head, carry):
        columns = head_columns(head)
        value_rows = with_ones(value_ref[:, columns])
        tops, all_sums = [], []
        for at in range(0, rows, tile):
            reach = at + tile
            scores = raw_scores(query_ref[at:reach, columns], key_ref[:reach, columns])
            row_ids = lax.broadcasted_iota(jnp.int32, scores.shape, 0) + at
            seen = row_ids >= lax.broadcasted_iota(jnp.int32, scores.shape, 1)
            outputs, top, sums = soft_part(jnp.where(seen, scores, -jnp.inf), value_rows[:reach])
            out_ref[head, at:reach, :] = outputs.astype(jnp.bfloat16)
            tops.append(top)
            all_sums.append(sums)
        out_ref[head, rows:, :] = three_parts(log_sums(tops, all_sums))
        return carry

    lax.fori_loop(0, HEADS, one_head, 0, unroll=4)


def own_part(here, queries, keys, values):
    rows = queries.shape[0]
    return call(
        own_kernel,
        [SCALARS, IN_VMEM, IN_VMEM, IN_VMEM],
        jax.ShapeDtypeStruct((HEADS, rows + STAT_ROWS, HD), jnp.bfloat16),
        IN_VMEM,
        flops=4 * HEADS * rows * rows * HD,
        moved=8 * HEADS * rows * HD,
        exps=HEADS * rows * rows,
    )(here, queries, keys, values)


def near_kernel(here_ref, picks_ref, query_ref, near_ref, out_ref, heads_ref, *, shift, slots):
    rows = query_ref.shape[0]
    here = here_ref[0]
    list_heads(heads_ref, 0, picks_ref, here, here - shift, slots)
    for slot in range(slots):
        columns = head_columns(jnp.maximum(heads_ref[slot], 0))
        outputs, lines = attend_rows(
            query_ref[:, columns], near_ref[2 * slot], with_ones(near_ref[2 * slot + 1]), rows
        )
        out_ref[slot, :rows, :] = outputs.astype(jnp.bfloat16)
        out_ref[slot, rows:, :] = three_parts(lines)


def near_part(here, picks, queries, near, shift, slots):
    rows = queries.shape[0]
    return call(
        functools.partial(near_kernel, shift=shift, slots=slots),
        [SCALARS, SCALARS, IN_VMEM, IN_VMEM],
        jax.ShapeDtypeStruct((slots, rows + STAT_ROWS, HD), jnp.bfloat16),
        IN_VMEM,
        [pltpu.SMEM((slots + 1,), jnp.int32)],
        flops=4 * slots * rows * rows * HD,
        moved=12 * slots * rows * HD,
        exps=slots * rows * rows,
    )(here, picks, queries, near)


def find_spots(spots_ref, found_ref, picks_ref, here, shifts, slots):
    for owner in range(picks_ref.shape[0]):
        found_ref[owner] = 0

    for pick in range(PICKS):
        for head in range(HEADS):
            owner = picks_ref[here, pick, head]
            safe = jnp.maximum(owner, 0)
            order = found_ref[safe]
            found_ref[safe] = order + (owner >= 0).astype(jnp.int32)
            spot = jnp.int32(-1)
            for place, shift in enumerate(shifts):
                spot = jnp.where(here - safe == shift, place * slots + order, spot)
            spots_ref[head * PICKS + pick] = jnp.where(owner >= 0, spot, -1)


def merge_kernel(here_ref, picks_ref, *refs, places, shifts, slots):
    count = len(places)
    parts = refs[:count]
    result_ref, out_ref, sums_ref, held, spots_ref, found_ref, sems = refs[count:]
    groups = sums_ref.shape[1]
    rows = groups * LANES
    copies = [
        pltpu.make_async_copy(part, held.at[pl.ds(place, part.shape[0])], sems.at[number])
        for number, (part, place) in enumerate(zip(parts, places))
    ]
    for copy in copies:
        copy.start()
    find_spots(spots_ref, found_ref, picks_ref, here_ref[0], shifts, slots)
    for copy in copies:
        copy.wait()

    def one_head(head, carry):
        found = [spots_ref[head * PICKS + pick] for pick in range(PICKS)]
        spots = [head] + [jnp.where(spot >= 0, HEADS + spot, head) for spot in found]
        sums = [stats_of(held[spot, rows:, :], groups) for spot in spots]
        for pick, spot in enumerate(found):
            sums[1 + pick] = jnp.where(spot >= 0, sums[1 + pick], -jnp.inf)
        top = functools.reduce(jnp.maximum, sums)
        shares = [jnp.exp2(part - top) for part in sums]
        whole = functools.reduce(jnp.add, shares)
        sums_ref[head] = top + jnp.log2(whole)
        for group in range(groups):
            span = pl.ds(group * LANES, LANES)
            own = held[head, span, :].astype(jnp.float32)
            mixed = own
            for spot, share in zip(spots[1:], shares[1:]):
                weight = down_rows((share / whole)[group : group + 1, :])
                mixed = mixed + (held[spot, span, :].astype(jnp.float32) - own) * weight
            out_ref[head, span, :] = mixed
            result_ref[span, head_columns(head)] = mixed.astype(jnp.bfloat16)
        return carry

    lax.fori_loop(0, HEADS, one_head, 0, unroll=2)


def merge(here, picks, parts, places, shifts, slots):
    rows = parts[0].shape[1] - STAT_ROWS
    width = picks.shape[0]
    total = HEADS + len(shifts) * slots
    return call(
        functools.partial(merge_kernel, places=tuple(places), shifts=shifts, slots=slots),
        [SCALARS, SCALARS] + [pl.BlockSpec(memory_space=pl.ANY)] * len(parts),
        [
            jax.ShapeDtypeStruct((rows, HEADS * HD), jnp.bfloat16),
            jax.ShapeDtypeStruct((HEADS, rows, HD), jnp.float32),
            jax.ShapeDtypeStruct((HEADS, rows // LANES, LANES), jnp.float32),
        ],
        [IN_VMEM, IN_VMEM, IN_VMEM],
        [
            pltpu.VMEM((total, rows + STAT_ROWS, HD), jnp.bfloat16),
            pltpu.SMEM((PICKS * HEADS,), jnp.int32),
            pltpu.SMEM((width,), jnp.int32),
            pltpu.SemaphoreType.DMA((len(parts),)),
        ],
        flops=6 * HEADS * rows * HD,
        moved=2 * (HEADS * 2 + total) * rows * HD,
    )(here, picks, *parts)


def finish_kernel(
    here_ref, picks_ref, mixed_ref, sums_ref, part_ref, old_ref, out_ref, heads_ref, held, sems, *, shift, slots
):
    del old_ref
    groups = sums_ref.shape[1]
    rows = groups * LANES
    here = here_ref[0]
    list_heads(heads_ref, 0, picks_ref, here, here - shift, slots)

    def patch(slot):
        columns = head_columns(jnp.maximum(heads_ref[slot], 0))
        return pltpu.make_async_copy(held.at[slot], out_ref.at[:, columns], sems.at[slot])

    for slot in range(slots):

        @pl.when(heads_ref[slot] >= 0)
        def _():
            head = heads_ref[slot]
            added = stats_of(part_ref[slot, rows:, :], groups)
            share = 1.0 / (1.0 + jnp.exp2(sums_ref[head] - added))
            for group in range(groups):
                span = pl.ds(group * LANES, LANES)
                old = mixed_ref[head, span, :]
                new = part_ref[slot, span, :].astype(jnp.float32)
                mixed = old + (new - old) * down_rows(share[group : group + 1, :])
                held[slot, span, :] = mixed.astype(jnp.bfloat16)
            patch(slot).start()

    for slot in range(slots):

        @pl.when(heads_ref[slot] >= 0)
        def _():
            patch(slot).wait()


def finish(here, picks, result, mixed, sums, part, shift, slots):
    heads, rows, _ = mixed.shape
    return pl.pallas_call(
        functools.partial(finish_kernel, shift=shift, slots=slots),
        in_specs=[SCALARS, SCALARS, IN_VMEM, IN_VMEM, IN_VMEM, IN_HBM],
        out_specs=IN_HBM,
        out_shape=jax.ShapeDtypeStruct(result.shape, result.dtype),
        scratch_shapes=[
            pltpu.SMEM((slots + 1,), jnp.int32),
            pltpu.VMEM((slots, rows, HD), jnp.bfloat16),
            pltpu.SemaphoreType.DMA((slots,)),
        ],
        input_output_aliases={5: 0},
        compiler_params=pltpu.CompilerParams(vmem_limit_bytes=VMEM_BYTES),
        cost_estimate=pl.CostEstimate(
            flops=2 * slots * rows * HD, bytes_accessed=8 * slots * rows * HD, transcendentals=0
        ),
    )(here, picks, mixed, sums, part, result)


def after(value, *earlier):
    return lax.optimization_barrier((value,) + earlier)[0]


def groups_in_order(width, slots):
    middle = width // 2
    groups = [[(middle, 0, slots)], [(shift, 0, slots) for shift in (1, width - 1)]]
    for low in range(3, middle):
        size = max(1, slots // 2)
        for first in range(0, slots, size):
            count = min(size, slots - first)
            groups.append([(low, first, count), (width - low, first, count)])
    return groups + [[(width - 2, 0, slots)]]


def travelling_queries(queries, keys, values, picks):
    width = lax.axis_size("ctx")
    sections = lax.axis_size("pipe")
    slots = max(1, PICKS * HEADS // width)
    here = lax.axis_index("ctx").astype(jnp.int32).reshape(1)
    queries, keys, values = queries[0], keys[0], values[0]
    own_picks = picks[0].transpose(0, 2, 1)

    groups = groups_in_order(width, slots)
    near_shift = 2
    near_jobs = [(near_shift, 0, slots, True)]
    query_jobs = [piece + (False,) for group in groups for piece in group]

    def up(value, shift):
        return lax.ppermute(value, "ctx", [(at, at + shift) for at in range(width - shift)])

    def down(value, shift):
        return lax.ppermute(value, "ctx", [(at, at - shift) for at in range(shift, width)])

    def up_and_on(value, shift):
        pairs = [
            (at * sections + section, (at + shift) * sections + (section + 1) % sections)
            for at in range(width - shift)
            for section in range(sections)
        ]
        return lax.ppermute(value, ("ctx", "pipe"), pairs)

    near_send = pack(here, own_picks, [keys, values], near_jobs, slots)[0]
    near = up(near_send, near_shift)
    sends, now = {}, after(here, near_send)
    for jobs in (query_jobs[:1], query_jobs[1:]):
        packed = pack(now, own_picks, [queries], jobs, slots)
        sends |= {job[:3]: send for job, send in zip(jobs, packed)}
        now = after(now, *packed)
    arrived = {}

    def attend_group(token, group, is_anchor=False):
        return dict(
            zip(
                group,
                attend(
                    token,
                    own_picks,
                    keys,
                    values,
                    [arrived[piece] for piece in group],
                    tuple(group),
                    slots,
                    is_anchor,
                ),
            )
        )

    def ask_for(group, *earlier):
        for piece in group:
            send = after(sends[piece], *earlier) if earlier else sends[piece]
            arrived[piece] = down(send, piece[0])

    def send_back(parts):
        for piece, part in parts.items():
            if len(returned) >= 3:
                part = after(part, list(returned.values())[-3])
            returned[piece] = up_and_on(part, piece[0])

    def those(found, group):
        return [found[piece] for piece in group]

    returned = {}
    ask_for(groups[0])
    own = own_part(now, queries, keys, values)
    own_back = passed_along(own, "pipe", 1)
    ask_for(groups[1], own)
    now = after(here, own)
    for number, group in enumerate(groups):
        if number == 0:
            ask_for(groups[2][:1], now, *those(arrived, group))
        elif number == 1:
            ask_for(groups[2][1:], now, *those(arrived, group))
        elif number + 1 < len(groups):
            ask_for(groups[number + 1], now, *those(arrived, group))
        if number == 2:
            now = after(now, own_back)
        if number == len(groups) - 1:
            now = tick(now, *list(returned.values())[-4:-2])
        parts = attend_group(now, group, is_anchor=number in (1, 2))
        send_back(parts)
        now = after(now, *parts.values())
        if number == 0:
            beside = near_part(now, own_picks, queries, near, near_shift, slots)
            now = after(now, beside)
        if number == 3:
            beside_back = passed_along(after(beside, *parts.values()), "pipe", 1)
    before = passed_along(after(own_picks, now), "pipe", 1)
    now = tick(now)

    final = groups[-1][0]
    others = [shift for shift in range(1, width) if shift not in (near_shift, final[0])]
    merged_shifts = (near_shift,) + tuple(others)
    pieces = [piece for piece in returned if piece != final]
    places = [HEADS + merged_shifts.index(shift) * slots + first for shift, first, _ in pieces]
    parts = [own_back, beside_back] + [returned[piece] for piece in pieces]
    result, mixed, sums = merge(now, before, parts, [0, HEADS] + places, merged_shifts, slots)
    result = finish(now, before, result, mixed, sums, returned[final], final[0], slots)
    return result[None]


def travelling_keys(queries, keys, values, picks):
    ctx_width = lax.axis_size("ctx")
    rank_here = lax.axis_index("ctx")
    slot_count = max(1, PICKS * HEADS // ctx_width)
    block_rows = queries.shape[1]
    score_scale = HD ** (-0.5)
    every_pick = picks[0].reshape(ctx_width, HEADS * PICKS)
    chosen = lax.dynamic_slice_in_dim(every_pick, rank_here, 1, 0)
    pick_order = request_table(chosen, lax.iota(jnp.int32, ctx_width), slot_count)[1]
    asked_table = request_table(every_pick, rank_here.reshape(1), slot_count)[0]
    asked_heads = asked_table[:, 0, :]
    safe_asked = jnp.maximum(asked_heads, 0)
    query_heads = queries[0].reshape(block_rows, HEADS, HD).transpose(1, 0, 2)
    key_heads = keys[0].reshape(block_rows, HEADS, HD).transpose(1, 0, 2)
    value_heads = values[0].reshape(block_rows, HEADS, HD).transpose(1, 0, 2)
    is_live = chosen[0] >= 0
    flat_slot = jnp.where(is_live, chosen[0] * slot_count + pick_order[0], 0)
    remote_mask = jnp.repeat(is_live.reshape(HEADS, PICKS), block_rows, axis=1)
    row_index = lax.iota(jnp.int32, block_rows)
    causal = row_index[:, None] >= row_index[None, :]

    def masked_scores(query_head, key_rows, mask_row):
        scores = lax.dot_general(
            query_head, key_rows, (((1,), (1,)), ((), ())), preferred_element_type=jnp.float32
        )
        allowed = jnp.concatenate(
            [causal, jnp.broadcast_to(mask_row[None, :], (block_rows, PICKS * block_rows))], axis=1
        )
        return jnp.where(allowed, scores * score_scale, -jnp.inf)

    def row_stats(scores):
        row_top = jnp.max(scores, axis=1)
        row_total = jnp.sum(jnp.exp(scores - row_top[:, None]), axis=1)
        return (row_top, row_total)

    def weighted(scores, row_top, row_total, value_rows):
        prob_rows = (jnp.exp(scores - row_top[:, None]) / row_total[:, None]).astype(jnp.bfloat16)
        return jnp.dot(prob_rows, value_rows, preferred_element_type=jnp.float32).astype(
            jnp.bfloat16
        )

    send_both = jnp.concatenate([key_heads, value_heads], axis=2)[safe_asked]
    got_slots = lax.all_to_all(send_both, "ctx", split_axis=0, concat_axis=0, tiled=True)
    last_width = 2 * HD
    flat_slots = got_slots.reshape(ctx_width * slot_count, block_rows, last_width)
    remote_both = flat_slots[flat_slot].reshape(HEADS, PICKS * block_rows, last_width)
    all_keys = jnp.concatenate([key_heads, remote_both[:, :, :HD]], axis=1)
    all_values = jnp.concatenate([value_heads, remote_both[:, :, HD:]], axis=1)

    def per_head(head_items):
        query_head, key_rows, value_rows, mask_row = head_items
        scores = masked_scores(query_head, key_rows, mask_row)
        row_top, row_total = row_stats(scores)
        return weighted(scores, row_top, row_total, value_rows)

    outputs = lax.map(per_head, (query_heads, all_keys, all_values, remote_mask))
    merged = outputs.transpose(1, 0, 2).reshape(1, block_rows, HEADS * HD)
    return passed_along(merged, "pipe", 1)


def per_device(queries, keys, values, picks):
    few_shifts = 8 <= lax.axis_size("ctx") <= 16
    run = travelling_queries if few_shifts else travelling_keys
    return run(queries, keys, values, picks)


def solution(mesh):
    placed = (
        P("pipe", "ctx", None),
        P("pipe", "ctx", None),
        P("pipe", "ctx", None),
        P("pipe", None, None, None),
    )
    return jax.shard_map(
        per_device, mesh=mesh, in_specs=placed, out_specs=P("pipe", "ctx", None), check_vma=False
    )
```

```python
import functools
import math

import jax
import jax.numpy as jnp
from jax import lax
from jax.experimental import pallas as pl
from jax.experimental.pallas import tpu as pltpu
from jax.sharding import PartitionSpec as P

HEADS = 16
HD = 128
PICKS = 2
EXP2_SCALE = HD ** -0.5 * math.log2(math.e)
LANES = 128
STAT_ROWS = 16
VMEM_BYTES = 24 * 1024 * 1024
HIGH_COST = 10**12


def passed_along(value, axis, steps):
    count = lax.axis_size(axis)
    pairs = [(source, (source + steps) % count) for source in range(count)]
    return lax.ppermute(value, axis, pairs)


def request_table(chosen, owners, slot_count):
    pick_count = chosen.shape[1]
    pick_ids = lax.iota(jnp.int32, pick_count)
    is_live = chosen >= 0
    earlier = pick_ids[None, :] < pick_ids[:, None]
    same_owner = (chosen[:, :, None] == chosen[:, None, :]) & earlier[None]
    pick_order = jnp.sum(same_owner.astype(jnp.int32), axis=2)
    head_ids = pick_ids // PICKS
    slot_ranks = lax.iota(jnp.int32, slot_count)
    matches = (
        is_live[:, None, None, :]
        & (chosen[:, None, None, :] == owners[None, :, None, None])
        & (pick_order[:, None, None, :] == slot_ranks[None, None, :, None])
    )
    was_found = jnp.any(matches, axis=3)
    head_table = jnp.sum(jnp.where(matches, head_ids[None, None, None, :], 0), axis=3)
    return (jnp.where(was_found, head_table, -1), pick_order)


def call(
    kernel, name_space, outputs, out_specs, scratch=(), flops=0, moved=0, exps=0
):
    return pl.pallas_call(
        kernel,
        in_specs=name_space,
        out_specs=out_specs,
        out_shape=outputs,
        scratch_shapes=list(scratch),
        compiler_params=pltpu.CompilerParams(vmem_limit_bytes=VMEM_BYTES),
        cost_estimate=pl.CostEstimate(flops=flops, bytes_accessed=moved, transcendentals=exps),
    )


SCALARS = pl.BlockSpec(memory_space=pltpu.SMEM)
IN_HBM = pl.BlockSpec(memory_space=pltpu.HBM)
IN_VMEM = pl.BlockSpec(memory_space=pltpu.VMEM)


def tick_kernel(here_ref, out_ref):
    out_ref[0] = here_ref[0]


def tick(here, *earlier):
    return call(
        tick_kernel,
        [SCALARS],
        jax.ShapeDtypeStruct((1,), jnp.int32),
        SCALARS,
        flops=0,
    )(after(here, *earlier))


def list_heads(heads_ref, start, picks_ref, block, owner, slots):
    width = picks_ref.shape[0]
    spare = heads_ref.shape[0] - 1
    for slot in range(slots):
        heads_ref[start + slot] = -1
    valid = (block >= 0) & (block < width) & (owner >= 0) & (owner < width)
    row = jnp.clip(block, 0, width - 1)
    wanted = jnp.where(valid, owner, -2)
    found = jnp.int32(0)
    for pick in range(PICKS):
        for head in range(HEADS):
            hit = picks_ref[row, pick, head] == wanted
            heads_ref[jnp.where(hit, start + found, spare)] = head
            found = found + hit.astype(jnp.int32)


def pack_kernel(here_ref, picks_ref, *refs, jobs, slots):
    is_near = jobs[0][3]
    sources = refs[: 1 + is_near]
    outputs = refs[1 + is_near : 1 + is_near + len(jobs)]
    heads_ref, sems = refs[-2], refs[-1]
    here = here_ref[0]
    listed = {}
    for shift, first, count, is_near in jobs:
        key = (shift, is_near)
        if key not in listed:
            listed[key] = len(listed) * slots
            block, owner = (here + shift, here) if is_near else (here, here - shift)
            list_heads(heads_ref, listed[key], picks_ref, block, owner, slots)
    copies = []
    for (shift, first, count, is_near), output in zip(jobs, outputs):
        for slot in range(count):
            head = jnp.maximum(heads_ref[listed[shift, is_near] + first + slot], 0)
            columns = pl.ds(pl.multiple_of(head * HD, HD), HD)
            for place, source in enumerate(sources):
                target = output.at[2 * slot + place if is_near else slot]
                copy = pltpu.make_async_copy(
                    source.at[:, columns], target, sems.at[len(copies)]
                )
                copy.start()
                copies.append(copy)
    for copy in copies:
        copy.wait()


def pack(here, picks, sources, jobs, slots):
    rows = sources[0].shape[0]
    sizes = [len(sources) * count for _, _, count, _ in jobs]
    return call(
        functools.partial(pack_kernel, jobs=jobs, slots=slots),
        [SCALARS, SCALARS] + [IN_VMEM] * len(sources),
        [jax.ShapeDtypeStruct((size, rows, HD), jnp.bfloat16) for size in sizes],
        [IN_VMEM] * len(sizes),
        [pltpu.SMEM((len(jobs) * slots + 1,), jnp.int32), pltpu.SemaphoreType.DMA((sum(sizes),))],
        moved=4 * rows * HD * sum(sizes),
    )(here, picks, *sources)


def diagonal():
    shape = (LANES, LANES)
    return lax.broadcasted_iota(jnp.int32, shape, 0) == lax.broadcasted_iota(jnp.int32, shape, 1)


def raw_scores(query_rows, key_rows):
    return lax.dot_general(
        query_rows, key_rows, (((1,), (1,)), ((), ())), preferred_element_type=jnp.float32
    )


def with_ones(value_rows):
    return jnp.concatenate([value_rows, jnp.ones_like(value_rows)], axis=1)


def soft_part(scores, value_rows):
    top = jnp.max(scores, axis=1, keepdims=True)
    weights = jnp.exp2((scores - top) * EXP2_SCALE).astype(jnp.bfloat16)
    total = jnp.dot(weights, value_rows, preferred_element_type=jnp.float32)
    sums = total[:, HD:]
    return total[:, :HD] * pl.reciprocal(sums), top * EXP2_SCALE, sums


def across_lanes(column):
    eye = diagonal()
    spread = jnp.broadcast_to(column, (column.shape[0], LANES))
    return [
        jnp.sum(jnp.where(eye, spread[at : at + LANES], 0.0), axis=0, keepdims=True)
        for at in range(0, column.shape[0], LANES)
    ]


def down_rows(line):
    spread = jnp.broadcast_to(line, (LANES, LANES))
    return jnp.sum(jnp.where(diagonal(), spread, 0.0), axis=1, keepdims=True)


def three_parts(stats):
    first = stats.astype(jnp.bfloat16).astype(jnp.float32)
    second = (stats - first).astype(jnp.bfloat16).astype(jnp.float32)
    third = stats - first - second
    parts = jnp.concatenate([first, second, third], axis=0)
    pad = jnp.zeros((STAT_ROWS - parts.shape[0], LANES), jnp.float32)
    return jnp.concatenate([parts, pad], axis=0).astype(jnp.bfloat16)


def stats_of(block, groups):
    stats = block.astype(jnp.float32)
    return stats[:groups] + stats[groups : 2 * groups] + stats[2 * groups : 3 * groups]


def log_sums(tops, sums):
    top_lines = [line for top in tops for line in across_lanes(top)]
    sum_lines = [line for part in sums for line in across_lanes(part)]
    return jnp.concatenate(top_lines, axis=0) + jnp.log2(jnp.concatenate(sum_lines, axis=0))


def attend_rows(query_rows, key_rows, value_rows, tile):
    found = [
        soft_part(raw_scores(query_rows[at : at + tile], key_rows), value_rows)
        for at in range(0, query_rows.shape[0], tile)
    ]
    outputs, tops, sums = zip(*found)
    return jnp.concatenate(outputs, axis=0), log_sums(tops, sums)


def head_columns(head):
    return pl.ds(pl.multiple_of(head * HD, HD), HD)


def attend_kernel(here_ref, picks_ref, key_ref, value_ref, *refs, group, slots):
    heads_ref = refs[-1]
    here = here_ref[0]
    for number, (shift, first, count) in enumerate(group):
        query_ref, out_ref = refs[number], refs[len(group) + number]
        rows = query_ref.shape[1]
        list_heads(heads_ref, 0, picks_ref, here + shift, here, slots)
        for slot in range(count):
            columns = head_columns(jnp.maximum(heads_ref[first + slot], 0))
            outputs, lines = attend_rows(
                query_ref[slot], key_ref[:, columns], with_ones(value_ref[:, columns]), rows
            )
            out_ref[slot, :rows, :] = outputs.astype(jnp.bfloat16)
            out_ref[slot, rows:, :] = three_parts(lines)


def attend(here, picks, keys, values, arrived, group, slots, is_anchor):
    rows = keys.shape[0]
    total = sum(count for _, _, count in group)
    return call(
        functools.partial(attend_kernel, group=group, slots=slots),
        [SCALARS, SCALARS, IN_VMEM, IN_VMEM] + [IN_VMEM] * len(group),
        [
            jax.ShapeDtypeStruct((count, rows + STAT_ROWS, HD), jnp.bfloat16)
            for _, _, count in group
        ],
        [IN_VMEM] * len(group),
        [pltpu.SMEM((slots + 1,), jnp.int32)],
        flops=HIGH_COST if is_anchor else 4 * total * rows * rows * HD,
        moved=8 * total * rows * HD,
        exps=total * rows * rows,
    )(here, picks, keys, values, *arrived)


def own_kernel(here_ref, query_ref, key_ref, value_ref, out_ref):
    rows = query_ref.shape[0]
    tile = min(rows, 256)

    def one_head(head, carry):
        columns = head_columns(head)
        value_rows = with_ones(value_ref[:, columns])
        tops, all_sums = [], []
        for at in range(0, rows, tile):
            reach = at + tile
            scores = raw_scores(query_ref[at:reach, columns], key_ref[:reach, columns])
            row_ids = lax.broadcasted_iota(jnp.int32, scores.shape, 0) + at
            seen = row_ids >= lax.broadcasted_iota(jnp.int32, scores.shape, 1)
            outputs, top, sums = soft_part(jnp.where(seen, scores, -jnp.inf), value_rows[:reach])
            out_ref[head, at:reach, :] = outputs.astype(jnp.bfloat16)
            tops.append(top)
            all_sums.append(sums)
        out_ref[head, rows:, :] = three_parts(log_sums(tops, all_sums))
        return carry

    lax.fori_loop(0, HEADS, one_head, 0, unroll=4)


def own_part(here, queries, keys, values):
    rows = queries.shape[0]
    return call(
        own_kernel,
        [SCALARS, IN_VMEM, IN_VMEM, IN_VMEM],
        jax.ShapeDtypeStruct((HEADS, rows + STAT_ROWS, HD), jnp.bfloat16),
        IN_VMEM,
        flops=4 * HEADS * rows * rows * HD,
        moved=8 * HEADS * rows * HD,
        exps=HEADS * rows * rows,
    )(here, queries, keys, values)


def near_kernel(here_ref, picks_ref, query_ref, *refs, shifts, slots):
    near_refs, out_ref, heads_ref = refs[: len(shifts)], refs[-2], refs[-1]
    rows = query_ref.shape[0]
    here = here_ref[0]
    for place, (shift, near_ref) in enumerate(zip(shifts, near_refs)):
        list_heads(heads_ref, 0, picks_ref, here, here - shift, slots)
        for slot in range(slots):
            columns = head_columns(jnp.maximum(heads_ref[slot], 0))
            outputs, lines = attend_rows(
                query_ref[:, columns], near_ref[2 * slot], with_ones(near_ref[2 * slot + 1]), rows
            )
            out_ref[place * slots + slot, :rows, :] = outputs.astype(jnp.bfloat16)
            out_ref[place * slots + slot, rows:, :] = three_parts(lines)


def near_part(here, picks, queries, near, shifts, slots):
    rows = queries.shape[0]
    total = len(shifts) * slots
    return call(
        functools.partial(near_kernel, shifts=shifts, slots=slots),
        [SCALARS, SCALARS, IN_VMEM] + [IN_VMEM] * len(shifts),
        jax.ShapeDtypeStruct((total, rows + STAT_ROWS, HD), jnp.bfloat16),
        IN_VMEM,
        [pltpu.SMEM((slots + 1,), jnp.int32)],
        flops=4 * total * rows * rows * HD,
        moved=12 * total * rows * HD,
        exps=total * rows * rows,
    )(here, picks, queries, *near)


def find_spots(spots_ref, found_ref, picks_ref, here, shifts, slots):
    for owner in range(picks_ref.shape[0]):
        found_ref[owner] = 0

    for pick in range(PICKS):
        for head in range(HEADS):
            owner = picks_ref[here, pick, head]
            safe = jnp.maximum(owner, 0)
            order = found_ref[safe]
            found_ref[safe] = order + (owner >= 0).astype(jnp.int32)
            spot = jnp.int32(-1)
            for place, shift in enumerate(shifts):
                spot = jnp.where(here - safe == shift, place * slots + order, spot)
            spots_ref[head * PICKS + pick] = jnp.where(owner >= 0, spot, -1)


def merge_kernel(here_ref, picks_ref, *refs, places, shifts, slots):
    count = len(places)
    parts = refs[:count]
    result_ref, out_ref, sums_ref, held, spots_ref, found_ref, sems = refs[count:]
    groups = sums_ref.shape[1]
    rows = groups * LANES
    copies = [
        pltpu.make_async_copy(part, held.at[pl.ds(place, part.shape[0])], sems.at[number])
        for number, (part, place) in enumerate(zip(parts, places))
    ]
    for copy in copies:
        copy.start()
    find_spots(spots_ref, found_ref, picks_ref, here_ref[0], shifts, slots)
    for copy in copies:
        copy.wait()

    def one_head(head, carry):
        found = [spots_ref[head * PICKS + pick] for pick in range(PICKS)]
        spots = [head] + [jnp.where(spot >= 0, HEADS + spot, head) for spot in found]
        sums = [stats_of(held[spot, rows:, :], groups) for spot in spots]
        for pick, spot in enumerate(found):
            sums[1 + pick] = jnp.where(spot >= 0, sums[1 + pick], -jnp.inf)
        top = functools.reduce(jnp.maximum, sums)
        shares = [jnp.exp2(part - top) for part in sums]
        whole = functools.reduce(jnp.add, shares)
        sums_ref[head] = top + jnp.log2(whole)
        for group in range(groups):
            span = pl.ds(group * LANES, LANES)
            own = held[head, span, :].astype(jnp.float32)
            mixed = own
            for spot, share in zip(spots[1:], shares[1:]):
                weight = down_rows((share / whole)[group : group + 1, :])
                mixed = mixed + (held[spot, span, :].astype(jnp.float32) - own) * weight
            out_ref[head, span, :] = mixed
            result_ref[span, head_columns(head)] = mixed.astype(jnp.bfloat16)
        return carry

    lax.fori_loop(0, HEADS, one_head, 0, unroll=2)


def merge(here, picks, parts, places, shifts, slots):
    rows = parts[0].shape[1] - STAT_ROWS
    width = picks.shape[0]
    total = HEADS + len(shifts) * slots
    return call(
        functools.partial(merge_kernel, places=tuple(places), shifts=shifts, slots=slots),
        [SCALARS, SCALARS] + [pl.BlockSpec(memory_space=pl.ANY)] * len(parts),
        [
            jax.ShapeDtypeStruct((rows, HEADS * HD), jnp.bfloat16),
            jax.ShapeDtypeStruct((HEADS, rows, HD), jnp.float32),
            jax.ShapeDtypeStruct((HEADS, rows // LANES, LANES), jnp.float32),
        ],
        [IN_VMEM, IN_VMEM, IN_VMEM],
        [
            pltpu.VMEM((total, rows + STAT_ROWS, HD), jnp.bfloat16),
            pltpu.SMEM((PICKS * HEADS,), jnp.int32),
            pltpu.SMEM((width,), jnp.int32),
            pltpu.SemaphoreType.DMA((len(parts),)),
        ],
        flops=6 * HEADS * rows * HD,
        moved=2 * (HEADS * 2 + total) * rows * HD,
    )(here, picks, *parts)


def finish_kernel(here_ref, picks_ref, mixed_ref, sums_ref, *refs, shifts, slots):
    count = len(shifts)
    parts, out_ref, (heads_ref, held, sems) = refs[:count], refs[count + 1], refs[count + 2 :]
    groups = sums_ref.shape[1]
    rows = groups * LANES
    here = here_ref[0]
    for number, shift in enumerate(shifts):
        list_heads(heads_ref, number * slots, picks_ref, here, here - shift, slots)

    def slot_of(head, number):
        found = jnp.int32(-1)
        for slot in range(slots):
            found = jnp.where(heads_ref[number * slots + slot] == head, slot, found)
        return found

    def is_first(head, number):
        first = head >= 0
        for earlier in range(number):
            first = first & (slot_of(head, earlier) < 0)
        return first

    def patch(place):
        columns = head_columns(jnp.maximum(heads_ref[place], 0))
        return pltpu.make_async_copy(held.at[place], out_ref.at[:, columns], sems.at[place])

    places = [(number, number * slots + slot) for number in range(count) for slot in range(slots)]
    for number, place in places:
        head = heads_ref[place]

        @pl.when(is_first(head, number))
        def _():
            found = [slot_of(head, later) for later in range(number, count)]
            spots = [jnp.maximum(spot, 0) for spot in found]
            sums = [sums_ref[head]]
            for part, spot, safe in zip(parts[number:], found, spots):
                added = stats_of(part[safe, rows:, :], groups)
                sums.append(jnp.where(spot >= 0, added, -jnp.inf))
            top = functools.reduce(jnp.maximum, sums)
            shares = [jnp.exp2(part - top) for part in sums]
            whole = functools.reduce(jnp.add, shares)
            for group in range(groups):
                span = pl.ds(group * LANES, LANES)
                before = mixed_ref[head, span, :]
                mixed = before
                for part, spot, safe, share in zip(parts[number:], found, spots, shares[1:]):
                    new = jnp.where(spot >= 0, part[safe, span, :].astype(jnp.float32), 0.0)
                    weight = down_rows((share / whole)[group : group + 1, :])
                    mixed = mixed + (new - before) * weight
                held[place, span, :] = mixed.astype(jnp.bfloat16)
            patch(place).start()

    for number, place in places:

        @pl.when(is_first(heads_ref[place], number))
        def _():
            patch(place).wait()


def finish(here, picks, result, mixed, sums, parts, shifts, slots):
    rows = mixed.shape[1]
    total = len(shifts) * slots
    return pl.pallas_call(
        functools.partial(finish_kernel, shifts=shifts, slots=slots),
        in_specs=[SCALARS, SCALARS] + [IN_VMEM] * (2 + len(parts)) + [IN_HBM],
        out_specs=IN_HBM,
        out_shape=jax.ShapeDtypeStruct(result.shape, result.dtype),
        scratch_shapes=[
            pltpu.SMEM((total + 1,), jnp.int32),
            pltpu.VMEM((total, rows, HD), jnp.bfloat16),
            pltpu.SemaphoreType.DMA((total,)),
        ],
        input_output_aliases={4 + len(parts): 0},
        compiler_params=pltpu.CompilerParams(vmem_limit_bytes=VMEM_BYTES),
        cost_estimate=pl.CostEstimate(
            flops=2 * total * rows * HD, bytes_accessed=8 * total * rows * HD, transcendentals=0
        ),
    )(here, picks, mixed, sums, *parts, result)


def after(value, *earlier):
    return lax.optimization_barrier((value,) + earlier)[0]


def travelling_queries(queries, keys, values, picks):
    width = lax.axis_size("ctx")
    sections = lax.axis_size("pipe")
    slots = max(1, PICKS * HEADS // width)
    here = lax.axis_index("ctx").astype(jnp.int32).reshape(1)
    queries, keys, values = queries[0], keys[0], values[0]
    own_picks = picks[0].transpose(0, 2, 1)

    near_shifts = (2, width - 2)
    middle = width // 2
    far_shifts = [middle, 1, width - 1]
    for low in range(middle - 1, 2, -1):
        far_shifts += [low, width - low]
    final_shifts = tuple(far_shifts[-2:])

    def up(value, shift):
        return lax.ppermute(value, "ctx", [(at, at + shift) for at in range(width - shift)])

    def down(value, shift):
        return lax.ppermute(value, "ctx", [(at, at - shift) for at in range(shift, width)])

    def up_and_on(value, shift):
        pairs = [
            (at * sections + section, (at + shift) * sections + (section + 1) % sections)
            for at in range(width - shift)
            for section in range(sections)
        ]
        return lax.ppermute(value, ("ctx", "pipe"), pairs)

    near_jobs = [(shift, 0, slots, True) for shift in near_shifts]
    near_sends = pack(here, own_picks, [keys, values], near_jobs, slots)
    near = [up(near_sends[0], near_shifts[0])]
    before = passed_along(own_picks, "pipe", 1)
    sends, now = {}, after(here, *near_sends)
    for shifts in (far_shifts[:1], far_shifts[1:]):
        jobs = [(shift, 0, slots, False) for shift in shifts]
        packed = pack(now, own_picks, [queries], jobs, slots)
        sends |= zip(shifts, packed)
        now = after(now, *packed)
    arrived, returned = {}, {}

    def ask_for(shift, *earlier):
        arrived[shift] = down(after(sends[shift], *earlier), shift)

    def work(token, shift, is_anchor=False):
        return attend(
            token, own_picks, keys, values, [arrived[shift]], ((shift, 0, slots),), slots, is_anchor
        )[0]

    four, one, seven, three, five = far_shifts
    ask_for(four, near_sends[0])
    own = own_part(after(now, before), queries, keys, values)
    own_back = passed_along(own, "pipe", 1)
    near.append(up(after(near_sends[1], own), near_shifts[1]))
    ask_for(one, arrived[four], near[0], own)
    ask_for(seven, arrived[four], near[0], own)
    part_four = work(after(here, own, near[0]), four, is_anchor=True)
    returned[four] = up_and_on(after(part_four, own_back), four)
    part_one = work(after(here, part_four, own_back), one, is_anchor=True)
    ask_for(three, own_back, part_four, arrived[one])
    part_seven = work(after(here, part_one, own_back), seven, is_anchor=True)
    ask_for(five, arrived[one], part_four)
    returned[one] = up_and_on(after(part_one, *near), one)
    returned[seven] = up_and_on(after(part_seven, *near), seven)
    beside = near_part(after(here, part_seven), own_picks, queries, near, near_shifts, slots)
    part_three = work(after(here, beside, returned[four]), three, is_anchor=True)
    returned[three] = up_and_on(after(part_three, returned[four]), three)
    beside_back = passed_along(after(beside, arrived[three]), "pipe", 1)
    part_five = work(after(here, part_three, returned[one]), five, is_anchor=True)
    returned[five] = up_and_on(after(part_five, returned[one]), five)
    now = after(here, part_five)

    merged_shifts = near_shifts + (four, one, seven)
    places = [HEADS + place * slots for place in range(2, 5)]
    parts = [own_back, beside_back] + [returned[shift] for shift in (four, one, seven)]
    result, mixed, sums = merge(now, before, parts, [0, HEADS] + places, merged_shifts, slots)
    lasts = [returned[shift] for shift in final_shifts]
    now = tick(now, sums, returned[three])
    return finish(now, before, result, mixed, sums, lasts, final_shifts, slots)[None]


def travelling_keys(queries, keys, values, picks):
    ctx_width = lax.axis_size("ctx")
    rank_here = lax.axis_index("ctx")
    slot_count = max(1, PICKS * HEADS // ctx_width)
    block_rows = queries.shape[1]
    score_scale = HD ** (-0.5)
    every_pick = picks[0].reshape(ctx_width, HEADS * PICKS)
    chosen = lax.dynamic_slice_in_dim(every_pick, rank_here, 1, 0)
    pick_order = request_table(chosen, lax.iota(jnp.int32, ctx_width), slot_count)[1]
    asked_table = request_table(every_pick, rank_here.reshape(1), slot_count)[0]
    asked_heads = asked_table[:, 0, :]
    safe_asked = jnp.maximum(asked_heads, 0)
    query_heads = queries[0].reshape(block_rows, HEADS, HD).transpose(1, 0, 2)
    key_heads = keys[0].reshape(block_rows, HEADS, HD).transpose(1, 0, 2)
    value_heads = values[0].reshape(block_rows, HEADS, HD).transpose(1, 0, 2)
    is_live = chosen[0] >= 0
    flat_slot = jnp.where(is_live, chosen[0] * slot_count + pick_order[0], 0)
    remote_mask = jnp.repeat(is_live.reshape(HEADS, PICKS), block_rows, axis=1)
    row_index = lax.iota(jnp.int32, block_rows)
    causal = row_index[:, None] >= row_index[None, :]

    def masked_scores(query_head, key_rows, mask_row):
        scores = lax.dot_general(
            query_head, key_rows, (((1,), (1,)), ((), ())), preferred_element_type=jnp.float32
        )
        allowed = jnp.concatenate(
            [causal, jnp.broadcast_to(mask_row[None, :], (block_rows, PICKS * block_rows))], axis=1
        )
        return jnp.where(allowed, scores * score_scale, -jnp.inf)

    def row_stats(scores):
        row_top = jnp.max(scores, axis=1)
        row_total = jnp.sum(jnp.exp(scores - row_top[:, None]), axis=1)
        return (row_top, row_total)

    def weighted(scores, row_top, row_total, value_rows):
        prob_rows = (jnp.exp(scores - row_top[:, None]) / row_total[:, None]).astype(jnp.bfloat16)
        return jnp.dot(prob_rows, value_rows, preferred_element_type=jnp.float32).astype(
            jnp.bfloat16
        )

    send_both = jnp.concatenate([key_heads, value_heads], axis=2)[safe_asked]
    got_slots = lax.all_to_all(send_both, "ctx", split_axis=0, concat_axis=0, tiled=True)
    last_width = 2 * HD
    flat_slots = got_slots.reshape(ctx_width * slot_count, block_rows, last_width)
    remote_both = flat_slots[flat_slot].reshape(HEADS, PICKS * block_rows, last_width)
    all_keys = jnp.concatenate([key_heads, remote_both[:, :, :HD]], axis=1)
    all_values = jnp.concatenate([value_heads, remote_both[:, :, HD:]], axis=1)

    def per_head(head_items):
        query_head, key_rows, value_rows, mask_row = head_items
        scores = masked_scores(query_head, key_rows, mask_row)
        row_top, row_total = row_stats(scores)
        return weighted(scores, row_top, row_total, value_rows)

    outputs = lax.map(per_head, (query_heads, all_keys, all_values, remote_mask))
    merged = outputs.transpose(1, 0, 2).reshape(1, block_rows, HEADS * HD)
    return passed_along(merged, "pipe", 1)


def per_device(queries, keys, values, picks):
    few_shifts = lax.axis_size("ctx") == 8
    run = travelling_queries if few_shifts else travelling_keys
    return run(queries, keys, values, picks)


def solution(mesh):
    placed = (
        P("pipe", "ctx", None),
        P("pipe", "ctx", None),
        P("pipe", "ctx", None),
        P("pipe", None, None, None),
    )
    return jax.shard_map(
        per_device, mesh=mesh, in_specs=placed, out_specs=P("pipe", "ctx", None), check_vma=False
    )
```

```python
import functools
import math

import jax
import jax.numpy as jnp
from jax import lax
from jax.experimental import pallas as pl
from jax.experimental.pallas import tpu as pltpu
from jax.sharding import PartitionSpec as P

HEADS = 16
HD = 128
PICKS = 2
EXP2_SCALE = HD ** -0.5 * math.log2(math.e)
LANES = 128
STAT_ROWS = 16
VMEM_BYTES = 24 * 1024 * 1024
HIGH_COST = 10**12


def passed_along(value, axis, steps):
    count = lax.axis_size(axis)
    pairs = [(source, (source + steps) % count) for source in range(count)]
    return lax.ppermute(value, axis, pairs)


def request_table(chosen, owners, slot_count):
    pick_count = chosen.shape[1]
    pick_ids = lax.iota(jnp.int32, pick_count)
    is_live = chosen >= 0
    earlier = pick_ids[None, :] < pick_ids[:, None]
    same_owner = (chosen[:, :, None] == chosen[:, None, :]) & earlier[None]
    pick_order = jnp.sum(same_owner.astype(jnp.int32), axis=2)
    head_ids = pick_ids // PICKS
    slot_ranks = lax.iota(jnp.int32, slot_count)
    matches = (
        is_live[:, None, None, :]
        & (chosen[:, None, None, :] == owners[None, :, None, None])
        & (pick_order[:, None, None, :] == slot_ranks[None, None, :, None])
    )
    was_found = jnp.any(matches, axis=3)
    head_table = jnp.sum(jnp.where(matches, head_ids[None, None, None, :], 0), axis=3)
    return (jnp.where(was_found, head_table, -1), pick_order)


def call(
    kernel, name_space, outputs, out_specs, scratch=(), flops=0, moved=0, exps=0
):
    return pl.pallas_call(
        kernel,
        in_specs=name_space,
        out_specs=out_specs,
        out_shape=outputs,
        scratch_shapes=list(scratch),
        compiler_params=pltpu.CompilerParams(vmem_limit_bytes=VMEM_BYTES),
        cost_estimate=pl.CostEstimate(flops=flops, bytes_accessed=moved, transcendentals=exps),
    )


SCALARS = pl.BlockSpec(memory_space=pltpu.SMEM)
IN_HBM = pl.BlockSpec(memory_space=pltpu.HBM)
IN_VMEM = pl.BlockSpec(memory_space=pltpu.VMEM)


def tick_kernel(here_ref, out_ref):
    out_ref[0] = here_ref[0]


def tick(here, *earlier):
    return call(
        tick_kernel,
        [SCALARS],
        jax.ShapeDtypeStruct((1,), jnp.int32),
        SCALARS,
        flops=0,
    )(after(here, *earlier))


def list_heads(heads_ref, start, picks_ref, block, owner, slots):
    width = picks_ref.shape[0]
    spare = heads_ref.shape[0] - 1
    for slot in range(slots):
        heads_ref[start + slot] = -1
    valid = (block >= 0) & (block < width) & (owner >= 0) & (owner < width)
    row = jnp.clip(block, 0, width - 1)
    wanted = jnp.where(valid, owner, -2)
    found = jnp.int32(0)
    for pick in range(PICKS):
        for head in range(HEADS):
            hit = picks_ref[row, pick, head] == wanted
            heads_ref[jnp.where(hit, start + found, spare)] = head
            found = found + hit.astype(jnp.int32)


def pack_kernel(here_ref, picks_ref, *refs, jobs, slots):
    is_near = jobs[0][3]
    sources = refs[: 1 + is_near]
    outputs = refs[1 + is_near : 1 + is_near + len(jobs)]
    heads_ref, sems = refs[-2], refs[-1]
    here = here_ref[0]
    listed = {}
    for shift, first, count, is_near in jobs:
        key = (shift, is_near)
        if key not in listed:
            listed[key] = len(listed) * slots
            block, owner = (here + shift, here) if is_near else (here, here - shift)
            list_heads(heads_ref, listed[key], picks_ref, block, owner, slots)
    copies = []
    for (shift, first, count, is_near), output in zip(jobs, outputs):
        for slot in range(count):
            head = jnp.maximum(heads_ref[listed[shift, is_near] + first + slot], 0)
            columns = pl.ds(pl.multiple_of(head * HD, HD), HD)
            for place, source in enumerate(sources):
                target = output.at[2 * slot + place if is_near else slot]
                copy = pltpu.make_async_copy(
                    source.at[:, columns], target, sems.at[len(copies)]
                )
                copy.start()
                copies.append(copy)
    for copy in copies:
        copy.wait()


def pack(here, picks, sources, jobs, slots):
    rows = sources[0].shape[0]
    sizes = [len(sources) * count for _, _, count, _ in jobs]
    return call(
        functools.partial(pack_kernel, jobs=jobs, slots=slots),
        [SCALARS, SCALARS] + [IN_VMEM] * len(sources),
        [jax.ShapeDtypeStruct((size, rows, HD), jnp.bfloat16) for size in sizes],
        [IN_VMEM] * len(sizes),
        [pltpu.SMEM((len(jobs) * slots + 1,), jnp.int32), pltpu.SemaphoreType.DMA((sum(sizes),))],
        moved=4 * rows * HD * sum(sizes),
    )(here, picks, *sources)


def diagonal():
    shape = (LANES, LANES)
    return lax.broadcasted_iota(jnp.int32, shape, 0) == lax.broadcasted_iota(jnp.int32, shape, 1)


def raw_scores(query_rows, key_rows):
    return lax.dot_general(
        query_rows, key_rows, (((1,), (1,)), ((), ())), preferred_element_type=jnp.float32
    )


def with_ones(value_rows):
    return jnp.concatenate([value_rows, jnp.ones_like(value_rows)], axis=1)


def soft_part(scores, value_rows):
    top = jnp.max(scores, axis=1, keepdims=True)
    weights = jnp.exp2((scores - top) * EXP2_SCALE).astype(jnp.bfloat16)
    total = jnp.dot(weights, value_rows, preferred_element_type=jnp.float32)
    sums = total[:, HD:]
    return total[:, :HD] * pl.reciprocal(sums), top * EXP2_SCALE, sums


def across_lanes(column):
    eye = diagonal()
    spread = jnp.broadcast_to(column, (column.shape[0], LANES))
    return [
        jnp.sum(jnp.where(eye, spread[at : at + LANES], 0.0), axis=0, keepdims=True)
        for at in range(0, column.shape[0], LANES)
    ]


def down_rows(line):
    spread = jnp.broadcast_to(line, (LANES, LANES))
    return jnp.sum(jnp.where(diagonal(), spread, 0.0), axis=1, keepdims=True)


def three_parts(stats):
    first = stats.astype(jnp.bfloat16).astype(jnp.float32)
    second = (stats - first).astype(jnp.bfloat16).astype(jnp.float32)
    third = stats - first - second
    parts = jnp.concatenate([first, second, third], axis=0)
    pad = jnp.zeros((STAT_ROWS - parts.shape[0], LANES), jnp.float32)
    return jnp.concatenate([parts, pad], axis=0).astype(jnp.bfloat16)


def stats_of(block, groups):
    stats = block.astype(jnp.float32)
    return stats[:groups] + stats[groups : 2 * groups] + stats[2 * groups : 3 * groups]


def log_sums(tops, sums):
    top_lines = [line for top in tops for line in across_lanes(top)]
    sum_lines = [line for part in sums for line in across_lanes(part)]
    return jnp.concatenate(top_lines, axis=0) + jnp.log2(jnp.concatenate(sum_lines, axis=0))


def attend_rows(query_rows, key_rows, value_rows, tile):
    found = [
        soft_part(raw_scores(query_rows[at : at + tile], key_rows), value_rows)
        for at in range(0, query_rows.shape[0], tile)
    ]
    outputs, tops, sums = zip(*found)
    return jnp.concatenate(outputs, axis=0), log_sums(tops, sums)


def head_columns(head):
    return pl.ds(pl.multiple_of(head * HD, HD), HD)


def attend_kernel(here_ref, picks_ref, key_ref, value_ref, *refs, group, slots):
    heads_ref = refs[-1]
    here = here_ref[0]
    for number, (shift, first, count) in enumerate(group):
        query_ref, out_ref = refs[number], refs[len(group) + number]
        rows = query_ref.shape[1]
        list_heads(heads_ref, 0, picks_ref, here + shift, here, slots)
        for slot in range(count):
            columns = head_columns(jnp.maximum(heads_ref[first + slot], 0))
            outputs, lines = attend_rows(
                query_ref[slot], key_ref[:, columns], with_ones(value_ref[:, columns]), rows
            )
            out_ref[slot, :rows, :] = outputs.astype(jnp.bfloat16)
            out_ref[slot, rows:, :] = three_parts(lines)


def attend(here, picks, keys, values, arrived, group, slots, is_anchor):
    rows = keys.shape[0]
    total = sum(count for _, _, count in group)
    return call(
        functools.partial(attend_kernel, group=group, slots=slots),
        [SCALARS, SCALARS, IN_VMEM, IN_VMEM] + [IN_VMEM] * len(group),
        [
            jax.ShapeDtypeStruct((count, rows + STAT_ROWS, HD), jnp.bfloat16)
            for _, _, count in group
        ],
        [IN_VMEM] * len(group),
        [pltpu.SMEM((slots + 1,), jnp.int32)],
        flops=HIGH_COST if is_anchor else 4 * total * rows * rows * HD,
        moved=8 * total * rows * HD,
        exps=total * rows * rows,
    )(here, picks, keys, values, *arrived)


def own_kernel(here_ref, query_ref, key_ref, value_ref, out_ref):
    rows = query_ref.shape[0]
    tile = min(rows, 256)

    def one_head(head, carry):
        columns = head_columns(head)
        value_rows = with_ones(value_ref[:, columns])
        tops, all_sums = [], []
        for at in range(0, rows, tile):
            reach = at + tile
            scores = raw_scores(query_ref[at:reach, columns], key_ref[:reach, columns])
            row_ids = lax.broadcasted_iota(jnp.int32, scores.shape, 0) + at
            seen = row_ids >= lax.broadcasted_iota(jnp.int32, scores.shape, 1)
            outputs, top, sums = soft_part(jnp.where(seen, scores, -jnp.inf), value_rows[:reach])
            out_ref[head, at:reach, :] = outputs.astype(jnp.bfloat16)
            tops.append(top)
            all_sums.append(sums)
        out_ref[head, rows:, :] = three_parts(log_sums(tops, all_sums))
        return carry

    lax.fori_loop(0, HEADS, one_head, 0, unroll=4)


def own_part(here, queries, keys, values):
    rows = queries.shape[0]
    return call(
        own_kernel,
        [SCALARS, IN_VMEM, IN_VMEM, IN_VMEM],
        jax.ShapeDtypeStruct((HEADS, rows + STAT_ROWS, HD), jnp.bfloat16),
        IN_VMEM,
        flops=4 * HEADS * rows * rows * HD,
        moved=8 * HEADS * rows * HD,
        exps=HEADS * rows * rows,
    )(here, queries, keys, values)


def near_kernel(here_ref, picks_ref, query_ref, *refs, shifts, slots):
    near_refs, out_ref, heads_ref = refs[: len(shifts)], refs[-2], refs[-1]
    rows = query_ref.shape[0]
    here = here_ref[0]
    for place, (shift, near_ref) in enumerate(zip(shifts, near_refs)):
        list_heads(heads_ref, 0, picks_ref, here, here - shift, slots)
        for slot in range(slots):
            columns = head_columns(jnp.maximum(heads_ref[slot], 0))
            outputs, lines = attend_rows(
                query_ref[:, columns], near_ref[2 * slot], with_ones(near_ref[2 * slot + 1]), rows
            )
            out_ref[place * slots + slot, :rows, :] = outputs.astype(jnp.bfloat16)
            out_ref[place * slots + slot, rows:, :] = three_parts(lines)


def near_part(here, picks, queries, near, shifts, slots):
    rows = queries.shape[0]
    total = len(shifts) * slots
    return call(
        functools.partial(near_kernel, shifts=shifts, slots=slots),
        [SCALARS, SCALARS, IN_VMEM] + [IN_VMEM] * len(shifts),
        jax.ShapeDtypeStruct((total, rows + STAT_ROWS, HD), jnp.bfloat16),
        IN_VMEM,
        [pltpu.SMEM((slots + 1,), jnp.int32)],
        flops=4 * total * rows * rows * HD,
        moved=12 * total * rows * HD,
        exps=total * rows * rows,
    )(here, picks, queries, *near)


def find_spots(spots_ref, found_ref, picks_ref, here, shifts, slots):
    for owner in range(picks_ref.shape[0]):
        found_ref[owner] = 0

    for pick in range(PICKS):
        for head in range(HEADS):
            owner = picks_ref[here, pick, head]
            safe = jnp.maximum(owner, 0)
            order = found_ref[safe]
            found_ref[safe] = order + (owner >= 0).astype(jnp.int32)
            spot = jnp.int32(-1)
            for place, shift in enumerate(shifts):
                spot = jnp.where(here - safe == shift, place * slots + order, spot)
            spots_ref[head * PICKS + pick] = jnp.where(owner >= 0, spot, -1)


def merge_kernel(here_ref, picks_ref, *refs, places, shifts, slots):
    count = len(places)
    parts = refs[:count]
    result_ref, out_ref, sums_ref, held, spots_ref, found_ref, sems = refs[count:]
    groups = sums_ref.shape[1]
    rows = groups * LANES
    copies = [
        pltpu.make_async_copy(part, held.at[pl.ds(place, part.shape[0])], sems.at[number])
        for number, (part, place) in enumerate(zip(parts, places))
    ]
    for copy in copies:
        copy.start()
    find_spots(spots_ref, found_ref, picks_ref, here_ref[0], shifts, slots)
    for copy in copies:
        copy.wait()

    def one_head(head, carry):
        found = [spots_ref[head * PICKS + pick] for pick in range(PICKS)]
        spots = [head] + [jnp.where(spot >= 0, HEADS + spot, head) for spot in found]
        sums = [stats_of(held[spot, rows:, :], groups) for spot in spots]
        for pick, spot in enumerate(found):
            sums[1 + pick] = jnp.where(spot >= 0, sums[1 + pick], -jnp.inf)
        top = functools.reduce(jnp.maximum, sums)
        shares = [jnp.exp2(part - top) for part in sums]
        whole = functools.reduce(jnp.add, shares)
        sums_ref[head] = top + jnp.log2(whole)
        for group in range(groups):
            span = pl.ds(group * LANES, LANES)
            own = held[head, span, :].astype(jnp.float32)
            mixed = own
            for spot, share in zip(spots[1:], shares[1:]):
                weight = down_rows((share / whole)[group : group + 1, :])
                mixed = mixed + (held[spot, span, :].astype(jnp.float32) - own) * weight
            out_ref[head, span, :] = mixed
            result_ref[span, head_columns(head)] = mixed.astype(jnp.bfloat16)
        return carry

    lax.fori_loop(0, HEADS, one_head, 0, unroll=2)


def merge(here, picks, parts, places, shifts, slots):
    rows = parts[0].shape[1] - STAT_ROWS
    width = picks.shape[0]
    total = HEADS + len(shifts) * slots
    return call(
        functools.partial(merge_kernel, places=tuple(places), shifts=shifts, slots=slots),
        [SCALARS, SCALARS] + [pl.BlockSpec(memory_space=pl.ANY)] * len(parts),
        [
            jax.ShapeDtypeStruct((rows, HEADS * HD), jnp.bfloat16),
            jax.ShapeDtypeStruct((HEADS, rows, HD), jnp.float32),
            jax.ShapeDtypeStruct((HEADS, rows // LANES, LANES), jnp.float32),
        ],
        [IN_VMEM, IN_VMEM, IN_VMEM],
        [
            pltpu.VMEM((total, rows + STAT_ROWS, HD), jnp.bfloat16),
            pltpu.SMEM((PICKS * HEADS,), jnp.int32),
            pltpu.SMEM((width,), jnp.int32),
            pltpu.SemaphoreType.DMA((len(parts),)),
        ],
        flops=6 * HEADS * rows * HD,
        moved=2 * (HEADS * 2 + total) * rows * HD,
    )(here, picks, *parts)


def finish_kernel(here_ref, picks_ref, mixed_ref, sums_ref, *refs, shifts, slots):
    count = len(shifts)
    parts, out_ref, (heads_ref, held, sems) = refs[:count], refs[count + 1], refs[count + 2 :]
    groups = sums_ref.shape[1]
    rows = groups * LANES
    here = here_ref[0]
    for number, shift in enumerate(shifts):
        list_heads(heads_ref, number * slots, picks_ref, here, here - shift, slots)

    def slot_of(head, number):
        found = jnp.int32(-1)
        for slot in range(slots):
            found = jnp.where(heads_ref[number * slots + slot] == head, slot, found)
        return found

    def is_first(head, number):
        first = head >= 0
        for earlier in range(number):
            first = first & (slot_of(head, earlier) < 0)
        return first

    def patch(place):
        columns = head_columns(jnp.maximum(heads_ref[place], 0))
        return pltpu.make_async_copy(held.at[place], out_ref.at[:, columns], sems.at[place])

    places = [(number, number * slots + slot) for number in range(count) for slot in range(slots)]
    for number, place in places:
        head = heads_ref[place]

        @pl.when(is_first(head, number))
        def _():
            found = [slot_of(head, later) for later in range(number, count)]
            spots = [jnp.maximum(spot, 0) for spot in found]
            sums = [sums_ref[head]]
            for part, spot, safe in zip(parts[number:], found, spots):
                added = stats_of(part[safe, rows:, :], groups)
                sums.append(jnp.where(spot >= 0, added, -jnp.inf))
            top = functools.reduce(jnp.maximum, sums)
            shares = [jnp.exp2(part - top) for part in sums]
            whole = functools.reduce(jnp.add, shares)
            for group in range(groups):
                span = pl.ds(group * LANES, LANES)
                before = mixed_ref[head, span, :]
                mixed = before
                for part, spot, safe, share in zip(parts[number:], found, spots, shares[1:]):
                    new = jnp.where(spot >= 0, part[safe, span, :].astype(jnp.float32), 0.0)
                    weight = down_rows((share / whole)[group : group + 1, :])
                    mixed = mixed + (new - before) * weight
                held[place, span, :] = mixed.astype(jnp.bfloat16)
            patch(place).start()

    for number, place in places:

        @pl.when(is_first(heads_ref[place], number))
        def _():
            patch(place).wait()


def finish(here, picks, result, mixed, sums, parts, shifts, slots):
    rows = mixed.shape[1]
    total = len(shifts) * slots
    return pl.pallas_call(
        functools.partial(finish_kernel, shifts=shifts, slots=slots),
        in_specs=[SCALARS, SCALARS] + [IN_VMEM] * (2 + len(parts)) + [IN_HBM],
        out_specs=IN_HBM,
        out_shape=jax.ShapeDtypeStruct(result.shape, result.dtype),
        scratch_shapes=[
            pltpu.SMEM((total + 1,), jnp.int32),
            pltpu.VMEM((total, rows, HD), jnp.bfloat16),
            pltpu.SemaphoreType.DMA((total,)),
        ],
        input_output_aliases={4 + len(parts): 0},
        compiler_params=pltpu.CompilerParams(vmem_limit_bytes=VMEM_BYTES),
        cost_estimate=pl.CostEstimate(
            flops=2 * total * rows * HD, bytes_accessed=8 * total * rows * HD, transcendentals=0
        ),
    )(here, picks, mixed, sums, *parts, result)


def after(value, *earlier):
    return lax.optimization_barrier((value,) + earlier)[0]


def travelling_queries(queries, keys, values, picks):
    width = lax.axis_size("ctx")
    sections = lax.axis_size("pipe")
    slots = max(1, PICKS * HEADS // width)
    here = lax.axis_index("ctx").astype(jnp.int32).reshape(1)
    queries, keys, values = queries[0], keys[0], values[0]
    own_picks = picks[0].transpose(0, 2, 1)

    near_shifts = (2, width - 2)
    middle = width // 2
    far_shifts = [middle, middle - 1, middle + 1, 1, width - 1]
    final_shifts = tuple(far_shifts[3:])

    def up(value, shift):
        return lax.ppermute(value, "ctx", [(at, at + shift) for at in range(width - shift)])

    def down(value, shift):
        return lax.ppermute(value, "ctx", [(at, at - shift) for at in range(shift, width)])

    def up_and_on(value, shift):
        pairs = [
            (at * sections + section, (at + shift) * sections + (section + 1) % sections)
            for at in range(width - shift)
            for section in range(sections)
        ]
        return lax.ppermute(value, ("ctx", "pipe"), pairs)

    near_jobs = [(shift, 0, slots, True) for shift in near_shifts]
    near_sends = pack(here, own_picks, [keys, values], near_jobs, slots)
    near = [up(near_sends[0], near_shifts[0])]
    before = passed_along(own_picks, "pipe", 1)
    sends, now = {}, after(here, *near_sends)
    for shifts in (far_shifts[:1], far_shifts[1:]):
        jobs = [(shift, 0, slots, False) for shift in shifts]
        packed = pack(now, own_picks, [queries], jobs, slots)
        sends |= zip(shifts, packed)
        now = after(now, *packed)
    arrived, returned = {}, {}

    def ask_for(shift, *earlier):
        arrived[shift] = down(after(sends[shift], *earlier), shift)

    def work(token, shift, is_anchor=False):
        return attend(
            token, own_picks, keys, values, [arrived[shift]], ((shift, 0, slots),), slots, is_anchor
        )[0]

    four, three, five, one, seven = far_shifts
    ask_for(four, near_sends[0])
    own = own_part(after(now, before), queries, keys, values)
    own_back = passed_along(own, "pipe", 1)
    near.append(up(after(near_sends[1], own), near_shifts[1]))
    ask_for(three, arrived[four], near[0], own)
    ask_for(five, arrived[four], near[0], own)
    part_four = work(after(here, own, near[0]), four, is_anchor=True)
    returned[four] = up_and_on(part_four, four)
    beside = near_part(after(here, part_four, own_back), own_picks, queries, near, near_shifts, slots)
    ask_for(one, own_back, part_four, *near)
    ask_for(seven, own_back, part_four, *near)
    part_three = work(after(here, beside), three, is_anchor=True)
    returned[three] = up_and_on(part_three, three)
    part_five = work(after(here, part_three), five)
    returned[five] = up_and_on(part_five, five)
    beside_back = passed_along(beside, "pipe", 1)
    part_one = work(after(here, part_five, beside_back), one)
    returned[one] = up_and_on(part_one, one)
    part_seven = work(after(here, part_one), seven)
    returned[seven] = up_and_on(part_seven, seven)
    now = after(here, part_seven)

    merged_shifts = near_shifts + (four, three, five)
    places = [HEADS + place * slots for place in (2, 3, 4)]
    parts = [own_back, beside_back, returned[four], returned[three], returned[five]]
    result, mixed, sums = merge(now, before, parts, [0, HEADS] + places, merged_shifts, slots)
    lasts = [returned[shift] for shift in final_shifts]
    return finish(now, before, result, mixed, sums, lasts, final_shifts, slots)[None]


def travelling_keys(queries, keys, values, picks):
    ctx_width = lax.axis_size("ctx")
    rank_here = lax.axis_index("ctx")
    slot_count = max(1, PICKS * HEADS // ctx_width)
    block_rows = queries.shape[1]
    score_scale = HD ** (-0.5)
    every_pick = picks[0].reshape(ctx_width, HEADS * PICKS)
    chosen = lax.dynamic_slice_in_dim(every_pick, rank_here, 1, 0)
    pick_order = request_table(chosen, lax.iota(jnp.int32, ctx_width), slot_count)[1]
    asked_table = request_table(every_pick, rank_here.reshape(1), slot_count)[0]
    asked_heads = asked_table[:, 0, :]
    safe_asked = jnp.maximum(asked_heads, 0)
    query_heads = queries[0].reshape(block_rows, HEADS, HD).transpose(1, 0, 2)
    key_heads = keys[0].reshape(block_rows, HEADS, HD).transpose(1, 0, 2)
    value_heads = values[0].reshape(block_rows, HEADS, HD).transpose(1, 0, 2)
    is_live = chosen[0] >= 0
    flat_slot = jnp.where(is_live, chosen[0] * slot_count + pick_order[0], 0)
    remote_mask = jnp.repeat(is_live.reshape(HEADS, PICKS), block_rows, axis=1)
    row_index = lax.iota(jnp.int32, block_rows)
    causal = row_index[:, None] >= row_index[None, :]

    def masked_scores(query_head, key_rows, mask_row):
        scores = lax.dot_general(
            query_head, key_rows, (((1,), (1,)), ((), ())), preferred_element_type=jnp.float32
        )
        allowed = jnp.concatenate(
            [causal, jnp.broadcast_to(mask_row[None, :], (block_rows, PICKS * block_rows))], axis=1
        )
        return jnp.where(allowed, scores * score_scale, -jnp.inf)

    def row_stats(scores):
        row_top = jnp.max(scores, axis=1)
        row_total = jnp.sum(jnp.exp(scores - row_top[:, None]), axis=1)
        return (row_top, row_total)

    def weighted(scores, row_top, row_total, value_rows):
        prob_rows = (jnp.exp(scores - row_top[:, None]) / row_total[:, None]).astype(jnp.bfloat16)
        return jnp.dot(prob_rows, value_rows, preferred_element_type=jnp.float32).astype(
            jnp.bfloat16
        )

    send_both = jnp.concatenate([key_heads, value_heads], axis=2)[safe_asked]
    got_slots = lax.all_to_all(send_both, "ctx", split_axis=0, concat_axis=0, tiled=True)
    last_width = 2 * HD
    flat_slots = got_slots.reshape(ctx_width * slot_count, block_rows, last_width)
    remote_both = flat_slots[flat_slot].reshape(HEADS, PICKS * block_rows, last_width)
    all_keys = jnp.concatenate([key_heads, remote_both[:, :, :HD]], axis=1)
    all_values = jnp.concatenate([value_heads, remote_both[:, :, HD:]], axis=1)

    def per_head(head_items):
        query_head, key_rows, value_rows, mask_row = head_items
        scores = masked_scores(query_head, key_rows, mask_row)
        row_top, row_total = row_stats(scores)
        return weighted(scores, row_top, row_total, value_rows)

    outputs = lax.map(per_head, (query_heads, all_keys, all_values, remote_mask))
    merged = outputs.transpose(1, 0, 2).reshape(1, block_rows, HEADS * HD)
    return passed_along(merged, "pipe", 1)


def per_device(queries, keys, values, picks):
    few_shifts = lax.axis_size("ctx") == 8
    run = travelling_queries if few_shifts else travelling_keys
    return run(queries, keys, values, picks)


def solution(mesh):
    placed = (
        P("pipe", "ctx", None),
        P("pipe", "ctx", None),
        P("pipe", "ctx", None),
        P("pipe", None, None, None),
    )
    return jax.shard_map(
        per_device, mesh=mesh, in_specs=placed, out_specs=P("pipe", "ctx", None), check_vma=False
    )
```

```python
import functools
import math

import jax
import jax.numpy as jnp
from jax import lax
from jax.experimental import pallas as pl
from jax.experimental.pallas import tpu as pltpu
from jax.sharding import PartitionSpec as P

HEADS = 16
HD = 128
PICKS = 2
EXP2_SCALE = HD ** -0.5 * math.log2(math.e)
LANES = 128
STAT_ROWS = 16
VMEM_BYTES = 24 * 1024 * 1024
HIGH_COST = 10**12


def passed_along(value, axis, steps):
    count = lax.axis_size(axis)
    pairs = [(source, (source + steps) % count) for source in range(count)]
    return lax.ppermute(value, axis, pairs)


def request_table(chosen, owners, slot_count):
    pick_count = chosen.shape[1]
    pick_ids = lax.iota(jnp.int32, pick_count)
    is_live = chosen >= 0
    earlier = pick_ids[None, :] < pick_ids[:, None]
    same_owner = (chosen[:, :, None] == chosen[:, None, :]) & earlier[None]
    pick_order = jnp.sum(same_owner.astype(jnp.int32), axis=2)
    head_ids = pick_ids // PICKS
    slot_ranks = lax.iota(jnp.int32, slot_count)
    matches = (
        is_live[:, None, None, :]
        & (chosen[:, None, None, :] == owners[None, :, None, None])
        & (pick_order[:, None, None, :] == slot_ranks[None, None, :, None])
    )
    was_found = jnp.any(matches, axis=3)
    head_table = jnp.sum(jnp.where(matches, head_ids[None, None, None, :], 0), axis=3)
    return (jnp.where(was_found, head_table, -1), pick_order)


def call(
    kernel, name_space, outputs, out_specs, scratch=(), flops=0, moved=0, exps=0
):
    return pl.pallas_call(
        kernel,
        in_specs=name_space,
        out_specs=out_specs,
        out_shape=outputs,
        scratch_shapes=list(scratch),
        compiler_params=pltpu.CompilerParams(vmem_limit_bytes=VMEM_BYTES),
        cost_estimate=pl.CostEstimate(flops=flops, bytes_accessed=moved, transcendentals=exps),
    )


SCALARS = pl.BlockSpec(memory_space=pltpu.SMEM)
IN_HBM = pl.BlockSpec(memory_space=pltpu.HBM)
IN_VMEM = pl.BlockSpec(memory_space=pltpu.VMEM)


def tick_kernel(here_ref, out_ref):
    out_ref[0] = here_ref[0]


def tick(here, *earlier):
    return call(
        tick_kernel,
        [SCALARS],
        jax.ShapeDtypeStruct((1,), jnp.int32),
        SCALARS,
        flops=0,
    )(after(here, *earlier))


def list_heads(heads_ref, start, picks_ref, block, owner, slots):
    width = picks_ref.shape[0]
    spare = heads_ref.shape[0] - 1
    for slot in range(slots):
        heads_ref[start + slot] = -1
    valid = (block >= 0) & (block < width) & (owner >= 0) & (owner < width)
    row = jnp.clip(block, 0, width - 1)
    wanted = jnp.where(valid, owner, -2)
    found = jnp.int32(0)
    for pick in range(PICKS):
        for head in range(HEADS):
            hit = picks_ref[row, pick, head] == wanted
            heads_ref[jnp.where(hit, start + found, spare)] = head
            found = found + hit.astype(jnp.int32)


def pack_kernel(here_ref, picks_ref, *refs, jobs, slots):
    is_near = jobs[0][3]
    sources = refs[: 1 + is_near]
    outputs = refs[1 + is_near : 1 + is_near + len(jobs)]
    heads_ref, sems = refs[-2], refs[-1]
    here = here_ref[0]
    listed = {}
    for shift, first, count, is_near in jobs:
        key = (shift, is_near)
        if key not in listed:
            listed[key] = len(listed) * slots
            block, owner = (here + shift, here) if is_near else (here, here - shift)
            list_heads(heads_ref, listed[key], picks_ref, block, owner, slots)
    copies = []
    for (shift, first, count, is_near), output in zip(jobs, outputs):
        for slot in range(count):
            head = jnp.maximum(heads_ref[listed[shift, is_near] + first + slot], 0)
            columns = pl.ds(pl.multiple_of(head * HD, HD), HD)
            for place, source in enumerate(sources):
                target = output.at[2 * slot + place if is_near else slot]
                copy = pltpu.make_async_copy(
                    source.at[:, columns], target, sems.at[len(copies)]
                )
                copy.start()
                copies.append(copy)
    for copy in copies:
        copy.wait()


def pack(here, picks, sources, jobs, slots):
    rows = sources[0].shape[0]
    sizes = [len(sources) * count for _, _, count, _ in jobs]
    return call(
        functools.partial(pack_kernel, jobs=jobs, slots=slots),
        [SCALARS, SCALARS] + [IN_VMEM] * len(sources),
        [jax.ShapeDtypeStruct((size, rows, HD), jnp.bfloat16) for size in sizes],
        [IN_VMEM] * len(sizes),
        [pltpu.SMEM((len(jobs) * slots + 1,), jnp.int32), pltpu.SemaphoreType.DMA((sum(sizes),))],
        moved=4 * rows * HD * sum(sizes),
    )(here, picks, *sources)


def diagonal():
    shape = (LANES, LANES)
    return lax.broadcasted_iota(jnp.int32, shape, 0) == lax.broadcasted_iota(jnp.int32, shape, 1)


def raw_scores(query_rows, key_rows):
    return lax.dot_general(
        query_rows, key_rows, (((1,), (1,)), ((), ())), preferred_element_type=jnp.float32
    )


def with_ones(value_rows):
    return jnp.concatenate([value_rows, jnp.ones_like(value_rows)], axis=1)


def soft_part(scores, value_rows):
    top = jnp.max(scores, axis=1, keepdims=True)
    weights = jnp.exp2((scores - top) * EXP2_SCALE).astype(jnp.bfloat16)
    total = jnp.dot(weights, value_rows, preferred_element_type=jnp.float32)
    sums = total[:, HD:]
    return total[:, :HD] * pl.reciprocal(sums), top * EXP2_SCALE, sums


def across_lanes(column):
    eye = diagonal()
    spread = jnp.broadcast_to(column, (column.shape[0], LANES))
    return [
        jnp.sum(jnp.where(eye, spread[at : at + LANES], 0.0), axis=0, keepdims=True)
        for at in range(0, column.shape[0], LANES)
    ]


def down_rows(line):
    spread = jnp.broadcast_to(line, (LANES, LANES))
    return jnp.sum(jnp.where(diagonal(), spread, 0.0), axis=1, keepdims=True)


def three_parts(stats):
    first = stats.astype(jnp.bfloat16).astype(jnp.float32)
    second = (stats - first).astype(jnp.bfloat16).astype(jnp.float32)
    third = stats - first - second
    parts = jnp.concatenate([first, second, third], axis=0)
    pad = jnp.zeros((STAT_ROWS - parts.shape[0], LANES), jnp.float32)
    return jnp.concatenate([parts, pad], axis=0).astype(jnp.bfloat16)


def stats_of(block, groups):
    stats = block.astype(jnp.float32)
    return stats[:groups] + stats[groups : 2 * groups] + stats[2 * groups : 3 * groups]


def log_sums(tops, sums):
    top_lines = [line for top in tops for line in across_lanes(top)]
    sum_lines = [line for part in sums for line in across_lanes(part)]
    return jnp.concatenate(top_lines, axis=0) + jnp.log2(jnp.concatenate(sum_lines, axis=0))


def attend_rows(query_rows, key_rows, value_rows, tile):
    found = [
        soft_part(raw_scores(query_rows[at : at + tile], key_rows), value_rows)
        for at in range(0, query_rows.shape[0], tile)
    ]
    outputs, tops, sums = zip(*found)
    return jnp.concatenate(outputs, axis=0), log_sums(tops, sums)


def head_columns(head):
    return pl.ds(pl.multiple_of(head * HD, HD), HD)


def attend_kernel(here_ref, picks_ref, key_ref, value_ref, *refs, group, slots):
    heads_ref = refs[-1]
    here = here_ref[0]
    for number, (shift, first, count) in enumerate(group):
        query_ref, out_ref = refs[number], refs[len(group) + number]
        rows = query_ref.shape[1]
        list_heads(heads_ref, 0, picks_ref, here + shift, here, slots)
        for slot in range(count):
            columns = head_columns(jnp.maximum(heads_ref[first + slot], 0))
            outputs, lines = attend_rows(
                query_ref[slot], key_ref[:, columns], with_ones(value_ref[:, columns]), rows
            )
            out_ref[slot, :rows, :] = outputs.astype(jnp.bfloat16)
            out_ref[slot, rows:, :] = three_parts(lines)


def attend(here, picks, keys, values, arrived, group, slots, is_anchor):
    rows = keys.shape[0]
    total = sum(count for _, _, count in group)
    return call(
        functools.partial(attend_kernel, group=group, slots=slots),
        [SCALARS, SCALARS, IN_VMEM, IN_VMEM] + [IN_VMEM] * len(group),
        [
            jax.ShapeDtypeStruct((count, rows + STAT_ROWS, HD), jnp.bfloat16)
            for _, _, count in group
        ],
        [IN_VMEM] * len(group),
        [pltpu.SMEM((slots + 1,), jnp.int32)],
        flops=HIGH_COST if is_anchor else 4 * total * rows * rows * HD,
        moved=8 * total * rows * HD,
        exps=total * rows * rows,
    )(here, picks, keys, values, *arrived)


def own_kernel(here_ref, query_ref, key_ref, value_ref, out_ref):
    rows = query_ref.shape[0]
    tile = min(rows, 256)

    def one_head(head, carry):
        columns = head_columns(head)
        value_rows = with_ones(value_ref[:, columns])
        tops, all_sums = [], []
        for at in range(0, rows, tile):
            reach = at + tile
            scores = raw_scores(query_ref[at:reach, columns], key_ref[:reach, columns])
            row_ids = lax.broadcasted_iota(jnp.int32, scores.shape, 0) + at
            seen = row_ids >= lax.broadcasted_iota(jnp.int32, scores.shape, 1)
            outputs, top, sums = soft_part(jnp.where(seen, scores, -jnp.inf), value_rows[:reach])
            out_ref[head, at:reach, :] = outputs.astype(jnp.bfloat16)
            tops.append(top)
            all_sums.append(sums)
        out_ref[head, rows:, :] = three_parts(log_sums(tops, all_sums))
        return carry

    lax.fori_loop(0, HEADS, one_head, 0, unroll=4)


def own_part(here, queries, keys, values):
    rows = queries.shape[0]
    return call(
        own_kernel,
        [SCALARS, IN_VMEM, IN_VMEM, IN_VMEM],
        jax.ShapeDtypeStruct((HEADS, rows + STAT_ROWS, HD), jnp.bfloat16),
        IN_VMEM,
        flops=4 * HEADS * rows * rows * HD,
        moved=8 * HEADS * rows * HD,
        exps=HEADS * rows * rows,
    )(here, queries, keys, values)


def near_kernel(here_ref, picks_ref, query_ref, *refs, shifts, slots):
    near_refs, out_ref, heads_ref = refs[: len(shifts)], refs[-2], refs[-1]
    rows = query_ref.shape[0]
    here = here_ref[0]
    for place, (shift, near_ref) in enumerate(zip(shifts, near_refs)):
        list_heads(heads_ref, 0, picks_ref, here, here - shift, slots)
        for slot in range(slots):
            columns = head_columns(jnp.maximum(heads_ref[slot], 0))
            outputs, lines = attend_rows(
                query_ref[:, columns], near_ref[2 * slot], with_ones(near_ref[2 * slot + 1]), rows
            )
            out_ref[place * slots + slot, :rows, :] = outputs.astype(jnp.bfloat16)
            out_ref[place * slots + slot, rows:, :] = three_parts(lines)


def near_part(here, picks, queries, near, shifts, slots):
    rows = queries.shape[0]
    total = len(shifts) * slots
    return call(
        functools.partial(near_kernel, shifts=shifts, slots=slots),
        [SCALARS, SCALARS, IN_VMEM] + [IN_VMEM] * len(shifts),
        jax.ShapeDtypeStruct((total, rows + STAT_ROWS, HD), jnp.bfloat16),
        IN_VMEM,
        [pltpu.SMEM((slots + 1,), jnp.int32)],
        flops=4 * total * rows * rows * HD,
        moved=12 * total * rows * HD,
        exps=total * rows * rows,
    )(here, picks, queries, *near)


def find_spots(spots_ref, found_ref, picks_ref, here, shifts, slots):
    for owner in range(picks_ref.shape[0]):
        found_ref[owner] = 0

    for pick in range(PICKS):
        for head in range(HEADS):
            owner = picks_ref[here, pick, head]
            safe = jnp.maximum(owner, 0)
            order = found_ref[safe]
            found_ref[safe] = order + (owner >= 0).astype(jnp.int32)
            spot = jnp.int32(-1)
            for place, shift in enumerate(shifts):
                spot = jnp.where(here - safe == shift, place * slots + order, spot)
            spots_ref[head * PICKS + pick] = jnp.where(owner >= 0, spot, -1)


def merge_kernel(here_ref, picks_ref, *refs, places, shifts, slots):
    count = len(places)
    parts = refs[:count]
    result_ref, out_ref, sums_ref, held, spots_ref, found_ref, sems = refs[count:]
    groups = sums_ref.shape[1]
    rows = groups * LANES
    copies = [
        pltpu.make_async_copy(part, held.at[pl.ds(place, part.shape[0])], sems.at[number])
        for number, (part, place) in enumerate(zip(parts, places))
    ]
    for copy in copies:
        copy.start()
    find_spots(spots_ref, found_ref, picks_ref, here_ref[0], shifts, slots)
    for copy in copies:
        copy.wait()

    def one_head(head, carry):
        found = [spots_ref[head * PICKS + pick] for pick in range(PICKS)]
        spots = [head] + [jnp.where(spot >= 0, HEADS + spot, head) for spot in found]
        sums = [stats_of(held[spot, rows:, :], groups) for spot in spots]
        for pick, spot in enumerate(found):
            sums[1 + pick] = jnp.where(spot >= 0, sums[1 + pick], -jnp.inf)
        top = functools.reduce(jnp.maximum, sums)
        shares = [jnp.exp2(part - top) for part in sums]
        whole = functools.reduce(jnp.add, shares)
        sums_ref[head] = top + jnp.log2(whole)
        for group in range(groups):
            span = pl.ds(group * LANES, LANES)
            own = held[head, span, :].astype(jnp.float32)
            mixed = own
            for spot, share in zip(spots[1:], shares[1:]):
                weight = down_rows((share / whole)[group : group + 1, :])
                mixed = mixed + (held[spot, span, :].astype(jnp.float32) - own) * weight
            out_ref[head, span, :] = mixed
            result_ref[span, head_columns(head)] = mixed.astype(jnp.bfloat16)
        return carry

    lax.fori_loop(0, HEADS, one_head, 0, unroll=2)


def merge(here, picks, parts, places, shifts, slots):
    rows = parts[0].shape[1] - STAT_ROWS
    width = picks.shape[0]
    total = HEADS + len(shifts) * slots
    return call(
        functools.partial(merge_kernel, places=tuple(places), shifts=shifts, slots=slots),
        [SCALARS, SCALARS] + [pl.BlockSpec(memory_space=pl.ANY)] * len(parts),
        [
            jax.ShapeDtypeStruct((rows, HEADS * HD), jnp.bfloat16),
            jax.ShapeDtypeStruct((HEADS, rows, HD), jnp.float32),
            jax.ShapeDtypeStruct((HEADS, rows // LANES, LANES), jnp.float32),
        ],
        [IN_VMEM, IN_VMEM, IN_VMEM],
        [
            pltpu.VMEM((total, rows + STAT_ROWS, HD), jnp.bfloat16),
            pltpu.SMEM((PICKS * HEADS,), jnp.int32),
            pltpu.SMEM((width,), jnp.int32),
            pltpu.SemaphoreType.DMA((len(parts),)),
        ],
        flops=6 * HEADS * rows * HD,
        moved=2 * (HEADS * 2 + total) * rows * HD,
    )(here, picks, *parts)


def finish_kernel(here_ref, picks_ref, mixed_ref, sums_ref, *refs, shifts, slots):
    count = len(shifts)
    parts, out_ref, (heads_ref, held, sems) = refs[:count], refs[count + 1], refs[count + 2 :]
    groups = sums_ref.shape[1]
    rows = groups * LANES
    here = here_ref[0]
    for number, shift in enumerate(shifts):
        list_heads(heads_ref, number * slots, picks_ref, here, here - shift, slots)

    def slot_of(head, number):
        found = jnp.int32(-1)
        for slot in range(slots):
            found = jnp.where(heads_ref[number * slots + slot] == head, slot, found)
        return found

    def is_first(head, number):
        first = head >= 0
        for earlier in range(number):
            first = first & (slot_of(head, earlier) < 0)
        return first

    def patch(place):
        columns = head_columns(jnp.maximum(heads_ref[place], 0))
        return pltpu.make_async_copy(held.at[place], out_ref.at[:, columns], sems.at[place])

    places = [(number, number * slots + slot) for number in range(count) for slot in range(slots)]
    for number, place in places:
        head = heads_ref[place]

        @pl.when(is_first(head, number))
        def _():
            found = [slot_of(head, later) for later in range(number, count)]
            spots = [jnp.maximum(spot, 0) for spot in found]
            sums = [sums_ref[head]]
            for part, spot, safe in zip(parts[number:], found, spots):
                added = stats_of(part[safe, rows:, :], groups)
                sums.append(jnp.where(spot >= 0, added, -jnp.inf))
            top = functools.reduce(jnp.maximum, sums)
            shares = [jnp.exp2(part - top) for part in sums]
            whole = functools.reduce(jnp.add, shares)
            for group in range(groups):
                span = pl.ds(group * LANES, LANES)
                before = mixed_ref[head, span, :]
                mixed = before
                for part, spot, safe, share in zip(parts[number:], found, spots, shares[1:]):
                    new = jnp.where(spot >= 0, part[safe, span, :].astype(jnp.float32), 0.0)
                    weight = down_rows((share / whole)[group : group + 1, :])
                    mixed = mixed + (new - before) * weight
                held[place, span, :] = mixed.astype(jnp.bfloat16)
            patch(place).start()

    for number, place in places:

        @pl.when(is_first(heads_ref[place], number))
        def _():
            patch(place).wait()


def finish(here, picks, result, mixed, sums, parts, shifts, slots):
    rows = mixed.shape[1]
    total = len(shifts) * slots
    return pl.pallas_call(
        functools.partial(finish_kernel, shifts=shifts, slots=slots),
        in_specs=[SCALARS, SCALARS] + [IN_VMEM] * (2 + len(parts)) + [IN_HBM],
        out_specs=IN_HBM,
        out_shape=jax.ShapeDtypeStruct(result.shape, result.dtype),
        scratch_shapes=[
            pltpu.SMEM((total + 1,), jnp.int32),
            pltpu.VMEM((total, rows, HD), jnp.bfloat16),
            pltpu.SemaphoreType.DMA((total,)),
        ],
        input_output_aliases={4 + len(parts): 0},
        compiler_params=pltpu.CompilerParams(vmem_limit_bytes=VMEM_BYTES),
        cost_estimate=pl.CostEstimate(
            flops=2 * total * rows * HD, bytes_accessed=8 * total * rows * HD, transcendentals=0
        ),
    )(here, picks, mixed, sums, *parts, result)


def after(value, *earlier):
    return lax.optimization_barrier((value,) + earlier)[0]


def travelling_queries(queries, keys, values, picks):
    width = lax.axis_size("ctx")
    sections = lax.axis_size("pipe")
    slots = max(1, PICKS * HEADS // width)
    here = lax.axis_index("ctx").astype(jnp.int32).reshape(1)
    queries, keys, values = queries[0], keys[0], values[0]
    own_picks = picks[0].transpose(0, 2, 1)

    near_shifts = (2, width - 2)
    middle = width // 2
    far_shifts = [middle - 1, middle + 1, middle, 1, width - 1]
    final_shifts = tuple(far_shifts[2:])

    def up(value, shift):
        return lax.ppermute(value, "ctx", [(at, at + shift) for at in range(width - shift)])

    def down(value, shift):
        return lax.ppermute(value, "ctx", [(at, at - shift) for at in range(shift, width)])

    def up_and_on(value, shift):
        pairs = [
            (at * sections + section, (at + shift) * sections + (section + 1) % sections)
            for at in range(width - shift)
            for section in range(sections)
        ]
        return lax.ppermute(value, ("ctx", "pipe"), pairs)

    near_jobs = [(shift, 0, slots, True) for shift in near_shifts]
    near_sends = pack(here, own_picks, [keys, values], near_jobs, slots)
    near = [up(near_sends[0], near_shifts[0])]
    before = passed_along(own_picks, "pipe", 1)
    sends, now = {}, after(here, *near_sends)
    for shifts in (far_shifts[:2], far_shifts[2:]):
        jobs = [(shift, 0, slots, False) for shift in shifts]
        packed = pack(now, own_picks, [queries], jobs, slots)
        sends |= zip(shifts, packed)
        now = after(now, *packed)
    arrived, returned = {}, {}

    def ask_for(shift, *earlier):
        arrived[shift] = down(after(sends[shift], *earlier), shift)

    def work(token, shift, is_anchor=False):
        return attend(
            token, own_picks, keys, values, [arrived[shift]], ((shift, 0, slots),), slots, is_anchor
        )[0]

    three, five, four, one, seven = far_shifts
    ask_for(three, near_sends[0])
    ask_for(five, near_sends[0])
    own = own_part(after(now, before), queries, keys, values)
    own_back = passed_along(own, "pipe", 1)
    near.append(up(after(near_sends[1], own), near_shifts[1]))
    part_three = work(after(here, own, near[0]), three, is_anchor=True)
    returned[three] = up_and_on(part_three, three)
    part_five = work(after(here, part_three), five, is_anchor=True)
    returned[five] = up_and_on(part_five, five)
    ask_for(four, arrived[three], arrived[five], near[0])
    beside = near_part(after(here, part_five, own_back), own_picks, queries, near, near_shifts, slots)
    ask_for(one, own_back, part_five, *near)
    ask_for(seven, own_back, part_five, *near)
    beside_back = passed_along(beside, "pipe", 1)
    part_four = work(after(here, beside), four, is_anchor=True)
    returned[four] = up_and_on(part_four, four)
    part_one = work(after(here, part_four, beside_back), one)
    returned[one] = up_and_on(part_one, one)
    part_seven = work(after(here, part_one), seven)
    returned[seven] = up_and_on(part_seven, seven)
    now = after(here, part_seven)

    merged_shifts = near_shifts + (three, five)
    places = [HEADS + place * slots for place in (2, 3)]
    parts = [own_back, beside_back, returned[three], returned[five]]
    result, mixed, sums = merge(now, before, parts, [0, HEADS] + places, merged_shifts, slots)
    lasts = [returned[shift] for shift in final_shifts]
    return finish(now, before, result, mixed, sums, lasts, final_shifts, slots)[None]


def travelling_keys(queries, keys, values, picks):
    ctx_width = lax.axis_size("ctx")
    rank_here = lax.axis_index("ctx")
    slot_count = max(1, PICKS * HEADS // ctx_width)
    block_rows = queries.shape[1]
    score_scale = HD ** (-0.5)
    every_pick = picks[0].reshape(ctx_width, HEADS * PICKS)
    chosen = lax.dynamic_slice_in_dim(every_pick, rank_here, 1, 0)
    pick_order = request_table(chosen, lax.iota(jnp.int32, ctx_width), slot_count)[1]
    asked_table = request_table(every_pick, rank_here.reshape(1), slot_count)[0]
    asked_heads = asked_table[:, 0, :]
    safe_asked = jnp.maximum(asked_heads, 0)
    query_heads = queries[0].reshape(block_rows, HEADS, HD).transpose(1, 0, 2)
    key_heads = keys[0].reshape(block_rows, HEADS, HD).transpose(1, 0, 2)
    value_heads = values[0].reshape(block_rows, HEADS, HD).transpose(1, 0, 2)
    is_live = chosen[0] >= 0
    flat_slot = jnp.where(is_live, chosen[0] * slot_count + pick_order[0], 0)
    remote_mask = jnp.repeat(is_live.reshape(HEADS, PICKS), block_rows, axis=1)
    row_index = lax.iota(jnp.int32, block_rows)
    causal = row_index[:, None] >= row_index[None, :]

    def masked_scores(query_head, key_rows, mask_row):
        scores = lax.dot_general(
            query_head, key_rows, (((1,), (1,)), ((), ())), preferred_element_type=jnp.float32
        )
        allowed = jnp.concatenate(
            [causal, jnp.broadcast_to(mask_row[None, :], (block_rows, PICKS * block_rows))], axis=1
        )
        return jnp.where(allowed, scores * score_scale, -jnp.inf)

    def row_stats(scores):
        row_top = jnp.max(scores, axis=1)
        row_total = jnp.sum(jnp.exp(scores - row_top[:, None]), axis=1)
        return (row_top, row_total)

    def weighted(scores, row_top, row_total, value_rows):
        prob_rows = (jnp.exp(scores - row_top[:, None]) / row_total[:, None]).astype(jnp.bfloat16)
        return jnp.dot(prob_rows, value_rows, preferred_element_type=jnp.float32).astype(
            jnp.bfloat16
        )

    send_both = jnp.concatenate([key_heads, value_heads], axis=2)[safe_asked]
    got_slots = lax.all_to_all(send_both, "ctx", split_axis=0, concat_axis=0, tiled=True)
    last_width = 2 * HD
    flat_slots = got_slots.reshape(ctx_width * slot_count, block_rows, last_width)
    remote_both = flat_slots[flat_slot].reshape(HEADS, PICKS * block_rows, last_width)
    all_keys = jnp.concatenate([key_heads, remote_both[:, :, :HD]], axis=1)
    all_values = jnp.concatenate([value_heads, remote_both[:, :, HD:]], axis=1)

    def per_head(head_items):
        query_head, key_rows, value_rows, mask_row = head_items
        scores = masked_scores(query_head, key_rows, mask_row)
        row_top, row_total = row_stats(scores)
        return weighted(scores, row_top, row_total, value_rows)

    outputs = lax.map(per_head, (query_heads, all_keys, all_values, remote_mask))
    merged = outputs.transpose(1, 0, 2).reshape(1, block_rows, HEADS * HD)
    return passed_along(merged, "pipe", 1)


def per_device(queries, keys, values, picks):
    few_shifts = lax.axis_size("ctx") == 8
    run = travelling_queries if few_shifts else travelling_keys
    return run(queries, keys, values, picks)


def solution(mesh):
    placed = (
        P("pipe", "ctx", None),
        P("pipe", "ctx", None),
        P("pipe", "ctx", None),
        P("pipe", None, None, None),
    )
    return jax.shard_map(
        per_device, mesh=mesh, in_specs=placed, out_specs=P("pipe", "ctx", None), check_vma=False
    )
```

```python
import functools
import math

import jax
import jax.numpy as jnp
from jax import lax
from jax.experimental import pallas as pl
from jax.experimental.pallas import tpu as pltpu
from jax.sharding import PartitionSpec as P

HEADS = 16
HD = 128
PICKS = 2
EXP2_SCALE = HD ** -0.5 * math.log2(math.e)
LANES = 128
STAT_ROWS = 16
VMEM_BYTES = 24 * 1024 * 1024
HIGH_COST = 10**12


def passed_along(value, axis, steps):
    count = lax.axis_size(axis)
    pairs = [(source, (source + steps) % count) for source in range(count)]
    return lax.ppermute(value, axis, pairs)


def request_table(chosen, owners, slot_count):
    pick_count = chosen.shape[1]
    pick_ids = lax.iota(jnp.int32, pick_count)
    is_live = chosen >= 0
    earlier = pick_ids[None, :] < pick_ids[:, None]
    same_owner = (chosen[:, :, None] == chosen[:, None, :]) & earlier[None]
    pick_order = jnp.sum(same_owner.astype(jnp.int32), axis=2)
    head_ids = pick_ids // PICKS
    slot_ranks = lax.iota(jnp.int32, slot_count)
    matches = (
        is_live[:, None, None, :]
        & (chosen[:, None, None, :] == owners[None, :, None, None])
        & (pick_order[:, None, None, :] == slot_ranks[None, None, :, None])
    )
    was_found = jnp.any(matches, axis=3)
    head_table = jnp.sum(jnp.where(matches, head_ids[None, None, None, :], 0), axis=3)
    return (jnp.where(was_found, head_table, -1), pick_order)


def call(
    kernel, name_space, outputs, out_specs, scratch=(), flops=0, moved=0, exps=0
):
    return pl.pallas_call(
        kernel,
        in_specs=name_space,
        out_specs=out_specs,
        out_shape=outputs,
        scratch_shapes=list(scratch),
        compiler_params=pltpu.CompilerParams(vmem_limit_bytes=VMEM_BYTES),
        cost_estimate=pl.CostEstimate(flops=flops, bytes_accessed=moved, transcendentals=exps),
    )


SCALARS = pl.BlockSpec(memory_space=pltpu.SMEM)
IN_HBM = pl.BlockSpec(memory_space=pltpu.HBM)
IN_VMEM = pl.BlockSpec(memory_space=pltpu.VMEM)


def tick_kernel(here_ref, out_ref):
    out_ref[0] = here_ref[0]


def tick(here, *earlier):
    return call(
        tick_kernel,
        [SCALARS],
        jax.ShapeDtypeStruct((1,), jnp.int32),
        SCALARS,
        flops=0,
    )(after(here, *earlier))


def list_heads(heads_ref, start, picks_ref, block, owner, slots):
    width = picks_ref.shape[0]
    spare = heads_ref.shape[0] - 1
    for slot in range(slots):
        heads_ref[start + slot] = -1
    valid = (block >= 0) & (block < width) & (owner >= 0) & (owner < width)
    row = jnp.clip(block, 0, width - 1)
    wanted = jnp.where(valid, owner, -2)
    found = jnp.int32(0)
    for pick in range(PICKS):
        for head in range(HEADS):
            hit = picks_ref[row, pick, head] == wanted
            heads_ref[jnp.where(hit, start + found, spare)] = head
            found = found + hit.astype(jnp.int32)


def pack_kernel(here_ref, picks_ref, *refs, jobs, slots):
    is_near = jobs[0][3]
    sources = refs[: 1 + is_near]
    outputs = refs[1 + is_near : 1 + is_near + len(jobs)]
    heads_ref, sems = refs[-2], refs[-1]
    here = here_ref[0]
    listed = {}
    for shift, first, count, is_near in jobs:
        key = (shift, is_near)
        if key not in listed:
            listed[key] = len(listed) * slots
            block, owner = (here + shift, here) if is_near else (here, here - shift)
            list_heads(heads_ref, listed[key], picks_ref, block, owner, slots)
    copies = []
    for (shift, first, count, is_near), output in zip(jobs, outputs):
        for slot in range(count):
            head = jnp.maximum(heads_ref[listed[shift, is_near] + first + slot], 0)
            columns = pl.ds(pl.multiple_of(head * HD, HD), HD)
            for place, source in enumerate(sources):
                target = output.at[2 * slot + place if is_near else slot]
                copy = pltpu.make_async_copy(
                    source.at[:, columns], target, sems.at[len(copies)]
                )
                copy.start()
                copies.append(copy)
    for copy in copies:
        copy.wait()


def pack(here, picks, sources, jobs, slots):
    rows = sources[0].shape[0]
    sizes = [len(sources) * count for _, _, count, _ in jobs]
    return call(
        functools.partial(pack_kernel, jobs=jobs, slots=slots),
        [SCALARS, SCALARS] + [IN_VMEM] * len(sources),
        [jax.ShapeDtypeStruct((size, rows, HD), jnp.bfloat16) for size in sizes],
        [IN_VMEM] * len(sizes),
        [pltpu.SMEM((len(jobs) * slots + 1,), jnp.int32), pltpu.SemaphoreType.DMA((sum(sizes),))],
        moved=4 * rows * HD * sum(sizes),
    )(here, picks, *sources)


def diagonal():
    shape = (LANES, LANES)
    return lax.broadcasted_iota(jnp.int32, shape, 0) == lax.broadcasted_iota(jnp.int32, shape, 1)


def raw_scores(query_rows, key_rows):
    return lax.dot_general(
        query_rows, key_rows, (((1,), (1,)), ((), ())), preferred_element_type=jnp.float32
    )


def with_ones(value_rows):
    return jnp.concatenate([value_rows, jnp.ones_like(value_rows)], axis=1)


def soft_part(scores, value_rows):
    top = jnp.max(scores, axis=1, keepdims=True)
    weights = jnp.exp2((scores - top) * EXP2_SCALE).astype(jnp.bfloat16)
    total = jnp.dot(weights, value_rows, preferred_element_type=jnp.float32)
    sums = total[:, HD:]
    return total[:, :HD] * pl.reciprocal(sums), top * EXP2_SCALE, sums


def across_lanes(column):
    eye = diagonal()
    spread = jnp.broadcast_to(column, (column.shape[0], LANES))
    return [
        jnp.sum(jnp.where(eye, spread[at : at + LANES], 0.0), axis=0, keepdims=True)
        for at in range(0, column.shape[0], LANES)
    ]


def down_rows(line):
    spread = jnp.broadcast_to(line, (LANES, LANES))
    return jnp.sum(jnp.where(diagonal(), spread, 0.0), axis=1, keepdims=True)


def three_parts(stats):
    first = stats.astype(jnp.bfloat16).astype(jnp.float32)
    second = (stats - first).astype(jnp.bfloat16).astype(jnp.float32)
    third = stats - first - second
    parts = jnp.concatenate([first, second, third], axis=0)
    pad = jnp.zeros((STAT_ROWS - parts.shape[0], LANES), jnp.float32)
    return jnp.concatenate([parts, pad], axis=0).astype(jnp.bfloat16)


def stats_of(block, groups):
    stats = block.astype(jnp.float32)
    return stats[:groups] + stats[groups : 2 * groups] + stats[2 * groups : 3 * groups]


def log_sums(tops, sums):
    top_lines = [line for top in tops for line in across_lanes(top)]
    sum_lines = [line for part in sums for line in across_lanes(part)]
    return jnp.concatenate(top_lines, axis=0) + jnp.log2(jnp.concatenate(sum_lines, axis=0))


def attend_rows(query_rows, key_rows, value_rows, tile):
    found = [
        soft_part(raw_scores(query_rows[at : at + tile], key_rows), value_rows)
        for at in range(0, query_rows.shape[0], tile)
    ]
    outputs, tops, sums = zip(*found)
    return jnp.concatenate(outputs, axis=0), log_sums(tops, sums)


def head_columns(head):
    return pl.ds(pl.multiple_of(head * HD, HD), HD)


def attend_kernel(here_ref, picks_ref, key_ref, value_ref, *refs, group, slots):
    heads_ref = refs[-1]
    here = here_ref[0]
    for number, (shift, first, count) in enumerate(group):
        query_ref, out_ref = refs[number], refs[len(group) + number]
        rows = query_ref.shape[1]
        list_heads(heads_ref, 0, picks_ref, here + shift, here, slots)
        for slot in range(count):
            columns = head_columns(jnp.maximum(heads_ref[first + slot], 0))
            outputs, lines = attend_rows(
                query_ref[slot], key_ref[:, columns], with_ones(value_ref[:, columns]), rows
            )
            out_ref[slot, :rows, :] = outputs.astype(jnp.bfloat16)
            out_ref[slot, rows:, :] = three_parts(lines)


def attend(here, picks, keys, values, arrived, group, slots, is_anchor):
    rows = keys.shape[0]
    total = sum(count for _, _, count in group)
    return call(
        functools.partial(attend_kernel, group=group, slots=slots),
        [SCALARS, SCALARS, IN_VMEM, IN_VMEM] + [IN_VMEM] * len(group),
        [
            jax.ShapeDtypeStruct((count, rows + STAT_ROWS, HD), jnp.bfloat16)
            for _, _, count in group
        ],
        [IN_VMEM] * len(group),
        [pltpu.SMEM((slots + 1,), jnp.int32)],
        flops=HIGH_COST if is_anchor else 4 * total * rows * rows * HD,
        moved=8 * total * rows * HD,
        exps=total * rows * rows,
    )(here, picks, keys, values, *arrived)


def own_kernel(here_ref, query_ref, key_ref, value_ref, out_ref):
    rows = query_ref.shape[0]
    tile = min(rows, 256)

    def one_head(head, carry):
        columns = head_columns(head)
        value_rows = with_ones(value_ref[:, columns])
        tops, all_sums = [], []
        for at in range(0, rows, tile):
            reach = at + tile
            scores = raw_scores(query_ref[at:reach, columns], key_ref[:reach, columns])
            row_ids = lax.broadcasted_iota(jnp.int32, scores.shape, 0) + at
            seen = row_ids >= lax.broadcasted_iota(jnp.int32, scores.shape, 1)
            outputs, top, sums = soft_part(jnp.where(seen, scores, -jnp.inf), value_rows[:reach])
            out_ref[head, at:reach, :] = outputs.astype(jnp.bfloat16)
            tops.append(top)
            all_sums.append(sums)
        out_ref[head, rows:, :] = three_parts(log_sums(tops, all_sums))
        return carry

    lax.fori_loop(0, HEADS, one_head, 0, unroll=4)


def own_part(here, queries, keys, values):
    rows = queries.shape[0]
    return call(
        own_kernel,
        [SCALARS, IN_VMEM, IN_VMEM, IN_VMEM],
        jax.ShapeDtypeStruct((HEADS, rows + STAT_ROWS, HD), jnp.bfloat16),
        IN_VMEM,
        flops=4 * HEADS * rows * rows * HD,
        moved=8 * HEADS * rows * HD,
        exps=HEADS * rows * rows,
    )(here, queries, keys, values)


def near_kernel(here_ref, picks_ref, query_ref, *refs, shifts, slots):
    near_refs, out_ref, heads_ref = refs[: len(shifts)], refs[-2], refs[-1]
    rows = query_ref.shape[0]
    here = here_ref[0]
    for place, (shift, near_ref) in enumerate(zip(shifts, near_refs)):
        list_heads(heads_ref, 0, picks_ref, here, here - shift, slots)
        for slot in range(slots):
            columns = head_columns(jnp.maximum(heads_ref[slot], 0))
            outputs, lines = attend_rows(
                query_ref[:, columns], near_ref[2 * slot], with_ones(near_ref[2 * slot + 1]), rows
            )
            out_ref[place * slots + slot, :rows, :] = outputs.astype(jnp.bfloat16)
            out_ref[place * slots + slot, rows:, :] = three_parts(lines)


def near_part(here, picks, queries, near, shifts, slots):
    rows = queries.shape[0]
    total = len(shifts) * slots
    return call(
        functools.partial(near_kernel, shifts=shifts, slots=slots),
        [SCALARS, SCALARS, IN_VMEM] + [IN_VMEM] * len(shifts),
        jax.ShapeDtypeStruct((total, rows + STAT_ROWS, HD), jnp.bfloat16),
        IN_VMEM,
        [pltpu.SMEM((slots + 1,), jnp.int32)],
        flops=HIGH_COST,
        moved=12 * total * rows * HD,
        exps=total * rows * rows,
    )(here, picks, queries, *near)


def find_spots(spots_ref, found_ref, picks_ref, here, shifts, slots):
    for owner in range(picks_ref.shape[0]):
        found_ref[owner] = 0

    for pick in range(PICKS):
        for head in range(HEADS):
            owner = picks_ref[here, pick, head]
            safe = jnp.maximum(owner, 0)
            order = found_ref[safe]
            found_ref[safe] = order + (owner >= 0).astype(jnp.int32)
            spot = jnp.int32(-1)
            for place, shift in enumerate(shifts):
                spot = jnp.where(here - safe == shift, place * slots + order, spot)
            spots_ref[head * PICKS + pick] = jnp.where(owner >= 0, spot, -1)


def merge_kernel(here_ref, picks_ref, *refs, places, shifts, slots):
    count = len(places)
    parts = refs[:count]
    result_ref, out_ref, sums_ref, held, spots_ref, found_ref, sems = refs[count:]
    groups = sums_ref.shape[1]
    rows = groups * LANES
    copies = [
        pltpu.make_async_copy(part, held.at[pl.ds(place, part.shape[0])], sems.at[number])
        for number, (part, place) in enumerate(zip(parts, places))
    ]
    for copy in copies:
        copy.start()
    find_spots(spots_ref, found_ref, picks_ref, here_ref[0], shifts, slots)
    for copy in copies:
        copy.wait()

    def one_head(head, carry):
        found = [spots_ref[head * PICKS + pick] for pick in range(PICKS)]
        spots = [head] + [jnp.where(spot >= 0, HEADS + spot, head) for spot in found]
        sums = [stats_of(held[spot, rows:, :], groups) for spot in spots]
        for pick, spot in enumerate(found):
            sums[1 + pick] = jnp.where(spot >= 0, sums[1 + pick], -jnp.inf)
        top = functools.reduce(jnp.maximum, sums)
        shares = [jnp.exp2(part - top) for part in sums]
        whole = functools.reduce(jnp.add, shares)
        sums_ref[head] = top + jnp.log2(whole)
        for group in range(groups):
            span = pl.ds(group * LANES, LANES)
            own = held[head, span, :].astype(jnp.float32)
            mixed = own
            for spot, share in zip(spots[1:], shares[1:]):
                weight = down_rows((share / whole)[group : group + 1, :])
                mixed = mixed + (held[spot, span, :].astype(jnp.float32) - own) * weight
            out_ref[head, span, :] = mixed
            result_ref[span, head_columns(head)] = mixed.astype(jnp.bfloat16)
        return carry

    lax.fori_loop(0, HEADS, one_head, 0, unroll=2)


def merge(here, picks, parts, places, shifts, slots):
    rows = parts[0].shape[1] - STAT_ROWS
    width = picks.shape[0]
    total = HEADS + len(shifts) * slots
    return call(
        functools.partial(merge_kernel, places=tuple(places), shifts=shifts, slots=slots),
        [SCALARS, SCALARS] + [pl.BlockSpec(memory_space=pl.ANY)] * len(parts),
        [
            jax.ShapeDtypeStruct((rows, HEADS * HD), jnp.bfloat16),
            jax.ShapeDtypeStruct((HEADS, rows, HD), jnp.float32),
            jax.ShapeDtypeStruct((HEADS, rows // LANES, LANES), jnp.float32),
        ],
        [IN_VMEM, IN_VMEM, IN_VMEM],
        [
            pltpu.VMEM((total, rows + STAT_ROWS, HD), jnp.bfloat16),
            pltpu.SMEM((PICKS * HEADS,), jnp.int32),
            pltpu.SMEM((width,), jnp.int32),
            pltpu.SemaphoreType.DMA((len(parts),)),
        ],
        flops=6 * HEADS * rows * HD,
        moved=2 * (HEADS * 2 + total) * rows * HD,
    )(here, picks, *parts)


def finish_kernel(here_ref, picks_ref, mixed_ref, sums_ref, *refs, shifts, slots):
    count = len(shifts)
    parts, out_ref, (heads_ref, held, sems) = refs[:count], refs[count + 1], refs[count + 2 :]
    groups = sums_ref.shape[1]
    rows = groups * LANES
    here = here_ref[0]
    for number, shift in enumerate(shifts):
        list_heads(heads_ref, number * slots, picks_ref, here, here - shift, slots)

    def slot_of(head, number):
        found = jnp.int32(-1)
        for slot in range(slots):
            found = jnp.where(heads_ref[number * slots + slot] == head, slot, found)
        return found

    def is_first(head, number):
        first = head >= 0
        for earlier in range(number):
            first = first & (slot_of(head, earlier) < 0)
        return first

    def patch(place):
        columns = head_columns(jnp.maximum(heads_ref[place], 0))
        return pltpu.make_async_copy(held.at[place], out_ref.at[:, columns], sems.at[place])

    places = [(number, number * slots + slot) for number in range(count) for slot in range(slots)]
    for number, place in places:
        head = heads_ref[place]

        @pl.when(is_first(head, number))
        def _():
            found = [slot_of(head, later) for later in range(number, count)]
            spots = [jnp.maximum(spot, 0) for spot in found]
            sums = [sums_ref[head]]
            for part, spot, safe in zip(parts[number:], found, spots):
                added = stats_of(part[safe, rows:, :], groups)
                sums.append(jnp.where(spot >= 0, added, -jnp.inf))
            top = functools.reduce(jnp.maximum, sums)
            shares = [jnp.exp2(part - top) for part in sums]
            whole = functools.reduce(jnp.add, shares)
            for group in range(groups):
                span = pl.ds(group * LANES, LANES)
                before = mixed_ref[head, span, :]
                mixed = before
                for part, spot, safe, share in zip(parts[number:], found, spots, shares[1:]):
                    new = jnp.where(spot >= 0, part[safe, span, :].astype(jnp.float32), 0.0)
                    weight = down_rows((share / whole)[group : group + 1, :])
                    mixed = mixed + (new - before) * weight
                held[place, span, :] = mixed.astype(jnp.bfloat16)
            patch(place).start()

    for number, place in places:

        @pl.when(is_first(heads_ref[place], number))
        def _():
            patch(place).wait()


def finish(here, picks, result, mixed, sums, parts, shifts, slots):
    rows = mixed.shape[1]
    total = len(shifts) * slots
    return pl.pallas_call(
        functools.partial(finish_kernel, shifts=shifts, slots=slots),
        in_specs=[SCALARS, SCALARS] + [IN_VMEM] * (2 + len(parts)) + [IN_HBM],
        out_specs=IN_HBM,
        out_shape=jax.ShapeDtypeStruct(result.shape, result.dtype),
        scratch_shapes=[
            pltpu.SMEM((total + 1,), jnp.int32),
            pltpu.VMEM((total, rows, HD), jnp.bfloat16),
            pltpu.SemaphoreType.DMA((total,)),
        ],
        input_output_aliases={4 + len(parts): 0},
        compiler_params=pltpu.CompilerParams(vmem_limit_bytes=VMEM_BYTES),
        cost_estimate=pl.CostEstimate(
            flops=2 * total * rows * HD, bytes_accessed=8 * total * rows * HD, transcendentals=0
        ),
    )(here, picks, mixed, sums, *parts, result)


def after(value, *earlier):
    return lax.optimization_barrier((value,) + earlier)[0]


def travelling_queries(queries, keys, values, picks):
    width = lax.axis_size("ctx")
    sections = lax.axis_size("pipe")
    slots = max(1, PICKS * HEADS // width)
    here = lax.axis_index("ctx").astype(jnp.int32).reshape(1)
    queries, keys, values = queries[0], keys[0], values[0]
    own_picks = picks[0].transpose(0, 2, 1)

    near_shifts = (2, width - 2)
    middle = width // 2
    far_shifts = [middle - 1, middle + 1, 1, width - 1, middle]
    final_shifts = tuple(far_shifts[2:])

    def up(value, shift):
        return lax.ppermute(value, "ctx", [(at, at + shift) for at in range(width - shift)])

    def down(value, shift):
        return lax.ppermute(value, "ctx", [(at, at - shift) for at in range(shift, width)])

    def up_and_on(value, shift):
        pairs = [
            (at * sections + section, (at + shift) * sections + (section + 1) % sections)
            for at in range(width - shift)
            for section in range(sections)
        ]
        return lax.ppermute(value, ("ctx", "pipe"), pairs)

    near_jobs = [(shift, 0, slots, True) for shift in near_shifts]
    near_sends = pack(here, own_picks, [keys, values], near_jobs, slots)
    near = [up(near_sends[0], near_shifts[0])]
    before = passed_along(own_picks, "pipe", 1)
    sends, now = {}, after(here, *near_sends)
    for shifts in (far_shifts[:2], far_shifts[2:]):
        jobs = [(shift, 0, slots, False) for shift in shifts]
        packed = pack(now, own_picks, [queries], jobs, slots)
        sends |= zip(shifts, packed)
        now = after(now, *packed)
    arrived, returned = {}, {}

    def ask_for(shift, *earlier):
        arrived[shift] = down(after(sends[shift], *earlier), shift)

    def work(token, shift, is_anchor=False):
        return attend(
            token, own_picks, keys, values, [arrived[shift]], ((shift, 0, slots),), slots, is_anchor
        )[0]

    three, five, one, seven, four = far_shifts
    ask_for(three, near_sends[0])
    ask_for(five, near_sends[0])
    own = own_part(after(now, before), queries, keys, values)
    own_back = passed_along(own, "pipe", 1)
    near.append(up(after(near_sends[1], own), near_shifts[1]))
    part_three = work(after(here, own, near[0]), three, is_anchor=True)
    returned[three] = up_and_on(part_three, three)
    part_five = work(after(here, part_three), five, is_anchor=True)
    returned[five] = up_and_on(part_five, five)
    ask_for(one, arrived[three], arrived[five], near[0])
    beside = near_part(after(here, part_five, own_back), own_picks, queries, near, near_shifts, slots)
    ask_for(seven, own_back, part_five)
    beside_back = passed_along(after(beside, arrived[seven]), "pipe", 1)
    part_one = work(after(here, beside), one)
    returned[one] = up_and_on(part_one, one)
    ask_for(four, arrived[one], beside)
    part_seven = work(after(here, part_one), seven, is_anchor=True)
    returned[seven] = up_and_on(part_seven, seven)
    part_four = work(after(here, part_seven, beside_back), four)
    returned[four] = up_and_on(part_four, four)
    now = after(here, part_four)

    merged_shifts = near_shifts + (three, five)
    places = [HEADS + place * slots for place in (2, 3)]
    parts = [own_back, beside_back, returned[three], returned[five]]
    result, mixed, sums = merge(now, before, parts, [0, HEADS] + places, merged_shifts, slots)
    lasts = [returned[shift] for shift in final_shifts]
    return finish(now, before, result, mixed, sums, lasts, final_shifts, slots)[None]


def travelling_keys(queries, keys, values, picks):
    ctx_width = lax.axis_size("ctx")
    rank_here = lax.axis_index("ctx")
    slot_count = max(1, PICKS * HEADS // ctx_width)
    block_rows = queries.shape[1]
    score_scale = HD ** (-0.5)
    every_pick = picks[0].reshape(ctx_width, HEADS * PICKS)
    chosen = lax.dynamic_slice_in_dim(every_pick, rank_here, 1, 0)
    pick_order = request_table(chosen, lax.iota(jnp.int32, ctx_width), slot_count)[1]
    asked_table = request_table(every_pick, rank_here.reshape(1), slot_count)[0]
    asked_heads = asked_table[:, 0, :]
    safe_asked = jnp.maximum(asked_heads, 0)
    query_heads = queries[0].reshape(block_rows, HEADS, HD).transpose(1, 0, 2)
    key_heads = keys[0].reshape(block_rows, HEADS, HD).transpose(1, 0, 2)
    value_heads = values[0].reshape(block_rows, HEADS, HD).transpose(1, 0, 2)
    is_live = chosen[0] >= 0
    flat_slot = jnp.where(is_live, chosen[0] * slot_count + pick_order[0], 0)
    remote_mask = jnp.repeat(is_live.reshape(HEADS, PICKS), block_rows, axis=1)
    row_index = lax.iota(jnp.int32, block_rows)
    causal = row_index[:, None] >= row_index[None, :]

    def masked_scores(query_head, key_rows, mask_row):
        scores = lax.dot_general(
            query_head, key_rows, (((1,), (1,)), ((), ())), preferred_element_type=jnp.float32
        )
        allowed = jnp.concatenate(
            [causal, jnp.broadcast_to(mask_row[None, :], (block_rows, PICKS * block_rows))], axis=1
        )
        return jnp.where(allowed, scores * score_scale, -jnp.inf)

    def row_stats(scores):
        row_top = jnp.max(scores, axis=1)
        row_total = jnp.sum(jnp.exp(scores - row_top[:, None]), axis=1)
        return (row_top, row_total)

    def weighted(scores, row_top, row_total, value_rows):
        prob_rows = (jnp.exp(scores - row_top[:, None]) / row_total[:, None]).astype(jnp.bfloat16)
        return jnp.dot(prob_rows, value_rows, preferred_element_type=jnp.float32).astype(
            jnp.bfloat16
        )

    send_both = jnp.concatenate([key_heads, value_heads], axis=2)[safe_asked]
    got_slots = lax.all_to_all(send_both, "ctx", split_axis=0, concat_axis=0, tiled=True)
    last_width = 2 * HD
    flat_slots = got_slots.reshape(ctx_width * slot_count, block_rows, last_width)
    remote_both = flat_slots[flat_slot].reshape(HEADS, PICKS * block_rows, last_width)
    all_keys = jnp.concatenate([key_heads, remote_both[:, :, :HD]], axis=1)
    all_values = jnp.concatenate([value_heads, remote_both[:, :, HD:]], axis=1)

    def per_head(head_items):
        query_head, key_rows, value_rows, mask_row = head_items
        scores = masked_scores(query_head, key_rows, mask_row)
        row_top, row_total = row_stats(scores)
        return weighted(scores, row_top, row_total, value_rows)

    outputs = lax.map(per_head, (query_heads, all_keys, all_values, remote_mask))
    merged = outputs.transpose(1, 0, 2).reshape(1, block_rows, HEADS * HD)
    return passed_along(merged, "pipe", 1)


def per_device(queries, keys, values, picks):
    few_shifts = lax.axis_size("ctx") == 8
    run = travelling_queries if few_shifts else travelling_keys
    return run(queries, keys, values, picks)


def solution(mesh):
    placed = (
        P("pipe", "ctx", None),
        P("pipe", "ctx", None),
        P("pipe", "ctx", None),
        P("pipe", None, None, None),
    )
    return jax.shard_map(
        per_device, mesh=mesh, in_specs=placed, out_specs=P("pipe", "ctx", None), check_vma=False
    )
```

```python
import functools
import math

import jax
import jax.numpy as jnp
from jax import lax
from jax.experimental import pallas as pl
from jax.experimental.pallas import tpu as pltpu
from jax.sharding import PartitionSpec as P

HEADS = 16
HD = 128
PICKS = 2
EXP2_SCALE = HD ** -0.5 * math.log2(math.e)
LANES = 128
STAT_ROWS = 16
VMEM_BYTES = 24 * 1024 * 1024
HIGH_COST = 10**12


def passed_along(value, axis, steps):
    count = lax.axis_size(axis)
    pairs = [(source, (source + steps) % count) for source in range(count)]
    return lax.ppermute(value, axis, pairs)


def request_table(chosen, owners, slot_count):
    pick_count = chosen.shape[1]
    pick_ids = lax.iota(jnp.int32, pick_count)
    is_live = chosen >= 0
    earlier = pick_ids[None, :] < pick_ids[:, None]
    same_owner = (chosen[:, :, None] == chosen[:, None, :]) & earlier[None]
    pick_order = jnp.sum(same_owner.astype(jnp.int32), axis=2)
    head_ids = pick_ids // PICKS
    slot_ranks = lax.iota(jnp.int32, slot_count)
    matches = (
        is_live[:, None, None, :]
        & (chosen[:, None, None, :] == owners[None, :, None, None])
        & (pick_order[:, None, None, :] == slot_ranks[None, None, :, None])
    )
    was_found = jnp.any(matches, axis=3)
    head_table = jnp.sum(jnp.where(matches, head_ids[None, None, None, :], 0), axis=3)
    return (jnp.where(was_found, head_table, -1), pick_order)


def call(
    kernel, name_space, outputs, out_specs, scratch=(), flops=0, moved=0, exps=0
):
    return pl.pallas_call(
        kernel,
        in_specs=name_space,
        out_specs=out_specs,
        out_shape=outputs,
        scratch_shapes=list(scratch),
        compiler_params=pltpu.CompilerParams(vmem_limit_bytes=VMEM_BYTES),
        cost_estimate=pl.CostEstimate(flops=flops, bytes_accessed=moved, transcendentals=exps),
    )


SCALARS = pl.BlockSpec(memory_space=pltpu.SMEM)
IN_HBM = pl.BlockSpec(memory_space=pltpu.HBM)
IN_VMEM = pl.BlockSpec(memory_space=pltpu.VMEM)


def tick_kernel(here_ref, out_ref):
    out_ref[0] = here_ref[0]


def tick(here, *earlier):
    return call(
        tick_kernel,
        [SCALARS],
        jax.ShapeDtypeStruct((1,), jnp.int32),
        SCALARS,
        flops=0,
    )(after(here, *earlier))


def list_heads(heads_ref, start, picks_ref, block, owner, slots):
    width = picks_ref.shape[0]
    spare = heads_ref.shape[0] - 1
    for slot in range(slots):
        heads_ref[start + slot] = -1
    valid = (block >= 0) & (block < width) & (owner >= 0) & (owner < width)
    row = jnp.clip(block, 0, width - 1)
    wanted = jnp.where(valid, owner, -2)
    found = jnp.int32(0)
    for pick in range(PICKS):
        for head in range(HEADS):
            hit = picks_ref[row, pick, head] == wanted
            heads_ref[jnp.where(hit, start + found, spare)] = head
            found = found + hit.astype(jnp.int32)


def pack_kernel(here_ref, picks_ref, *refs, jobs, slots):
    is_near = jobs[0][3]
    sources = refs[: 1 + is_near]
    outputs = refs[1 + is_near : 1 + is_near + len(jobs)]
    heads_ref, sems = refs[-2], refs[-1]
    here = here_ref[0]
    listed = {}
    for shift, first, count, is_near in jobs:
        key = (shift, is_near)
        if key not in listed:
            listed[key] = len(listed) * slots
            block, owner = (here + shift, here) if is_near else (here, here - shift)
            list_heads(heads_ref, listed[key], picks_ref, block, owner, slots)
    copies = []
    for (shift, first, count, is_near), output in zip(jobs, outputs):
        for slot in range(count):
            head = jnp.maximum(heads_ref[listed[shift, is_near] + first + slot], 0)
            columns = pl.ds(pl.multiple_of(head * HD, HD), HD)
            for place, source in enumerate(sources):
                target = output.at[2 * slot + place if is_near else slot]
                copy = pltpu.make_async_copy(
                    source.at[:, columns], target, sems.at[len(copies)]
                )
                copy.start()
                copies.append(copy)
    for copy in copies:
        copy.wait()


def pack(here, picks, sources, jobs, slots):
    rows = sources[0].shape[0]
    sizes = [len(sources) * count for _, _, count, _ in jobs]
    return call(
        functools.partial(pack_kernel, jobs=jobs, slots=slots),
        [SCALARS, SCALARS] + [IN_VMEM] * len(sources),
        [jax.ShapeDtypeStruct((size, rows, HD), jnp.bfloat16) for size in sizes],
        [IN_VMEM] * len(sizes),
        [pltpu.SMEM((len(jobs) * slots + 1,), jnp.int32), pltpu.SemaphoreType.DMA((sum(sizes),))],
        moved=4 * rows * HD * sum(sizes),
    )(here, picks, *sources)


def diagonal():
    shape = (LANES, LANES)
    return lax.broadcasted_iota(jnp.int32, shape, 0) == lax.broadcasted_iota(jnp.int32, shape, 1)


def raw_scores(query_rows, key_rows):
    return lax.dot_general(
        query_rows, key_rows, (((1,), (1,)), ((), ())), preferred_element_type=jnp.float32
    )


def with_ones(value_rows):
    return jnp.concatenate([value_rows, jnp.ones_like(value_rows)], axis=1)


def soft_part(scores, value_rows):
    top = jnp.max(scores, axis=1, keepdims=True)
    weights = jnp.exp2((scores - top) * EXP2_SCALE).astype(jnp.bfloat16)
    total = jnp.dot(weights, value_rows, preferred_element_type=jnp.float32)
    sums = total[:, HD:]
    return total[:, :HD] * pl.reciprocal(sums), top * EXP2_SCALE, sums


def across_lanes(column):
    eye = diagonal()
    spread = jnp.broadcast_to(column, (column.shape[0], LANES))
    return [
        jnp.sum(jnp.where(eye, spread[at : at + LANES], 0.0), axis=0, keepdims=True)
        for at in range(0, column.shape[0], LANES)
    ]


def down_rows(line):
    spread = jnp.broadcast_to(line, (LANES, LANES))
    return jnp.sum(jnp.where(diagonal(), spread, 0.0), axis=1, keepdims=True)


def three_parts(stats):
    first = stats.astype(jnp.bfloat16).astype(jnp.float32)
    second = (stats - first).astype(jnp.bfloat16).astype(jnp.float32)
    third = stats - first - second
    parts = jnp.concatenate([first, second, third], axis=0)
    pad = jnp.zeros((STAT_ROWS - parts.shape[0], LANES), jnp.float32)
    return jnp.concatenate([parts, pad], axis=0).astype(jnp.bfloat16)


def stats_of(block, groups):
    stats = block.astype(jnp.float32)
    return stats[:groups] + stats[groups : 2 * groups] + stats[2 * groups : 3 * groups]


def log_sums(tops, sums):
    top_lines = [line for top in tops for line in across_lanes(top)]
    sum_lines = [line for part in sums for line in across_lanes(part)]
    return jnp.concatenate(top_lines, axis=0) + jnp.log2(jnp.concatenate(sum_lines, axis=0))


def attend_rows(query_rows, key_rows, value_rows, tile):
    found = [
        soft_part(raw_scores(query_rows[at : at + tile], key_rows), value_rows)
        for at in range(0, query_rows.shape[0], tile)
    ]
    outputs, tops, sums = zip(*found)
    return jnp.concatenate(outputs, axis=0), log_sums(tops, sums)


def head_columns(head):
    return pl.ds(pl.multiple_of(head * HD, HD), HD)


def attend_kernel(here_ref, picks_ref, key_ref, value_ref, *refs, group, slots):
    heads_ref = refs[-1]
    here = here_ref[0]
    for number, (shift, first, count) in enumerate(group):
        query_ref, out_ref = refs[number], refs[len(group) + number]
        rows = query_ref.shape[1]
        list_heads(heads_ref, 0, picks_ref, here + shift, here, slots)
        for slot in range(count):
            columns = head_columns(jnp.maximum(heads_ref[first + slot], 0))
            outputs, lines = attend_rows(
                query_ref[slot], key_ref[:, columns], with_ones(value_ref[:, columns]), rows
            )
            out_ref[slot, :rows, :] = outputs.astype(jnp.bfloat16)
            out_ref[slot, rows:, :] = three_parts(lines)


def attend(here, picks, keys, values, arrived, group, slots, is_anchor):
    rows = keys.shape[0]
    total = sum(count for _, _, count in group)
    return call(
        functools.partial(attend_kernel, group=group, slots=slots),
        [SCALARS, SCALARS, IN_VMEM, IN_VMEM] + [IN_VMEM] * len(group),
        [
            jax.ShapeDtypeStruct((count, rows + STAT_ROWS, HD), jnp.bfloat16)
            for _, _, count in group
        ],
        [IN_VMEM] * len(group),
        [pltpu.SMEM((slots + 1,), jnp.int32)],
        flops=HIGH_COST if is_anchor else 4 * total * rows * rows * HD,
        moved=8 * total * rows * HD,
        exps=total * rows * rows,
    )(here, picks, keys, values, *arrived)


def own_kernel(here_ref, query_ref, key_ref, value_ref, out_ref):
    rows = query_ref.shape[0]
    tile = min(rows, 256)

    def one_head(head, carry):
        columns = head_columns(head)
        value_rows = with_ones(value_ref[:, columns])
        tops, all_sums = [], []
        for at in range(0, rows, tile):
            reach = at + tile
            scores = raw_scores(query_ref[at:reach, columns], key_ref[:reach, columns])
            row_ids = lax.broadcasted_iota(jnp.int32, scores.shape, 0) + at
            seen = row_ids >= lax.broadcasted_iota(jnp.int32, scores.shape, 1)
            outputs, top, sums = soft_part(jnp.where(seen, scores, -jnp.inf), value_rows[:reach])
            out_ref[head, at:reach, :] = outputs.astype(jnp.bfloat16)
            tops.append(top)
            all_sums.append(sums)
        out_ref[head, rows:, :] = three_parts(log_sums(tops, all_sums))
        return carry

    lax.fori_loop(0, HEADS, one_head, 0, unroll=4)


def own_part(here, queries, keys, values):
    rows = queries.shape[0]
    return call(
        own_kernel,
        [SCALARS, IN_VMEM, IN_VMEM, IN_VMEM],
        jax.ShapeDtypeStruct((HEADS, rows + STAT_ROWS, HD), jnp.bfloat16),
        IN_VMEM,
        flops=4 * HEADS * rows * rows * HD,
        moved=8 * HEADS * rows * HD,
        exps=HEADS * rows * rows,
    )(here, queries, keys, values)


def near_kernel(here_ref, picks_ref, query_ref, *refs, shifts, slots):
    near_refs, out_ref, heads_ref = refs[: len(shifts)], refs[-2], refs[-1]
    rows = query_ref.shape[0]
    here = here_ref[0]
    for place, (shift, near_ref) in enumerate(zip(shifts, near_refs)):
        list_heads(heads_ref, 0, picks_ref, here, here - shift, slots)
        for slot in range(slots):
            columns = head_columns(jnp.maximum(heads_ref[slot], 0))
            outputs, lines = attend_rows(
                query_ref[:, columns], near_ref[2 * slot], with_ones(near_ref[2 * slot + 1]), rows
            )
            out_ref[place * slots + slot, :rows, :] = outputs.astype(jnp.bfloat16)
            out_ref[place * slots + slot, rows:, :] = three_parts(lines)


def near_part(here, picks, queries, near, shifts, slots):
    rows = queries.shape[0]
    total = len(shifts) * slots
    return call(
        functools.partial(near_kernel, shifts=shifts, slots=slots),
        [SCALARS, SCALARS, IN_VMEM] + [IN_VMEM] * len(shifts),
        jax.ShapeDtypeStruct((total, rows + STAT_ROWS, HD), jnp.bfloat16),
        IN_VMEM,
        [pltpu.SMEM((slots + 1,), jnp.int32)],
        flops=HIGH_COST,
        moved=12 * total * rows * HD,
        exps=total * rows * rows,
    )(here, picks, queries, *near)


def find_spots(spots_ref, found_ref, picks_ref, here, shifts, slots):
    for owner in range(picks_ref.shape[0]):
        found_ref[owner] = 0

    for pick in range(PICKS):
        for head in range(HEADS):
            owner = picks_ref[here, pick, head]
            safe = jnp.maximum(owner, 0)
            order = found_ref[safe]
            found_ref[safe] = order + (owner >= 0).astype(jnp.int32)
            spot = jnp.int32(-1)
            for place, shift in enumerate(shifts):
                spot = jnp.where(here - safe == shift, place * slots + order, spot)
            spots_ref[head * PICKS + pick] = jnp.where(owner >= 0, spot, -1)


def merge_kernel(here_ref, picks_ref, *refs, places, shifts, slots):
    count = len(places)
    parts = refs[:count]
    result_ref, out_ref, sums_ref, held, spots_ref, found_ref, sems = refs[count:]
    groups = sums_ref.shape[1]
    rows = groups * LANES
    copies = [
        pltpu.make_async_copy(part, held.at[pl.ds(place, part.shape[0])], sems.at[number])
        for number, (part, place) in enumerate(zip(parts, places))
    ]
    for copy in copies:
        copy.start()
    find_spots(spots_ref, found_ref, picks_ref, here_ref[0], shifts, slots)
    for copy in copies:
        copy.wait()

    def one_head(head, carry):
        found = [spots_ref[head * PICKS + pick] for pick in range(PICKS)]
        spots = [head] + [jnp.where(spot >= 0, HEADS + spot, head) for spot in found]
        sums = [stats_of(held[spot, rows:, :], groups) for spot in spots]
        for pick, spot in enumerate(found):
            sums[1 + pick] = jnp.where(spot >= 0, sums[1 + pick], -jnp.inf)
        top = functools.reduce(jnp.maximum, sums)
        shares = [jnp.exp2(part - top) for part in sums]
        whole = functools.reduce(jnp.add, shares)
        sums_ref[head] = top + jnp.log2(whole)
        for group in range(groups):
            span = pl.ds(group * LANES, LANES)
            own = held[head, span, :].astype(jnp.float32)
            mixed = own
            for spot, share in zip(spots[1:], shares[1:]):
                weight = down_rows((share / whole)[group : group + 1, :])
                mixed = mixed + (held[spot, span, :].astype(jnp.float32) - own) * weight
            out_ref[head, span, :] = mixed
            result_ref[span, head_columns(head)] = mixed.astype(jnp.bfloat16)
        return carry

    lax.fori_loop(0, HEADS, one_head, 0, unroll=2)


def merge(here, picks, parts, places, shifts, slots):
    rows = parts[0].shape[1] - STAT_ROWS
    width = picks.shape[0]
    total = HEADS + len(shifts) * slots
    return call(
        functools.partial(merge_kernel, places=tuple(places), shifts=shifts, slots=slots),
        [SCALARS, SCALARS] + [pl.BlockSpec(memory_space=pl.ANY)] * len(parts),
        [
            jax.ShapeDtypeStruct((rows, HEADS * HD), jnp.bfloat16),
            jax.ShapeDtypeStruct((HEADS, rows, HD), jnp.float32),
            jax.ShapeDtypeStruct((HEADS, rows // LANES, LANES), jnp.float32),
        ],
        [IN_VMEM, IN_VMEM, IN_VMEM],
        [
            pltpu.VMEM((total, rows + STAT_ROWS, HD), jnp.bfloat16),
            pltpu.SMEM((PICKS * HEADS,), jnp.int32),
            pltpu.SMEM((width,), jnp.int32),
            pltpu.SemaphoreType.DMA((len(parts),)),
        ],
        flops=6 * HEADS * rows * HD,
        moved=2 * (HEADS * 2 + total) * rows * HD,
    )(here, picks, *parts)


def finish_kernel(here_ref, picks_ref, mixed_ref, sums_ref, *refs, shifts, slots):
    count = len(shifts)
    parts, out_ref, (heads_ref, held, sems) = refs[:count], refs[count + 1], refs[count + 2 :]
    groups = sums_ref.shape[1]
    rows = groups * LANES
    here = here_ref[0]
    for number, shift in enumerate(shifts):
        list_heads(heads_ref, number * slots, picks_ref, here, here - shift, slots)

    def slot_of(head, number):
        found = jnp.int32(-1)
        for slot in range(slots):
            found = jnp.where(heads_ref[number * slots + slot] == head, slot, found)
        return found

    def is_first(head, number):
        first = head >= 0
        for earlier in range(number):
            first = first & (slot_of(head, earlier) < 0)
        return first

    def patch(place):
        columns = head_columns(jnp.maximum(heads_ref[place], 0))
        return pltpu.make_async_copy(held.at[place], out_ref.at[:, columns], sems.at[place])

    places = [(number, number * slots + slot) for number in range(count) for slot in range(slots)]
    for number, place in places:
        head = heads_ref[place]

        @pl.when(is_first(head, number))
        def _():
            found = [slot_of(head, later) for later in range(number, count)]
            spots = [jnp.maximum(spot, 0) for spot in found]
            sums = [sums_ref[head]]
            for part, spot, safe in zip(parts[number:], found, spots):
                added = stats_of(part[safe, rows:, :], groups)
                sums.append(jnp.where(spot >= 0, added, -jnp.inf))
            top = functools.reduce(jnp.maximum, sums)
            shares = [jnp.exp2(part - top) for part in sums]
            whole = functools.reduce(jnp.add, shares)
            for group in range(groups):
                span = pl.ds(group * LANES, LANES)
                before = mixed_ref[head, span, :]
                mixed = before
                for part, spot, safe, share in zip(parts[number:], found, spots, shares[1:]):
                    new = jnp.where(spot >= 0, part[safe, span, :].astype(jnp.float32), 0.0)
                    weight = down_rows((share / whole)[group : group + 1, :])
                    mixed = mixed + (new - before) * weight
                held[place, span, :] = mixed.astype(jnp.bfloat16)
            patch(place).start()

    for number, place in places:

        @pl.when(is_first(heads_ref[place], number))
        def _():
            patch(place).wait()


def finish(here, picks, result, mixed, sums, parts, shifts, slots):
    rows = mixed.shape[1]
    total = len(shifts) * slots
    return pl.pallas_call(
        functools.partial(finish_kernel, shifts=shifts, slots=slots),
        in_specs=[SCALARS, SCALARS] + [IN_VMEM] * (2 + len(parts)) + [IN_HBM],
        out_specs=IN_HBM,
        out_shape=jax.ShapeDtypeStruct(result.shape, result.dtype),
        scratch_shapes=[
            pltpu.SMEM((total + 1,), jnp.int32),
            pltpu.VMEM((total, rows, HD), jnp.bfloat16),
            pltpu.SemaphoreType.DMA((total,)),
        ],
        input_output_aliases={4 + len(parts): 0},
        compiler_params=pltpu.CompilerParams(vmem_limit_bytes=VMEM_BYTES),
        cost_estimate=pl.CostEstimate(
            flops=2 * total * rows * HD, bytes_accessed=8 * total * rows * HD, transcendentals=0
        ),
    )(here, picks, mixed, sums, *parts, result)


def after(value, *earlier):
    return lax.optimization_barrier((value,) + earlier)[0]


def travelling_queries(queries, keys, values, picks):
    width = lax.axis_size("ctx")
    sections = lax.axis_size("pipe")
    slots = max(1, PICKS * HEADS // width)
    here = lax.axis_index("ctx").astype(jnp.int32).reshape(1)
    queries, keys, values = queries[0], keys[0], values[0]
    own_picks = picks[0].transpose(0, 2, 1)

    near_shifts = (2, width - 2)
    middle = width // 2
    far_shifts = [middle - 1, middle + 1, middle, 1, width - 1]
    final_shifts = tuple(far_shifts[2:])

    def up(value, shift):
        return lax.ppermute(value, "ctx", [(at, at + shift) for at in range(width - shift)])

    def down(value, shift):
        return lax.ppermute(value, "ctx", [(at, at - shift) for at in range(shift, width)])

    def up_and_on(value, shift):
        pairs = [
            (at * sections + section, (at + shift) * sections + (section + 1) % sections)
            for at in range(width - shift)
            for section in range(sections)
        ]
        return lax.ppermute(value, ("ctx", "pipe"), pairs)

    near_jobs = [(shift, 0, slots, True) for shift in near_shifts]
    near_sends = pack(here, own_picks, [keys, values], near_jobs, slots)
    near = [up(near_sends[0], near_shifts[0])]
    before = passed_along(own_picks, "pipe", 1)
    sends, now = {}, after(here, *near_sends)
    for shifts in (far_shifts[:2], far_shifts[2:]):
        jobs = [(shift, 0, slots, False) for shift in shifts]
        packed = pack(now, own_picks, [queries], jobs, slots)
        sends |= zip(shifts, packed)
        now = after(now, *packed)
    arrived, returned = {}, {}

    def ask_for(shift, *earlier):
        arrived[shift] = down(after(sends[shift], *earlier), shift)

    def work(token, shift, is_anchor=False):
        return attend(
            token, own_picks, keys, values, [arrived[shift]], ((shift, 0, slots),), slots, is_anchor
        )[0]

    three, five, four, one, seven = far_shifts
    ask_for(three, near_sends[0])
    ask_for(five, near_sends[0])
    own = own_part(after(now, before), queries, keys, values)
    own_back = passed_along(own, "pipe", 1)
    near.append(up(after(near_sends[1], own), near_shifts[1]))
    part_three = work(after(here, own, near[0]), three, is_anchor=True)
    returned[three] = up_and_on(part_three, three)
    part_five = work(after(here, part_three), five, is_anchor=True)
    returned[five] = up_and_on(part_five, five)
    ask_for(four, arrived[three], arrived[five], part_five, own_back, *near)
    beside = near_part(after(here, part_five, own_back), own_picks, queries, near, near_shifts, slots)
    ask_for(one, own_back, part_five, *near)
    ask_for(seven, own_back, part_five, *near)
    beside_back = passed_along(beside, "pipe", 1)
    part_four = work(after(here, beside), four, is_anchor=True)
    returned[four] = up_and_on(part_four, four)
    part_one = work(after(here, part_four, beside_back), one)
    returned[one] = up_and_on(part_one, one)
    part_seven = work(after(here, part_one), seven)
    returned[seven] = up_and_on(part_seven, seven)
    now = after(here, part_seven)

    merged_shifts = near_shifts + (three, five)
    places = [HEADS + place * slots for place in (2, 3)]
    parts = [own_back, beside_back, returned[three], returned[five]]
    result, mixed, sums = merge(now, before, parts, [0, HEADS] + places, merged_shifts, slots)
    lasts = [returned[shift] for shift in final_shifts]
    return finish(now, before, result, mixed, sums, lasts, final_shifts, slots)[None]


def travelling_keys(queries, keys, values, picks):
    ctx_width = lax.axis_size("ctx")
    rank_here = lax.axis_index("ctx")
    slot_count = max(1, PICKS * HEADS // ctx_width)
    block_rows = queries.shape[1]
    score_scale = HD ** (-0.5)
    every_pick = picks[0].reshape(ctx_width, HEADS * PICKS)
    chosen = lax.dynamic_slice_in_dim(every_pick, rank_here, 1, 0)
    pick_order = request_table(chosen, lax.iota(jnp.int32, ctx_width), slot_count)[1]
    asked_table = request_table(every_pick, rank_here.reshape(1), slot_count)[0]
    asked_heads = asked_table[:, 0, :]
    safe_asked = jnp.maximum(asked_heads, 0)
    query_heads = queries[0].reshape(block_rows, HEADS, HD).transpose(1, 0, 2)
    key_heads = keys[0].reshape(block_rows, HEADS, HD).transpose(1, 0, 2)
    value_heads = values[0].reshape(block_rows, HEADS, HD).transpose(1, 0, 2)
    is_live = chosen[0] >= 0
    flat_slot = jnp.where(is_live, chosen[0] * slot_count + pick_order[0], 0)
    remote_mask = jnp.repeat(is_live.reshape(HEADS, PICKS), block_rows, axis=1)
    row_index = lax.iota(jnp.int32, block_rows)
    causal = row_index[:, None] >= row_index[None, :]

    def masked_scores(query_head, key_rows, mask_row):
        scores = lax.dot_general(
            query_head, key_rows, (((1,), (1,)), ((), ())), preferred_element_type=jnp.float32
        )
        allowed = jnp.concatenate(
            [causal, jnp.broadcast_to(mask_row[None, :], (block_rows, PICKS * block_rows))], axis=1
        )
        return jnp.where(allowed, scores * score_scale, -jnp.inf)

    def row_stats(scores):
        row_top = jnp.max(scores, axis=1)
        row_total = jnp.sum(jnp.exp(scores - row_top[:, None]), axis=1)
        return (row_top, row_total)

    def weighted(scores, row_top, row_total, value_rows):
        prob_rows = (jnp.exp(scores - row_top[:, None]) / row_total[:, None]).astype(jnp.bfloat16)
        return jnp.dot(prob_rows, value_rows, preferred_element_type=jnp.float32).astype(
            jnp.bfloat16
        )

    send_both = jnp.concatenate([key_heads, value_heads], axis=2)[safe_asked]
    got_slots = lax.all_to_all(send_both, "ctx", split_axis=0, concat_axis=0, tiled=True)
    last_width = 2 * HD
    flat_slots = got_slots.reshape(ctx_width * slot_count, block_rows, last_width)
    remote_both = flat_slots[flat_slot].reshape(HEADS, PICKS * block_rows, last_width)
    all_keys = jnp.concatenate([key_heads, remote_both[:, :, :HD]], axis=1)
    all_values = jnp.concatenate([value_heads, remote_both[:, :, HD:]], axis=1)

    def per_head(head_items):
        query_head, key_rows, value_rows, mask_row = head_items
        scores = masked_scores(query_head, key_rows, mask_row)
        row_top, row_total = row_stats(scores)
        return weighted(scores, row_top, row_total, value_rows)

    outputs = lax.map(per_head, (query_heads, all_keys, all_values, remote_mask))
    merged = outputs.transpose(1, 0, 2).reshape(1, block_rows, HEADS * HD)
    return passed_along(merged, "pipe", 1)


def per_device(queries, keys, values, picks):
    few_shifts = lax.axis_size("ctx") == 8
    run = travelling_queries if few_shifts else travelling_keys
    return run(queries, keys, values, picks)


def solution(mesh):
    placed = (
        P("pipe", "ctx", None),
        P("pipe", "ctx", None),
        P("pipe", "ctx", None),
        P("pipe", None, None, None),
    )
    return jax.shard_map(
        per_device, mesh=mesh, in_specs=placed, out_specs=P("pipe", "ctx", None), check_vma=False
    )
```

```python
import functools
import math

import jax
import jax.numpy as jnp
from jax import lax
from jax.experimental import pallas as pl
from jax.experimental.pallas import tpu as pltpu
from jax.sharding import PartitionSpec as P

HEADS = 16
HD = 128
PICKS = 2
EXP2_SCALE = HD ** -0.5 * math.log2(math.e)
LANES = 128
STAT_ROWS = 16
VMEM_BYTES = 24 * 1024 * 1024
HIGH_COST = 10**12


def passed_along(value, axis, steps):
    count = lax.axis_size(axis)
    pairs = [(source, (source + steps) % count) for source in range(count)]
    return lax.ppermute(value, axis, pairs)


def request_table(chosen, owners, slot_count):
    pick_count = chosen.shape[1]
    pick_ids = lax.iota(jnp.int32, pick_count)
    is_live = chosen >= 0
    earlier = pick_ids[None, :] < pick_ids[:, None]
    same_owner = (chosen[:, :, None] == chosen[:, None, :]) & earlier[None]
    pick_order = jnp.sum(same_owner.astype(jnp.int32), axis=2)
    head_ids = pick_ids // PICKS
    slot_ranks = lax.iota(jnp.int32, slot_count)
    matches = (
        is_live[:, None, None, :]
        & (chosen[:, None, None, :] == owners[None, :, None, None])
        & (pick_order[:, None, None, :] == slot_ranks[None, None, :, None])
    )
    was_found = jnp.any(matches, axis=3)
    head_table = jnp.sum(jnp.where(matches, head_ids[None, None, None, :], 0), axis=3)
    return (jnp.where(was_found, head_table, -1), pick_order)


def call(
    kernel, name_space, outputs, out_specs, scratch=(), flops=0, moved=0, exps=0
):
    return pl.pallas_call(
        kernel,
        in_specs=name_space,
        out_specs=out_specs,
        out_shape=outputs,
        scratch_shapes=list(scratch),
        compiler_params=pltpu.CompilerParams(vmem_limit_bytes=VMEM_BYTES),
        cost_estimate=pl.CostEstimate(flops=flops, bytes_accessed=moved, transcendentals=exps),
    )


SCALARS = pl.BlockSpec(memory_space=pltpu.SMEM)
IN_HBM = pl.BlockSpec(memory_space=pltpu.HBM)
IN_VMEM = pl.BlockSpec(memory_space=pltpu.VMEM)


def tick_kernel(here_ref, out_ref):
    out_ref[0] = here_ref[0]


def tick(here, *earlier):
    return call(
        tick_kernel,
        [SCALARS],
        jax.ShapeDtypeStruct((1,), jnp.int32),
        SCALARS,
        flops=0,
    )(after(here, *earlier))


def list_heads(heads_ref, start, picks_ref, block, owner, slots):
    width = picks_ref.shape[0]
    spare = heads_ref.shape[0] - 1
    for slot in range(slots):
        heads_ref[start + slot] = -1
    valid = (block >= 0) & (block < width) & (owner >= 0) & (owner < width)
    row = jnp.clip(block, 0, width - 1)
    wanted = jnp.where(valid, owner, -2)
    found = jnp.int32(0)
    for pick in range(PICKS):
        for head in range(HEADS):
            hit = picks_ref[row, pick, head] == wanted
            heads_ref[jnp.where(hit, start + found, spare)] = head
            found = found + hit.astype(jnp.int32)


def pack_kernel(here_ref, picks_ref, *refs, jobs, slots):
    is_near = jobs[0][3]
    sources = refs[: 1 + is_near]
    outputs = refs[1 + is_near : 1 + is_near + len(jobs)]
    heads_ref, sems = refs[-2], refs[-1]
    here = here_ref[0]
    listed = {}
    for shift, first, count, is_near in jobs:
        key = (shift, is_near)
        if key not in listed:
            listed[key] = len(listed) * slots
            block, owner = (here + shift, here) if is_near else (here, here - shift)
            list_heads(heads_ref, listed[key], picks_ref, block, owner, slots)
    copies = []
    for (shift, first, count, is_near), output in zip(jobs, outputs):
        for slot in range(count):
            head = jnp.maximum(heads_ref[listed[shift, is_near] + first + slot], 0)
            columns = pl.ds(pl.multiple_of(head * HD, HD), HD)
            for place, source in enumerate(sources):
                target = output.at[2 * slot + place if is_near else slot]
                copy = pltpu.make_async_copy(
                    source.at[:, columns], target, sems.at[len(copies)]
                )
                copy.start()
                copies.append(copy)
    for copy in copies:
        copy.wait()


def pack(here, picks, sources, jobs, slots, is_anchor=False):
    rows = sources[0].shape[0]
    sizes = [len(sources) * count for _, _, count, _ in jobs]
    return call(
        functools.partial(pack_kernel, jobs=jobs, slots=slots),
        [SCALARS, SCALARS] + [IN_VMEM] * len(sources),
        [jax.ShapeDtypeStruct((size, rows, HD), jnp.bfloat16) for size in sizes],
        [IN_VMEM] * len(sizes),
        [pltpu.SMEM((len(jobs) * slots + 1,), jnp.int32), pltpu.SemaphoreType.DMA((sum(sizes),))],
        flops=HIGH_COST if is_anchor else 0,
        moved=4 * rows * HD * sum(sizes),
    )(here, picks, *sources)


def diagonal():
    shape = (LANES, LANES)
    return lax.broadcasted_iota(jnp.int32, shape, 0) == lax.broadcasted_iota(jnp.int32, shape, 1)


def raw_scores(query_rows, key_rows):
    return lax.dot_general(
        query_rows, key_rows, (((1,), (1,)), ((), ())), preferred_element_type=jnp.float32
    )


def with_ones(value_rows):
    return jnp.concatenate([value_rows, jnp.ones_like(value_rows)], axis=1)


def soft_part(scores, value_rows):
    top = jnp.max(scores, axis=1, keepdims=True)
    weights = jnp.exp2((scores - top) * EXP2_SCALE).astype(jnp.bfloat16)
    total = jnp.dot(weights, value_rows, preferred_element_type=jnp.float32)
    sums = total[:, HD:]
    return total[:, :HD] * pl.reciprocal(sums), top * EXP2_SCALE, sums


def across_lanes(column):
    eye = diagonal()
    spread = jnp.broadcast_to(column, (column.shape[0], LANES))
    return [
        jnp.sum(jnp.where(eye, spread[at : at + LANES], 0.0), axis=0, keepdims=True)
        for at in range(0, column.shape[0], LANES)
    ]


def down_rows(line):
    spread = jnp.broadcast_to(line, (LANES, LANES))
    return jnp.sum(jnp.where(diagonal(), spread, 0.0), axis=1, keepdims=True)


def three_parts(stats):
    first = stats.astype(jnp.bfloat16).astype(jnp.float32)
    second = (stats - first).astype(jnp.bfloat16).astype(jnp.float32)
    third = stats - first - second
    parts = jnp.concatenate([first, second, third], axis=0)
    pad = jnp.zeros((STAT_ROWS - parts.shape[0], LANES), jnp.float32)
    return jnp.concatenate([parts, pad], axis=0).astype(jnp.bfloat16)


def stats_of(block, groups):
    stats = block.astype(jnp.float32)
    return stats[:groups] + stats[groups : 2 * groups] + stats[2 * groups : 3 * groups]


def log_sums(tops, sums):
    top_lines = [line for top in tops for line in across_lanes(top)]
    sum_lines = [line for part in sums for line in across_lanes(part)]
    return jnp.concatenate(top_lines, axis=0) + jnp.log2(jnp.concatenate(sum_lines, axis=0))


def attend_rows(query_rows, key_rows, value_rows, tile):
    found = [
        soft_part(raw_scores(query_rows[at : at + tile], key_rows), value_rows)
        for at in range(0, query_rows.shape[0], tile)
    ]
    outputs, tops, sums = zip(*found)
    return jnp.concatenate(outputs, axis=0), log_sums(tops, sums)


def head_columns(head):
    return pl.ds(pl.multiple_of(head * HD, HD), HD)


def attend_kernel(here_ref, picks_ref, key_ref, value_ref, *refs, group, slots):
    heads_ref = refs[-1]
    here = here_ref[0]
    for number, (shift, first, count) in enumerate(group):
        query_ref, out_ref = refs[number], refs[len(group) + number]
        rows = query_ref.shape[1]
        list_heads(heads_ref, 0, picks_ref, here + shift, here, slots)
        for slot in range(count):
            columns = head_columns(jnp.maximum(heads_ref[first + slot], 0))
            outputs, lines = attend_rows(
                query_ref[slot], key_ref[:, columns], with_ones(value_ref[:, columns]), rows
            )
            out_ref[slot, :rows, :] = outputs.astype(jnp.bfloat16)
            out_ref[slot, rows:, :] = three_parts(lines)


def attend(here, picks, keys, values, arrived, group, slots, is_anchor):
    rows = keys.shape[0]
    total = sum(count for _, _, count in group)
    return call(
        functools.partial(attend_kernel, group=group, slots=slots),
        [SCALARS, SCALARS, IN_VMEM, IN_VMEM] + [IN_VMEM] * len(group),
        [
            jax.ShapeDtypeStruct((count, rows + STAT_ROWS, HD), jnp.bfloat16)
            for _, _, count in group
        ],
        [IN_VMEM] * len(group),
        [pltpu.SMEM((slots + 1,), jnp.int32)],
        flops=HIGH_COST if is_anchor else 4 * total * rows * rows * HD,
        moved=8 * total * rows * HD,
        exps=total * rows * rows,
    )(here, picks, keys, values, *arrived)


def own_kernel(here_ref, query_ref, key_ref, value_ref, out_ref):
    rows = query_ref.shape[0]
    tile = min(rows, 256)

    def one_head(head, carry):
        columns = head_columns(head)
        value_rows = with_ones(value_ref[:, columns])
        tops, all_sums = [], []
        for at in range(0, rows, tile):
            reach = at + tile
            scores = raw_scores(query_ref[at:reach, columns], key_ref[:reach, columns])
            row_ids = lax.broadcasted_iota(jnp.int32, scores.shape, 0) + at
            seen = row_ids >= lax.broadcasted_iota(jnp.int32, scores.shape, 1)
            outputs, top, sums = soft_part(jnp.where(seen, scores, -jnp.inf), value_rows[:reach])
            out_ref[head, at:reach, :] = outputs.astype(jnp.bfloat16)
            tops.append(top)
            all_sums.append(sums)
        out_ref[head, rows:, :] = three_parts(log_sums(tops, all_sums))
        return carry

    lax.fori_loop(0, HEADS, one_head, 0, unroll=4)


def own_part(here, queries, keys, values):
    rows = queries.shape[0]
    return call(
        own_kernel,
        [SCALARS, IN_VMEM, IN_VMEM, IN_VMEM],
        jax.ShapeDtypeStruct((HEADS, rows + STAT_ROWS, HD), jnp.bfloat16),
        IN_VMEM,
        flops=4 * HEADS * rows * rows * HD,
        moved=8 * HEADS * rows * HD,
        exps=HEADS * rows * rows,
    )(here, queries, keys, values)


def near_kernel(here_ref, picks_ref, query_ref, *refs, shifts, slots):
    near_refs, out_ref, heads_ref = refs[: len(shifts)], refs[-2], refs[-1]
    rows = query_ref.shape[0]
    here = here_ref[0]
    for place, (shift, near_ref) in enumerate(zip(shifts, near_refs)):
        list_heads(heads_ref, 0, picks_ref, here, here - shift, slots)
        for slot in range(slots):
            columns = head_columns(jnp.maximum(heads_ref[slot], 0))
            outputs, lines = attend_rows(
                query_ref[:, columns], near_ref[2 * slot], with_ones(near_ref[2 * slot + 1]), rows
            )
            out_ref[place * slots + slot, :rows, :] = outputs.astype(jnp.bfloat16)
            out_ref[place * slots + slot, rows:, :] = three_parts(lines)


def near_part(here, picks, queries, near, shifts, slots):
    rows = queries.shape[0]
    total = len(shifts) * slots
    return call(
        functools.partial(near_kernel, shifts=shifts, slots=slots),
        [SCALARS, SCALARS, IN_VMEM] + [IN_VMEM] * len(shifts),
        jax.ShapeDtypeStruct((total, rows + STAT_ROWS, HD), jnp.bfloat16),
        IN_VMEM,
        [pltpu.SMEM((slots + 1,), jnp.int32)],
        flops=HIGH_COST,
        moved=12 * total * rows * HD,
        exps=total * rows * rows,
    )(here, picks, queries, *near)


def find_spots(spots_ref, found_ref, picks_ref, here, shifts, slots):
    for owner in range(picks_ref.shape[0]):
        found_ref[owner] = 0

    for pick in range(PICKS):
        for head in range(HEADS):
            owner = picks_ref[here, pick, head]
            safe = jnp.maximum(owner, 0)
            order = found_ref[safe]
            found_ref[safe] = order + (owner >= 0).astype(jnp.int32)
            spot = jnp.int32(-1)
            for place, shift in enumerate(shifts):
                spot = jnp.where(here - safe == shift, place * slots + order, spot)
            spots_ref[head * PICKS + pick] = jnp.where(owner >= 0, spot, -1)


def merge_kernel(here_ref, picks_ref, *refs, places, shifts, slots):
    count = len(places)
    parts = refs[:count]
    result_ref, out_ref, sums_ref, held, spots_ref, found_ref, sems = refs[count:]
    groups = sums_ref.shape[1]
    rows = groups * LANES
    copies = [
        pltpu.make_async_copy(part, held.at[pl.ds(place, part.shape[0])], sems.at[number])
        for number, (part, place) in enumerate(zip(parts, places))
    ]
    for copy in copies:
        copy.start()
    find_spots(spots_ref, found_ref, picks_ref, here_ref[0], shifts, slots)
    for copy in copies:
        copy.wait()

    def one_head(head, carry):
        found = [spots_ref[head * PICKS + pick] for pick in range(PICKS)]
        spots = [head] + [jnp.where(spot >= 0, HEADS + spot, head) for spot in found]
        sums = [stats_of(held[spot, rows:, :], groups) for spot in spots]
        for pick, spot in enumerate(found):
            sums[1 + pick] = jnp.where(spot >= 0, sums[1 + pick], -jnp.inf)
        top = functools.reduce(jnp.maximum, sums)
        shares = [jnp.exp2(part - top) for part in sums]
        whole = functools.reduce(jnp.add, shares)
        sums_ref[head] = top + jnp.log2(whole)
        for group in range(groups):
            span = pl.ds(group * LANES, LANES)
            own = held[head, span, :].astype(jnp.float32)
            mixed = own
            for spot, share in zip(spots[1:], shares[1:]):
                weight = down_rows((share / whole)[group : group + 1, :])
                mixed = mixed + (held[spot, span, :].astype(jnp.float32) - own) * weight
            out_ref[head, span, :] = mixed
            result_ref[span, head_columns(head)] = mixed.astype(jnp.bfloat16)
        return carry

    lax.fori_loop(0, HEADS, one_head, 0, unroll=2)


def merge(here, picks, parts, places, shifts, slots):
    rows = parts[0].shape[1] - STAT_ROWS
    width = picks.shape[0]
    total = HEADS + len(shifts) * slots
    return call(
        functools.partial(merge_kernel, places=tuple(places), shifts=shifts, slots=slots),
        [SCALARS, SCALARS] + [pl.BlockSpec(memory_space=pl.ANY)] * len(parts),
        [
            jax.ShapeDtypeStruct((rows, HEADS * HD), jnp.bfloat16),
            jax.ShapeDtypeStruct((HEADS, rows, HD), jnp.float32),
            jax.ShapeDtypeStruct((HEADS, rows // LANES, LANES), jnp.float32),
        ],
        [IN_VMEM, IN_VMEM, IN_VMEM],
        [
            pltpu.VMEM((total, rows + STAT_ROWS, HD), jnp.bfloat16),
            pltpu.SMEM((PICKS * HEADS,), jnp.int32),
            pltpu.SMEM((width,), jnp.int32),
            pltpu.SemaphoreType.DMA((len(parts),)),
        ],
        flops=6 * HEADS * rows * HD,
        moved=2 * (HEADS * 2 + total) * rows * HD,
    )(here, picks, *parts)


def finish_kernel(here_ref, picks_ref, mixed_ref, sums_ref, *refs, shifts, slots):
    count = len(shifts)
    parts, out_ref, (heads_ref, held, sems) = refs[:count], refs[count + 1], refs[count + 2 :]
    groups = sums_ref.shape[1]
    rows = groups * LANES
    here = here_ref[0]
    for number, shift in enumerate(shifts):
        list_heads(heads_ref, number * slots, picks_ref, here, here - shift, slots)

    def slot_of(head, number):
        found = jnp.int32(-1)
        for slot in range(slots):
            found = jnp.where(heads_ref[number * slots + slot] == head, slot, found)
        return found

    def is_first(head, number):
        first = head >= 0
        for earlier in range(number):
            first = first & (slot_of(head, earlier) < 0)
        return first

    def patch(place):
        columns = head_columns(jnp.maximum(heads_ref[place], 0))
        return pltpu.make_async_copy(held.at[place], out_ref.at[:, columns], sems.at[place])

    places = [(number, number * slots + slot) for number in range(count) for slot in range(slots)]
    for number, place in places:
        head = heads_ref[place]

        @pl.when(is_first(head, number))
        def _():
            found = [slot_of(head, later) for later in range(number, count)]
            spots = [jnp.maximum(spot, 0) for spot in found]
            sums = [sums_ref[head]]
            for part, spot, safe in zip(parts[number:], found, spots):
                added = stats_of(part[safe, rows:, :], groups)
                sums.append(jnp.where(spot >= 0, added, -jnp.inf))
            top = functools.reduce(jnp.maximum, sums)
            shares = [jnp.exp2(part - top) for part in sums]
            whole = functools.reduce(jnp.add, shares)
            for group in range(groups):
                span = pl.ds(group * LANES, LANES)
                before = mixed_ref[head, span, :]
                mixed = before
                for part, spot, safe, share in zip(parts[number:], found, spots, shares[1:]):
                    new = jnp.where(spot >= 0, part[safe, span, :].astype(jnp.float32), 0.0)
                    weight = down_rows((share / whole)[group : group + 1, :])
                    mixed = mixed + (new - before) * weight
                held[place, span, :] = mixed.astype(jnp.bfloat16)
            patch(place).start()

    for number, place in places:

        @pl.when(is_first(heads_ref[place], number))
        def _():
            patch(place).wait()


def finish(here, picks, result, mixed, sums, parts, shifts, slots):
    rows = mixed.shape[1]
    total = len(shifts) * slots
    return pl.pallas_call(
        functools.partial(finish_kernel, shifts=shifts, slots=slots),
        in_specs=[SCALARS, SCALARS] + [IN_VMEM] * (2 + len(parts)) + [IN_HBM],
        out_specs=IN_HBM,
        out_shape=jax.ShapeDtypeStruct(result.shape, result.dtype),
        scratch_shapes=[
            pltpu.SMEM((total + 1,), jnp.int32),
            pltpu.VMEM((total, rows, HD), jnp.bfloat16),
            pltpu.SemaphoreType.DMA((total,)),
        ],
        input_output_aliases={4 + len(parts): 0},
        compiler_params=pltpu.CompilerParams(vmem_limit_bytes=VMEM_BYTES),
        cost_estimate=pl.CostEstimate(
            flops=2 * total * rows * HD, bytes_accessed=8 * total * rows * HD, transcendentals=0
        ),
    )(here, picks, mixed, sums, *parts, result)


def after(value, *earlier):
    return lax.optimization_barrier((value,) + earlier)[0]


def travelling_queries(queries, keys, values, picks):
    width = lax.axis_size("ctx")
    sections = lax.axis_size("pipe")
    slots = max(1, PICKS * HEADS // width)
    here = lax.axis_index("ctx").astype(jnp.int32).reshape(1)
    queries, keys, values = queries[0], keys[0], values[0]
    own_picks = picks[0].transpose(0, 2, 1)

    near_shifts = (2, width - 2)
    middle = width // 2
    far_shifts = [middle - 1, middle + 1, middle, 1, width - 1]
    final_shifts = tuple(far_shifts[2:])

    def up(value, shift):
        return lax.ppermute(value, "ctx", [(at, at + shift) for at in range(width - shift)])

    def down(value, shift):
        return lax.ppermute(value, "ctx", [(at, at - shift) for at in range(shift, width)])

    def up_and_on(value, shift):
        pairs = [
            (at * sections + section, (at + shift) * sections + (section + 1) % sections)
            for at in range(width - shift)
            for section in range(sections)
        ]
        return lax.ppermute(value, ("ctx", "pipe"), pairs)

    near_jobs = [(shift, 0, slots, True) for shift in near_shifts]
    near_sends = pack(here, own_picks, [keys, values], near_jobs, slots)
    near = [up(send, shift) for send, shift in zip(near_sends, near_shifts)]
    before = passed_along(after(own_picks, near_sends[0]), "pipe", 1)
    sends, now = {}, after(here, *near_sends)
    for shifts in (far_shifts[:2], far_shifts[2:]):
        jobs = [(shift, 0, slots, False) for shift in shifts]
        packed = pack(now, own_picks, [queries], jobs, slots, is_anchor=len(shifts) > 2)
        sends |= zip(shifts, packed)
        now = after(now, *packed)
    arrived, returned = {}, {}

    def ask_for(shift, *earlier):
        arrived[shift] = down(after(sends[shift], *earlier), shift)

    def work(token, shift, is_anchor=False):
        return attend(
            token, own_picks, keys, values, [arrived[shift]], ((shift, 0, slots),), slots, is_anchor
        )[0]

    three, five, four, one, seven = far_shifts
    ask_for(three, near_sends[0])
    ask_for(five, near_sends[0])
    own = own_part(after(now, before), queries, keys, values)
    own_back = passed_along(own, "pipe", 1)
    part_three = work(after(here, own, near[0]), three, is_anchor=True)
    returned[three] = up_and_on(part_three, three)
    part_five = work(after(here, part_three), five, is_anchor=True)
    returned[five] = up_and_on(part_five, five)
    for shift in (four, one, seven):
        ask_for(shift, arrived[three], arrived[five], part_five, own_back, *near)
    beside = near_part(after(here, part_five, own_back), own_picks, queries, near, near_shifts, slots)
    part_four = work(after(here, beside), four, is_anchor=True)
    returned[four] = up_and_on(part_four, four)
    part_one = work(after(here, part_four), one, is_anchor=True)
    returned[one] = up_and_on(part_one, one)
    beside_back = passed_along(after(beside, part_one), "pipe", 1)
    part_seven = work(after(here, part_one), seven, is_anchor=True)
    returned[seven] = up_and_on(part_seven, seven)
    now = after(here, part_seven)

    merged_shifts = near_shifts + (three, five)
    places = [HEADS + place * slots for place in (2, 3)]
    parts = [own_back, beside_back, returned[three], returned[five]]
    result, mixed, sums = merge(now, before, parts, [0, HEADS] + places, merged_shifts, slots)
    lasts = [returned[shift] for shift in final_shifts]
    now = tick(now, sums, returned[four])
    now = tick(now, returned[one])
    return finish(now, before, result, mixed, sums, lasts, final_shifts, slots)[None]


def travelling_keys(queries, keys, values, picks):
    ctx_width = lax.axis_size("ctx")
    rank_here = lax.axis_index("ctx")
    slot_count = max(1, PICKS * HEADS // ctx_width)
    block_rows = queries.shape[1]
    score_scale = HD ** (-0.5)
    every_pick = picks[0].reshape(ctx_width, HEADS * PICKS)
    chosen = lax.dynamic_slice_in_dim(every_pick, rank_here, 1, 0)
    pick_order = request_table(chosen, lax.iota(jnp.int32, ctx_width), slot_count)[1]
    asked_table = request_table(every_pick, rank_here.reshape(1), slot_count)[0]
    asked_heads = asked_table[:, 0, :]
    safe_asked = jnp.maximum(asked_heads, 0)
    query_heads = queries[0].reshape(block_rows, HEADS, HD).transpose(1, 0, 2)
    key_heads = keys[0].reshape(block_rows, HEADS, HD).transpose(1, 0, 2)
    value_heads = values[0].reshape(block_rows, HEADS, HD).transpose(1, 0, 2)
    is_live = chosen[0] >= 0
    flat_slot = jnp.where(is_live, chosen[0] * slot_count + pick_order[0], 0)
    remote_mask = jnp.repeat(is_live.reshape(HEADS, PICKS), block_rows, axis=1)
    row_index = lax.iota(jnp.int32, block_rows)
    causal = row_index[:, None] >= row_index[None, :]

    def masked_scores(query_head, key_rows, mask_row):
        scores = lax.dot_general(
            query_head, key_rows, (((1,), (1,)), ((), ())), preferred_element_type=jnp.float32
        )
        allowed = jnp.concatenate(
            [causal, jnp.broadcast_to(mask_row[None, :], (block_rows, PICKS * block_rows))], axis=1
        )
        return jnp.where(allowed, scores * score_scale, -jnp.inf)

    def row_stats(scores):
        row_top = jnp.max(scores, axis=1)
        row_total = jnp.sum(jnp.exp(scores - row_top[:, None]), axis=1)
        return (row_top, row_total)

    def weighted(scores, row_top, row_total, value_rows):
        prob_rows = (jnp.exp(scores - row_top[:, None]) / row_total[:, None]).astype(jnp.bfloat16)
        return jnp.dot(prob_rows, value_rows, preferred_element_type=jnp.float32).astype(
            jnp.bfloat16
        )

    send_both = jnp.concatenate([key_heads, value_heads], axis=2)[safe_asked]
    got_slots = lax.all_to_all(send_both, "ctx", split_axis=0, concat_axis=0, tiled=True)
    last_width = 2 * HD
    flat_slots = got_slots.reshape(ctx_width * slot_count, block_rows, last_width)
    remote_both = flat_slots[flat_slot].reshape(HEADS, PICKS * block_rows, last_width)
    all_keys = jnp.concatenate([key_heads, remote_both[:, :, :HD]], axis=1)
    all_values = jnp.concatenate([value_heads, remote_both[:, :, HD:]], axis=1)

    def per_head(head_items):
        query_head, key_rows, value_rows, mask_row = head_items
        scores = masked_scores(query_head, key_rows, mask_row)
        row_top, row_total = row_stats(scores)
        return weighted(scores, row_top, row_total, value_rows)

    outputs = lax.map(per_head, (query_heads, all_keys, all_values, remote_mask))
    merged = outputs.transpose(1, 0, 2).reshape(1, block_rows, HEADS * HD)
    return passed_along(merged, "pipe", 1)


def per_device(queries, keys, values, picks):
    few_shifts = lax.axis_size("ctx") == 8
    run = travelling_queries if few_shifts else travelling_keys
    return run(queries, keys, values, picks)


def solution(mesh):
    placed = (
        P("pipe", "ctx", None),
        P("pipe", "ctx", None),
        P("pipe", "ctx", None),
        P("pipe", None, None, None),
    )
    return jax.shard_map(
        per_device, mesh=mesh, in_specs=placed, out_specs=P("pipe", "ctx", None), check_vma=False
    )
```

```python
import functools
import math

import jax
import jax.numpy as jnp
from jax import lax
from jax.experimental import pallas as pl
from jax.experimental.pallas import tpu as pltpu
from jax.sharding import PartitionSpec as P

HEADS = 16
HD = 128
PICKS = 2
EXP2_SCALE = HD ** -0.5 * math.log2(math.e)
LANES = 128
STAT_ROWS = 16
VMEM_BYTES = 24 * 1024 * 1024
HIGH_COST = 10**12


def passed_along(value, axis, steps):
    count = lax.axis_size(axis)
    pairs = [(source, (source + steps) % count) for source in range(count)]
    return lax.ppermute(value, axis, pairs)


def request_table(chosen, owners, slot_count):
    pick_count = chosen.shape[1]
    pick_ids = lax.iota(jnp.int32, pick_count)
    is_live = chosen >= 0
    earlier = pick_ids[None, :] < pick_ids[:, None]
    same_owner = (chosen[:, :, None] == chosen[:, None, :]) & earlier[None]
    pick_order = jnp.sum(same_owner.astype(jnp.int32), axis=2)
    head_ids = pick_ids // PICKS
    slot_ranks = lax.iota(jnp.int32, slot_count)
    matches = (
        is_live[:, None, None, :]
        & (chosen[:, None, None, :] == owners[None, :, None, None])
        & (pick_order[:, None, None, :] == slot_ranks[None, None, :, None])
    )
    was_found = jnp.any(matches, axis=3)
    head_table = jnp.sum(jnp.where(matches, head_ids[None, None, None, :], 0), axis=3)
    return (jnp.where(was_found, head_table, -1), pick_order)


def call(
    kernel, name_space, outputs, out_specs, scratch=(), flops=0, moved=0, exps=0
):
    return pl.pallas_call(
        kernel,
        in_specs=name_space,
        out_specs=out_specs,
        out_shape=outputs,
        scratch_shapes=list(scratch),
        compiler_params=pltpu.CompilerParams(vmem_limit_bytes=VMEM_BYTES),
        cost_estimate=pl.CostEstimate(flops=flops, bytes_accessed=moved, transcendentals=exps),
    )


SCALARS = pl.BlockSpec(memory_space=pltpu.SMEM)
IN_HBM = pl.BlockSpec(memory_space=pltpu.HBM)
IN_VMEM = pl.BlockSpec(memory_space=pltpu.VMEM)


def tick_kernel(here_ref, out_ref):
    out_ref[0] = here_ref[0]


def tick(here, *earlier):
    return call(
        tick_kernel,
        [SCALARS],
        jax.ShapeDtypeStruct((1,), jnp.int32),
        SCALARS,
        flops=0,
    )(after(here, *earlier))


def list_heads(heads_ref, start, picks_ref, block, owner, slots):
    width = picks_ref.shape[0]
    spare = heads_ref.shape[0] - 1
    for slot in range(slots):
        heads_ref[start + slot] = -1
    valid = (block >= 0) & (block < width) & (owner >= 0) & (owner < width)
    row = jnp.clip(block, 0, width - 1)
    wanted = jnp.where(valid, owner, -2)
    found = jnp.int32(0)
    for pick in range(PICKS):
        for head in range(HEADS):
            hit = picks_ref[row, pick, head] == wanted
            heads_ref[jnp.where(hit, start + found, spare)] = head
            found = found + hit.astype(jnp.int32)


def pack_kernel(here_ref, picks_ref, *refs, jobs, slots):
    is_near = jobs[0][3]
    sources = refs[: 1 + is_near]
    outputs = refs[1 + is_near : 1 + is_near + len(jobs)]
    heads_ref, sems = refs[-2], refs[-1]
    here = here_ref[0]
    listed = {}
    for shift, first, count, is_near in jobs:
        key = (shift, is_near)
        if key not in listed:
            listed[key] = len(listed) * slots
            block, owner = (here + shift, here) if is_near else (here, here - shift)
            list_heads(heads_ref, listed[key], picks_ref, block, owner, slots)
    copies = []
    for (shift, first, count, is_near), output in zip(jobs, outputs):
        for slot in range(count):
            head = jnp.maximum(heads_ref[listed[shift, is_near] + first + slot], 0)
            columns = pl.ds(pl.multiple_of(head * HD, HD), HD)
            for place, source in enumerate(sources):
                target = output.at[2 * slot + place if is_near else slot]
                copy = pltpu.make_async_copy(
                    source.at[:, columns], target, sems.at[len(copies)]
                )
                copy.start()
                copies.append(copy)
    for copy in copies:
        copy.wait()


def pack(here, picks, sources, jobs, slots):
    rows = sources[0].shape[0]
    sizes = [len(sources) * count for _, _, count, _ in jobs]
    return call(
        functools.partial(pack_kernel, jobs=jobs, slots=slots),
        [SCALARS, SCALARS] + [IN_VMEM] * len(sources),
        [jax.ShapeDtypeStruct((size, rows, HD), jnp.bfloat16) for size in sizes],
        [IN_VMEM] * len(sizes),
        [pltpu.SMEM((len(jobs) * slots + 1,), jnp.int32), pltpu.SemaphoreType.DMA((sum(sizes),))],
        moved=4 * rows * HD * sum(sizes),
    )(here, picks, *sources)


def diagonal():
    shape = (LANES, LANES)
    return lax.broadcasted_iota(jnp.int32, shape, 0) == lax.broadcasted_iota(jnp.int32, shape, 1)


def raw_scores(query_rows, key_rows):
    return lax.dot_general(
        query_rows, key_rows, (((1,), (1,)), ((), ())), preferred_element_type=jnp.float32
    )


def with_ones(value_rows):
    return jnp.concatenate([value_rows, jnp.ones_like(value_rows)], axis=1)


def soft_part(scores, value_rows):
    top = jnp.max(scores, axis=1, keepdims=True)
    weights = jnp.exp2((scores - top) * EXP2_SCALE).astype(jnp.bfloat16)
    total = jnp.dot(weights, value_rows, preferred_element_type=jnp.float32)
    sums = total[:, HD:]
    return total[:, :HD] * pl.reciprocal(sums), top * EXP2_SCALE, sums


def across_lanes(column):
    eye = diagonal()
    spread = jnp.broadcast_to(column, (column.shape[0], LANES))
    return [
        jnp.sum(jnp.where(eye, spread[at : at + LANES], 0.0), axis=0, keepdims=True)
        for at in range(0, column.shape[0], LANES)
    ]


def down_rows(line):
    spread = jnp.broadcast_to(line, (LANES, LANES))
    return jnp.sum(jnp.where(diagonal(), spread, 0.0), axis=1, keepdims=True)


def three_parts(stats):
    first = stats.astype(jnp.bfloat16).astype(jnp.float32)
    second = (stats - first).astype(jnp.bfloat16).astype(jnp.float32)
    third = stats - first - second
    parts = jnp.concatenate([first, second, third], axis=0)
    pad = jnp.zeros((STAT_ROWS - parts.shape[0], LANES), jnp.float32)
    return jnp.concatenate([parts, pad], axis=0).astype(jnp.bfloat16)


def stats_of(block, groups):
    stats = block.astype(jnp.float32)
    return stats[:groups] + stats[groups : 2 * groups] + stats[2 * groups : 3 * groups]


def log_sums(tops, sums):
    top_lines = [line for top in tops for line in across_lanes(top)]
    sum_lines = [line for part in sums for line in across_lanes(part)]
    return jnp.concatenate(top_lines, axis=0) + jnp.log2(jnp.concatenate(sum_lines, axis=0))


def attend_rows(query_rows, key_rows, value_rows, tile):
    found = [
        soft_part(raw_scores(query_rows[at : at + tile], key_rows), value_rows)
        for at in range(0, query_rows.shape[0], tile)
    ]
    outputs, tops, sums = zip(*found)
    return jnp.concatenate(outputs, axis=0), log_sums(tops, sums)


def head_columns(head):
    return pl.ds(pl.multiple_of(head * HD, HD), HD)


def attend_kernel(here_ref, picks_ref, key_ref, value_ref, *refs, group, slots):
    heads_ref = refs[-1]
    here = here_ref[0]
    for number, (shift, first, count) in enumerate(group):
        query_ref, out_ref = refs[number], refs[len(group) + number]
        rows = query_ref.shape[1]
        list_heads(heads_ref, 0, picks_ref, here + shift, here, slots)
        for slot in range(count):
            columns = head_columns(jnp.maximum(heads_ref[first + slot], 0))
            outputs, lines = attend_rows(
                query_ref[slot], key_ref[:, columns], with_ones(value_ref[:, columns]), rows
            )
            out_ref[slot, :rows, :] = outputs.astype(jnp.bfloat16)
            out_ref[slot, rows:, :] = three_parts(lines)


def attend(here, picks, keys, values, arrived, group, slots, is_anchor):
    rows = keys.shape[0]
    total = sum(count for _, _, count in group)
    return call(
        functools.partial(attend_kernel, group=group, slots=slots),
        [SCALARS, SCALARS, IN_VMEM, IN_VMEM] + [IN_VMEM] * len(group),
        [
            jax.ShapeDtypeStruct((count, rows + STAT_ROWS, HD), jnp.bfloat16)
            for _, _, count in group
        ],
        [IN_VMEM] * len(group),
        [pltpu.SMEM((slots + 1,), jnp.int32)],
        flops=HIGH_COST if is_anchor else 4 * total * rows * rows * HD,
        moved=8 * total * rows * HD,
        exps=total * rows * rows,
    )(here, picks, keys, values, *arrived)


def own_kernel(here_ref, query_ref, key_ref, value_ref, out_ref):
    rows = query_ref.shape[0]
    tile = min(rows, 256)

    def one_head(head, carry):
        columns = head_columns(head)
        value_rows = with_ones(value_ref[:, columns])
        tops, all_sums = [], []
        for at in range(0, rows, tile):
            reach = at + tile
            scores = raw_scores(query_ref[at:reach, columns], key_ref[:reach, columns])
            row_ids = lax.broadcasted_iota(jnp.int32, scores.shape, 0) + at
            seen = row_ids >= lax.broadcasted_iota(jnp.int32, scores.shape, 1)
            outputs, top, sums = soft_part(jnp.where(seen, scores, -jnp.inf), value_rows[:reach])
            out_ref[head, at:reach, :] = outputs.astype(jnp.bfloat16)
            tops.append(top)
            all_sums.append(sums)
        out_ref[head, rows:, :] = three_parts(log_sums(tops, all_sums))
        return carry

    lax.fori_loop(0, HEADS, one_head, 0, unroll=4)


def own_part(here, queries, keys, values):
    rows = queries.shape[0]
    return call(
        own_kernel,
        [SCALARS, IN_VMEM, IN_VMEM, IN_VMEM],
        jax.ShapeDtypeStruct((HEADS, rows + STAT_ROWS, HD), jnp.bfloat16),
        IN_VMEM,
        flops=4 * HEADS * rows * rows * HD,
        moved=8 * HEADS * rows * HD,
        exps=HEADS * rows * rows,
    )(here, queries, keys, values)


def near_kernel(here_ref, picks_ref, query_ref, *refs, shifts, slots):
    near_refs, out_ref, heads_ref = refs[: len(shifts)], refs[-2], refs[-1]
    rows = query_ref.shape[0]
    here = here_ref[0]
    for place, (shift, near_ref) in enumerate(zip(shifts, near_refs)):
        list_heads(heads_ref, 0, picks_ref, here, here - shift, slots)
        for slot in range(slots):
            columns = head_columns(jnp.maximum(heads_ref[slot], 0))
            outputs, lines = attend_rows(
                query_ref[:, columns], near_ref[2 * slot], with_ones(near_ref[2 * slot + 1]), rows
            )
            out_ref[place * slots + slot, :rows, :] = outputs.astype(jnp.bfloat16)
            out_ref[place * slots + slot, rows:, :] = three_parts(lines)


def near_part(here, picks, queries, near, shifts, slots):
    rows = queries.shape[0]
    total = len(shifts) * slots
    return call(
        functools.partial(near_kernel, shifts=shifts, slots=slots),
        [SCALARS, SCALARS, IN_VMEM] + [IN_VMEM] * len(shifts),
        jax.ShapeDtypeStruct((total, rows + STAT_ROWS, HD), jnp.bfloat16),
        IN_VMEM,
        [pltpu.SMEM((slots + 1,), jnp.int32)],
        flops=4 * total * rows * rows * HD,
        moved=12 * total * rows * HD,
        exps=total * rows * rows,
    )(here, picks, queries, *near)


def find_spots(spots_ref, found_ref, picks_ref, here, shifts, slots):
    for owner in range(picks_ref.shape[0]):
        found_ref[owner] = 0

    for pick in range(PICKS):
        for head in range(HEADS):
            owner = picks_ref[here, pick, head]
            safe = jnp.maximum(owner, 0)
            order = found_ref[safe]
            found_ref[safe] = order + (owner >= 0).astype(jnp.int32)
            spot = jnp.int32(-1)
            for place, shift in enumerate(shifts):
                spot = jnp.where(here - safe == shift, place * slots + order, spot)
            spots_ref[head * PICKS + pick] = jnp.where(owner >= 0, spot, -1)


def merge_kernel(here_ref, picks_ref, *refs, places, shifts, slots):
    count = len(places)
    parts = refs[:count]
    result_ref, out_ref, sums_ref, held, spots_ref, found_ref, sems = refs[count:]
    groups = sums_ref.shape[1]
    rows = groups * LANES
    copies = [
        pltpu.make_async_copy(part, held.at[pl.ds(place, part.shape[0])], sems.at[number])
        for number, (part, place) in enumerate(zip(parts, places))
    ]
    for copy in copies:
        copy.start()
    find_spots(spots_ref, found_ref, picks_ref, here_ref[0], shifts, slots)
    for copy in copies:
        copy.wait()

    def one_head(head, carry):
        found = [spots_ref[head * PICKS + pick] for pick in range(PICKS)]
        spots = [head] + [jnp.where(spot >= 0, HEADS + spot, head) for spot in found]
        sums = [stats_of(held[spot, rows:, :], groups) for spot in spots]
        for pick, spot in enumerate(found):
            sums[1 + pick] = jnp.where(spot >= 0, sums[1 + pick], -jnp.inf)
        top = functools.reduce(jnp.maximum, sums)
        shares = [jnp.exp2(part - top) for part in sums]
        whole = functools.reduce(jnp.add, shares)
        sums_ref[head] = top + jnp.log2(whole)
        for group in range(groups):
            span = pl.ds(group * LANES, LANES)
            own = held[head, span, :].astype(jnp.float32)
            mixed = own
            for spot, share in zip(spots[1:], shares[1:]):
                weight = down_rows((share / whole)[group : group + 1, :])
                mixed = mixed + (held[spot, span, :].astype(jnp.float32) - own) * weight
            out_ref[head, span, :] = mixed
            result_ref[span, head_columns(head)] = mixed.astype(jnp.bfloat16)
        return carry

    lax.fori_loop(0, HEADS, one_head, 0, unroll=2)


def merge(here, picks, parts, places, shifts, slots):
    rows = parts[0].shape[1] - STAT_ROWS
    width = picks.shape[0]
    total = HEADS + len(shifts) * slots
    return call(
        functools.partial(merge_kernel, places=tuple(places), shifts=shifts, slots=slots),
        [SCALARS, SCALARS] + [pl.BlockSpec(memory_space=pl.ANY)] * len(parts),
        [
            jax.ShapeDtypeStruct((rows, HEADS * HD), jnp.bfloat16),
            jax.ShapeDtypeStruct((HEADS, rows, HD), jnp.float32),
            jax.ShapeDtypeStruct((HEADS, rows // LANES, LANES), jnp.float32),
        ],
        [IN_VMEM, IN_VMEM, IN_VMEM],
        [
            pltpu.VMEM((total, rows + STAT_ROWS, HD), jnp.bfloat16),
            pltpu.SMEM((PICKS * HEADS,), jnp.int32),
            pltpu.SMEM((width,), jnp.int32),
            pltpu.SemaphoreType.DMA((len(parts),)),
        ],
        flops=6 * HEADS * rows * HD,
        moved=2 * (HEADS * 2 + total) * rows * HD,
    )(here, picks, *parts)


def finish_kernel(here_ref, picks_ref, mixed_ref, sums_ref, *refs, shifts, slots):
    count = len(shifts)
    parts, out_ref, (heads_ref, held, sems) = refs[:count], refs[count + 1], refs[count + 2 :]
    groups = sums_ref.shape[1]
    rows = groups * LANES
    here = here_ref[0]
    for number, shift in enumerate(shifts):
        list_heads(heads_ref, number * slots, picks_ref, here, here - shift, slots)

    def slot_of(head, number):
        found = jnp.int32(-1)
        for slot in range(slots):
            found = jnp.where(heads_ref[number * slots + slot] == head, slot, found)
        return found

    def is_first(head, number):
        first = head >= 0
        for earlier in range(number):
            first = first & (slot_of(head, earlier) < 0)
        return first

    def patch(place):
        columns = head_columns(jnp.maximum(heads_ref[place], 0))
        return pltpu.make_async_copy(held.at[place], out_ref.at[:, columns], sems.at[place])

    places = [(number, number * slots + slot) for number in range(count) for slot in range(slots)]
    for number, place in places:
        head = heads_ref[place]

        @pl.when(is_first(head, number))
        def _():
            found = [slot_of(head, later) for later in range(number, count)]
            spots = [jnp.maximum(spot, 0) for spot in found]
            sums = [sums_ref[head]]
            for part, spot, safe in zip(parts[number:], found, spots):
                added = stats_of(part[safe, rows:, :], groups)
                sums.append(jnp.where(spot >= 0, added, -jnp.inf))
            top = functools.reduce(jnp.maximum, sums)
            shares = [jnp.exp2(part - top) for part in sums]
            whole = functools.reduce(jnp.add, shares)
            for group in range(groups):
                span = pl.ds(group * LANES, LANES)
                before = mixed_ref[head, span, :]
                mixed = before
                for part, spot, safe, share in zip(parts[number:], found, spots, shares[1:]):
                    new = jnp.where(spot >= 0, part[safe, span, :].astype(jnp.float32), 0.0)
                    weight = down_rows((share / whole)[group : group + 1, :])
                    mixed = mixed + (new - before) * weight
                held[place, span, :] = mixed.astype(jnp.bfloat16)
            patch(place).start()

    for number, place in places:

        @pl.when(is_first(heads_ref[place], number))
        def _():
            patch(place).wait()


def finish(here, picks, result, mixed, sums, parts, shifts, slots):
    rows = mixed.shape[1]
    total = len(shifts) * slots
    return pl.pallas_call(
        functools.partial(finish_kernel, shifts=shifts, slots=slots),
        in_specs=[SCALARS, SCALARS] + [IN_VMEM] * (2 + len(parts)) + [IN_HBM],
        out_specs=IN_HBM,
        out_shape=jax.ShapeDtypeStruct(result.shape, result.dtype),
        scratch_shapes=[
            pltpu.SMEM((total + 1,), jnp.int32),
            pltpu.VMEM((total, rows, HD), jnp.bfloat16),
            pltpu.SemaphoreType.DMA((total,)),
        ],
        input_output_aliases={4 + len(parts): 0},
        compiler_params=pltpu.CompilerParams(vmem_limit_bytes=VMEM_BYTES),
        cost_estimate=pl.CostEstimate(
            flops=2 * total * rows * HD, bytes_accessed=8 * total * rows * HD, transcendentals=0
        ),
    )(here, picks, mixed, sums, *parts, result)


def after(value, *earlier):
    return lax.optimization_barrier((value,) + earlier)[0]


def travelling_queries(queries, keys, values, picks):
    width = lax.axis_size("ctx")
    sections = lax.axis_size("pipe")
    slots = max(1, PICKS * HEADS // width)
    here = lax.axis_index("ctx").astype(jnp.int32).reshape(1)
    queries, keys, values = queries[0], keys[0], values[0]
    own_picks = picks[0].transpose(0, 2, 1)

    near_shifts = (2, width - 2)
    middle = width // 2
    far_shifts = [middle, middle - 1, middle + 1, 1, width - 1]
    final_shifts = tuple(far_shifts[1:])

    def up(value, shift):
        return lax.ppermute(value, "ctx", [(at, at + shift) for at in range(width - shift)])

    def down(value, shift):
        return lax.ppermute(value, "ctx", [(at, at - shift) for at in range(shift, width)])

    def up_and_on(value, shift):
        pairs = [
            (at * sections + section, (at + shift) * sections + (section + 1) % sections)
            for at in range(width - shift)
            for section in range(sections)
        ]
        return lax.ppermute(value, ("ctx", "pipe"), pairs)

    near_jobs = [(shift, 0, slots, True) for shift in near_shifts]
    near_sends = pack(here, own_picks, [keys, values], near_jobs, slots)
    near = [up(near_sends[0], near_shifts[0])]
    before = passed_along(own_picks, "pipe", 1)
    sends, now = {}, after(here, *near_sends)
    for shifts in (far_shifts[:1], far_shifts[1:]):
        jobs = [(shift, 0, slots, False) for shift in shifts]
        packed = pack(now, own_picks, [queries], jobs, slots)
        sends |= zip(shifts, packed)
        now = after(now, *packed)
    arrived, returned = {}, {}

    def ask_for(shift, *earlier):
        arrived[shift] = down(after(sends[shift], *earlier), shift)

    def work(token, shift, is_anchor=False):
        return attend(
            token, own_picks, keys, values, [arrived[shift]], ((shift, 0, slots),), slots, is_anchor
        )[0]

    four, three, five, one, seven = far_shifts
    ask_for(four, near_sends[0])
    own = own_part(after(now, before), queries, keys, values)
    own_back = passed_along(own, "pipe", 1)
    near.append(up(after(near_sends[1], now), near_shifts[1]))
    ask_for(three, arrived[four], near[0], own)
    ask_for(five, arrived[four], near[0], own)
    part_four = work(after(here, own, near[0]), four, is_anchor=True)
    returned[four] = up_and_on(part_four, four)
    beside = near_part(after(here, part_four, own_back), own_picks, queries, near, near_shifts, slots)
    ask_for(one, own_back, part_four, *near)
    ask_for(seven, own_back, part_four, *near)
    part_three = work(after(here, beside), three, is_anchor=True)
    returned[three] = up_and_on(part_three, three)
    part_five = work(after(here, part_three), five)
    returned[five] = up_and_on(part_five, five)
    beside_back = passed_along(beside, "pipe", 1)
    part_one = work(after(here, part_five, beside_back), one)
    returned[one] = up_and_on(part_one, one)
    part_seven = work(after(here, part_one), seven)
    returned[seven] = up_and_on(part_seven, seven)
    now = after(here, part_seven)

    merged_shifts = near_shifts + (four,)
    places = [HEADS + 2 * slots]
    parts = [own_back, beside_back, returned[four]]
    result, mixed, sums = merge(now, before, parts, [0, HEADS] + places, merged_shifts, slots)
    lasts = [returned[shift] for shift in final_shifts]
    return finish(now, before, result, mixed, sums, lasts, final_shifts, slots)[None]


def travelling_keys(queries, keys, values, picks):
    ctx_width = lax.axis_size("ctx")
    rank_here = lax.axis_index("ctx")
    slot_count = max(1, PICKS * HEADS // ctx_width)
    block_rows = queries.shape[1]
    score_scale = HD ** (-0.5)
    every_pick = picks[0].reshape(ctx_width, HEADS * PICKS)
    chosen = lax.dynamic_slice_in_dim(every_pick, rank_here, 1, 0)
    pick_order = request_table(chosen, lax.iota(jnp.int32, ctx_width), slot_count)[1]
    asked_table = request_table(every_pick, rank_here.reshape(1), slot_count)[0]
    asked_heads = asked_table[:, 0, :]
    safe_asked = jnp.maximum(asked_heads, 0)
    query_heads = queries[0].reshape(block_rows, HEADS, HD).transpose(1, 0, 2)
    key_heads = keys[0].reshape(block_rows, HEADS, HD).transpose(1, 0, 2)
    value_heads = values[0].reshape(block_rows, HEADS, HD).transpose(1, 0, 2)
    is_live = chosen[0] >= 0
    flat_slot = jnp.where(is_live, chosen[0] * slot_count + pick_order[0], 0)
    remote_mask = jnp.repeat(is_live.reshape(HEADS, PICKS), block_rows, axis=1)
    row_index = lax.iota(jnp.int32, block_rows)
    causal = row_index[:, None] >= row_index[None, :]

    def masked_scores(query_head, key_rows, mask_row):
        scores = lax.dot_general(
            query_head, key_rows, (((1,), (1,)), ((), ())), preferred_element_type=jnp.float32
        )
        allowed = jnp.concatenate(
            [causal, jnp.broadcast_to(mask_row[None, :], (block_rows, PICKS * block_rows))], axis=1
        )
        return jnp.where(allowed, scores * score_scale, -jnp.inf)

    def row_stats(scores):
        row_top = jnp.max(scores, axis=1)
        row_total = jnp.sum(jnp.exp(scores - row_top[:, None]), axis=1)
        return (row_top, row_total)

    def weighted(scores, row_top, row_total, value_rows):
        prob_rows = (jnp.exp(scores - row_top[:, None]) / row_total[:, None]).astype(jnp.bfloat16)
        return jnp.dot(prob_rows, value_rows, preferred_element_type=jnp.float32).astype(
            jnp.bfloat16
        )

    send_both = jnp.concatenate([key_heads, value_heads], axis=2)[safe_asked]
    got_slots = lax.all_to_all(send_both, "ctx", split_axis=0, concat_axis=0, tiled=True)
    last_width = 2 * HD
    flat_slots = got_slots.reshape(ctx_width * slot_count, block_rows, last_width)
    remote_both = flat_slots[flat_slot].reshape(HEADS, PICKS * block_rows, last_width)
    all_keys = jnp.concatenate([key_heads, remote_both[:, :, :HD]], axis=1)
    all_values = jnp.concatenate([value_heads, remote_both[:, :, HD:]], axis=1)

    def per_head(head_items):
        query_head, key_rows, value_rows, mask_row = head_items
        scores = masked_scores(query_head, key_rows, mask_row)
        row_top, row_total = row_stats(scores)
        return weighted(scores, row_top, row_total, value_rows)

    outputs = lax.map(per_head, (query_heads, all_keys, all_values, remote_mask))
    merged = outputs.transpose(1, 0, 2).reshape(1, block_rows, HEADS * HD)
    return passed_along(merged, "pipe", 1)


def per_device(queries, keys, values, picks):
    few_shifts = lax.axis_size("ctx") == 8
    run = travelling_queries if few_shifts else travelling_keys
    return run(queries, keys, values, picks)


def solution(mesh):
    placed = (
        P("pipe", "ctx", None),
        P("pipe", "ctx", None),
        P("pipe", "ctx", None),
        P("pipe", None, None, None),
    )
    return jax.shard_map(
        per_device, mesh=mesh, in_specs=placed, out_specs=P("pipe", "ctx", None), check_vma=False
    )
```

```python
import functools
import math

import jax
import jax.numpy as jnp
from jax import lax
from jax.experimental import pallas as pl
from jax.experimental.pallas import tpu as pltpu
from jax.sharding import PartitionSpec as P

HEADS = 16
HD = 128
PICKS = 2
EXP2_SCALE = HD ** -0.5 * math.log2(math.e)
LANES = 128
STAT_ROWS = 16
VMEM_BYTES = 24 * 1024 * 1024
HIGH_COST = 10**12


def passed_along(value, axis, steps):
    count = lax.axis_size(axis)
    pairs = [(source, (source + steps) % count) for source in range(count)]
    return lax.ppermute(value, axis, pairs)


def request_table(chosen, owners, slot_count):
    pick_count = chosen.shape[1]
    pick_ids = lax.iota(jnp.int32, pick_count)
    is_live = chosen >= 0
    earlier = pick_ids[None, :] < pick_ids[:, None]
    same_owner = (chosen[:, :, None] == chosen[:, None, :]) & earlier[None]
    pick_order = jnp.sum(same_owner.astype(jnp.int32), axis=2)
    head_ids = pick_ids // PICKS
    slot_ranks = lax.iota(jnp.int32, slot_count)
    matches = (
        is_live[:, None, None, :]
        & (chosen[:, None, None, :] == owners[None, :, None, None])
        & (pick_order[:, None, None, :] == slot_ranks[None, None, :, None])
    )
    was_found = jnp.any(matches, axis=3)
    head_table = jnp.sum(jnp.where(matches, head_ids[None, None, None, :], 0), axis=3)
    return (jnp.where(was_found, head_table, -1), pick_order)


def call(
    kernel, name_space, outputs, out_specs, scratch=(), flops=0, moved=0, exps=0
):
    return pl.pallas_call(
        kernel,
        in_specs=name_space,
        out_specs=out_specs,
        out_shape=outputs,
        scratch_shapes=list(scratch),
        compiler_params=pltpu.CompilerParams(vmem_limit_bytes=VMEM_BYTES),
        cost_estimate=pl.CostEstimate(flops=flops, bytes_accessed=moved, transcendentals=exps),
    )


SCALARS = pl.BlockSpec(memory_space=pltpu.SMEM)
IN_HBM = pl.BlockSpec(memory_space=pltpu.HBM)
IN_VMEM = pl.BlockSpec(memory_space=pltpu.VMEM)


def tick_kernel(here_ref, out_ref):
    out_ref[0] = here_ref[0]


def tick(here, *earlier):
    return call(
        tick_kernel,
        [SCALARS],
        jax.ShapeDtypeStruct((1,), jnp.int32),
        SCALARS,
        flops=0,
    )(after(here, *earlier))


def list_heads(heads_ref, start, picks_ref, block, owner, slots):
    width = picks_ref.shape[0]
    spare = heads_ref.shape[0] - 1
    for slot in range(slots):
        heads_ref[start + slot] = -1
    valid = (block >= 0) & (block < width) & (owner >= 0) & (owner < width)
    row = jnp.clip(block, 0, width - 1)
    wanted = jnp.where(valid, owner, -2)
    found = jnp.int32(0)
    for pick in range(PICKS):
        for head in range(HEADS):
            hit = picks_ref[row, pick, head] == wanted
            heads_ref[jnp.where(hit, start + found, spare)] = head
            found = found + hit.astype(jnp.int32)


def pack_kernel(here_ref, picks_ref, *refs, jobs, slots):
    is_near = jobs[0][3]
    sources = refs[: 1 + is_near]
    outputs = refs[1 + is_near : 1 + is_near + len(jobs)]
    heads_ref, sems = refs[-2], refs[-1]
    here = here_ref[0]
    listed = {}
    for shift, first, count, is_near in jobs:
        key = (shift, is_near)
        if key not in listed:
            listed[key] = len(listed) * slots
            block, owner = (here + shift, here) if is_near else (here, here - shift)
            list_heads(heads_ref, listed[key], picks_ref, block, owner, slots)
    copies = []
    for (shift, first, count, is_near), output in zip(jobs, outputs):
        for slot in range(count):
            head = jnp.maximum(heads_ref[listed[shift, is_near] + first + slot], 0)
            columns = pl.ds(pl.multiple_of(head * HD, HD), HD)
            for place, source in enumerate(sources):
                target = output.at[2 * slot + place if is_near else slot]
                copy = pltpu.make_async_copy(
                    source.at[:, columns], target, sems.at[len(copies)]
                )
                copy.start()
                copies.append(copy)
    for copy in copies:
        copy.wait()


def pack(here, picks, sources, jobs, slots):
    rows = sources[0].shape[0]
    sizes = [len(sources) * count for _, _, count, _ in jobs]
    return call(
        functools.partial(pack_kernel, jobs=jobs, slots=slots),
        [SCALARS, SCALARS] + [IN_VMEM] * len(sources),
        [jax.ShapeDtypeStruct((size, rows, HD), jnp.bfloat16) for size in sizes],
        [IN_VMEM] * len(sizes),
        [pltpu.SMEM((len(jobs) * slots + 1,), jnp.int32), pltpu.SemaphoreType.DMA((sum(sizes),))],
        moved=4 * rows * HD * sum(sizes),
    )(here, picks, *sources)


def diagonal():
    shape = (LANES, LANES)
    return lax.broadcasted_iota(jnp.int32, shape, 0) == lax.broadcasted_iota(jnp.int32, shape, 1)


def raw_scores(query_rows, key_rows):
    return lax.dot_general(
        query_rows, key_rows, (((1,), (1,)), ((), ())), preferred_element_type=jnp.float32
    )


def with_ones(value_rows):
    return jnp.concatenate([value_rows, jnp.ones_like(value_rows)], axis=1)


def soft_part(scores, value_rows):
    top = jnp.max(scores, axis=1, keepdims=True)
    weights = jnp.exp2((scores - top) * EXP2_SCALE).astype(jnp.bfloat16)
    total = jnp.dot(weights, value_rows, preferred_element_type=jnp.float32)
    sums = total[:, HD:]
    return total[:, :HD] * pl.reciprocal(sums), top * EXP2_SCALE, sums


def across_lanes(column):
    eye = diagonal()
    spread = jnp.broadcast_to(column, (column.shape[0], LANES))
    return [
        jnp.sum(jnp.where(eye, spread[at : at + LANES], 0.0), axis=0, keepdims=True)
        for at in range(0, column.shape[0], LANES)
    ]


def down_rows(line):
    spread = jnp.broadcast_to(line, (LANES, LANES))
    return jnp.sum(jnp.where(diagonal(), spread, 0.0), axis=1, keepdims=True)


def three_parts(stats):
    first = stats.astype(jnp.bfloat16).astype(jnp.float32)
    second = (stats - first).astype(jnp.bfloat16).astype(jnp.float32)
    third = stats - first - second
    parts = jnp.concatenate([first, second, third], axis=0)
    pad = jnp.zeros((STAT_ROWS - parts.shape[0], LANES), jnp.float32)
    return jnp.concatenate([parts, pad], axis=0).astype(jnp.bfloat16)


def stats_of(block, groups):
    stats = block.astype(jnp.float32)
    return stats[:groups] + stats[groups : 2 * groups] + stats[2 * groups : 3 * groups]


def log_sums(tops, sums):
    top_lines = [line for top in tops for line in across_lanes(top)]
    sum_lines = [line for part in sums for line in across_lanes(part)]
    return jnp.concatenate(top_lines, axis=0) + jnp.log2(jnp.concatenate(sum_lines, axis=0))


def attend_rows(query_rows, key_rows, value_rows, tile):
    found = [
        soft_part(raw_scores(query_rows[at : at + tile], key_rows), value_rows)
        for at in range(0, query_rows.shape[0], tile)
    ]
    outputs, tops, sums = zip(*found)
    return jnp.concatenate(outputs, axis=0), log_sums(tops, sums)


def head_columns(head):
    return pl.ds(pl.multiple_of(head * HD, HD), HD)


def attend_kernel(here_ref, picks_ref, key_ref, value_ref, *refs, group, slots):
    heads_ref = refs[-1]
    here = here_ref[0]
    for number, (shift, first, count) in enumerate(group):
        query_ref, out_ref = refs[number], refs[len(group) + number]
        rows = query_ref.shape[1]
        list_heads(heads_ref, 0, picks_ref, here + shift, here, slots)
        for slot in range(count):
            columns = head_columns(jnp.maximum(heads_ref[first + slot], 0))
            outputs, lines = attend_rows(
                query_ref[slot], key_ref[:, columns], with_ones(value_ref[:, columns]), rows
            )
            out_ref[slot, :rows, :] = outputs.astype(jnp.bfloat16)
            out_ref[slot, rows:, :] = three_parts(lines)


def attend(here, picks, keys, values, arrived, group, slots, is_anchor):
    rows = keys.shape[0]
    total = sum(count for _, _, count in group)
    return call(
        functools.partial(attend_kernel, group=group, slots=slots),
        [SCALARS, SCALARS, IN_VMEM, IN_VMEM] + [IN_VMEM] * len(group),
        [
            jax.ShapeDtypeStruct((count, rows + STAT_ROWS, HD), jnp.bfloat16)
            for _, _, count in group
        ],
        [IN_VMEM] * len(group),
        [pltpu.SMEM((slots + 1,), jnp.int32)],
        flops=HIGH_COST if is_anchor else 4 * total * rows * rows * HD,
        moved=8 * total * rows * HD,
        exps=total * rows * rows,
    )(here, picks, keys, values, *arrived)


def own_kernel(here_ref, query_ref, key_ref, value_ref, out_ref):
    rows = query_ref.shape[0]
    tile = min(rows, 256)

    def one_head(head, carry):
        columns = head_columns(head)
        value_rows = with_ones(value_ref[:, columns])
        tops, all_sums = [], []
        for at in range(0, rows, tile):
            reach = at + tile
            scores = raw_scores(query_ref[at:reach, columns], key_ref[:reach, columns])
            row_ids = lax.broadcasted_iota(jnp.int32, scores.shape, 0) + at
            seen = row_ids >= lax.broadcasted_iota(jnp.int32, scores.shape, 1)
            outputs, top, sums = soft_part(jnp.where(seen, scores, -jnp.inf), value_rows[:reach])
            out_ref[head, at:reach, :] = outputs.astype(jnp.bfloat16)
            tops.append(top)
            all_sums.append(sums)
        out_ref[head, rows:, :] = three_parts(log_sums(tops, all_sums))
        return carry

    lax.fori_loop(0, HEADS, one_head, 0, unroll=4)


def own_part(here, queries, keys, values):
    rows = queries.shape[0]
    return call(
        own_kernel,
        [SCALARS, IN_VMEM, IN_VMEM, IN_VMEM],
        jax.ShapeDtypeStruct((HEADS, rows + STAT_ROWS, HD), jnp.bfloat16),
        IN_VMEM,
        flops=4 * HEADS * rows * rows * HD,
        moved=8 * HEADS * rows * HD,
        exps=HEADS * rows * rows,
    )(here, queries, keys, values)


def near_kernel(here_ref, picks_ref, query_ref, *refs, shifts, slots):
    near_refs, out_ref, heads_ref = refs[: len(shifts)], refs[-2], refs[-1]
    rows = query_ref.shape[0]
    here = here_ref[0]
    for place, (shift, near_ref) in enumerate(zip(shifts, near_refs)):
        list_heads(heads_ref, 0, picks_ref, here, here - shift, slots)
        for slot in range(slots):
            columns = head_columns(jnp.maximum(heads_ref[slot], 0))
            outputs, lines = attend_rows(
                query_ref[:, columns], near_ref[2 * slot], with_ones(near_ref[2 * slot + 1]), rows
            )
            out_ref[place * slots + slot, :rows, :] = outputs.astype(jnp.bfloat16)
            out_ref[place * slots + slot, rows:, :] = three_parts(lines)


def near_part(here, picks, queries, near, shifts, slots):
    rows = queries.shape[0]
    total = len(shifts) * slots
    return call(
        functools.partial(near_kernel, shifts=shifts, slots=slots),
        [SCALARS, SCALARS, IN_VMEM] + [IN_VMEM] * len(shifts),
        jax.ShapeDtypeStruct((total, rows + STAT_ROWS, HD), jnp.bfloat16),
        IN_VMEM,
        [pltpu.SMEM((slots + 1,), jnp.int32)],
        flops=4 * total * rows * rows * HD,
        moved=12 * total * rows * HD,
        exps=total * rows * rows,
    )(here, picks, queries, *near)


def find_spots(spots_ref, found_ref, picks_ref, here, shifts, slots):
    for owner in range(picks_ref.shape[0]):
        found_ref[owner] = 0

    for pick in range(PICKS):
        for head in range(HEADS):
            owner = picks_ref[here, pick, head]
            safe = jnp.maximum(owner, 0)
            order = found_ref[safe]
            found_ref[safe] = order + (owner >= 0).astype(jnp.int32)
            spot = jnp.int32(-1)
            for place, shift in enumerate(shifts):
                spot = jnp.where(here - safe == shift, place * slots + order, spot)
            spots_ref[head * PICKS + pick] = jnp.where(owner >= 0, spot, -1)


def merge_kernel(here_ref, picks_ref, *refs, places, shifts, slots):
    count = len(places)
    parts = refs[:count]
    result_ref, out_ref, sums_ref, held, spots_ref, found_ref, sems = refs[count:]
    groups = sums_ref.shape[1]
    rows = groups * LANES
    copies = [
        pltpu.make_async_copy(part, held.at[pl.ds(place, part.shape[0])], sems.at[number])
        for number, (part, place) in enumerate(zip(parts, places))
    ]
    for copy in copies:
        copy.start()
    find_spots(spots_ref, found_ref, picks_ref, here_ref[0], shifts, slots)
    for copy in copies:
        copy.wait()

    def one_head(head, carry):
        found = [spots_ref[head * PICKS + pick] for pick in range(PICKS)]
        spots = [head] + [jnp.where(spot >= 0, HEADS + spot, head) for spot in found]
        sums = [stats_of(held[spot, rows:, :], groups) for spot in spots]
        for pick, spot in enumerate(found):
            sums[1 + pick] = jnp.where(spot >= 0, sums[1 + pick], -jnp.inf)
        top = functools.reduce(jnp.maximum, sums)
        shares = [jnp.exp2(part - top) for part in sums]
        whole = functools.reduce(jnp.add, shares)
        sums_ref[head] = top + jnp.log2(whole)
        for group in range(groups):
            span = pl.ds(group * LANES, LANES)
            own = held[head, span, :].astype(jnp.float32)
            mixed = own
            for spot, share in zip(spots[1:], shares[1:]):
                weight = down_rows((share / whole)[group : group + 1, :])
                mixed = mixed + (held[spot, span, :].astype(jnp.float32) - own) * weight
            out_ref[head, span, :] = mixed
            result_ref[span, head_columns(head)] = mixed.astype(jnp.bfloat16)
        return carry

    lax.fori_loop(0, HEADS, one_head, 0, unroll=2)


def merge(here, picks, parts, places, shifts, slots):
    rows = parts[0].shape[1] - STAT_ROWS
    width = picks.shape[0]
    total = HEADS + len(shifts) * slots
    return call(
        functools.partial(merge_kernel, places=tuple(places), shifts=shifts, slots=slots),
        [SCALARS, SCALARS] + [pl.BlockSpec(memory_space=pl.ANY)] * len(parts),
        [
            jax.ShapeDtypeStruct((rows, HEADS * HD), jnp.bfloat16),
            jax.ShapeDtypeStruct((HEADS, rows, HD), jnp.float32),
            jax.ShapeDtypeStruct((HEADS, rows // LANES, LANES), jnp.float32),
        ],
        [IN_VMEM, IN_VMEM, IN_VMEM],
        [
            pltpu.VMEM((total, rows + STAT_ROWS, HD), jnp.bfloat16),
            pltpu.SMEM((PICKS * HEADS,), jnp.int32),
            pltpu.SMEM((width,), jnp.int32),
            pltpu.SemaphoreType.DMA((len(parts),)),
        ],
        flops=6 * HEADS * rows * HD,
        moved=2 * (HEADS * 2 + total) * rows * HD,
    )(here, picks, *parts)


def finish_kernel(here_ref, picks_ref, mixed_ref, sums_ref, *refs, shifts, slots):
    count = len(shifts)
    parts, out_ref, (heads_ref, held, sems) = refs[:count], refs[count + 1], refs[count + 2 :]
    groups = sums_ref.shape[1]
    rows = groups * LANES
    here = here_ref[0]
    for number, shift in enumerate(shifts):
        list_heads(heads_ref, number * slots, picks_ref, here, here - shift, slots)

    def slot_of(head, number):
        found = jnp.int32(-1)
        for slot in range(slots):
            found = jnp.where(heads_ref[number * slots + slot] == head, slot, found)
        return found

    def is_first(head, number):
        first = head >= 0
        for earlier in range(number):
            first = first & (slot_of(head, earlier) < 0)
        return first

    def patch(place):
        columns = head_columns(jnp.maximum(heads_ref[place], 0))
        return pltpu.make_async_copy(held.at[place], out_ref.at[:, columns], sems.at[place])

    places = [(number, number * slots + slot) for number in range(count) for slot in range(slots)]
    for number, place in places:
        head = heads_ref[place]

        @pl.when(is_first(head, number))
        def _():
            found = [slot_of(head, later) for later in range(number, count)]
            spots = [jnp.maximum(spot, 0) for spot in found]
            sums = [sums_ref[head]]
            for part, spot, safe in zip(parts[number:], found, spots):
                added = stats_of(part[safe, rows:, :], groups)
                sums.append(jnp.where(spot >= 0, added, -jnp.inf))
            top = functools.reduce(jnp.maximum, sums)
            shares = [jnp.exp2(part - top) for part in sums]
            whole = functools.reduce(jnp.add, shares)
            for group in range(groups):
                span = pl.ds(group * LANES, LANES)
                before = mixed_ref[head, span, :]
                mixed = before
                for part, spot, safe, share in zip(parts[number:], found, spots, shares[1:]):
                    new = jnp.where(spot >= 0, part[safe, span, :].astype(jnp.float32), 0.0)
                    weight = down_rows((share / whole)[group : group + 1, :])
                    mixed = mixed + (new - before) * weight
                held[place, span, :] = mixed.astype(jnp.bfloat16)
            patch(place).start()

    for number, place in places:

        @pl.when(is_first(heads_ref[place], number))
        def _():
            patch(place).wait()


def finish(here, picks, result, mixed, sums, parts, shifts, slots):
    rows = mixed.shape[1]
    total = len(shifts) * slots
    return pl.pallas_call(
        functools.partial(finish_kernel, shifts=shifts, slots=slots),
        in_specs=[SCALARS, SCALARS] + [IN_VMEM] * (2 + len(parts)) + [IN_HBM],
        out_specs=IN_HBM,
        out_shape=jax.ShapeDtypeStruct(result.shape, result.dtype),
        scratch_shapes=[
            pltpu.SMEM((total + 1,), jnp.int32),
            pltpu.VMEM((total, rows, HD), jnp.bfloat16),
            pltpu.SemaphoreType.DMA((total,)),
        ],
        input_output_aliases={4 + len(parts): 0},
        compiler_params=pltpu.CompilerParams(vmem_limit_bytes=VMEM_BYTES),
        cost_estimate=pl.CostEstimate(
            flops=2 * total * rows * HD, bytes_accessed=8 * total * rows * HD, transcendentals=0
        ),
    )(here, picks, mixed, sums, *parts, result)


def after(value, *earlier):
    return lax.optimization_barrier((value,) + earlier)[0]


def travelling_queries(queries, keys, values, picks):
    width = lax.axis_size("ctx")
    sections = lax.axis_size("pipe")
    slots = max(1, PICKS * HEADS // width)
    here = lax.axis_index("ctx").astype(jnp.int32).reshape(1)
    queries, keys, values = queries[0], keys[0], values[0]
    own_picks = picks[0].transpose(0, 2, 1)

    near_shifts = (2, width - 2)
    middle = width // 2
    far_shifts = [middle, middle - 1, middle + 1, 1, width - 1]
    final_shifts = tuple(far_shifts[1:])

    def up(value, shift):
        return lax.ppermute(value, "ctx", [(at, at + shift) for at in range(width - shift)])

    def down(value, shift):
        return lax.ppermute(value, "ctx", [(at, at - shift) for at in range(shift, width)])

    def up_and_on(value, shift):
        pairs = [
            (at * sections + section, (at + shift) * sections + (section + 1) % sections)
            for at in range(width - shift)
            for section in range(sections)
        ]
        return lax.ppermute(value, ("ctx", "pipe"), pairs)

    near_jobs = [(shift, 0, slots, True) for shift in near_shifts]
    near_sends = pack(here, own_picks, [keys, values], near_jobs, slots)
    near = [up(near_sends[0], near_shifts[0])]
    before = passed_along(own_picks, "pipe", 1)
    sends, now = {}, after(here, *near_sends)
    for shifts in (far_shifts[:1], far_shifts[1:]):
        jobs = [(shift, 0, slots, False) for shift in shifts]
        packed = pack(now, own_picks, [queries], jobs, slots)
        sends |= zip(shifts, packed)
        now = after(now, *packed)
    arrived, returned = {}, {}

    def ask_for(shift, *earlier):
        arrived[shift] = down(after(sends[shift], *earlier), shift)

    def work(token, shift, is_anchor=False):
        return attend(
            token, own_picks, keys, values, [arrived[shift]], ((shift, 0, slots),), slots, is_anchor
        )[0]

    four, three, five, one, seven = far_shifts
    ask_for(four, near_sends[0])
    own = own_part(after(now, before), queries, keys, values)
    own_back = passed_along(own, "pipe", 1)
    near.append(up(after(near_sends[1], own), near_shifts[1]))
    ask_for(three, arrived[four], near[0], own)
    ask_for(five, arrived[four], near[0], own)
    part_four = work(after(here, own, near[0]), four, is_anchor=True)
    returned[four] = up_and_on(part_four, four)
    beside = near_part(after(here, part_four, own_back), own_picks, queries, near, near_shifts, slots)
    ask_for(one, own_back, part_four, *near)
    ask_for(seven, own_back, part_four, *near)
    part_three = work(after(here, beside), three, is_anchor=True)
    returned[three] = up_and_on(part_three, three)
    part_five = work(after(here, part_three), five)
    returned[five] = up_and_on(part_five, five)
    beside_back = passed_along(beside, "pipe", 1)
    part_one = work(after(here, part_five, beside_back), one)
    returned[one] = up_and_on(part_one, one)
    part_seven = work(after(here, part_one), seven)
    returned[seven] = up_and_on(part_seven, seven)
    now = after(here, part_seven)

    merged_shifts = near_shifts + (four,)
    places = [HEADS + 2 * slots]
    parts = [own_back, beside_back, returned[four]]
    result, mixed, sums = merge(now, before, parts, [0, HEADS] + places, merged_shifts, slots)
    lasts = [returned[shift] for shift in final_shifts]
    return finish(now, before, result, mixed, sums, lasts, final_shifts, slots)[None]


def travelling_keys(queries, keys, values, picks):
    ctx_width = lax.axis_size("ctx")
    rank_here = lax.axis_index("ctx")
    slot_count = max(1, PICKS * HEADS // ctx_width)
    block_rows = queries.shape[1]
    score_scale = HD ** (-0.5)
    every_pick = picks[0].reshape(ctx_width, HEADS * PICKS)
    chosen = lax.dynamic_slice_in_dim(every_pick, rank_here, 1, 0)
    pick_order = request_table(chosen, lax.iota(jnp.int32, ctx_width), slot_count)[1]
    asked_table = request_table(every_pick, rank_here.reshape(1), slot_count)[0]
    asked_heads = asked_table[:, 0, :]
    safe_asked = jnp.maximum(asked_heads, 0)
    query_heads = queries[0].reshape(block_rows, HEADS, HD).transpose(1, 0, 2)
    key_heads = keys[0].reshape(block_rows, HEADS, HD).transpose(1, 0, 2)
    value_heads = values[0].reshape(block_rows, HEADS, HD).transpose(1, 0, 2)
    is_live = chosen[0] >= 0
    flat_slot = jnp.where(is_live, chosen[0] * slot_count + pick_order[0], 0)
    remote_mask = jnp.repeat(is_live.reshape(HEADS, PICKS), block_rows, axis=1)
    row_index = lax.iota(jnp.int32, block_rows)
    causal = row_index[:, None] >= row_index[None, :]

    def masked_scores(query_head, key_rows, mask_row):
        scores = lax.dot_general(
            query_head, key_rows, (((1,), (1,)), ((), ())), preferred_element_type=jnp.float32
        )
        allowed = jnp.concatenate(
            [causal, jnp.broadcast_to(mask_row[None, :], (block_rows, PICKS * block_rows))], axis=1
        )
        return jnp.where(allowed, scores * score_scale, -jnp.inf)

    def row_stats(scores):
        row_top = jnp.max(scores, axis=1)
        row_total = jnp.sum(jnp.exp(scores - row_top[:, None]), axis=1)
        return (row_top, row_total)

    def weighted(scores, row_top, row_total, value_rows):
        prob_rows = (jnp.exp(scores - row_top[:, None]) / row_total[:, None]).astype(jnp.bfloat16)
        return jnp.dot(prob_rows, value_rows, preferred_element_type=jnp.float32).astype(
            jnp.bfloat16
        )

    send_both = jnp.concatenate([key_heads, value_heads], axis=2)[safe_asked]
    got_slots = lax.all_to_all(send_both, "ctx", split_axis=0, concat_axis=0, tiled=True)
    last_width = 2 * HD
    flat_slots = got_slots.reshape(ctx_width * slot_count, block_rows, last_width)
    remote_both = flat_slots[flat_slot].reshape(HEADS, PICKS * block_rows, last_width)
    all_keys = jnp.concatenate([key_heads, remote_both[:, :, :HD]], axis=1)
    all_values = jnp.concatenate([value_heads, remote_both[:, :, HD:]], axis=1)

    def per_head(head_items):
        query_head, key_rows, value_rows, mask_row = head_items
        scores = masked_scores(query_head, key_rows, mask_row)
        row_top, row_total = row_stats(scores)
        return weighted(scores, row_top, row_total, value_rows)

    outputs = lax.map(per_head, (query_heads, all_keys, all_values, remote_mask))
    merged = outputs.transpose(1, 0, 2).reshape(1, block_rows, HEADS * HD)
    return passed_along(merged, "pipe", 1)


def per_device(queries, keys, values, picks):
    few_shifts = lax.axis_size("ctx") == 8
    run = travelling_queries if few_shifts else travelling_keys
    return run(queries, keys, values, picks)


def solution(mesh):
    placed = (
        P("pipe", "ctx", None),
        P("pipe", "ctx", None),
        P("pipe", "ctx", None),
        P("pipe", None, None, None),
    )
    return jax.shard_map(
        per_device, mesh=mesh, in_specs=placed, out_specs=P("pipe", "ctx", None), check_vma=False
    )
```

```python
import functools
import math

import jax
import jax.numpy as jnp
from jax import lax
from jax.experimental import pallas as pl
from jax.experimental.pallas import tpu as pltpu
from jax.sharding import PartitionSpec as P

HEADS = 16
HD = 128
PICKS = 2
EXP2_SCALE = HD ** -0.5 * math.log2(math.e)
LANES = 128
STAT_ROWS = 16
VMEM_BYTES = 24 * 1024 * 1024
HIGH_COST = 10**12


def passed_along(value, axis, steps):
    count = lax.axis_size(axis)
    pairs = [(source, (source + steps) % count) for source in range(count)]
    return lax.ppermute(value, axis, pairs)


def request_table(chosen, owners, slot_count):
    pick_count = chosen.shape[1]
    pick_ids = lax.iota(jnp.int32, pick_count)
    is_live = chosen >= 0
    earlier = pick_ids[None, :] < pick_ids[:, None]
    same_owner = (chosen[:, :, None] == chosen[:, None, :]) & earlier[None]
    pick_order = jnp.sum(same_owner.astype(jnp.int32), axis=2)
    head_ids = pick_ids // PICKS
    slot_ranks = lax.iota(jnp.int32, slot_count)
    matches = (
        is_live[:, None, None, :]
        & (chosen[:, None, None, :] == owners[None, :, None, None])
        & (pick_order[:, None, None, :] == slot_ranks[None, None, :, None])
    )
    was_found = jnp.any(matches, axis=3)
    head_table = jnp.sum(jnp.where(matches, head_ids[None, None, None, :], 0), axis=3)
    return (jnp.where(was_found, head_table, -1), pick_order)


def call(
    kernel, name_space, outputs, out_specs, scratch=(), flops=0, moved=0, exps=0
):
    return pl.pallas_call(
        kernel,
        in_specs=name_space,
        out_specs=out_specs,
        out_shape=outputs,
        scratch_shapes=list(scratch),
        compiler_params=pltpu.CompilerParams(vmem_limit_bytes=VMEM_BYTES),
        cost_estimate=pl.CostEstimate(flops=flops, bytes_accessed=moved, transcendentals=exps),
    )


SCALARS = pl.BlockSpec(memory_space=pltpu.SMEM)
IN_HBM = pl.BlockSpec(memory_space=pltpu.HBM)
IN_VMEM = pl.BlockSpec(memory_space=pltpu.VMEM)


def tick_kernel(here_ref, out_ref):
    out_ref[0] = here_ref[0]


def tick(here, *earlier):
    return call(
        tick_kernel,
        [SCALARS],
        jax.ShapeDtypeStruct((1,), jnp.int32),
        SCALARS,
        flops=0,
    )(after(here, *earlier))


def list_heads(heads_ref, start, picks_ref, block, owner, slots):
    width = picks_ref.shape[0]
    spare = heads_ref.shape[0] - 1
    for slot in range(slots):
        heads_ref[start + slot] = -1
    valid = (block >= 0) & (block < width) & (owner >= 0) & (owner < width)
    row = jnp.clip(block, 0, width - 1)
    wanted = jnp.where(valid, owner, -2)
    found = jnp.int32(0)
    for pick in range(PICKS):
        for head in range(HEADS):
            hit = picks_ref[row, pick, head] == wanted
            heads_ref[jnp.where(hit, start + found, spare)] = head
            found = found + hit.astype(jnp.int32)


def pack_kernel(here_ref, picks_ref, *refs, jobs, slots):
    is_near = jobs[0][3]
    sources = refs[: 1 + is_near]
    outputs = refs[1 + is_near : 1 + is_near + len(jobs)]
    heads_ref, sems = refs[-2], refs[-1]
    here = here_ref[0]
    listed = {}
    for shift, first, count, is_near in jobs:
        key = (shift, is_near)
        if key not in listed:
            listed[key] = len(listed) * slots
            block, owner = (here + shift, here) if is_near else (here, here - shift)
            list_heads(heads_ref, listed[key], picks_ref, block, owner, slots)
    copies = []
    for (shift, first, count, is_near), output in zip(jobs, outputs):
        for slot in range(count):
            head = jnp.maximum(heads_ref[listed[shift, is_near] + first + slot], 0)
            columns = pl.ds(pl.multiple_of(head * HD, HD), HD)
            for place, source in enumerate(sources):
                target = output.at[2 * slot + place if is_near else slot]
                copy = pltpu.make_async_copy(
                    source.at[:, columns], target, sems.at[len(copies)]
                )
                copy.start()
                copies.append(copy)
    for copy in copies:
        copy.wait()


def pack(here, picks, sources, jobs, slots):
    rows = sources[0].shape[0]
    sizes = [len(sources) * count for _, _, count, _ in jobs]
    return call(
        functools.partial(pack_kernel, jobs=jobs, slots=slots),
        [SCALARS, SCALARS] + [IN_VMEM] * len(sources),
        [jax.ShapeDtypeStruct((size, rows, HD), jnp.bfloat16) for size in sizes],
        [IN_VMEM] * len(sizes),
        [pltpu.SMEM((len(jobs) * slots + 1,), jnp.int32), pltpu.SemaphoreType.DMA((sum(sizes),))],
        moved=4 * rows * HD * sum(sizes),
    )(here, picks, *sources)


def diagonal():
    shape = (LANES, LANES)
    return lax.broadcasted_iota(jnp.int32, shape, 0) == lax.broadcasted_iota(jnp.int32, shape, 1)


def raw_scores(query_rows, key_rows):
    return lax.dot_general(
        query_rows, key_rows, (((1,), (1,)), ((), ())), preferred_element_type=jnp.float32
    )


def with_ones(value_rows):
    return jnp.concatenate([value_rows, jnp.ones_like(value_rows)], axis=1)


def soft_part(scores, value_rows):
    top = jnp.max(scores, axis=1, keepdims=True)
    weights = jnp.exp2((scores - top) * EXP2_SCALE).astype(jnp.bfloat16)
    total = jnp.dot(weights, value_rows, preferred_element_type=jnp.float32)
    sums = total[:, HD:]
    return total[:, :HD] * pl.reciprocal(sums), top * EXP2_SCALE, sums


def across_lanes(column):
    eye = diagonal()
    spread = jnp.broadcast_to(column, (column.shape[0], LANES))
    return [
        jnp.sum(jnp.where(eye, spread[at : at + LANES], 0.0), axis=0, keepdims=True)
        for at in range(0, column.shape[0], LANES)
    ]


def down_rows(line):
    spread = jnp.broadcast_to(line, (LANES, LANES))
    return jnp.sum(jnp.where(diagonal(), spread, 0.0), axis=1, keepdims=True)


def three_parts(stats):
    first = stats.astype(jnp.bfloat16).astype(jnp.float32)
    second = (stats - first).astype(jnp.bfloat16).astype(jnp.float32)
    third = stats - first - second
    parts = jnp.concatenate([first, second, third], axis=0)
    pad = jnp.zeros((STAT_ROWS - parts.shape[0], LANES), jnp.float32)
    return jnp.concatenate([parts, pad], axis=0).astype(jnp.bfloat16)


def stats_of(block, groups):
    stats = block.astype(jnp.float32)
    return stats[:groups] + stats[groups : 2 * groups] + stats[2 * groups : 3 * groups]


def log_sums(tops, sums):
    top_lines = [line for top in tops for line in across_lanes(top)]
    sum_lines = [line for part in sums for line in across_lanes(part)]
    return jnp.concatenate(top_lines, axis=0) + jnp.log2(jnp.concatenate(sum_lines, axis=0))


def attend_rows(query_rows, key_rows, value_rows, tile):
    found = [
        soft_part(raw_scores(query_rows[at : at + tile], key_rows), value_rows)
        for at in range(0, query_rows.shape[0], tile)
    ]
    outputs, tops, sums = zip(*found)
    return jnp.concatenate(outputs, axis=0), log_sums(tops, sums)


def head_columns(head):
    return pl.ds(pl.multiple_of(head * HD, HD), HD)


def attend_kernel(here_ref, picks_ref, key_ref, value_ref, *refs, group, slots):
    heads_ref = refs[-1]
    here = here_ref[0]
    for number, (shift, first, count) in enumerate(group):
        query_ref, out_ref = refs[number], refs[len(group) + number]
        rows = query_ref.shape[1]
        list_heads(heads_ref, 0, picks_ref, here + shift, here, slots)
        for slot in range(count):
            columns = head_columns(jnp.maximum(heads_ref[first + slot], 0))
            outputs, lines = attend_rows(
                query_ref[slot], key_ref[:, columns], with_ones(value_ref[:, columns]), rows
            )
            out_ref[slot, :rows, :] = outputs.astype(jnp.bfloat16)
            out_ref[slot, rows:, :] = three_parts(lines)


def attend(here, picks, keys, values, arrived, group, slots, is_anchor):
    rows = keys.shape[0]
    total = sum(count for _, _, count in group)
    return call(
        functools.partial(attend_kernel, group=group, slots=slots),
        [SCALARS, SCALARS, IN_VMEM, IN_VMEM] + [IN_VMEM] * len(group),
        [
            jax.ShapeDtypeStruct((count, rows + STAT_ROWS, HD), jnp.bfloat16)
            for _, _, count in group
        ],
        [IN_VMEM] * len(group),
        [pltpu.SMEM((slots + 1,), jnp.int32)],
        flops=HIGH_COST if is_anchor else 4 * total * rows * rows * HD,
        moved=8 * total * rows * HD,
        exps=total * rows * rows,
    )(here, picks, keys, values, *arrived)


def own_kernel(here_ref, query_ref, key_ref, value_ref, out_ref):
    rows = query_ref.shape[0]
    tile = min(rows, 256)

    def one_head(head, carry):
        columns = head_columns(head)
        value_rows = with_ones(value_ref[:, columns])
        tops, all_sums = [], []
        for at in range(0, rows, tile):
            reach = at + tile
            scores = raw_scores(query_ref[at:reach, columns], key_ref[:reach, columns])
            row_ids = lax.broadcasted_iota(jnp.int32, scores.shape, 0) + at
            seen = row_ids >= lax.broadcasted_iota(jnp.int32, scores.shape, 1)
            outputs, top, sums = soft_part(jnp.where(seen, scores, -jnp.inf), value_rows[:reach])
            out_ref[head, at:reach, :] = outputs.astype(jnp.bfloat16)
            tops.append(top)
            all_sums.append(sums)
        out_ref[head, rows:, :] = three_parts(log_sums(tops, all_sums))
        return carry

    lax.fori_loop(0, HEADS, one_head, 0, unroll=4)


def own_part(here, queries, keys, values):
    rows = queries.shape[0]
    return call(
        own_kernel,
        [SCALARS, IN_VMEM, IN_VMEM, IN_VMEM],
        jax.ShapeDtypeStruct((HEADS, rows + STAT_ROWS, HD), jnp.bfloat16),
        IN_VMEM,
        flops=4 * HEADS * rows * rows * HD,
        moved=8 * HEADS * rows * HD,
        exps=HEADS * rows * rows,
    )(here, queries, keys, values)


def near_kernel(here_ref, picks_ref, query_ref, *refs, shifts, slots):
    near_refs, out_ref, heads_ref = refs[: len(shifts)], refs[-2], refs[-1]
    rows = query_ref.shape[0]
    here = here_ref[0]
    for place, (shift, near_ref) in enumerate(zip(shifts, near_refs)):
        list_heads(heads_ref, 0, picks_ref, here, here - shift, slots)
        for slot in range(slots):
            columns = head_columns(jnp.maximum(heads_ref[slot], 0))
            outputs, lines = attend_rows(
                query_ref[:, columns], near_ref[2 * slot], with_ones(near_ref[2 * slot + 1]), rows
            )
            out_ref[place * slots + slot, :rows, :] = outputs.astype(jnp.bfloat16)
            out_ref[place * slots + slot, rows:, :] = three_parts(lines)


def near_part(here, picks, queries, near, shifts, slots):
    rows = queries.shape[0]
    total = len(shifts) * slots
    return call(
        functools.partial(near_kernel, shifts=shifts, slots=slots),
        [SCALARS, SCALARS, IN_VMEM] + [IN_VMEM] * len(shifts),
        jax.ShapeDtypeStruct((total, rows + STAT_ROWS, HD), jnp.bfloat16),
        IN_VMEM,
        [pltpu.SMEM((slots + 1,), jnp.int32)],
        flops=HIGH_COST,
        moved=12 * total * rows * HD,
        exps=total * rows * rows,
    )(here, picks, queries, *near)


def find_spots(spots_ref, found_ref, picks_ref, here, shifts, slots):
    for owner in range(picks_ref.shape[0]):
        found_ref[owner] = 0

    for pick in range(PICKS):
        for head in range(HEADS):
            owner = picks_ref[here, pick, head]
            safe = jnp.maximum(owner, 0)
            order = found_ref[safe]
            found_ref[safe] = order + (owner >= 0).astype(jnp.int32)
            spot = jnp.int32(-1)
            for place, shift in enumerate(shifts):
                spot = jnp.where(here - safe == shift, place * slots + order, spot)
            spots_ref[head * PICKS + pick] = jnp.where(owner >= 0, spot, -1)


def merge_kernel(here_ref, picks_ref, *refs, places, shifts, slots):
    count = len(places)
    parts = refs[:count]
    result_ref, out_ref, sums_ref, held, spots_ref, found_ref, sems = refs[count:]
    groups = sums_ref.shape[1]
    rows = groups * LANES
    copies = [
        pltpu.make_async_copy(part, held.at[pl.ds(place, part.shape[0])], sems.at[number])
        for number, (part, place) in enumerate(zip(parts, places))
    ]
    for copy in copies:
        copy.start()
    find_spots(spots_ref, found_ref, picks_ref, here_ref[0], shifts, slots)
    for copy in copies:
        copy.wait()

    def one_head(head, carry):
        found = [spots_ref[head * PICKS + pick] for pick in range(PICKS)]
        spots = [head] + [jnp.where(spot >= 0, HEADS + spot, head) for spot in found]
        sums = [stats_of(held[spot, rows:, :], groups) for spot in spots]
        for pick, spot in enumerate(found):
            sums[1 + pick] = jnp.where(spot >= 0, sums[1 + pick], -jnp.inf)
        top = functools.reduce(jnp.maximum, sums)
        shares = [jnp.exp2(part - top) for part in sums]
        whole = functools.reduce(jnp.add, shares)
        sums_ref[head] = top + jnp.log2(whole)
        for group in range(groups):
            span = pl.ds(group * LANES, LANES)
            own = held[head, span, :].astype(jnp.float32)
            mixed = own
            for spot, share in zip(spots[1:], shares[1:]):
                weight = down_rows((share / whole)[group : group + 1, :])
                mixed = mixed + (held[spot, span, :].astype(jnp.float32) - own) * weight
            out_ref[head, span, :] = mixed
            result_ref[span, head_columns(head)] = mixed.astype(jnp.bfloat16)
        return carry

    lax.fori_loop(0, HEADS, one_head, 0, unroll=2)


def merge(here, picks, parts, places, shifts, slots):
    rows = parts[0].shape[1] - STAT_ROWS
    width = picks.shape[0]
    total = HEADS + len(shifts) * slots
    return call(
        functools.partial(merge_kernel, places=tuple(places), shifts=shifts, slots=slots),
        [SCALARS, SCALARS] + [pl.BlockSpec(memory_space=pl.ANY)] * len(parts),
        [
            jax.ShapeDtypeStruct((rows, HEADS * HD), jnp.bfloat16),
            jax.ShapeDtypeStruct((HEADS, rows, HD), jnp.float32),
            jax.ShapeDtypeStruct((HEADS, rows // LANES, LANES), jnp.float32),
        ],
        [IN_VMEM, IN_VMEM, IN_VMEM],
        [
            pltpu.VMEM((total, rows + STAT_ROWS, HD), jnp.bfloat16),
            pltpu.SMEM((PICKS * HEADS,), jnp.int32),
            pltpu.SMEM((width,), jnp.int32),
            pltpu.SemaphoreType.DMA((len(parts),)),
        ],
        flops=6 * HEADS * rows * HD,
        moved=2 * (HEADS * 2 + total) * rows * HD,
    )(here, picks, *parts)


def finish_kernel(here_ref, picks_ref, mixed_ref, sums_ref, *refs, shifts, slots):
    count = len(shifts)
    parts, out_ref, (heads_ref, held, sems) = refs[:count], refs[count + 1], refs[count + 2 :]
    groups = sums_ref.shape[1]
    rows = groups * LANES
    here = here_ref[0]
    for number, shift in enumerate(shifts):
        list_heads(heads_ref, number * slots, picks_ref, here, here - shift, slots)

    def slot_of(head, number):
        found = jnp.int32(-1)
        for slot in range(slots):
            found = jnp.where(heads_ref[number * slots + slot] == head, slot, found)
        return found

    def is_first(head, number):
        first = head >= 0
        for earlier in range(number):
            first = first & (slot_of(head, earlier) < 0)
        return first

    def patch(place):
        columns = head_columns(jnp.maximum(heads_ref[place], 0))
        return pltpu.make_async_copy(held.at[place], out_ref.at[:, columns], sems.at[place])

    places = [(number, number * slots + slot) for number in range(count) for slot in range(slots)]
    for number, place in places:
        head = heads_ref[place]

        @pl.when(is_first(head, number))
        def _():
            found = [slot_of(head, later) for later in range(number, count)]
            spots = [jnp.maximum(spot, 0) for spot in found]
            sums = [sums_ref[head]]
            for part, spot, safe in zip(parts[number:], found, spots):
                added = stats_of(part[safe, rows:, :], groups)
                sums.append(jnp.where(spot >= 0, added, -jnp.inf))
            top = functools.reduce(jnp.maximum, sums)
            shares = [jnp.exp2(part - top) for part in sums]
            whole = functools.reduce(jnp.add, shares)
            for group in range(groups):
                span = pl.ds(group * LANES, LANES)
                before = mixed_ref[head, span, :]
                mixed = before
                for part, spot, safe, share in zip(parts[number:], found, spots, shares[1:]):
                    new = jnp.where(spot >= 0, part[safe, span, :].astype(jnp.float32), 0.0)
                    weight = down_rows((share / whole)[group : group + 1, :])
                    mixed = mixed + (new - before) * weight
                held[place, span, :] = mixed.astype(jnp.bfloat16)
            patch(place).start()

    for number, place in places:

        @pl.when(is_first(heads_ref[place], number))
        def _():
            patch(place).wait()


def finish(here, picks, result, mixed, sums, parts, shifts, slots):
    rows = mixed.shape[1]
    total = len(shifts) * slots
    return pl.pallas_call(
        functools.partial(finish_kernel, shifts=shifts, slots=slots),
        in_specs=[SCALARS, SCALARS] + [IN_VMEM] * (2 + len(parts)) + [IN_HBM],
        out_specs=IN_HBM,
        out_shape=jax.ShapeDtypeStruct(result.shape, result.dtype),
        scratch_shapes=[
            pltpu.SMEM((total + 1,), jnp.int32),
            pltpu.VMEM((total, rows, HD), jnp.bfloat16),
            pltpu.SemaphoreType.DMA((total,)),
        ],
        input_output_aliases={4 + len(parts): 0},
        compiler_params=pltpu.CompilerParams(vmem_limit_bytes=VMEM_BYTES),
        cost_estimate=pl.CostEstimate(
            flops=2 * total * rows * HD, bytes_accessed=8 * total * rows * HD, transcendentals=0
        ),
    )(here, picks, mixed, sums, *parts, result)


def after(value, *earlier):
    return lax.optimization_barrier((value,) + earlier)[0]


def travelling_queries(queries, keys, values, picks):
    width = lax.axis_size("ctx")
    sections = lax.axis_size("pipe")
    slots = max(1, PICKS * HEADS // width)
    here = lax.axis_index("ctx").astype(jnp.int32).reshape(1)
    queries, keys, values = queries[0], keys[0], values[0]
    own_picks = picks[0].transpose(0, 2, 1)

    near_shifts = (2, width - 2)
    middle = width // 2
    far_shifts = [middle - 1, middle + 1, middle, 1, width - 1]
    final_shifts = tuple(far_shifts[2:])

    def up(value, shift):
        return lax.ppermute(value, "ctx", [(at, at + shift) for at in range(width - shift)])

    def down(value, shift):
        return lax.ppermute(value, "ctx", [(at, at - shift) for at in range(shift, width)])

    def up_and_on(value, shift):
        pairs = [
            (at * sections + section, (at + shift) * sections + (section + 1) % sections)
            for at in range(width - shift)
            for section in range(sections)
        ]
        return lax.ppermute(value, ("ctx", "pipe"), pairs)

    near_jobs = [(shift, 0, slots, True) for shift in near_shifts]
    near_sends = pack(here, own_picks, [keys, values], near_jobs, slots)
    near = [up(near_sends[0], near_shifts[0])]
    before = passed_along(own_picks, "pipe", 1)
    sends, now = {}, after(here, *near_sends)
    for shifts in (far_shifts[:2], far_shifts[2:]):
        jobs = [(shift, 0, slots, False) for shift in shifts]
        packed = pack(now, own_picks, [queries], jobs, slots)
        sends |= zip(shifts, packed)
        now = after(now, *packed)
    arrived, returned = {}, {}

    def ask_for(shift, *earlier):
        arrived[shift] = down(after(sends[shift], *earlier), shift)

    def work(token, shift, is_anchor=False):
        return attend(
            token, own_picks, keys, values, [arrived[shift]], ((shift, 0, slots),), slots, is_anchor
        )[0]

    three, five, four, one, seven = far_shifts
    ask_for(three, near_sends[0])
    ask_for(five, near_sends[0])
    own = own_part(after(now, before), queries, keys, values)
    own_back = passed_along(own, "pipe", 1)
    near.append(up(after(near_sends[1], now), near_shifts[1]))
    part_three = work(after(here, own), three, is_anchor=True)
    returned[three] = up_and_on(part_three, three)
    part_five = work(after(here, part_three), five, is_anchor=True)
    returned[five] = up_and_on(part_five, five)
    ask_for(four, arrived[three], arrived[five], part_five, own_back, *near)
    beside = near_part(after(here, part_five, own_back), own_picks, queries, near, near_shifts, slots)
    ask_for(one, own_back, part_five, *near)
    ask_for(seven, own_back, part_five, *near)
    beside_back = passed_along(beside, "pipe", 1)
    part_four = work(after(here, beside), four, is_anchor=True)
    returned[four] = up_and_on(part_four, four)
    part_one = work(after(here, part_four, beside_back), one)
    returned[one] = up_and_on(part_one, one)
    part_seven = work(after(here, part_one), seven)
    returned[seven] = up_and_on(part_seven, seven)
    now = after(here, part_seven)

    merged_shifts = near_shifts + (three, five)
    places = [HEADS + place * slots for place in (2, 3)]
    parts = [own_back, beside_back, returned[three], returned[five]]
    result, mixed, sums = merge(now, before, parts, [0, HEADS] + places, merged_shifts, slots)
    lasts = [returned[shift] for shift in final_shifts]
    return finish(now, before, result, mixed, sums, lasts, final_shifts, slots)[None]


def travelling_keys(queries, keys, values, picks):
    ctx_width = lax.axis_size("ctx")
    rank_here = lax.axis_index("ctx")
    slot_count = max(1, PICKS * HEADS // ctx_width)
    block_rows = queries.shape[1]
    score_scale = HD ** (-0.5)
    every_pick = picks[0].reshape(ctx_width, HEADS * PICKS)
    chosen = lax.dynamic_slice_in_dim(every_pick, rank_here, 1, 0)
    pick_order = request_table(chosen, lax.iota(jnp.int32, ctx_width), slot_count)[1]
    asked_table = request_table(every_pick, rank_here.reshape(1), slot_count)[0]
    asked_heads = asked_table[:, 0, :]
    safe_asked = jnp.maximum(asked_heads, 0)
    query_heads = queries[0].reshape(block_rows, HEADS, HD).transpose(1, 0, 2)
    key_heads = keys[0].reshape(block_rows, HEADS, HD).transpose(1, 0, 2)
    value_heads = values[0].reshape(block_rows, HEADS, HD).transpose(1, 0, 2)
    is_live = chosen[0] >= 0
    flat_slot = jnp.where(is_live, chosen[0] * slot_count + pick_order[0], 0)
    remote_mask = jnp.repeat(is_live.reshape(HEADS, PICKS), block_rows, axis=1)
    row_index = lax.iota(jnp.int32, block_rows)
    causal = row_index[:, None] >= row_index[None, :]

    def masked_scores(query_head, key_rows, mask_row):
        scores = lax.dot_general(
            query_head, key_rows, (((1,), (1,)), ((), ())), preferred_element_type=jnp.float32
        )
        allowed = jnp.concatenate(
            [causal, jnp.broadcast_to(mask_row[None, :], (block_rows, PICKS * block_rows))], axis=1
        )
        return jnp.where(allowed, scores * score_scale, -jnp.inf)

    def row_stats(scores):
        row_top = jnp.max(scores, axis=1)
        row_total = jnp.sum(jnp.exp(scores - row_top[:, None]), axis=1)
        return (row_top, row_total)

    def weighted(scores, row_top, row_total, value_rows):
        prob_rows = (jnp.exp(scores - row_top[:, None]) / row_total[:, None]).astype(jnp.bfloat16)
        return jnp.dot(prob_rows, value_rows, preferred_element_type=jnp.float32).astype(
            jnp.bfloat16
        )

    send_both = jnp.concatenate([key_heads, value_heads], axis=2)[safe_asked]
    got_slots = lax.all_to_all(send_both, "ctx", split_axis=0, concat_axis=0, tiled=True)
    last_width = 2 * HD
    flat_slots = got_slots.reshape(ctx_width * slot_count, block_rows, last_width)
    remote_both = flat_slots[flat_slot].reshape(HEADS, PICKS * block_rows, last_width)
    all_keys = jnp.concatenate([key_heads, remote_both[:, :, :HD]], axis=1)
    all_values = jnp.concatenate([value_heads, remote_both[:, :, HD:]], axis=1)

    def per_head(head_items):
        query_head, key_rows, value_rows, mask_row = head_items
        scores = masked_scores(query_head, key_rows, mask_row)
        row_top, row_total = row_stats(scores)
        return weighted(scores, row_top, row_total, value_rows)

    outputs = lax.map(per_head, (query_heads, all_keys, all_values, remote_mask))
    merged = outputs.transpose(1, 0, 2).reshape(1, block_rows, HEADS * HD)
    return passed_along(merged, "pipe", 1)


def per_device(queries, keys, values, picks):
    few_shifts = lax.axis_size("ctx") == 8
    run = travelling_queries if few_shifts else travelling_keys
    return run(queries, keys, values, picks)


def solution(mesh):
    placed = (
        P("pipe", "ctx", None),
        P("pipe", "ctx", None),
        P("pipe", "ctx", None),
        P("pipe", None, None, None),
    )
    return jax.shard_map(
        per_device, mesh=mesh, in_specs=placed, out_specs=P("pipe", "ctx", None), check_vma=False
    )
```

```python
import functools
import math

import jax
import jax.numpy as jnp
from jax import lax
from jax.experimental import pallas as pl
from jax.experimental.pallas import tpu as pltpu
from jax.sharding import PartitionSpec as P

HEADS = 16
HD = 128
PICKS = 2
EXP2_SCALE = HD ** -0.5 * math.log2(math.e)
LANES = 128
STAT_ROWS = 16
VMEM_BYTES = 24 * 1024 * 1024
HIGH_COST = 10**12


def passed_along(value, axis, steps):
    count = lax.axis_size(axis)
    pairs = [(source, (source + steps) % count) for source in range(count)]
    return lax.ppermute(value, axis, pairs)


def request_table(chosen, owners, slot_count):
    pick_count = chosen.shape[1]
    pick_ids = lax.iota(jnp.int32, pick_count)
    is_live = chosen >= 0
    earlier = pick_ids[None, :] < pick_ids[:, None]
    same_owner = (chosen[:, :, None] == chosen[:, None, :]) & earlier[None]
    pick_order = jnp.sum(same_owner.astype(jnp.int32), axis=2)
    head_ids = pick_ids // PICKS
    slot_ranks = lax.iota(jnp.int32, slot_count)
    matches = (
        is_live[:, None, None, :]
        & (chosen[:, None, None, :] == owners[None, :, None, None])
        & (pick_order[:, None, None, :] == slot_ranks[None, None, :, None])
    )
    was_found = jnp.any(matches, axis=3)
    head_table = jnp.sum(jnp.where(matches, head_ids[None, None, None, :], 0), axis=3)
    return (jnp.where(was_found, head_table, -1), pick_order)


def call(
    kernel, name_space, outputs, out_specs, scratch=(), flops=0, moved=0, exps=0
):
    return pl.pallas_call(
        kernel,
        in_specs=name_space,
        out_specs=out_specs,
        out_shape=outputs,
        scratch_shapes=list(scratch),
        compiler_params=pltpu.CompilerParams(vmem_limit_bytes=VMEM_BYTES),
        cost_estimate=pl.CostEstimate(flops=flops, bytes_accessed=moved, transcendentals=exps),
    )


SCALARS = pl.BlockSpec(memory_space=pltpu.SMEM)
IN_HBM = pl.BlockSpec(memory_space=pltpu.HBM)
IN_VMEM = pl.BlockSpec(memory_space=pltpu.VMEM)


def tick_kernel(here_ref, out_ref):
    out_ref[0] = here_ref[0]


def tick(here, *earlier):
    return call(
        tick_kernel,
        [SCALARS],
        jax.ShapeDtypeStruct((1,), jnp.int32),
        SCALARS,
        flops=0,
    )(after(here, *earlier))


def list_heads(heads_ref, start, picks_ref, block, owner, slots):
    width = picks_ref.shape[0]
    spare = heads_ref.shape[0] - 1
    for slot in range(slots):
        heads_ref[start + slot] = -1
    valid = (block >= 0) & (block < width) & (owner >= 0) & (owner < width)
    row = jnp.clip(block, 0, width - 1)
    wanted = jnp.where(valid, owner, -2)
    found = jnp.int32(0)
    for pick in range(PICKS):
        for head in range(HEADS):
            hit = picks_ref[row, pick, head] == wanted
            heads_ref[jnp.where(hit, start + found, spare)] = head
            found = found + hit.astype(jnp.int32)


def pack_kernel(here_ref, picks_ref, *refs, jobs, slots):
    is_near = jobs[0][3]
    sources = refs[: 1 + is_near]
    outputs = refs[1 + is_near : 1 + is_near + len(jobs)]
    heads_ref, sems = refs[-2], refs[-1]
    here = here_ref[0]
    listed = {}
    for shift, first, count, is_near in jobs:
        key = (shift, is_near)
        if key not in listed:
            listed[key] = len(listed) * slots
            block, owner = (here + shift, here) if is_near else (here, here - shift)
            list_heads(heads_ref, listed[key], picks_ref, block, owner, slots)
    copies = []
    for (shift, first, count, is_near), output in zip(jobs, outputs):
        for slot in range(count):
            head = jnp.maximum(heads_ref[listed[shift, is_near] + first + slot], 0)
            columns = pl.ds(pl.multiple_of(head * HD, HD), HD)
            for place, source in enumerate(sources):
                target = output.at[2 * slot + place if is_near else slot]
                copy = pltpu.make_async_copy(
                    source.at[:, columns], target, sems.at[len(copies)]
                )
                copy.start()
                copies.append(copy)
    for copy in copies:
        copy.wait()


def pack(here, picks, sources, jobs, slots):
    rows = sources[0].shape[0]
    sizes = [len(sources) * count for _, _, count, _ in jobs]
    return call(
        functools.partial(pack_kernel, jobs=jobs, slots=slots),
        [SCALARS, SCALARS] + [IN_VMEM] * len(sources),
        [jax.ShapeDtypeStruct((size, rows, HD), jnp.bfloat16) for size in sizes],
        [IN_VMEM] * len(sizes),
        [pltpu.SMEM((len(jobs) * slots + 1,), jnp.int32), pltpu.SemaphoreType.DMA((sum(sizes),))],
        moved=4 * rows * HD * sum(sizes),
    )(here, picks, *sources)


def diagonal():
    shape = (LANES, LANES)
    return lax.broadcasted_iota(jnp.int32, shape, 0) == lax.broadcasted_iota(jnp.int32, shape, 1)


def raw_scores(query_rows, key_rows):
    return lax.dot_general(
        query_rows, key_rows, (((1,), (1,)), ((), ())), preferred_element_type=jnp.float32
    )


def with_ones(value_rows):
    return jnp.concatenate([value_rows, jnp.ones_like(value_rows)], axis=1)


def soft_part(scores, value_rows):
    top = jnp.max(scores, axis=1, keepdims=True)
    weights = jnp.exp2((scores - top) * EXP2_SCALE).astype(jnp.bfloat16)
    total = jnp.dot(weights, value_rows, preferred_element_type=jnp.float32)
    sums = total[:, HD:]
    return total[:, :HD] * pl.reciprocal(sums), top * EXP2_SCALE, sums


def across_lanes(column):
    eye = diagonal()
    spread = jnp.broadcast_to(column, (column.shape[0], LANES))
    return [
        jnp.sum(jnp.where(eye, spread[at : at + LANES], 0.0), axis=0, keepdims=True)
        for at in range(0, column.shape[0], LANES)
    ]


def down_rows(line):
    spread = jnp.broadcast_to(line, (LANES, LANES))
    return jnp.sum(jnp.where(diagonal(), spread, 0.0), axis=1, keepdims=True)


def three_parts(stats):
    first = stats.astype(jnp.bfloat16).astype(jnp.float32)
    second = (stats - first).astype(jnp.bfloat16).astype(jnp.float32)
    third = stats - first - second
    parts = jnp.concatenate([first, second, third], axis=0)
    pad = jnp.zeros((STAT_ROWS - parts.shape[0], LANES), jnp.float32)
    return jnp.concatenate([parts, pad], axis=0).astype(jnp.bfloat16)


def stats_of(block, groups):
    stats = block.astype(jnp.float32)
    return stats[:groups] + stats[groups : 2 * groups] + stats[2 * groups : 3 * groups]


def log_sums(tops, sums):
    top_lines = [line for top in tops for line in across_lanes(top)]
    sum_lines = [line for part in sums for line in across_lanes(part)]
    return jnp.concatenate(top_lines, axis=0) + jnp.log2(jnp.concatenate(sum_lines, axis=0))


def attend_rows(query_rows, key_rows, value_rows, tile):
    found = [
        soft_part(raw_scores(query_rows[at : at + tile], key_rows), value_rows)
        for at in range(0, query_rows.shape[0], tile)
    ]
    outputs, tops, sums = zip(*found)
    return jnp.concatenate(outputs, axis=0), log_sums(tops, sums)


def head_columns(head):
    return pl.ds(pl.multiple_of(head * HD, HD), HD)


def attend_kernel(here_ref, picks_ref, key_ref, value_ref, *refs, group, slots):
    heads_ref = refs[-1]
    here = here_ref[0]
    for number, (shift, first, count) in enumerate(group):
        query_ref, out_ref = refs[number], refs[len(group) + number]
        rows = query_ref.shape[1]
        list_heads(heads_ref, 0, picks_ref, here + shift, here, slots)
        for slot in range(count):
            columns = head_columns(jnp.maximum(heads_ref[first + slot], 0))
            outputs, lines = attend_rows(
                query_ref[slot], key_ref[:, columns], with_ones(value_ref[:, columns]), rows
            )
            out_ref[slot, :rows, :] = outputs.astype(jnp.bfloat16)
            out_ref[slot, rows:, :] = three_parts(lines)


def attend(here, picks, keys, values, arrived, group, slots, is_anchor):
    rows = keys.shape[0]
    total = sum(count for _, _, count in group)
    return call(
        functools.partial(attend_kernel, group=group, slots=slots),
        [SCALARS, SCALARS, IN_VMEM, IN_VMEM] + [IN_VMEM] * len(group),
        [
            jax.ShapeDtypeStruct((count, rows + STAT_ROWS, HD), jnp.bfloat16)
            for _, _, count in group
        ],
        [IN_VMEM] * len(group),
        [pltpu.SMEM((slots + 1,), jnp.int32)],
        flops=HIGH_COST if is_anchor else 4 * total * rows * rows * HD,
        moved=8 * total * rows * HD,
        exps=total * rows * rows,
    )(here, picks, keys, values, *arrived)


def own_kernel(here_ref, query_ref, key_ref, value_ref, out_ref):
    rows = query_ref.shape[0]
    tile = min(rows, 256)

    def one_head(head, carry):
        columns = head_columns(head)
        value_rows = with_ones(value_ref[:, columns])
        tops, all_sums = [], []
        for at in range(0, rows, tile):
            reach = at + tile
            scores = raw_scores(query_ref[at:reach, columns], key_ref[:reach, columns])
            row_ids = lax.broadcasted_iota(jnp.int32, scores.shape, 0) + at
            seen = row_ids >= lax.broadcasted_iota(jnp.int32, scores.shape, 1)
            outputs, top, sums = soft_part(jnp.where(seen, scores, -jnp.inf), value_rows[:reach])
            out_ref[head, at:reach, :] = outputs.astype(jnp.bfloat16)
            tops.append(top)
            all_sums.append(sums)
        out_ref[head, rows:, :] = three_parts(log_sums(tops, all_sums))
        return carry

    lax.fori_loop(0, HEADS, one_head, 0, unroll=4)


def own_part(here, queries, keys, values):
    rows = queries.shape[0]
    return call(
        own_kernel,
        [SCALARS, IN_VMEM, IN_VMEM, IN_VMEM],
        jax.ShapeDtypeStruct((HEADS, rows + STAT_ROWS, HD), jnp.bfloat16),
        IN_VMEM,
        flops=4 * HEADS * rows * rows * HD,
        moved=8 * HEADS * rows * HD,
        exps=HEADS * rows * rows,
    )(here, queries, keys, values)


def near_kernel(here_ref, picks_ref, query_ref, *refs, shifts, slots):
    near_refs, out_ref, heads_ref = refs[: len(shifts)], refs[-2], refs[-1]
    rows = query_ref.shape[0]
    here = here_ref[0]
    for place, (shift, near_ref) in enumerate(zip(shifts, near_refs)):
        list_heads(heads_ref, 0, picks_ref, here, here - shift, slots)
        for slot in range(slots):
            columns = head_columns(jnp.maximum(heads_ref[slot], 0))
            outputs, lines = attend_rows(
                query_ref[:, columns], near_ref[2 * slot], with_ones(near_ref[2 * slot + 1]), rows
            )
            out_ref[place * slots + slot, :rows, :] = outputs.astype(jnp.bfloat16)
            out_ref[place * slots + slot, rows:, :] = three_parts(lines)


def near_part(here, picks, queries, near, shifts, slots):
    rows = queries.shape[0]
    total = len(shifts) * slots
    return call(
        functools.partial(near_kernel, shifts=shifts, slots=slots),
        [SCALARS, SCALARS, IN_VMEM] + [IN_VMEM] * len(shifts),
        jax.ShapeDtypeStruct((total, rows + STAT_ROWS, HD), jnp.bfloat16),
        IN_VMEM,
        [pltpu.SMEM((slots + 1,), jnp.int32)],
        flops=HIGH_COST,
        moved=12 * total * rows * HD,
        exps=total * rows * rows,
    )(here, picks, queries, *near)


def find_spots(spots_ref, found_ref, picks_ref, here, shifts, slots):
    for owner in range(picks_ref.shape[0]):
        found_ref[owner] = 0

    for pick in range(PICKS):
        for head in range(HEADS):
            owner = picks_ref[here, pick, head]
            safe = jnp.maximum(owner, 0)
            order = found_ref[safe]
            found_ref[safe] = order + (owner >= 0).astype(jnp.int32)
            spot = jnp.int32(-1)
            for place, shift in enumerate(shifts):
                spot = jnp.where(here - safe == shift, place * slots + order, spot)
            spots_ref[head * PICKS + pick] = jnp.where(owner >= 0, spot, -1)


def merge_kernel(here_ref, picks_ref, *refs, places, shifts, slots):
    count = len(places)
    parts = refs[:count]
    result_ref, out_ref, sums_ref, held, spots_ref, found_ref, sems = refs[count:]
    groups = sums_ref.shape[1]
    rows = groups * LANES
    copies = [
        pltpu.make_async_copy(part, held.at[pl.ds(place, part.shape[0])], sems.at[number])
        for number, (part, place) in enumerate(zip(parts, places))
    ]
    for copy in copies:
        copy.start()
    find_spots(spots_ref, found_ref, picks_ref, here_ref[0], shifts, slots)
    for copy in copies:
        copy.wait()

    def one_head(head, carry):
        found = [spots_ref[head * PICKS + pick] for pick in range(PICKS)]
        spots = [head] + [jnp.where(spot >= 0, HEADS + spot, head) for spot in found]
        sums = [stats_of(held[spot, rows:, :], groups) for spot in spots]
        for pick, spot in enumerate(found):
            sums[1 + pick] = jnp.where(spot >= 0, sums[1 + pick], -jnp.inf)
        top = functools.reduce(jnp.maximum, sums)
        shares = [jnp.exp2(part - top) for part in sums]
        whole = functools.reduce(jnp.add, shares)
        sums_ref[head] = top + jnp.log2(whole)
        for group in range(groups):
            span = pl.ds(group * LANES, LANES)
            own = held[head, span, :].astype(jnp.float32)
            mixed = own
            for spot, share in zip(spots[1:], shares[1:]):
                weight = down_rows((share / whole)[group : group + 1, :])
                mixed = mixed + (held[spot, span, :].astype(jnp.float32) - own) * weight
            out_ref[head, span, :] = mixed
            result_ref[span, head_columns(head)] = mixed.astype(jnp.bfloat16)
        return carry

    lax.fori_loop(0, HEADS, one_head, 0, unroll=2)


def merge(here, picks, parts, places, shifts, slots):
    rows = parts[0].shape[1] - STAT_ROWS
    width = picks.shape[0]
    total = HEADS + len(shifts) * slots
    return call(
        functools.partial(merge_kernel, places=tuple(places), shifts=shifts, slots=slots),
        [SCALARS, SCALARS] + [pl.BlockSpec(memory_space=pl.ANY)] * len(parts),
        [
            jax.ShapeDtypeStruct((rows, HEADS * HD), jnp.bfloat16),
            jax.ShapeDtypeStruct((HEADS, rows, HD), jnp.float32),
            jax.ShapeDtypeStruct((HEADS, rows // LANES, LANES), jnp.float32),
        ],
        [IN_VMEM, IN_VMEM, IN_VMEM],
        [
            pltpu.VMEM((total, rows + STAT_ROWS, HD), jnp.bfloat16),
            pltpu.SMEM((PICKS * HEADS,), jnp.int32),
            pltpu.SMEM((width,), jnp.int32),
            pltpu.SemaphoreType.DMA((len(parts),)),
        ],
        flops=6 * HEADS * rows * HD,
        moved=2 * (HEADS * 2 + total) * rows * HD,
    )(here, picks, *parts)


def finish_kernel(here_ref, picks_ref, mixed_ref, sums_ref, *refs, shifts, slots):
    count = len(shifts)
    parts, out_ref, (heads_ref, held, sems) = refs[:count], refs[count + 1], refs[count + 2 :]
    groups = sums_ref.shape[1]
    rows = groups * LANES
    here = here_ref[0]
    for number, shift in enumerate(shifts):
        list_heads(heads_ref, number * slots, picks_ref, here, here - shift, slots)

    def slot_of(head, number):
        found = jnp.int32(-1)
        for slot in range(slots):
            found = jnp.where(heads_ref[number * slots + slot] == head, slot, found)
        return found

    def is_first(head, number):
        first = head >= 0
        for earlier in range(number):
            first = first & (slot_of(head, earlier) < 0)
        return first

    def patch(place):
        columns = head_columns(jnp.maximum(heads_ref[place], 0))
        return pltpu.make_async_copy(held.at[place], out_ref.at[:, columns], sems.at[place])

    places = [(number, number * slots + slot) for number in range(count) for slot in range(slots)]
    for number, place in places:
        head = heads_ref[place]

        @pl.when(is_first(head, number))
        def _():
            found = [slot_of(head, later) for later in range(number, count)]
            spots = [jnp.maximum(spot, 0) for spot in found]
            sums = [sums_ref[head]]
            for part, spot, safe in zip(parts[number:], found, spots):
                added = stats_of(part[safe, rows:, :], groups)
                sums.append(jnp.where(spot >= 0, added, -jnp.inf))
            top = functools.reduce(jnp.maximum, sums)
            shares = [jnp.exp2(part - top) for part in sums]
            whole = functools.reduce(jnp.add, shares)
            for group in range(groups):
                span = pl.ds(group * LANES, LANES)
                before = mixed_ref[head, span, :]
                mixed = before
                for part, spot, safe, share in zip(parts[number:], found, spots, shares[1:]):
                    new = jnp.where(spot >= 0, part[safe, span, :].astype(jnp.float32), 0.0)
                    weight = down_rows((share / whole)[group : group + 1, :])
                    mixed = mixed + (new - before) * weight
                held[place, span, :] = mixed.astype(jnp.bfloat16)
            patch(place).start()

    for number, place in places:

        @pl.when(is_first(heads_ref[place], number))
        def _():
            patch(place).wait()


def finish(here, picks, result, mixed, sums, parts, shifts, slots):
    rows = mixed.shape[1]
    total = len(shifts) * slots
    return pl.pallas_call(
        functools.partial(finish_kernel, shifts=shifts, slots=slots),
        in_specs=[SCALARS, SCALARS] + [IN_VMEM] * (2 + len(parts)) + [IN_HBM],
        out_specs=IN_HBM,
        out_shape=jax.ShapeDtypeStruct(result.shape, result.dtype),
        scratch_shapes=[
            pltpu.SMEM((total + 1,), jnp.int32),
            pltpu.VMEM((total, rows, HD), jnp.bfloat16),
            pltpu.SemaphoreType.DMA((total,)),
        ],
        input_output_aliases={4 + len(parts): 0},
        compiler_params=pltpu.CompilerParams(vmem_limit_bytes=VMEM_BYTES),
        cost_estimate=pl.CostEstimate(
            flops=2 * total * rows * HD, bytes_accessed=8 * total * rows * HD, transcendentals=0
        ),
    )(here, picks, mixed, sums, *parts, result)


def after(value, *earlier):
    return lax.optimization_barrier((value,) + earlier)[0]


def travelling_queries(queries, keys, values, picks):
    width = lax.axis_size("ctx")
    sections = lax.axis_size("pipe")
    slots = max(1, PICKS * HEADS // width)
    here = lax.axis_index("ctx").astype(jnp.int32).reshape(1)
    queries, keys, values = queries[0], keys[0], values[0]
    own_picks = picks[0].transpose(0, 2, 1)

    near_shifts = (2, width - 2)
    middle = width // 2
    far_shifts = [middle - 1, middle + 1, middle, 1, width - 1]
    final_shifts = tuple(far_shifts[2:])

    def up(value, shift):
        return lax.ppermute(value, "ctx", [(at, at + shift) for at in range(width - shift)])

    def down(value, shift):
        return lax.ppermute(value, "ctx", [(at, at - shift) for at in range(shift, width)])

    def up_and_on(value, shift):
        pairs = [
            (at * sections + section, (at + shift) * sections + (section + 1) % sections)
            for at in range(width - shift)
            for section in range(sections)
        ]
        return lax.ppermute(value, ("ctx", "pipe"), pairs)

    near_jobs = [(shift, 0, slots, True) for shift in near_shifts]
    near_sends = pack(here, own_picks, [keys, values], near_jobs, slots)
    near = [up(near_sends[0], near_shifts[0])]
    before = passed_along(own_picks, "pipe", 1)
    sends, now = {}, after(here, *near_sends)
    for shifts in (far_shifts[:2], far_shifts[2:]):
        jobs = [(shift, 0, slots, False) for shift in shifts]
        packed = pack(now, own_picks, [queries], jobs, slots)
        sends |= zip(shifts, packed)
        now = after(now, *packed)
    arrived, returned = {}, {}

    def ask_for(shift, *earlier):
        arrived[shift] = down(after(sends[shift], *earlier), shift)

    def work(token, shift, is_anchor=False):
        return attend(
            token, own_picks, keys, values, [arrived[shift]], ((shift, 0, slots),), slots, is_anchor
        )[0]

    three, five, four, one, seven = far_shifts
    ask_for(three, near_sends[0])
    ask_for(five, near_sends[0])
    own = own_part(after(now, before), queries, keys, values)
    own_back = passed_along(own, "pipe", 1)
    near.append(up(after(near_sends[1], own), near_shifts[1]))
    part_three = work(after(here, own, near[0]), three, is_anchor=True)
    returned[three] = up_and_on(part_three, three)
    part_five = work(after(here, part_three), five, is_anchor=True)
    returned[five] = up_and_on(part_five, five)
    ask_for(four, arrived[three], arrived[five], part_five, own_back, near[0])
    beside = near_part(after(here, part_five, own_back), own_picks, queries, near, near_shifts, slots)
    ask_for(one, own_back, part_five, *near)
    ask_for(seven, own_back, part_five, *near)
    beside_back = passed_along(beside, "pipe", 1)
    part_four = work(after(here, beside), four, is_anchor=True)
    returned[four] = up_and_on(part_four, four)
    part_one = work(after(here, part_four, beside_back), one)
    returned[one] = up_and_on(part_one, one)
    part_seven = work(after(here, part_one), seven)
    returned[seven] = up_and_on(part_seven, seven)
    now = after(here, part_seven)

    merged_shifts = near_shifts + (three, five)
    places = [HEADS + place * slots for place in (2, 3)]
    parts = [own_back, beside_back, returned[three], returned[five]]
    result, mixed, sums = merge(now, before, parts, [0, HEADS] + places, merged_shifts, slots)
    lasts = [returned[shift] for shift in final_shifts]
    return finish(now, before, result, mixed, sums, lasts, final_shifts, slots)[None]


def travelling_keys(queries, keys, values, picks):
    ctx_width = lax.axis_size("ctx")
    rank_here = lax.axis_index("ctx")
    slot_count = max(1, PICKS * HEADS // ctx_width)
    block_rows = queries.shape[1]
    score_scale = HD ** (-0.5)
    every_pick = picks[0].reshape(ctx_width, HEADS * PICKS)
    chosen = lax.dynamic_slice_in_dim(every_pick, rank_here, 1, 0)
    pick_order = request_table(chosen, lax.iota(jnp.int32, ctx_width), slot_count)[1]
    asked_table = request_table(every_pick, rank_here.reshape(1), slot_count)[0]
    asked_heads = asked_table[:, 0, :]
    safe_asked = jnp.maximum(asked_heads, 0)
    query_heads = queries[0].reshape(block_rows, HEADS, HD).transpose(1, 0, 2)
    key_heads = keys[0].reshape(block_rows, HEADS, HD).transpose(1, 0, 2)
    value_heads = values[0].reshape(block_rows, HEADS, HD).transpose(1, 0, 2)
    is_live = chosen[0] >= 0
    flat_slot = jnp.where(is_live, chosen[0] * slot_count + pick_order[0], 0)
    remote_mask = jnp.repeat(is_live.reshape(HEADS, PICKS), block_rows, axis=1)
    row_index = lax.iota(jnp.int32, block_rows)
    causal = row_index[:, None] >= row_index[None, :]

    def masked_scores(query_head, key_rows, mask_row):
        scores = lax.dot_general(
            query_head, key_rows, (((1,), (1,)), ((), ())), preferred_element_type=jnp.float32
        )
        allowed = jnp.concatenate(
            [causal, jnp.broadcast_to(mask_row[None, :], (block_rows, PICKS * block_rows))], axis=1
        )
        return jnp.where(allowed, scores * score_scale, -jnp.inf)

    def row_stats(scores):
        row_top = jnp.max(scores, axis=1)
        row_total = jnp.sum(jnp.exp(scores - row_top[:, None]), axis=1)
        return (row_top, row_total)

    def weighted(scores, row_top, row_total, value_rows):
        prob_rows = (jnp.exp(scores - row_top[:, None]) / row_total[:, None]).astype(jnp.bfloat16)
        return jnp.dot(prob_rows, value_rows, preferred_element_type=jnp.float32).astype(
            jnp.bfloat16
        )

    send_both = jnp.concatenate([key_heads, value_heads], axis=2)[safe_asked]
    got_slots = lax.all_to_all(send_both, "ctx", split_axis=0, concat_axis=0, tiled=True)
    last_width = 2 * HD
    flat_slots = got_slots.reshape(ctx_width * slot_count, block_rows, last_width)
    remote_both = flat_slots[flat_slot].reshape(HEADS, PICKS * block_rows, last_width)
    all_keys = jnp.concatenate([key_heads, remote_both[:, :, :HD]], axis=1)
    all_values = jnp.concatenate([value_heads, remote_both[:, :, HD:]], axis=1)

    def per_head(head_items):
        query_head, key_rows, value_rows, mask_row = head_items
        scores = masked_scores(query_head, key_rows, mask_row)
        row_top, row_total = row_stats(scores)
        return weighted(scores, row_top, row_total, value_rows)

    outputs = lax.map(per_head, (query_heads, all_keys, all_values, remote_mask))
    merged = outputs.transpose(1, 0, 2).reshape(1, block_rows, HEADS * HD)
    return passed_along(merged, "pipe", 1)


def per_device(queries, keys, values, picks):
    few_shifts = lax.axis_size("ctx") == 8
    run = travelling_queries if few_shifts else travelling_keys
    return run(queries, keys, values, picks)


def solution(mesh):
    placed = (
        P("pipe", "ctx", None),
        P("pipe", "ctx", None),
        P("pipe", "ctx", None),
        P("pipe", None, None, None),
    )
    return jax.shard_map(
        per_device, mesh=mesh, in_specs=placed, out_specs=P("pipe", "ctx", None), check_vma=False
    )
```

```python
import functools
import math

import jax
import jax.numpy as jnp
from jax import lax
from jax.experimental import pallas as pl
from jax.experimental.pallas import tpu as pltpu
from jax.sharding import PartitionSpec as P

HEADS = 16
HD = 128
PICKS = 2
EXP2_SCALE = HD ** -0.5 * math.log2(math.e)
LANES = 128
STAT_ROWS = 16
VMEM_BYTES = 24 * 1024 * 1024
HIGH_COST = 10**12


def passed_along(value, axis, steps):
    count = lax.axis_size(axis)
    pairs = [(source, (source + steps) % count) for source in range(count)]
    return lax.ppermute(value, axis, pairs)


def request_table(chosen, owners, slot_count):
    pick_count = chosen.shape[1]
    pick_ids = lax.iota(jnp.int32, pick_count)
    is_live = chosen >= 0
    earlier = pick_ids[None, :] < pick_ids[:, None]
    same_owner = (chosen[:, :, None] == chosen[:, None, :]) & earlier[None]
    pick_order = jnp.sum(same_owner.astype(jnp.int32), axis=2)
    head_ids = pick_ids // PICKS
    slot_ranks = lax.iota(jnp.int32, slot_count)
    matches = (
        is_live[:, None, None, :]
        & (chosen[:, None, None, :] == owners[None, :, None, None])
        & (pick_order[:, None, None, :] == slot_ranks[None, None, :, None])
    )
    was_found = jnp.any(matches, axis=3)
    head_table = jnp.sum(jnp.where(matches, head_ids[None, None, None, :], 0), axis=3)
    return (jnp.where(was_found, head_table, -1), pick_order)


def call(
    kernel, name_space, outputs, out_specs, scratch=(), flops=0, moved=0, exps=0
):
    return pl.pallas_call(
        kernel,
        in_specs=name_space,
        out_specs=out_specs,
        out_shape=outputs,
        scratch_shapes=list(scratch),
        compiler_params=pltpu.CompilerParams(vmem_limit_bytes=VMEM_BYTES),
        cost_estimate=pl.CostEstimate(flops=flops, bytes_accessed=moved, transcendentals=exps),
    )


SCALARS = pl.BlockSpec(memory_space=pltpu.SMEM)
IN_HBM = pl.BlockSpec(memory_space=pltpu.HBM)
IN_VMEM = pl.BlockSpec(memory_space=pltpu.VMEM)


def tick_kernel(here_ref, out_ref):
    out_ref[0] = here_ref[0]


def tick(here, *earlier):
    return call(
        tick_kernel,
        [SCALARS],
        jax.ShapeDtypeStruct((1,), jnp.int32),
        SCALARS,
        flops=0,
    )(after(here, *earlier))


def list_heads(heads_ref, start, picks_ref, block, owner, slots):
    width = picks_ref.shape[0]
    spare = heads_ref.shape[0] - 1
    for slot in range(slots):
        heads_ref[start + slot] = -1
    valid = (block >= 0) & (block < width) & (owner >= 0) & (owner < width)
    row = jnp.clip(block, 0, width - 1)
    wanted = jnp.where(valid, owner, -2)
    found = jnp.int32(0)
    for pick in range(PICKS):
        for head in range(HEADS):
            hit = picks_ref[row, pick, head] == wanted
            heads_ref[jnp.where(hit, start + found, spare)] = head
            found = found + hit.astype(jnp.int32)


def pack_kernel(here_ref, picks_ref, *refs, jobs, slots):
    is_near = jobs[0][3]
    sources = refs[: 1 + is_near]
    outputs = refs[1 + is_near : 1 + is_near + len(jobs)]
    heads_ref, sems = refs[-2], refs[-1]
    here = here_ref[0]
    listed = {}
    for shift, first, count, is_near in jobs:
        key = (shift, is_near)
        if key not in listed:
            listed[key] = len(listed) * slots
            block, owner = (here + shift, here) if is_near else (here, here - shift)
            list_heads(heads_ref, listed[key], picks_ref, block, owner, slots)
    copies = []
    for (shift, first, count, is_near), output in zip(jobs, outputs):
        for slot in range(count):
            head = jnp.maximum(heads_ref[listed[shift, is_near] + first + slot], 0)
            columns = pl.ds(pl.multiple_of(head * HD, HD), HD)
            for place, source in enumerate(sources):
                target = output.at[2 * slot + place if is_near else slot]
                copy = pltpu.make_async_copy(
                    source.at[:, columns], target, sems.at[len(copies)]
                )
                copy.start()
                copies.append(copy)
    for copy in copies:
        copy.wait()


def pack(here, picks, sources, jobs, slots):
    rows = sources[0].shape[0]
    sizes = [len(sources) * count for _, _, count, _ in jobs]
    return call(
        functools.partial(pack_kernel, jobs=jobs, slots=slots),
        [SCALARS, SCALARS] + [IN_VMEM] * len(sources),
        [jax.ShapeDtypeStruct((size, rows, HD), jnp.bfloat16) for size in sizes],
        [IN_VMEM] * len(sizes),
        [pltpu.SMEM((len(jobs) * slots + 1,), jnp.int32), pltpu.SemaphoreType.DMA((sum(sizes),))],
        moved=4 * rows * HD * sum(sizes),
    )(here, picks, *sources)


def diagonal():
    shape = (LANES, LANES)
    return lax.broadcasted_iota(jnp.int32, shape, 0) == lax.broadcasted_iota(jnp.int32, shape, 1)


def raw_scores(query_rows, key_rows):
    return lax.dot_general(
        query_rows, key_rows, (((1,), (1,)), ((), ())), preferred_element_type=jnp.float32
    )


def with_ones(value_rows):
    return jnp.concatenate([value_rows, jnp.ones_like(value_rows)], axis=1)


def soft_part(scores, value_rows):
    top = jnp.max(scores, axis=1, keepdims=True)
    weights = jnp.exp2((scores - top) * EXP2_SCALE).astype(jnp.bfloat16)
    total = jnp.dot(weights, value_rows, preferred_element_type=jnp.float32)
    sums = total[:, HD:]
    return total[:, :HD] * pl.reciprocal(sums), top * EXP2_SCALE, sums


def across_lanes(column):
    eye = diagonal()
    spread = jnp.broadcast_to(column, (column.shape[0], LANES))
    return [
        jnp.sum(jnp.where(eye, spread[at : at + LANES], 0.0), axis=0, keepdims=True)
        for at in range(0, column.shape[0], LANES)
    ]


def down_rows(line):
    spread = jnp.broadcast_to(line, (LANES, LANES))
    return jnp.sum(jnp.where(diagonal(), spread, 0.0), axis=1, keepdims=True)


def three_parts(stats):
    first = stats.astype(jnp.bfloat16).astype(jnp.float32)
    second = (stats - first).astype(jnp.bfloat16).astype(jnp.float32)
    third = stats - first - second
    parts = jnp.concatenate([first, second, third], axis=0)
    pad = jnp.zeros((STAT_ROWS - parts.shape[0], LANES), jnp.float32)
    return jnp.concatenate([parts, pad], axis=0).astype(jnp.bfloat16)


def stats_of(block, groups):
    stats = block.astype(jnp.float32)
    return stats[:groups] + stats[groups : 2 * groups] + stats[2 * groups : 3 * groups]


def log_sums(tops, sums):
    top_lines = [line for top in tops for line in across_lanes(top)]
    sum_lines = [line for part in sums for line in across_lanes(part)]
    return jnp.concatenate(top_lines, axis=0) + jnp.log2(jnp.concatenate(sum_lines, axis=0))


def attend_rows(query_rows, key_rows, value_rows, tile):
    found = [
        soft_part(raw_scores(query_rows[at : at + tile], key_rows), value_rows)
        for at in range(0, query_rows.shape[0], tile)
    ]
    outputs, tops, sums = zip(*found)
    return jnp.concatenate(outputs, axis=0), log_sums(tops, sums)


def head_columns(head):
    return pl.ds(pl.multiple_of(head * HD, HD), HD)


def attend_kernel(here_ref, picks_ref, key_ref, value_ref, *refs, group, slots):
    heads_ref = refs[-1]
    here = here_ref[0]
    for number, (shift, first, count) in enumerate(group):
        query_ref, out_ref = refs[number], refs[len(group) + number]
        rows = query_ref.shape[1]
        list_heads(heads_ref, 0, picks_ref, here + shift, here, slots)
        for slot in range(count):
            columns = head_columns(jnp.maximum(heads_ref[first + slot], 0))
            outputs, lines = attend_rows(
                query_ref[slot], key_ref[:, columns], with_ones(value_ref[:, columns]), rows
            )
            out_ref[slot, :rows, :] = outputs.astype(jnp.bfloat16)
            out_ref[slot, rows:, :] = three_parts(lines)


def attend(here, picks, keys, values, arrived, group, slots, is_anchor):
    rows = keys.shape[0]
    total = sum(count for _, _, count in group)
    return call(
        functools.partial(attend_kernel, group=group, slots=slots),
        [SCALARS, SCALARS, IN_VMEM, IN_VMEM] + [IN_VMEM] * len(group),
        [
            jax.ShapeDtypeStruct((count, rows + STAT_ROWS, HD), jnp.bfloat16)
            for _, _, count in group
        ],
        [IN_VMEM] * len(group),
        [pltpu.SMEM((slots + 1,), jnp.int32)],
        flops=HIGH_COST if is_anchor else 4 * total * rows * rows * HD,
        moved=8 * total * rows * HD,
        exps=total * rows * rows,
    )(here, picks, keys, values, *arrived)


def own_kernel(here_ref, query_ref, key_ref, value_ref, out_ref):
    rows = query_ref.shape[0]
    tile = min(rows, 256)

    def one_head(head, carry):
        columns = head_columns(head)
        value_rows = with_ones(value_ref[:, columns])
        tops, all_sums = [], []
        for at in range(0, rows, tile):
            reach = at + tile
            scores = raw_scores(query_ref[at:reach, columns], key_ref[:reach, columns])
            row_ids = lax.broadcasted_iota(jnp.int32, scores.shape, 0) + at
            seen = row_ids >= lax.broadcasted_iota(jnp.int32, scores.shape, 1)
            outputs, top, sums = soft_part(jnp.where(seen, scores, -jnp.inf), value_rows[:reach])
            out_ref[head, at:reach, :] = outputs.astype(jnp.bfloat16)
            tops.append(top)
            all_sums.append(sums)
        out_ref[head, rows:, :] = three_parts(log_sums(tops, all_sums))
        return carry

    lax.fori_loop(0, HEADS, one_head, 0, unroll=4)


def own_part(here, queries, keys, values):
    rows = queries.shape[0]
    return call(
        own_kernel,
        [SCALARS, IN_VMEM, IN_VMEM, IN_VMEM],
        jax.ShapeDtypeStruct((HEADS, rows + STAT_ROWS, HD), jnp.bfloat16),
        IN_VMEM,
        flops=4 * HEADS * rows * rows * HD,
        moved=8 * HEADS * rows * HD,
        exps=HEADS * rows * rows,
    )(here, queries, keys, values)


def near_kernel(here_ref, picks_ref, query_ref, *refs, shifts, slots):
    near_refs, out_ref, heads_ref = refs[: len(shifts)], refs[-2], refs[-1]
    rows = query_ref.shape[0]
    here = here_ref[0]
    for place, (shift, near_ref) in enumerate(zip(shifts, near_refs)):
        list_heads(heads_ref, 0, picks_ref, here, here - shift, slots)
        for slot in range(slots):
            columns = head_columns(jnp.maximum(heads_ref[slot], 0))
            outputs, lines = attend_rows(
                query_ref[:, columns], near_ref[2 * slot], with_ones(near_ref[2 * slot + 1]), rows
            )
            out_ref[place * slots + slot, :rows, :] = outputs.astype(jnp.bfloat16)
            out_ref[place * slots + slot, rows:, :] = three_parts(lines)


def near_part(here, picks, queries, near, shifts, slots):
    rows = queries.shape[0]
    total = len(shifts) * slots
    return call(
        functools.partial(near_kernel, shifts=shifts, slots=slots),
        [SCALARS, SCALARS, IN_VMEM] + [IN_VMEM] * len(shifts),
        jax.ShapeDtypeStruct((total, rows + STAT_ROWS, HD), jnp.bfloat16),
        IN_VMEM,
        [pltpu.SMEM((slots + 1,), jnp.int32)],
        flops=HIGH_COST,
        moved=12 * total * rows * HD,
        exps=total * rows * rows,
    )(here, picks, queries, *near)


def find_spots(spots_ref, found_ref, picks_ref, here, shifts, slots):
    for owner in range(picks_ref.shape[0]):
        found_ref[owner] = 0

    for pick in range(PICKS):
        for head in range(HEADS):
            owner = picks_ref[here, pick, head]
            safe = jnp.maximum(owner, 0)
            order = found_ref[safe]
            found_ref[safe] = order + (owner >= 0).astype(jnp.int32)
            spot = jnp.int32(-1)
            for place, shift in enumerate(shifts):
                spot = jnp.where(here - safe == shift, place * slots + order, spot)
            spots_ref[head * PICKS + pick] = jnp.where(owner >= 0, spot, -1)


def merge_kernel(here_ref, picks_ref, *refs, places, shifts, slots):
    count = len(places)
    parts = refs[:count]
    result_ref, out_ref, sums_ref, held, spots_ref, found_ref, sems = refs[count:]
    groups = sums_ref.shape[1]
    rows = groups * LANES
    copies = [
        pltpu.make_async_copy(part, held.at[pl.ds(place, part.shape[0])], sems.at[number])
        for number, (part, place) in enumerate(zip(parts, places))
    ]
    for copy in copies:
        copy.start()
    find_spots(spots_ref, found_ref, picks_ref, here_ref[0], shifts, slots)
    for copy in copies:
        copy.wait()

    def one_head(head, carry):
        found = [spots_ref[head * PICKS + pick] for pick in range(PICKS)]
        spots = [head] + [jnp.where(spot >= 0, HEADS + spot, head) for spot in found]
        sums = [stats_of(held[spot, rows:, :], groups) for spot in spots]
        for pick, spot in enumerate(found):
            sums[1 + pick] = jnp.where(spot >= 0, sums[1 + pick], -jnp.inf)
        top = functools.reduce(jnp.maximum, sums)
        shares = [jnp.exp2(part - top) for part in sums]
        whole = functools.reduce(jnp.add, shares)
        sums_ref[head] = top + jnp.log2(whole)
        for group in range(groups):
            span = pl.ds(group * LANES, LANES)
            own = held[head, span, :].astype(jnp.float32)
            mixed = own
            for spot, share in zip(spots[1:], shares[1:]):
                weight = down_rows((share / whole)[group : group + 1, :])
                mixed = mixed + (held[spot, span, :].astype(jnp.float32) - own) * weight
            out_ref[head, span, :] = mixed
            result_ref[span, head_columns(head)] = mixed.astype(jnp.bfloat16)
        return carry

    lax.fori_loop(0, HEADS, one_head, 0, unroll=2)


def merge(here, picks, parts, places, shifts, slots):
    rows = parts[0].shape[1] - STAT_ROWS
    width = picks.shape[0]
    total = HEADS + len(shifts) * slots
    return call(
        functools.partial(merge_kernel, places=tuple(places), shifts=shifts, slots=slots),
        [SCALARS, SCALARS] + [pl.BlockSpec(memory_space=pl.ANY)] * len(parts),
        [
            jax.ShapeDtypeStruct((rows, HEADS * HD), jnp.bfloat16),
            jax.ShapeDtypeStruct((HEADS, rows, HD), jnp.float32),
            jax.ShapeDtypeStruct((HEADS, rows // LANES, LANES), jnp.float32),
        ],
        [IN_VMEM, IN_VMEM, IN_VMEM],
        [
            pltpu.VMEM((total, rows + STAT_ROWS, HD), jnp.bfloat16),
            pltpu.SMEM((PICKS * HEADS,), jnp.int32),
            pltpu.SMEM((width,), jnp.int32),
            pltpu.SemaphoreType.DMA((len(parts),)),
        ],
        flops=6 * HEADS * rows * HD,
        moved=2 * (HEADS * 2 + total) * rows * HD,
    )(here, picks, *parts)


def finish_kernel(here_ref, picks_ref, mixed_ref, sums_ref, *refs, shifts, slots):
    count = len(shifts)
    parts, out_ref, (heads_ref, held, sems) = refs[:count], refs[count + 1], refs[count + 2 :]
    groups = sums_ref.shape[1]
    rows = groups * LANES
    here = here_ref[0]
    for number, shift in enumerate(shifts):
        list_heads(heads_ref, number * slots, picks_ref, here, here - shift, slots)

    def slot_of(head, number):
        found = jnp.int32(-1)
        for slot in range(slots):
            found = jnp.where(heads_ref[number * slots + slot] == head, slot, found)
        return found

    def is_first(head, number):
        first = head >= 0
        for earlier in range(number):
            first = first & (slot_of(head, earlier) < 0)
        return first

    def patch(place):
        columns = head_columns(jnp.maximum(heads_ref[place], 0))
        return pltpu.make_async_copy(held.at[place], out_ref.at[:, columns], sems.at[place])

    places = [(number, number * slots + slot) for number in range(count) for slot in range(slots)]
    for number, place in places:
        head = heads_ref[place]

        @pl.when(is_first(head, number))
        def _():
            found = [slot_of(head, later) for later in range(number, count)]
            spots = [jnp.maximum(spot, 0) for spot in found]
            sums = [sums_ref[head]]
            for part, spot, safe in zip(parts[number:], found, spots):
                added = stats_of(part[safe, rows:, :], groups)
                sums.append(jnp.where(spot >= 0, added, -jnp.inf))
            top = functools.reduce(jnp.maximum, sums)
            shares = [jnp.exp2(part - top) for part in sums]
            whole = functools.reduce(jnp.add, shares)
            for group in range(groups):
                span = pl.ds(group * LANES, LANES)
                before = mixed_ref[head, span, :]
                mixed = before
                for part, spot, safe, share in zip(parts[number:], found, spots, shares[1:]):
                    new = jnp.where(spot >= 0, part[safe, span, :].astype(jnp.float32), 0.0)
                    weight = down_rows((share / whole)[group : group + 1, :])
                    mixed = mixed + (new - before) * weight
                held[place, span, :] = mixed.astype(jnp.bfloat16)
            patch(place).start()

    for number, place in places:

        @pl.when(is_first(heads_ref[place], number))
        def _():
            patch(place).wait()


def finish(here, picks, result, mixed, sums, parts, shifts, slots):
    rows = mixed.shape[1]
    total = len(shifts) * slots
    return pl.pallas_call(
        functools.partial(finish_kernel, shifts=shifts, slots=slots),
        in_specs=[SCALARS, SCALARS] + [IN_VMEM] * (2 + len(parts)) + [IN_HBM],
        out_specs=IN_HBM,
        out_shape=jax.ShapeDtypeStruct(result.shape, result.dtype),
        scratch_shapes=[
            pltpu.SMEM((total + 1,), jnp.int32),
            pltpu.VMEM((total, rows, HD), jnp.bfloat16),
            pltpu.SemaphoreType.DMA((total,)),
        ],
        input_output_aliases={4 + len(parts): 0},
        compiler_params=pltpu.CompilerParams(vmem_limit_bytes=VMEM_BYTES),
        cost_estimate=pl.CostEstimate(
            flops=2 * total * rows * HD, bytes_accessed=8 * total * rows * HD, transcendentals=0
        ),
    )(here, picks, mixed, sums, *parts, result)


def after(value, *earlier):
    return lax.optimization_barrier((value,) + earlier)[0]


def travelling_queries(queries, keys, values, picks):
    width = lax.axis_size("ctx")
    sections = lax.axis_size("pipe")
    slots = max(1, PICKS * HEADS // width)
    here = lax.axis_index("ctx").astype(jnp.int32).reshape(1)
    queries, keys, values = queries[0], keys[0], values[0]
    own_picks = picks[0].transpose(0, 2, 1)

    near_shifts = (2, width - 2)
    middle = width // 2
    far_shifts = [middle - 1, middle + 1, middle, 1, width - 1]
    final_shifts = tuple(far_shifts[2:])

    def up(value, shift):
        return lax.ppermute(value, "ctx", [(at, at + shift) for at in range(width - shift)])

    def down(value, shift):
        return lax.ppermute(value, "ctx", [(at, at - shift) for at in range(shift, width)])

    def up_and_on(value, shift):
        pairs = [
            (at * sections + section, (at + shift) * sections + (section + 1) % sections)
            for at in range(width - shift)
            for section in range(sections)
        ]
        return lax.ppermute(value, ("ctx", "pipe"), pairs)

    near_jobs = [(shift, 0, slots, True) for shift in near_shifts]
    near_sends = pack(here, own_picks, [keys, values], near_jobs, slots)
    near = [up(near_sends[0], near_shifts[0])]
    before = passed_along(own_picks, "pipe", 1)
    sends, now = {}, after(here, *near_sends)
    for shifts in (far_shifts[:2], far_shifts[2:]):
        jobs = [(shift, 0, slots, False) for shift in shifts]
        packed = pack(now, own_picks, [queries], jobs, slots)
        sends |= zip(shifts, packed)
        now = after(now, *packed)
    arrived, returned = {}, {}

    def ask_for(shift, *earlier):
        arrived[shift] = down(after(sends[shift], *earlier), shift)

    def work(token, shift, is_anchor=False):
        return attend(
            token, own_picks, keys, values, [arrived[shift]], ((shift, 0, slots),), slots, is_anchor
        )[0]

    three, five, four, one, seven = far_shifts
    ask_for(three, near_sends[0])
    ask_for(five, near_sends[0])
    own = own_part(after(now, before), queries, keys, values)
    own_back = passed_along(own, "pipe", 1)
    near.append(up(after(near_sends[1], own), near_shifts[1]))
    part_three = work(after(here, own, near[0]), three, is_anchor=True)
    returned[three] = up_and_on(part_three, three)
    part_five = work(after(here, part_three), five, is_anchor=True)
    returned[five] = up_and_on(part_five, five)
    ask_for(one, arrived[three], arrived[five], part_five)
    ask_for(four, arrived[three], arrived[five], part_five, own_back, near[0])
    beside = near_part(after(here, part_five, own_back), own_picks, queries, near, near_shifts, slots)
    ask_for(seven, own_back, part_five, *near)
    beside_back = passed_along(beside, "pipe", 1)
    part_one = work(after(here, beside), one, is_anchor=True)
    returned[one] = up_and_on(part_one, one)
    part_four = work(after(here, part_one, beside_back), four)
    returned[four] = up_and_on(part_four, four)
    part_seven = work(after(here, part_four), seven)
    returned[seven] = up_and_on(part_seven, seven)
    now = after(here, part_seven)

    merged_shifts = near_shifts + (three, five)
    places = [HEADS + place * slots for place in (2, 3)]
    parts = [own_back, beside_back, returned[three], returned[five]]
    result, mixed, sums = merge(now, before, parts, [0, HEADS] + places, merged_shifts, slots)
    lasts = [returned[shift] for shift in final_shifts]
    return finish(now, before, result, mixed, sums, lasts, final_shifts, slots)[None]


def travelling_keys(queries, keys, values, picks):
    ctx_width = lax.axis_size("ctx")
    rank_here = lax.axis_index("ctx")
    slot_count = max(1, PICKS * HEADS // ctx_width)
    block_rows = queries.shape[1]
    score_scale = HD ** (-0.5)
    every_pick = picks[0].reshape(ctx_width, HEADS * PICKS)
    chosen = lax.dynamic_slice_in_dim(every_pick, rank_here, 1, 0)
    pick_order = request_table(chosen, lax.iota(jnp.int32, ctx_width), slot_count)[1]
    asked_table = request_table(every_pick, rank_here.reshape(1), slot_count)[0]
    asked_heads = asked_table[:, 0, :]
    safe_asked = jnp.maximum(asked_heads, 0)
    query_heads = queries[0].reshape(block_rows, HEADS, HD).transpose(1, 0, 2)
    key_heads = keys[0].reshape(block_rows, HEADS, HD).transpose(1, 0, 2)
    value_heads = values[0].reshape(block_rows, HEADS, HD).transpose(1, 0, 2)
    is_live = chosen[0] >= 0
    flat_slot = jnp.where(is_live, chosen[0] * slot_count + pick_order[0], 0)
    remote_mask = jnp.repeat(is_live.reshape(HEADS, PICKS), block_rows, axis=1)
    row_index = lax.iota(jnp.int32, block_rows)
    causal = row_index[:, None] >= row_index[None, :]

    def masked_scores(query_head, key_rows, mask_row):
        scores = lax.dot_general(
            query_head, key_rows, (((1,), (1,)), ((), ())), preferred_element_type=jnp.float32
        )
        allowed = jnp.concatenate(
            [causal, jnp.broadcast_to(mask_row[None, :], (block_rows, PICKS * block_rows))], axis=1
        )
        return jnp.where(allowed, scores * score_scale, -jnp.inf)

    def row_stats(scores):
        row_top = jnp.max(scores, axis=1)
        row_total = jnp.sum(jnp.exp(scores - row_top[:, None]), axis=1)
        return (row_top, row_total)

    def weighted(scores, row_top, row_total, value_rows):
        prob_rows = (jnp.exp(scores - row_top[:, None]) / row_total[:, None]).astype(jnp.bfloat16)
        return jnp.dot(prob_rows, value_rows, preferred_element_type=jnp.float32).astype(
            jnp.bfloat16
        )

    send_both = jnp.concatenate([key_heads, value_heads], axis=2)[safe_asked]
    got_slots = lax.all_to_all(send_both, "ctx", split_axis=0, concat_axis=0, tiled=True)
    last_width = 2 * HD
    flat_slots = got_slots.reshape(ctx_width * slot_count, block_rows, last_width)
    remote_both = flat_slots[flat_slot].reshape(HEADS, PICKS * block_rows, last_width)
    all_keys = jnp.concatenate([key_heads, remote_both[:, :, :HD]], axis=1)
    all_values = jnp.concatenate([value_heads, remote_both[:, :, HD:]], axis=1)

    def per_head(head_items):
        query_head, key_rows, value_rows, mask_row = head_items
        scores = masked_scores(query_head, key_rows, mask_row)
        row_top, row_total = row_stats(scores)
        return weighted(scores, row_top, row_total, value_rows)

    outputs = lax.map(per_head, (query_heads, all_keys, all_values, remote_mask))
    merged = outputs.transpose(1, 0, 2).reshape(1, block_rows, HEADS * HD)
    return passed_along(merged, "pipe", 1)


def per_device(queries, keys, values, picks):
    few_shifts = lax.axis_size("ctx") == 8
    run = travelling_queries if few_shifts else travelling_keys
    return run(queries, keys, values, picks)


def solution(mesh):
    placed = (
        P("pipe", "ctx", None),
        P("pipe", "ctx", None),
        P("pipe", "ctx", None),
        P("pipe", None, None, None),
    )
    return jax.shard_map(
        per_device, mesh=mesh, in_specs=placed, out_specs=P("pipe", "ctx", None), check_vma=False
    )
```

```python
import functools
import math

import jax
import jax.numpy as jnp
from jax import lax
from jax.experimental import pallas as pl
from jax.experimental.pallas import tpu as pltpu
from jax.sharding import PartitionSpec as P

HEADS = 16
HD = 128
PICKS = 2
EXP2_SCALE = HD ** -0.5 * math.log2(math.e)
LANES = 128
STAT_ROWS = 16
VMEM_BYTES = 24 * 1024 * 1024
HIGH_COST = 10**12


def passed_along(value, axis, steps):
    count = lax.axis_size(axis)
    pairs = [(source, (source + steps) % count) for source in range(count)]
    return lax.ppermute(value, axis, pairs)


def request_table(chosen, owners, slot_count):
    pick_count = chosen.shape[1]
    pick_ids = lax.iota(jnp.int32, pick_count)
    is_live = chosen >= 0
    earlier = pick_ids[None, :] < pick_ids[:, None]
    same_owner = (chosen[:, :, None] == chosen[:, None, :]) & earlier[None]
    pick_order = jnp.sum(same_owner.astype(jnp.int32), axis=2)
    head_ids = pick_ids // PICKS
    slot_ranks = lax.iota(jnp.int32, slot_count)
    matches = (
        is_live[:, None, None, :]
        & (chosen[:, None, None, :] == owners[None, :, None, None])
        & (pick_order[:, None, None, :] == slot_ranks[None, None, :, None])
    )
    was_found = jnp.any(matches, axis=3)
    head_table = jnp.sum(jnp.where(matches, head_ids[None, None, None, :], 0), axis=3)
    return (jnp.where(was_found, head_table, -1), pick_order)


def call(
    kernel, name_space, outputs, out_specs, scratch=(), flops=0, moved=0, exps=0
):
    return pl.pallas_call(
        kernel,
        in_specs=name_space,
        out_specs=out_specs,
        out_shape=outputs,
        scratch_shapes=list(scratch),
        compiler_params=pltpu.CompilerParams(vmem_limit_bytes=VMEM_BYTES),
        cost_estimate=pl.CostEstimate(flops=flops, bytes_accessed=moved, transcendentals=exps),
    )


SCALARS = pl.BlockSpec(memory_space=pltpu.SMEM)
IN_HBM = pl.BlockSpec(memory_space=pltpu.HBM)
IN_VMEM = pl.BlockSpec(memory_space=pltpu.VMEM)


def tick_kernel(here_ref, out_ref):
    out_ref[0] = here_ref[0]


def tick(here, *earlier):
    return call(
        tick_kernel,
        [SCALARS],
        jax.ShapeDtypeStruct((1,), jnp.int32),
        SCALARS,
        flops=0,
    )(after(here, *earlier))


def list_heads(heads_ref, start, picks_ref, block, owner, slots):
    width = picks_ref.shape[0]
    spare = heads_ref.shape[0] - 1
    for slot in range(slots):
        heads_ref[start + slot] = -1
    valid = (block >= 0) & (block < width) & (owner >= 0) & (owner < width)
    row = jnp.clip(block, 0, width - 1)
    wanted = jnp.where(valid, owner, -2)
    found = jnp.int32(0)
    for pick in range(PICKS):
        for head in range(HEADS):
            hit = picks_ref[row, pick, head] == wanted
            heads_ref[jnp.where(hit, start + found, spare)] = head
            found = found + hit.astype(jnp.int32)


def pack_kernel(here_ref, picks_ref, *refs, jobs, slots):
    is_near = jobs[0][3]
    sources = refs[: 1 + is_near]
    outputs = refs[1 + is_near : 1 + is_near + len(jobs)]
    heads_ref, sems = refs[-2], refs[-1]
    here = here_ref[0]
    listed = {}
    for shift, first, count, is_near in jobs:
        key = (shift, is_near)
        if key not in listed:
            listed[key] = len(listed) * slots
            block, owner = (here + shift, here) if is_near else (here, here - shift)
            list_heads(heads_ref, listed[key], picks_ref, block, owner, slots)
    copies = []
    for (shift, first, count, is_near), output in zip(jobs, outputs):
        for slot in range(count):
            head = jnp.maximum(heads_ref[listed[shift, is_near] + first + slot], 0)
            columns = pl.ds(pl.multiple_of(head * HD, HD), HD)
            for place, source in enumerate(sources):
                target = output.at[2 * slot + place if is_near else slot]
                copy = pltpu.make_async_copy(
                    source.at[:, columns], target, sems.at[len(copies)]
                )
                copy.start()
                copies.append(copy)
    for copy in copies:
        copy.wait()


def pack(here, picks, sources, jobs, slots):
    rows = sources[0].shape[0]
    sizes = [len(sources) * count for _, _, count, _ in jobs]
    return call(
        functools.partial(pack_kernel, jobs=jobs, slots=slots),
        [SCALARS, SCALARS] + [IN_VMEM] * len(sources),
        [jax.ShapeDtypeStruct((size, rows, HD), jnp.bfloat16) for size in sizes],
        [IN_VMEM] * len(sizes),
        [pltpu.SMEM((len(jobs) * slots + 1,), jnp.int32), pltpu.SemaphoreType.DMA((sum(sizes),))],
        moved=4 * rows * HD * sum(sizes),
    )(here, picks, *sources)


def diagonal():
    shape = (LANES, LANES)
    return lax.broadcasted_iota(jnp.int32, shape, 0) == lax.broadcasted_iota(jnp.int32, shape, 1)


def raw_scores(query_rows, key_rows):
    return lax.dot_general(
        query_rows, key_rows, (((1,), (1,)), ((), ())), preferred_element_type=jnp.float32
    )


def with_ones(value_rows):
    return jnp.concatenate([value_rows, jnp.ones_like(value_rows)], axis=1)


def soft_part(scores, value_rows):
    top = jnp.max(scores, axis=1, keepdims=True)
    weights = jnp.exp2((scores - top) * EXP2_SCALE).astype(jnp.bfloat16)
    total = jnp.dot(weights, value_rows, preferred_element_type=jnp.float32)
    sums = total[:, HD:]
    return total[:, :HD] * pl.reciprocal(sums), top * EXP2_SCALE, sums


def across_lanes(column):
    eye = diagonal()
    spread = jnp.broadcast_to(column, (column.shape[0], LANES))
    return [
        jnp.sum(jnp.where(eye, spread[at : at + LANES], 0.0), axis=0, keepdims=True)
        for at in range(0, column.shape[0], LANES)
    ]


def down_rows(line):
    spread = jnp.broadcast_to(line, (LANES, LANES))
    return jnp.sum(jnp.where(diagonal(), spread, 0.0), axis=1, keepdims=True)


def three_parts(stats):
    first = stats.astype(jnp.bfloat16).astype(jnp.float32)
    second = (stats - first).astype(jnp.bfloat16).astype(jnp.float32)
    third = stats - first - second
    parts = jnp.concatenate([first, second, third], axis=0)
    pad = jnp.zeros((STAT_ROWS - parts.shape[0], LANES), jnp.float32)
    return jnp.concatenate([parts, pad], axis=0).astype(jnp.bfloat16)


def stats_of(block, groups):
    stats = block.astype(jnp.float32)
    return stats[:groups] + stats[groups : 2 * groups] + stats[2 * groups : 3 * groups]


def log_sums(tops, sums):
    top_lines = [line for top in tops for line in across_lanes(top)]
    sum_lines = [line for part in sums for line in across_lanes(part)]
    return jnp.concatenate(top_lines, axis=0) + jnp.log2(jnp.concatenate(sum_lines, axis=0))


def attend_rows(query_rows, key_rows, value_rows, tile):
    found = [
        soft_part(raw_scores(query_rows[at : at + tile], key_rows), value_rows)
        for at in range(0, query_rows.shape[0], tile)
    ]
    outputs, tops, sums = zip(*found)
    return jnp.concatenate(outputs, axis=0), log_sums(tops, sums)


def head_columns(head):
    return pl.ds(pl.multiple_of(head * HD, HD), HD)


def attend_kernel(here_ref, picks_ref, key_ref, value_ref, *refs, group, slots):
    heads_ref = refs[-1]
    here = here_ref[0]
    for number, (shift, first, count) in enumerate(group):
        query_ref, out_ref = refs[number], refs[len(group) + number]
        rows = query_ref.shape[1]
        list_heads(heads_ref, 0, picks_ref, here + shift, here, slots)
        for slot in range(count):
            columns = head_columns(jnp.maximum(heads_ref[first + slot], 0))
            outputs, lines = attend_rows(
                query_ref[slot], key_ref[:, columns], with_ones(value_ref[:, columns]), rows
            )
            out_ref[slot, :rows, :] = outputs.astype(jnp.bfloat16)
            out_ref[slot, rows:, :] = three_parts(lines)


def attend(here, picks, keys, values, arrived, group, slots, is_anchor):
    rows = keys.shape[0]
    total = sum(count for _, _, count in group)
    return call(
        functools.partial(attend_kernel, group=group, slots=slots),
        [SCALARS, SCALARS, IN_VMEM, IN_VMEM] + [IN_VMEM] * len(group),
        [
            jax.ShapeDtypeStruct((count, rows + STAT_ROWS, HD), jnp.bfloat16)
            for _, _, count in group
        ],
        [IN_VMEM] * len(group),
        [pltpu.SMEM((slots + 1,), jnp.int32)],
        flops=HIGH_COST if is_anchor else 4 * total * rows * rows * HD,
        moved=8 * total * rows * HD,
        exps=total * rows * rows,
    )(here, picks, keys, values, *arrived)


def own_kernel(here_ref, query_ref, key_ref, value_ref, out_ref):
    rows = query_ref.shape[0]
    tile = min(rows, 256)

    def one_head(head, carry):
        columns = head_columns(head)
        value_rows = with_ones(value_ref[:, columns])
        tops, all_sums = [], []
        for at in range(0, rows, tile):
            reach = at + tile
            scores = raw_scores(query_ref[at:reach, columns], key_ref[:reach, columns])
            row_ids = lax.broadcasted_iota(jnp.int32, scores.shape, 0) + at
            seen = row_ids >= lax.broadcasted_iota(jnp.int32, scores.shape, 1)
            outputs, top, sums = soft_part(jnp.where(seen, scores, -jnp.inf), value_rows[:reach])
            out_ref[head, at:reach, :] = outputs.astype(jnp.bfloat16)
            tops.append(top)
            all_sums.append(sums)
        out_ref[head, rows:, :] = three_parts(log_sums(tops, all_sums))
        return carry

    lax.fori_loop(0, HEADS, one_head, 0, unroll=4)


def own_part(here, queries, keys, values):
    rows = queries.shape[0]
    return call(
        own_kernel,
        [SCALARS, IN_VMEM, IN_VMEM, IN_VMEM],
        jax.ShapeDtypeStruct((HEADS, rows + STAT_ROWS, HD), jnp.bfloat16),
        IN_VMEM,
        flops=4 * HEADS * rows * rows * HD,
        moved=8 * HEADS * rows * HD,
        exps=HEADS * rows * rows,
    )(here, queries, keys, values)


def near_kernel(here_ref, picks_ref, query_ref, *refs, shifts, slots):
    near_refs, out_ref, heads_ref = refs[: len(shifts)], refs[-2], refs[-1]
    rows = query_ref.shape[0]
    here = here_ref[0]
    for place, (shift, near_ref) in enumerate(zip(shifts, near_refs)):
        list_heads(heads_ref, 0, picks_ref, here, here - shift, slots)
        for slot in range(slots):
            columns = head_columns(jnp.maximum(heads_ref[slot], 0))
            outputs, lines = attend_rows(
                query_ref[:, columns], near_ref[2 * slot], with_ones(near_ref[2 * slot + 1]), rows
            )
            out_ref[place * slots + slot, :rows, :] = outputs.astype(jnp.bfloat16)
            out_ref[place * slots + slot, rows:, :] = three_parts(lines)


def near_part(here, picks, queries, near, shifts, slots):
    rows = queries.shape[0]
    total = len(shifts) * slots
    return call(
        functools.partial(near_kernel, shifts=shifts, slots=slots),
        [SCALARS, SCALARS, IN_VMEM] + [IN_VMEM] * len(shifts),
        jax.ShapeDtypeStruct((total, rows + STAT_ROWS, HD), jnp.bfloat16),
        IN_VMEM,
        [pltpu.SMEM((slots + 1,), jnp.int32)],
        flops=HIGH_COST,
        moved=12 * total * rows * HD,
        exps=total * rows * rows,
    )(here, picks, queries, *near)


def find_spots(spots_ref, found_ref, picks_ref, here, shifts, slots):
    for owner in range(picks_ref.shape[0]):
        found_ref[owner] = 0

    for pick in range(PICKS):
        for head in range(HEADS):
            owner = picks_ref[here, pick, head]
            safe = jnp.maximum(owner, 0)
            order = found_ref[safe]
            found_ref[safe] = order + (owner >= 0).astype(jnp.int32)
            spot = jnp.int32(-1)
            for place, shift in enumerate(shifts):
                spot = jnp.where(here - safe == shift, place * slots + order, spot)
            spots_ref[head * PICKS + pick] = jnp.where(owner >= 0, spot, -1)


def merge_kernel(here_ref, picks_ref, *refs, places, shifts, slots):
    count = len(places)
    parts = refs[:count]
    result_ref, out_ref, sums_ref, held, spots_ref, found_ref, sems = refs[count:]
    groups = sums_ref.shape[1]
    rows = groups * LANES
    copies = [
        pltpu.make_async_copy(part, held.at[pl.ds(place, part.shape[0])], sems.at[number])
        for number, (part, place) in enumerate(zip(parts, places))
    ]
    for copy in copies:
        copy.start()
    find_spots(spots_ref, found_ref, picks_ref, here_ref[0], shifts, slots)
    for copy in copies:
        copy.wait()

    def one_head(head, carry):
        found = [spots_ref[head * PICKS + pick] for pick in range(PICKS)]
        spots = [head] + [jnp.where(spot >= 0, HEADS + spot, head) for spot in found]
        sums = [stats_of(held[spot, rows:, :], groups) for spot in spots]
        for pick, spot in enumerate(found):
            sums[1 + pick] = jnp.where(spot >= 0, sums[1 + pick], -jnp.inf)
        top = functools.reduce(jnp.maximum, sums)
        shares = [jnp.exp2(part - top) for part in sums]
        whole = functools.reduce(jnp.add, shares)
        sums_ref[head] = top + jnp.log2(whole)
        for group in range(groups):
            span = pl.ds(group * LANES, LANES)
            own = held[head, span, :].astype(jnp.float32)
            mixed = own
            for spot, share in zip(spots[1:], shares[1:]):
                weight = down_rows((share / whole)[group : group + 1, :])
                mixed = mixed + (held[spot, span, :].astype(jnp.float32) - own) * weight
            out_ref[head, span, :] = mixed
            result_ref[span, head_columns(head)] = mixed.astype(jnp.bfloat16)
        return carry

    lax.fori_loop(0, HEADS, one_head, 0, unroll=2)


def merge(here, picks, parts, places, shifts, slots):
    rows = parts[0].shape[1] - STAT_ROWS
    width = picks.shape[0]
    total = HEADS + len(shifts) * slots
    return call(
        functools.partial(merge_kernel, places=tuple(places), shifts=shifts, slots=slots),
        [SCALARS, SCALARS] + [pl.BlockSpec(memory_space=pl.ANY)] * len(parts),
        [
            jax.ShapeDtypeStruct((rows, HEADS * HD), jnp.bfloat16),
            jax.ShapeDtypeStruct((HEADS, rows, HD), jnp.float32),
            jax.ShapeDtypeStruct((HEADS, rows // LANES, LANES), jnp.float32),
        ],
        [IN_VMEM, IN_VMEM, IN_VMEM],
        [
            pltpu.VMEM((total, rows + STAT_ROWS, HD), jnp.bfloat16),
            pltpu.SMEM((PICKS * HEADS,), jnp.int32),
            pltpu.SMEM((width,), jnp.int32),
            pltpu.SemaphoreType.DMA((len(parts),)),
        ],
        flops=6 * HEADS * rows * HD,
        moved=2 * (HEADS * 2 + total) * rows * HD,
    )(here, picks, *parts)


def finish_kernel(here_ref, picks_ref, mixed_ref, sums_ref, *refs, shifts, slots):
    count = len(shifts)
    parts, out_ref, (heads_ref, held, sems) = refs[:count], refs[count + 1], refs[count + 2 :]
    groups = sums_ref.shape[1]
    rows = groups * LANES
    here = here_ref[0]
    for number, shift in enumerate(shifts):
        list_heads(heads_ref, number * slots, picks_ref, here, here - shift, slots)

    def slot_of(head, number):
        found = jnp.int32(-1)
        for slot in range(slots):
            found = jnp.where(heads_ref[number * slots + slot] == head, slot, found)
        return found

    def is_first(head, number):
        first = head >= 0
        for earlier in range(number):
            first = first & (slot_of(head, earlier) < 0)
        return first

    def patch(place):
        columns = head_columns(jnp.maximum(heads_ref[place], 0))
        return pltpu.make_async_copy(held.at[place], out_ref.at[:, columns], sems.at[place])

    places = [(number, number * slots + slot) for number in range(count) for slot in range(slots)]
    for number, place in places:
        head = heads_ref[place]

        @pl.when(is_first(head, number))
        def _():
            found = [slot_of(head, later) for later in range(number, count)]
            spots = [jnp.maximum(spot, 0) for spot in found]
            sums = [sums_ref[head]]
            for part, spot, safe in zip(parts[number:], found, spots):
                added = stats_of(part[safe, rows:, :], groups)
                sums.append(jnp.where(spot >= 0, added, -jnp.inf))
            top = functools.reduce(jnp.maximum, sums)
            shares = [jnp.exp2(part - top) for part in sums]
            whole = functools.reduce(jnp.add, shares)
            for group in range(groups):
                span = pl.ds(group * LANES, LANES)
                before = mixed_ref[head, span, :]
                mixed = before
                for part, spot, safe, share in zip(parts[number:], found, spots, shares[1:]):
                    new = jnp.where(spot >= 0, part[safe, span, :].astype(jnp.float32), 0.0)
                    weight = down_rows((share / whole)[group : group + 1, :])
                    mixed = mixed + (new - before) * weight
                held[place, span, :] = mixed.astype(jnp.bfloat16)
            patch(place).start()

    for number, place in places:

        @pl.when(is_first(heads_ref[place], number))
        def _():
            patch(place).wait()


def finish(here, picks, result, mixed, sums, parts, shifts, slots):
    rows = mixed.shape[1]
    total = len(shifts) * slots
    return pl.pallas_call(
        functools.partial(finish_kernel, shifts=shifts, slots=slots),
        in_specs=[SCALARS, SCALARS] + [IN_VMEM] * (2 + len(parts)) + [IN_HBM],
        out_specs=IN_HBM,
        out_shape=jax.ShapeDtypeStruct(result.shape, result.dtype),
        scratch_shapes=[
            pltpu.SMEM((total + 1,), jnp.int32),
            pltpu.VMEM((total, rows, HD), jnp.bfloat16),
            pltpu.SemaphoreType.DMA((total,)),
        ],
        input_output_aliases={4 + len(parts): 0},
        compiler_params=pltpu.CompilerParams(vmem_limit_bytes=VMEM_BYTES),
        cost_estimate=pl.CostEstimate(
            flops=2 * total * rows * HD, bytes_accessed=8 * total * rows * HD, transcendentals=0
        ),
    )(here, picks, mixed, sums, *parts, result)


def after(value, *earlier):
    return lax.optimization_barrier((value,) + earlier)[0]


def travelling_queries(queries, keys, values, picks):
    width = lax.axis_size("ctx")
    sections = lax.axis_size("pipe")
    slots = max(1, PICKS * HEADS // width)
    here = lax.axis_index("ctx").astype(jnp.int32).reshape(1)
    queries, keys, values = queries[0], keys[0], values[0]
    own_picks = picks[0].transpose(0, 2, 1)

    near_shifts = (2, width - 2)
    middle = width // 2
    far_shifts = [middle - 1, middle + 1, middle, 1, width - 1]
    final_shifts = tuple(far_shifts[2:])

    def up(value, shift):
        return lax.ppermute(value, "ctx", [(at, at + shift) for at in range(width - shift)])

    def down(value, shift):
        return lax.ppermute(value, "ctx", [(at, at - shift) for at in range(shift, width)])

    def up_and_on(value, shift):
        pairs = [
            (at * sections + section, (at + shift) * sections + (section + 1) % sections)
            for at in range(width - shift)
            for section in range(sections)
        ]
        return lax.ppermute(value, ("ctx", "pipe"), pairs)

    near_jobs = [(shift, 0, slots, True) for shift in near_shifts]
    near_sends = pack(here, own_picks, [keys, values], near_jobs, slots)
    near = [up(near_sends[0], near_shifts[0])]
    before = passed_along(own_picks, "pipe", 1)
    sends, now = {}, after(here, *near_sends)
    for shifts in (far_shifts[:2], far_shifts[2:]):
        jobs = [(shift, 0, slots, False) for shift in shifts]
        packed = pack(now, own_picks, [queries], jobs, slots)
        sends |= zip(shifts, packed)
        now = after(now, *packed)
    arrived, returned = {}, {}

    def ask_for(shift, *earlier):
        arrived[shift] = down(after(sends[shift], *earlier), shift)

    def work(token, shift, is_anchor=False):
        return attend(
            token, own_picks, keys, values, [arrived[shift]], ((shift, 0, slots),), slots, is_anchor
        )[0]

    three, five, four, one, seven = far_shifts
    ask_for(three, near_sends[0])
    ask_for(five, near_sends[0])
    own = own_part(after(now, before), queries, keys, values)
    own_back = passed_along(own, "pipe", 1)
    near.append(up(after(near_sends[1], own), near_shifts[1]))
    part_three = work(after(here, own, near[0]), three, is_anchor=True)
    returned[three] = up_and_on(part_three, three)
    part_five = work(after(here, part_three), five, is_anchor=True)
    returned[five] = up_and_on(part_five, five)
    ask_for(four, arrived[three], arrived[five], part_five, own_back, near[0])
    beside = near_part(after(here, part_five, own_back), own_picks, queries, near, near_shifts, slots)
    ask_for(seven, own_back, part_five, *near)
    ask_for(one, own_back, part_five, *near)
    beside_back = passed_along(beside, "pipe", 1)
    part_four = work(after(here, beside), four, is_anchor=True)
    returned[four] = up_and_on(part_four, four)
    part_seven = work(after(here, part_four, beside_back), seven)
    returned[seven] = up_and_on(part_seven, seven)
    part_one = work(after(here, part_seven), one)
    returned[one] = up_and_on(part_one, one)
    now = after(here, part_one)

    merged_shifts = near_shifts + (three, five)
    places = [HEADS + place * slots for place in (2, 3)]
    parts = [own_back, beside_back, returned[three], returned[five]]
    result, mixed, sums = merge(now, before, parts, [0, HEADS] + places, merged_shifts, slots)
    lasts = [returned[shift] for shift in final_shifts]
    return finish(now, before, result, mixed, sums, lasts, final_shifts, slots)[None]


def travelling_keys(queries, keys, values, picks):
    ctx_width = lax.axis_size("ctx")
    rank_here = lax.axis_index("ctx")
    slot_count = max(1, PICKS * HEADS // ctx_width)
    block_rows = queries.shape[1]
    score_scale = HD ** (-0.5)
    every_pick = picks[0].reshape(ctx_width, HEADS * PICKS)
    chosen = lax.dynamic_slice_in_dim(every_pick, rank_here, 1, 0)
    pick_order = request_table(chosen, lax.iota(jnp.int32, ctx_width), slot_count)[1]
    asked_table = request_table(every_pick, rank_here.reshape(1), slot_count)[0]
    asked_heads = asked_table[:, 0, :]
    safe_asked = jnp.maximum(asked_heads, 0)
    query_heads = queries[0].reshape(block_rows, HEADS, HD).transpose(1, 0, 2)
    key_heads = keys[0].reshape(block_rows, HEADS, HD).transpose(1, 0, 2)
    value_heads = values[0].reshape(block_rows, HEADS, HD).transpose(1, 0, 2)
    is_live = chosen[0] >= 0
    flat_slot = jnp.where(is_live, chosen[0] * slot_count + pick_order[0], 0)
    remote_mask = jnp.repeat(is_live.reshape(HEADS, PICKS), block_rows, axis=1)
    row_index = lax.iota(jnp.int32, block_rows)
    causal = row_index[:, None] >= row_index[None, :]

    def masked_scores(query_head, key_rows, mask_row):
        scores = lax.dot_general(
            query_head, key_rows, (((1,), (1,)), ((), ())), preferred_element_type=jnp.float32
        )
        allowed = jnp.concatenate(
            [causal, jnp.broadcast_to(mask_row[None, :], (block_rows, PICKS * block_rows))], axis=1
        )
        return jnp.where(allowed, scores * score_scale, -jnp.inf)

    def row_stats(scores):
        row_top = jnp.max(scores, axis=1)
        row_total = jnp.sum(jnp.exp(scores - row_top[:, None]), axis=1)
        return (row_top, row_total)

    def weighted(scores, row_top, row_total, value_rows):
        prob_rows = (jnp.exp(scores - row_top[:, None]) / row_total[:, None]).astype(jnp.bfloat16)
        return jnp.dot(prob_rows, value_rows, preferred_element_type=jnp.float32).astype(
            jnp.bfloat16
        )

    send_both = jnp.concatenate([key_heads, value_heads], axis=2)[safe_asked]
    got_slots = lax.all_to_all(send_both, "ctx", split_axis=0, concat_axis=0, tiled=True)
    last_width = 2 * HD
    flat_slots = got_slots.reshape(ctx_width * slot_count, block_rows, last_width)
    remote_both = flat_slots[flat_slot].reshape(HEADS, PICKS * block_rows, last_width)
    all_keys = jnp.concatenate([key_heads, remote_both[:, :, :HD]], axis=1)
    all_values = jnp.concatenate([value_heads, remote_both[:, :, HD:]], axis=1)

    def per_head(head_items):
        query_head, key_rows, value_rows, mask_row = head_items
        scores = masked_scores(query_head, key_rows, mask_row)
        row_top, row_total = row_stats(scores)
        return weighted(scores, row_top, row_total, value_rows)

    outputs = lax.map(per_head, (query_heads, all_keys, all_values, remote_mask))
    merged = outputs.transpose(1, 0, 2).reshape(1, block_rows, HEADS * HD)
    return passed_along(merged, "pipe", 1)


def per_device(queries, keys, values, picks):
    few_shifts = lax.axis_size("ctx") == 8
    run = travelling_queries if few_shifts else travelling_keys
    return run(queries, keys, values, picks)


def solution(mesh):
    placed = (
        P("pipe", "ctx", None),
        P("pipe", "ctx", None),
        P("pipe", "ctx", None),
        P("pipe", None, None, None),
    )
    return jax.shard_map(
        per_device, mesh=mesh, in_specs=placed, out_specs=P("pipe", "ctx", None), check_vma=False
    )
```
